32 devices in a mesh: lat: 4 (over y, core), lon: 8 (over z, x).
Axes of the slice: x: 2, y: 2, z: 4, core: 2. Of those that a mesh axis runs over, the one named last changes fastest.
Arguments:
- features: bfloat16 [64, 64, 1024], P(None, 'lat', 'lon'), may hold values from -6 to 6
- labels: int32 [64, 1024], P('lat', 'lon'), may hold values from 0 to 5
- tile_regions: int32 [4, 8, 6], P('lat', 'lon'), may hold values from 0 to 895, as said below
- bank_slot: int32 [896], replicated, may hold values from 0 to 895, as said below
- kernel_bank: bfloat16 [896, 32, 512], P('lon'), may hold values from -0.25 to 0.25
- in_factor: bfloat16 [32, 64], replicated, may hold values from -0.75 to 0.75
- tap_factor: bfloat16 [16, 25], replicated, may hold values from -1.25 to 1.25
- out_factor: bfloat16 [64, 32], replicated, may hold values from -1 to 1
- out_bias: float32 [64], replicated, may hold values from -4 to 4
Outputs:
- mixed: bfloat16 [64, 64, 1024], P(None, 'lat', 'lon')
The draws below stay inside these ranges and needn't reach their ends.
Inputs may be any that keep to these rules, and one draw needn't show every extreme that they name: `tile_regions`: each tile lists 6 distinct regions: exactly 2 held by the bank device of its own lon index, 2 by that of the next lon index and 2 by that of the previous one (lon indices wrap); within one latitude band the tiles ask each bank device for exactly 4 distinct regions in all. A permutation: region r is bank row bank_slot[r], held by the lon device bank_slot[r] // 112.
All inputs are finite; a program needn't handle non-finite values.
Results may differ from the reference program's by a relative error of at most 0.0056.
Values may be sent and summed in bfloat16 or wider, within the bound.
No kernel may reach another device: no remote copies, remote signals or barrier semaphores. Data moves between devices by JAX's collectives and lax.ppermute only.
A program may use at most 64 MiB of HBM per device.

```python
import jax
import jax.numpy as jnp
from jax import lax

CIN = 64
COUT = 64
RANK = 32
TAP_RANK = 16
KS = 5
TAPS = 25
REG_DEV = 112
REGIONS = 896
CAP = 2
CAPU = 4
MAXR = 6
LAT_DEV = 16
LON_DEV = 128
NLAT = 64
NLON = 1024
N_LAT = 4
N_LON = 8


def slot_plan(key):
    return jax.random.permutation(jax.random.fold_in(key, 11), REGIONS).astype(jnp.int32)


def draw_bank_slot(key, part):
    return slot_plan(key)


def draw_tile_regions(key, part):
    slot_of = slot_plan(key)
    region_of = jnp.argsort(slot_of, stable=True).astype(jnp.int32)
    pool_keys = jax.random.split(jax.random.fold_in(key, 12), N_LAT * N_LON)
    pools = jax.vmap(lambda single: jax.random.permutation(single, REG_DEV)[:CAPU])(pool_keys)
    pools = pools.reshape(N_LAT, N_LON, CAPU).astype(jnp.int32)
    next_pools = jnp.roll(pools, -1, axis=1)
    prev_pools = jnp.roll(pools, 1, axis=1)
    first = jax.random.randint(jax.random.fold_in(key, 13), (N_LAT, N_LON), 0, CAPU)
    stride = jax.random.randint(jax.random.fold_in(key, 14), (N_LAT, N_LON), 1, CAPU)
    second = (first + stride) % CAPU
    pair = jnp.stack([first, second], axis=-1).astype(jnp.int32)
    from_prev = jnp.take_along_axis(prev_pools, pair, axis=-1)
    local_rows = jnp.concatenate([pools[:, :, :CAP], next_pools[:, :, CAP:2 * CAP], from_prev], axis=-1)
    strips = jnp.arange(N_LON, dtype=jnp.int32)[None, :, None]
    offsets = jnp.array([0, 0, 1, 1, -1, -1], dtype=jnp.int32)[None, None, :]
    owners = (strips + offsets + N_LON) % N_LON
    slots = owners * REG_DEV + local_rows
    regions = region_of[slots]
    order_keys = jax.random.split(jax.random.fold_in(key, 15), N_LAT * N_LON)
    orders = jax.vmap(lambda single: jax.random.permutation(single, MAXR))(order_keys).reshape(N_LAT, N_LON, MAXR)
    return jnp.take_along_axis(regions, orders.astype(jnp.int32), axis=-1).astype(jnp.int32)


def with_ends(drawn, rng, smallest, top_value):
    dims = drawn.shape
    spot = [jax.random.randint(jax.random.fold_in(rng, axis), (), 0, dims[axis]) for axis in range(len(dims))]
    drawn = drawn.at[tuple(spot)].set(smallest)
    longest = dims.index(max(dims))
    spot[longest] = (spot[longest] + 1) % dims[longest]
    return drawn.at[tuple(spot)].set(top_value)


def block_scale(stream_key, shape, shards, low, top_value):
    level, own = 1.0, jax.random.fold_in(stream_key, 6)
    for position, shards_of in shards:
        heights = jnp.exp(jax.random.uniform(jax.random.fold_in(own, position), (shards_of,), jnp.float32, low / len(shards), top_value / len(shards)))
        level = level * jnp.repeat(heights, shape[position] // shards_of).reshape([-1 if axis == position else 1 for axis in range(len(shape))])
    return level


def normal_values(rng, extent, scale, limit, cuts=(), held_as=jnp.bfloat16):
    result = scale * jax.random.normal(rng, extent, jnp.float32)
    if cuts:
        result = result * block_scale(rng, extent, cuts, -0.22, 0.18)
    return jnp.clip(result, -limit, limit).astype(held_as)


def setup_inputs(seed: int = 0) -> dict:
    splits = jax.random.split(jax.random.key(seed), 10)
    return {
        "features": normal_values(splits[0], (CIN, NLAT, NLON), 1.0, 6.0, ((1, 4), (2, 8))),
        "labels": with_ends(jax.random.randint(splits[1], (NLAT, NLON), 0, MAXR), jax.random.fold_in(splits[1], 1), 0, MAXR - 1).astype(jnp.int32),
        "tile_regions": draw_tile_regions(jax.random.fold_in(splits[9], 71), 0),
        "bank_slot": draw_bank_slot(jax.random.fold_in(splits[9], 71), 0),
        "kernel_bank": normal_values(splits[4], (REGIONS, RANK, TAP_RANK * RANK), (TAP_RANK * RANK) ** -0.5, 0.25, ((0, 8),)),
        "in_factor": normal_values(splits[5], (RANK, CIN), CIN ** -0.5, 0.75),
        "tap_factor": normal_values(splits[6], (TAP_RANK, TAPS), TAPS ** -0.5, 1.25),
        "out_factor": normal_values(splits[7], (COUT, RANK), RANK ** -0.5, 1.0),
        "out_bias": normal_values(splits[8], (COUT,), 1.0, 4.0, (), jnp.float32),
    }


def tile_layer(window, tile_labels, region_cores, tap_factor, out_factor, out_bias):
    lat_len = window.shape[1] - KS + 1
    lon_len = window.shape[2] - KS + 1
    shifted = [window[:, row_off:row_off + lat_len, col_off:col_off + lon_len] for row_off in range(KS) for col_off in range(KS)]
    stacked = jnp.stack(shifted).reshape(KS * KS, -1)
    tapped = jnp.dot(tap_factor, stacked, preferred_element_type=jnp.float32).astype(jnp.bfloat16)
    tapped = tapped.reshape(-1, lat_len * lon_len)
    tucker_rank = region_cores.shape[1]
    list_len = region_cores.shape[0]
    flat_cores = region_cores.reshape(list_len * tucker_rank, -1)
    all_regions = jnp.dot(flat_cores, tapped, preferred_element_type=jnp.float32).reshape(list_len, tucker_rank, -1)
    onehot = (tile_labels.reshape(-1)[None, :] == jnp.arange(list_len, dtype=jnp.int32)[:, None]).astype(jnp.float32)
    hidden = jnp.sum(all_regions * onehot[:, None, :], axis=0).astype(jnp.bfloat16)
    output = jnp.dot(out_factor, hidden, preferred_element_type=jnp.float32) + out_bias[:, None]
    return jax.nn.silu(output).astype(jnp.bfloat16).reshape(-1, lat_len, lon_len)


def reference(features, labels, tile_regions, bank_slot, kernel_bank, in_factor, tap_factor, out_factor, out_bias):
    reach = KS // 2
    flat = features.reshape(CIN, -1)
    reduced = jnp.dot(in_factor, flat, preferred_element_type=jnp.float32).astype(jnp.bfloat16).reshape(RANK, NLAT, NLON)
    widened = jnp.concatenate([reduced[:, :, NLON - reach:], reduced, reduced[:, :, :reach]], axis=2)
    padded = jnp.pad(widened, ((0, 0), (reach, reach), (0, 0)))

    def one_tile(tile_index):
        band = (tile_index // N_LON).astype(jnp.int32)
        strip = (tile_index % N_LON).astype(jnp.int32)
        window = lax.dynamic_slice(padded, (jnp.int32(0), band * LAT_DEV, strip * LON_DEV), (RANK, LAT_DEV + 2 * reach, LON_DEV + 2 * reach))
        tile_labels = lax.dynamic_slice(labels, (band * LAT_DEV, strip * LON_DEV), (LAT_DEV, LON_DEV))
        region_cores = kernel_bank[bank_slot[tile_regions[band, strip]]]
        return tile_layer(window, tile_labels, region_cores, tap_factor, out_factor, out_bias)

    tiles = lax.map(one_tile, jnp.arange(N_LAT * N_LON, dtype=jnp.int32))
    tiles = tiles.reshape(N_LAT, N_LON, COUT, LAT_DEV, LON_DEV)
    return tiles.transpose(2, 0, 3, 1, 4).reshape(COUT, NLAT, NLON)
```

```python
import functools

import jax
import jax.numpy as jnp
from jax import lax
from jax.experimental import pallas as pl
from jax.experimental.pallas import tpu as pltpu
from jax.sharding import PartitionSpec as P

KS = 5
REACH = KS // 2
PER_OWNER = 2
LANES = 128
EDGE = 2 * REACH
F32 = jnp.float32
BF16 = jnp.bfloat16
VMEM = pl.BlockSpec(memory_space=pltpu.VMEM)
SMEM = pl.BlockSpec(memory_space=pltpu.SMEM)
HBM = pl.BlockSpec(memory_space=pl.ANY)
PARAMS = pltpu.CompilerParams(vmem_limit_bytes=58 * 1024 * 1024)


def swap_pairs(count, wrap):
    first = [(i, i ^ 1) for i in range(count)]
    second = []
    for i in range(1, count if wrap else count - 1, 2):
        second += [(i, (i + 1) % count), ((i + 1) % count, i)]
    return first, second


def lane_index(shape):
    return lax.broadcasted_iota(jnp.int32, shape, 1)


def reduce_kernel(
    lon_count, held, list_ref, slot_ref, feat_ref, in_ref, red_ref, pay_a_ref, pay_b_ref, meta_ref, rows_ref
):
    channels, lat_len, lon_len = feat_ref.shape
    rank = in_ref.shape[0]
    me = lax.axis_index("lon")
    even = (me % 2) == 0
    prev = lax.rem(me + lon_count - 1, lon_count)
    bases = (me * held, prev * held, lax.rem(me + 1, lon_count) * held)
    counts = [jnp.int32(0)] * 3
    places = [[jnp.int32(0)] * PER_OWNER for _ in range(3)]
    rows = [[jnp.int32(0)] * PER_OWNER for _ in range(3)]
    for i in range(list_ref.shape[2]):
        slot = slot_ref[list_ref[0, 0, i]]
        for group, base in enumerate(bases):
            local = slot - base
            hit = (local >= 0) & (local < held)
            for rank_here in range(PER_OWNER):
                take = hit & (counts[group] == rank_here)
                places[group][rank_here] = jnp.where(take, i, places[group][rank_here])
                rows[group][rank_here] = jnp.where(take, local, rows[group][rank_here])
            counts[group] = counts[group] + hit.astype(jnp.int32)
    for group in range(3):
        for rank_here in range(PER_OWNER):
            meta_ref[group * PER_OWNER + rank_here] = places[group][rank_here]
    for rank_here in range(PER_OWNER):
        meta_ref[3 * PER_OWNER + rank_here] = rows[0][rank_here]

    rows_ref[...] = feat_ref[...].astype(F32).reshape(channels * lat_len, lon_len)
    cells = jnp.concatenate(
        [rows_ref[pl.ds(p, channels, stride=lat_len), :].astype(BF16) for p in range(lat_len)], axis=1
    )
    reduced = jnp.dot(in_ref[...], cells, preferred_element_type=F32)
    red_ref[...] = reduced.astype(BF16)
    lane = lane_index((rank, LANES))
    pack = jnp.zeros((rank, LANES), F32)
    for p in range(lat_len):
        turned = pltpu.roll(reduced[:, p * lon_len : (p + 1) * lon_len], EDGE * p + REACH, 1)
        pack = jnp.where(lane // EDGE == p, turned, pack)
    for out_ref, wanted in ((pay_a_ref, even), (pay_b_ref, jnp.logical_not(even))):
        load = pack
        for rank_here in range(PER_OWNER):
            row = jnp.where(wanted, rows[2][rank_here], rows[1][rank_here]).astype(F32)
            load = jnp.where(lane == EDGE * lat_len + rank_here, row, load)
        out_ref[...] = load.astype(BF16)


def pick_kernel(
    lat_len, got_a_ref, got_b_ref, red_ref, bank_ref, core_a_ref, core_b_ref, edge_ref, row_a_ref, row_b_ref, sems
):
    lon_len = red_ref.shape[1] // lat_len
    rank = red_ref.shape[0]
    copies = []
    lane = lane_index((1, LANES))
    for side, (got_ref, core_ref) in enumerate(((got_a_ref, core_a_ref), (got_b_ref, core_b_ref))):
        head = got_ref[...].astype(F32)[0:1, :]
        for rank_here in range(PER_OWNER):
            row = jnp.sum(jnp.where(lane == EDGE * lat_len + rank_here, head, 0.0)).astype(jnp.int32)
            copy = pltpu.make_async_copy(bank_ref.at[row], core_ref.at[rank_here], sems.at[side, rank_here])
            copy.start()
            copies.append(copy)
    even_lon = (lax.axis_index("lon") % 2) == 0
    even_lat = (lax.axis_index("lat") % 2) == 0
    lane = lane_index((rank, LANES))
    got_a = got_a_ref[...].astype(F32)
    got_b = got_b_ref[...].astype(F32)
    from_prev = lane % EDGE < REACH
    edges = jnp.where(from_prev == even_lon, got_b, got_a).astype(BF16)
    edge_ref[...] = edges
    head = red_ref[:, : REACH * lon_len].astype(F32)
    tail = red_ref[:, (lat_len - REACH) * lon_len :].astype(F32)
    row_a_ref[:, : REACH * lon_len] = jnp.where(even_lat, tail, head).astype(BF16)
    row_b_ref[:, : REACH * lon_len] = jnp.where(even_lat, head, tail).astype(BF16)
    row_a_ref[:, REACH * lon_len :] = edges
    row_b_ref[:, REACH * lon_len :] = edges
    for copy in copies:
        copy.wait()


def tile_kernel(
    meta_ref,
    red_ref,
    edge_ref,
    row_a_ref,
    row_b_ref,
    core_a_ref,
    core_b_ref,
    bank_ref,
    labels_ref,
    tap_ref,
    out_factor_ref,
    bias_ref,
    out_ref,
    own_ref,
    stack_ref,
    mixed_ref,
    sems,
):
    lat_len, lon_len = labels_ref.shape
    rank = red_ref.shape[0]
    half = rank // 2
    tap_rank, taps = tap_ref.shape
    copies = []
    for rank_here in range(PER_OWNER):
        row = meta_ref[3 * PER_OWNER + rank_here]
        copy = pltpu.make_async_copy(bank_ref.at[row], own_ref.at[rank_here], sems.at[rank_here])
        copy.start()
        copies.append(copy)

    even_lat = (lax.axis_index("lat") % 2) == 0
    even_lon = (lax.axis_index("lon") % 2) == 0
    lane = lane_index((rank, LANES))
    row_a = row_a_ref[...].astype(F32)
    row_b = row_b_ref[...].astype(F32)
    above = jnp.where(even_lat, row_b, row_a)
    below = jnp.where(even_lat, row_a, row_b)
    inner_edges = edge_ref[...].astype(F32)
    for w in range(lat_len + KS - 1):
        p = w - REACH
        if p < 0:
            row = above[:, w * lon_len : (w + 1) * lon_len]
            edges, place = above[:, REACH * lon_len :], lat_len + p
        elif p >= lat_len:
            row = below[:, (p - lat_len) * lon_len : (p - lat_len + 1) * lon_len]
            edges, place = below[:, REACH * lon_len :], p - lat_len
        else:
            row = red_ref[:, p * lon_len : (p + 1) * lon_len].astype(F32)
            edges, place = inner_edges, p
        edges = pltpu.roll(edges, (LANES - REACH - EDGE * place) % LANES, 1)
        for col_off in range(KS):
            shift = REACH - col_off
            if shift > 0:
                moved = pltpu.roll(jnp.where(lane >= lon_len - shift, edges, row), shift, 1)
            elif shift < 0:
                moved = pltpu.roll(jnp.where(lane < -shift, edges, row), lon_len + shift, 1)
            else:
                moved = row
            moved = moved.astype(BF16)
            for row_off in range(KS):
                q = w - row_off
                if 0 <= q < lat_len:
                    k = row_off * KS + col_off
                    for h in range(2):
                        stack_ref[h, k * half : (k + 1) * half, q * lon_len : (q + 1) * lon_len] = moved[
                            h * half : (h + 1) * half
                        ]

    wide_rows, wide_cols = tap_rank * half, taps * half
    spread = (
        lax.broadcasted_iota(jnp.int32, (wide_rows, tap_rank), 0) // half == lane_index((wide_rows, tap_rank))
    ).astype(BF16)
    repeat = (
        lax.broadcasted_iota(jnp.int32, (taps, wide_cols), 0) == lane_index((taps, wide_cols)) // half
    ).astype(BF16)
    tall = jnp.dot(spread, tap_ref[...], preferred_element_type=F32).astype(BF16)
    wide = jnp.dot(tall, repeat, preferred_element_type=F32)
    same = (
        lax.broadcasted_iota(jnp.int32, (wide_rows, wide_cols), 0) % half
        == lane_index((wide_rows, wide_cols)) % half
    )
    weights = jnp.where(same, wide, 0.0).astype(BF16)

    out_channels = out_factor_ref.shape[0]
    square = (out_channels, out_channels)
    bias = jnp.sum(
        jnp.where(lax.broadcasted_iota(jnp.int32, square, 0) == lane_index(square), bias_ref[...], 0.0),
        axis=1,
        keepdims=True,
    )
    for copy in copies:
        copy.wait()
    core_a = core_a_ref[...].reshape(PER_OWNER * rank, -1)
    core_b = core_b_ref[...].reshape(PER_OWNER * rank, -1)
    cores = jnp.concatenate([own_ref[...].reshape(PER_OWNER * rank, -1), core_a, core_b], axis=0)
    places = []
    for rank_here in range(PER_OWNER):
        places.append(meta_ref[rank_here])
    for flip in (False, True):
        for rank_here in range(PER_OWNER):
            prev, following = meta_ref[PER_OWNER + rank_here], meta_ref[2 * PER_OWNER + rank_here]
            if flip:
                prev, following = following, prev
            places.append(jnp.where(even_lon, following, prev))

    step = 2
    for start in range(0, lat_len, step):
        span = slice(start * lon_len, (start + step) * lon_len)
        parts = [
            jnp.dot(weights, stack_ref[h, :, span], preferred_element_type=F32)
            .astype(BF16)
            .reshape(tap_rank, 1, half, step * lon_len)
            for h in range(2)
        ]
        tapped = jnp.concatenate(parts, axis=1).reshape(tap_rank * rank, step * lon_len)
        every = jnp.dot(cores, tapped, preferred_element_type=F32)
        chosen = jnp.concatenate([labels_ref[start + r : start + r + 1, :] for r in range(step)], axis=1)
        hidden = jnp.zeros((rank, step * lon_len), F32)
        for index, place in enumerate(places):
            hidden = jnp.where(chosen == place, every[index * rank : (index + 1) * rank], hidden)
        output = jnp.dot(out_factor_ref[...], hidden.astype(BF16), preferred_element_type=F32) + bias
        mixed = output / (1.0 + jnp.exp(-output))
        for r in range(step):
            mixed_ref[pl.ds(start + r, out_channels, stride=lat_len), :] = mixed[:, r * lon_len : (r + 1) * lon_len]
    out_ref[...] = mixed_ref[...].reshape(out_channels, lat_len, lon_len).astype(BF16)


def on_device(
    features, labels, tile_regions, bank_slot, kernel_bank, in_factor, tap_factor, out_factor, out_bias
):
    channels, lat_len, lon_len = features.shape
    rank = in_factor.shape[0]
    held, core_rows, core_cols = kernel_bank.shape
    cells = lat_len * lon_len
    lon_first, lon_second = swap_pairs(lax.axis_size("lon"), True)
    lat_first, lat_second = swap_pairs(lax.axis_size("lat"), False)
    edge_shape = jax.ShapeDtypeStruct((rank, LANES), BF16)
    reduced, pay_a, pay_b, meta = pl.pallas_call(
        functools.partial(reduce_kernel, lax.axis_size("lon"), held),
        out_shape=(
            jax.ShapeDtypeStruct((rank, cells), BF16),
            edge_shape,
            edge_shape,
            jax.ShapeDtypeStruct((4 * PER_OWNER,), jnp.int32),
        ),
        in_specs=[SMEM, SMEM, VMEM, VMEM],
        out_specs=(VMEM, VMEM, VMEM, SMEM),
        scratch_shapes=[pltpu.VMEM((channels * lat_len, lon_len), F32)],
        compiler_params=PARAMS,
    )(tile_regions, bank_slot, features, in_factor)
    got_b = lax.ppermute(pay_b, "lon", lon_second)
    got_a = lax.ppermute(pay_a, "lon", lon_first)
    core_shape = jax.ShapeDtypeStruct((PER_OWNER, core_rows, core_cols), BF16)
    row_shape = jax.ShapeDtypeStruct((rank, REACH * lon_len + LANES), BF16)
    core_a, core_b, edges, row_a, row_b = pl.pallas_call(
        functools.partial(pick_kernel, lat_len),
        out_shape=(core_shape, core_shape, edge_shape, row_shape, row_shape),
        in_specs=[VMEM, VMEM, VMEM, HBM],
        out_specs=(VMEM,) * 5,
        scratch_shapes=[pltpu.SemaphoreType.DMA((2, PER_OWNER))],
        compiler_params=PARAMS,
    )(got_a, got_b, reduced, kernel_bank)
    core_b = lax.ppermute(core_b, "lon", lon_second)
    core_a = lax.ppermute(core_a, "lon", lon_first)
    row_a = lax.ppermute(row_a, "lat", lat_first)
    row_b = lax.ppermute(row_b, "lat", lat_second)
    return pl.pallas_call(
        tile_kernel,
        out_shape=jax.ShapeDtypeStruct((out_factor.shape[0], lat_len, lon_len), BF16),
        in_specs=[SMEM] + [VMEM] * 6 + [HBM] + [VMEM] * 4,
        out_specs=VMEM,
        scratch_shapes=[
            pltpu.VMEM((PER_OWNER, core_rows, core_cols), BF16),
            pltpu.VMEM((2, tap_factor.shape[1] * rank // 2, cells), BF16),
            pltpu.VMEM((out_factor.shape[0] * lat_len, lon_len), F32),
            pltpu.SemaphoreType.DMA((PER_OWNER,)),
        ],
        compiler_params=PARAMS,
    )(
        meta,
        reduced,
        edges,
        row_a,
        row_b,
        core_a,
        core_b,
        kernel_bank,
        labels,
        tap_factor,
        out_factor,
        out_bias.reshape(1, -1),
    )


def solution(mesh):
    placed = (
        P(None, "lat", "lon"),
        P("lat", "lon"),
        P("lat", "lon", None),
        P(),
        P("lon", None, None),
        P(),
        P(),
        P(),
        P(),
    )
    return jax.shard_map(
        on_device, mesh=mesh, in_specs=placed, out_specs=P(None, "lat", "lon"), check_vma=False
    )
```

```python
import functools

import jax
import jax.numpy as jnp
from jax import lax
from jax.experimental import pallas as pl
from jax.experimental.pallas import tpu as pltpu
from jax.sharding import PartitionSpec as P

KS = 5
REACH = KS // 2
PER_OWNER = 2
LANES = 128
EDGE = 2 * REACH
F32 = jnp.float32
BF16 = jnp.bfloat16
VMEM = pl.BlockSpec(memory_space=pltpu.VMEM)
SMEM = pl.BlockSpec(memory_space=pltpu.SMEM)
HBM = pl.BlockSpec(memory_space=pltpu.HBM)
PARAMS = pltpu.CompilerParams(vmem_limit_bytes=24 * 1024 * 1024)


def swap_pairs(count, wrap):
    first = [(i, i ^ 1) for i in range(count)]
    second = []
    for i in range(1, count if wrap else count - 1, 2):
        second += [(i, (i + 1) % count), ((i + 1) % count, i)]
    return first, second


def lane_index(shape):
    return lax.broadcasted_iota(jnp.int32, shape, 1)


def reduce_kernel(
    lon_count, held, list_ref, slot_ref, feat_ref, in_ref, red_ref, pay_a_ref, pay_b_ref, meta_ref, rows_ref
):
    channels, lat_len, lon_len = feat_ref.shape
    rank = in_ref.shape[0]
    me = lax.axis_index("lon")
    even = (me % 2) == 0
    prev = lax.rem(me + lon_count - 1, lon_count)
    bases = (me * held, prev * held, lax.rem(me + 1, lon_count) * held)
    counts = [jnp.int32(0)] * 3
    places = [[jnp.int32(0)] * PER_OWNER for _ in range(3)]
    rows = [[jnp.int32(0)] * PER_OWNER for _ in range(3)]
    for i in range(list_ref.shape[2]):
        slot = slot_ref[list_ref[0, 0, i]]
        for group, base in enumerate(bases):
            local = slot - base
            hit = (local >= 0) & (local < held)
            for rank_here in range(PER_OWNER):
                take = hit & (counts[group] == rank_here)
                places[group][rank_here] = jnp.where(take, i, places[group][rank_here])
                rows[group][rank_here] = jnp.where(take, local, rows[group][rank_here])
            counts[group] = counts[group] + hit.astype(jnp.int32)
    for group in range(3):
        for rank_here in range(PER_OWNER):
            meta_ref[group * PER_OWNER + rank_here] = places[group][rank_here]
    for rank_here in range(PER_OWNER):
        meta_ref[3 * PER_OWNER + rank_here] = rows[0][rank_here]

    rows_ref[...] = feat_ref[...].astype(F32).reshape(channels * lat_len, lon_len)
    cells = jnp.concatenate(
        [rows_ref[pl.ds(p, channels, stride=lat_len), :].astype(BF16) for p in range(lat_len)], axis=1
    )
    reduced = jnp.dot(in_ref[...], cells, preferred_element_type=F32)
    red_ref[...] = reduced.astype(BF16)
    lane = lane_index((rank, LANES))
    pack = jnp.zeros((rank, LANES), F32)
    for p in range(lat_len):
        turned = pltpu.roll(reduced[:, p * lon_len : (p + 1) * lon_len], EDGE * p + REACH, 1)
        pack = jnp.where(lane // EDGE == p, turned, pack)
    for out_ref, wanted in ((pay_a_ref, even), (pay_b_ref, jnp.logical_not(even))):
        load = pack
        for rank_here in range(PER_OWNER):
            row = jnp.where(wanted, rows[2][rank_here], rows[1][rank_here]).astype(F32)
            load = jnp.where(lane == EDGE * lat_len + rank_here, row, load)
        out_ref[...] = load.astype(BF16)


def pick_kernel(
    lat_len,
    meta_ref,
    got_b_ref,
    got_a_ref,
    red_ref,
    bank_ref,
    core_b_ref,
    core_a_ref,
    own_ref,
    edge_ref,
    row_a_ref,
    row_b_ref,
    sems,
):
    lon_len = red_ref.shape[1] // lat_len
    rank = red_ref.shape[0]
    copies = []
    lane = lane_index((1, LANES))
    for side, (got_ref, core_ref) in enumerate(((got_b_ref, core_b_ref), (got_a_ref, core_a_ref))):
        head = got_ref[...].astype(F32)[0:1, :]
        for rank_here in range(PER_OWNER):
            row = jnp.sum(jnp.where(lane == EDGE * lat_len + rank_here, head, 0.0)).astype(jnp.int32)
            copy = pltpu.make_async_copy(bank_ref.at[row], core_ref.at[rank_here], sems.at[side, rank_here])
            copy.start()
            copies.append(copy)
    for rank_here in range(PER_OWNER):
        row = meta_ref[3 * PER_OWNER + rank_here]
        copy = pltpu.make_async_copy(bank_ref.at[row], own_ref.at[rank_here], sems.at[2, rank_here])
        copy.start()
        copies.append(copy)
    even_lon = (lax.axis_index("lon") % 2) == 0
    even_lat = (lax.axis_index("lat") % 2) == 0
    lane = lane_index((rank, LANES))
    got_a = got_a_ref[...].astype(F32)
    got_b = got_b_ref[...].astype(F32)
    from_prev = lane % EDGE < REACH
    edges = jnp.where(from_prev == even_lon, got_b, got_a).astype(BF16)
    edge_ref[...] = edges
    head = red_ref[:, : REACH * lon_len].astype(F32)
    tail = red_ref[:, (lat_len - REACH) * lon_len :].astype(F32)
    row_a_ref[:, : REACH * lon_len] = jnp.where(even_lat, tail, head).astype(BF16)
    row_b_ref[:, : REACH * lon_len] = jnp.where(even_lat, head, tail).astype(BF16)
    row_a_ref[:, REACH * lon_len :] = edges
    row_b_ref[:, REACH * lon_len :] = edges
    for copy in copies:
        copy.wait()


def stencil_kernel(red_ref, edge_ref, row_a_ref, row_b_ref, tap_ref, tapped_ref, stack_ref):
    rank = red_ref.shape[0]
    half = rank // 2
    tap_rank, taps = tap_ref.shape
    lon_len = (row_a_ref.shape[1] - LANES) // REACH
    lat_len = red_ref.shape[1] // lon_len
    even_lat = (lax.axis_index("lat") % 2) == 0
    lane = lane_index((rank, LANES))
    row_a = row_a_ref[...].astype(F32)
    row_b = row_b_ref[...].astype(F32)
    above = jnp.where(even_lat, row_b, row_a)
    below = jnp.where(even_lat, row_a, row_b)
    inner_edges = edge_ref[...].astype(F32)
    for w in range(lat_len + KS - 1):
        p = w - REACH
        if p < 0:
            row = above[:, w * lon_len : (w + 1) * lon_len]
            edges, place = above[:, REACH * lon_len :], lat_len + p
        elif p >= lat_len:
            row = below[:, (p - lat_len) * lon_len : (p - lat_len + 1) * lon_len]
            edges, place = below[:, REACH * lon_len :], p - lat_len
        else:
            row = red_ref[:, p * lon_len : (p + 1) * lon_len].astype(F32)
            edges, place = inner_edges, p
        edges = pltpu.roll(edges, (LANES - REACH - EDGE * place) % LANES, 1)
        for col_off in range(KS):
            shift = REACH - col_off
            if shift > 0:
                moved = pltpu.roll(jnp.where(lane >= lon_len - shift, edges, row), shift, 1)
            elif shift < 0:
                moved = pltpu.roll(jnp.where(lane < -shift, edges, row), lon_len + shift, 1)
            else:
                moved = row
            moved = moved.astype(BF16)
            for row_off in range(KS):
                q = w - row_off
                if 0 <= q < lat_len:
                    k = row_off * KS + col_off
                    for h in range(2):
                        stack_ref[h, k * half : (k + 1) * half, q * lon_len : (q + 1) * lon_len] = moved[
                            h * half : (h + 1) * half
                        ]

    wide_rows, wide_cols = tap_rank * half, taps * half
    spread = (
        lax.broadcasted_iota(jnp.int32, (wide_rows, tap_rank), 0) // half == lane_index((wide_rows, tap_rank))
    ).astype(BF16)
    repeat = (
        lax.broadcasted_iota(jnp.int32, (taps, wide_cols), 0) == lane_index((taps, wide_cols)) // half
    ).astype(BF16)
    tall = jnp.dot(spread, tap_ref[...], preferred_element_type=F32).astype(BF16)
    wide = jnp.dot(tall, repeat, preferred_element_type=F32)
    same = (
        lax.broadcasted_iota(jnp.int32, (wide_rows, wide_cols), 0) % half
        == lane_index((wide_rows, wide_cols)) % half
    )
    weights = jnp.where(same, wide, 0.0).astype(BF16)
    step = 2
    for start in range(0, lat_len, step):
        span = slice(start * lon_len, (start + step) * lon_len)
        parts = [
            jnp.dot(weights, stack_ref[h, :, span], preferred_element_type=F32)
            .astype(BF16)
            .reshape(tap_rank, 1, half, step * lon_len)
            for h in range(2)
        ]
        tapped_ref[:, span] = jnp.concatenate(parts, axis=1).reshape(tap_rank * rank, step * lon_len)


def mix_kernel(
    meta_ref, tapped_ref, core_a_ref, core_b_ref, own_ref, labels_ref, out_factor_ref, bias_ref, out_ref, mixed_ref
):
    lat_len, lon_len = labels_ref.shape
    rank, out_channels = out_factor_ref.shape
    even_lon = (lax.axis_index("lon") % 2) == 0
    square = (out_channels, out_channels)
    bias = jnp.sum(
        jnp.where(lax.broadcasted_iota(jnp.int32, square, 0) == lane_index(square), bias_ref[...], 0.0),
        axis=1,
        keepdims=True,
    )
    cores = jnp.concatenate(
        [ref[...].reshape(PER_OWNER * rank, -1) for ref in (own_ref, core_a_ref, core_b_ref)], axis=0
    )
    places = [meta_ref[rank_here] for rank_here in range(PER_OWNER)]
    for flip in (False, True):
        for rank_here in range(PER_OWNER):
            prev, following = meta_ref[PER_OWNER + rank_here], meta_ref[2 * PER_OWNER + rank_here]
            if flip:
                prev, following = following, prev
            places.append(jnp.where(even_lon, following, prev))
    step = 2
    for start in range(0, lat_len, step):
        span = slice(start * lon_len, (start + step) * lon_len)
        every = jnp.dot(cores, tapped_ref[:, span], preferred_element_type=F32)
        chosen = jnp.concatenate([labels_ref[start + r : start + r + 1, :] for r in range(step)], axis=1)
        hidden = jnp.zeros((rank, step * lon_len), F32)
        for index, place in enumerate(places):
            hidden = jnp.where(chosen == place, every[index * rank : (index + 1) * rank], hidden)
        output = (
            lax.dot_general(
                out_factor_ref[...], hidden.astype(BF16), (((0,), (0,)), ((), ())), preferred_element_type=F32
            )
            + bias
        )
        mixed = output / (1.0 + jnp.exp(-output))
        for r in range(step):
            mixed_ref[pl.ds(start + r, out_channels, stride=lat_len), :] = mixed[:, r * lon_len : (r + 1) * lon_len]
    out_ref[...] = mixed_ref[...].reshape(out_channels, lat_len, lon_len).astype(BF16)


def on_device(
    features, labels, tile_regions, bank_slot, kernel_bank, in_factor, tap_factor, out_factor, out_bias
):
    channels, lat_len, lon_len = features.shape
    rank = in_factor.shape[0]
    held, core_rows, core_cols = kernel_bank.shape
    cells = lat_len * lon_len
    lon_first, lon_second = swap_pairs(lax.axis_size("lon"), True)
    lat_first, lat_second = swap_pairs(lax.axis_size("lat"), False)
    edge_shape = jax.ShapeDtypeStruct((rank, LANES), BF16)
    reduced, pay_a, pay_b, meta = pl.pallas_call(
        functools.partial(reduce_kernel, lax.axis_size("lon"), held),
        out_shape=(
            jax.ShapeDtypeStruct((rank, cells), BF16),
            edge_shape,
            edge_shape,
            jax.ShapeDtypeStruct((4 * PER_OWNER,), jnp.int32),
        ),
        in_specs=[SMEM, SMEM, VMEM, VMEM],
        out_specs=(VMEM, VMEM, VMEM, SMEM),
        scratch_shapes=[pltpu.VMEM((channels * lat_len, lon_len), F32)],
        compiler_params=PARAMS,
    )(tile_regions, bank_slot, features, in_factor)
    got_b = lax.ppermute(pay_b, "lon", lon_second)
    got_a = lax.ppermute(pay_a, "lon", lon_first)
    core_shape = jax.ShapeDtypeStruct((PER_OWNER, core_rows, core_cols), BF16)
    row_shape = jax.ShapeDtypeStruct((rank, REACH * lon_len + LANES), BF16)
    core_b, core_a, own, edges, row_a, row_b = pl.pallas_call(
        functools.partial(pick_kernel, lat_len),
        out_shape=(core_shape, core_shape, core_shape, edge_shape, row_shape, row_shape),
        in_specs=[SMEM, VMEM, VMEM, VMEM, HBM],
        out_specs=(VMEM,) * 6,
        scratch_shapes=[pltpu.SemaphoreType.DMA((3, PER_OWNER))],
        compiler_params=PARAMS,
    )(meta, got_b, got_a, reduced, pltpu.with_memory_space_constraint(kernel_bank, pltpu.HBM))
    core_b = lax.ppermute(core_b, "lon", lon_second)
    core_a = lax.ppermute(core_a, "lon", lon_first)
    row_a = lax.ppermute(row_a, "lat", lat_first)
    row_b = lax.ppermute(row_b, "lat", lat_second)
    tap_rank, taps = tap_factor.shape
    tapped = pl.pallas_call(
        stencil_kernel,
        out_shape=jax.ShapeDtypeStruct((tap_rank * rank, cells), BF16),
        in_specs=[VMEM] * 5,
        out_specs=VMEM,
        scratch_shapes=[pltpu.VMEM((2, taps * rank // 2, cells), BF16)],
        compiler_params=PARAMS,
        cost_estimate=pl.CostEstimate(
            flops=2 * 16 * taps * tap_rank * rank * cells, bytes_accessed=4 * tap_rank * rank * cells, transcendentals=0
        ),
    )(reduced, edges, row_a, row_b, tap_factor)
    return pl.pallas_call(
        mix_kernel,
        out_shape=jax.ShapeDtypeStruct((out_factor.shape[0], lat_len, lon_len), BF16),
        in_specs=[SMEM] + [VMEM] * 7,
        out_specs=VMEM,
        scratch_shapes=[pltpu.VMEM((out_factor.shape[0] * lat_len, lon_len), F32)],
        compiler_params=PARAMS,
    )(meta, tapped, core_a, core_b, own, labels, out_factor.T, out_bias.reshape(1, -1))


def solution(mesh):
    placed = (
        P(None, "lat", "lon"),
        P("lat", "lon"),
        P("lat", "lon", None),
        P(),
        P("lon", None, None),
        P(),
        P(),
        P(),
        P(),
    )
    return jax.shard_map(
        on_device, mesh=mesh, in_specs=placed, out_specs=P(None, "lat", "lon"), check_vma=False
    )
```

```python
import functools

import jax
import jax.numpy as jnp
from jax import lax
from jax.experimental import pallas as pl
from jax.experimental.pallas import tpu as pltpu
from jax.sharding import PartitionSpec as P

KS = 5
REACH = KS // 2
PER_OWNER = 2
LANES = 128
EDGE = 2 * REACH
GROUP = 8
F32 = jnp.float32
BF16 = jnp.bfloat16
VMEM = pl.BlockSpec(memory_space=pltpu.VMEM)
SMEM = pl.BlockSpec(memory_space=pltpu.SMEM)
HBM = pl.BlockSpec(memory_space=pltpu.HBM)
PARAMS = pltpu.CompilerParams(vmem_limit_bytes=24 * 1024 * 1024)


def swap_pairs(count, wrap):
    first = [(i, i ^ 1) for i in range(count)]
    second = [] if wrap else [(0, 0), (count - 1, count - 1)]
    for i in range(1, count if wrap else count - 1, 2):
        second += [(i, (i + 1) % count), ((i + 1) % count, i)]
    return first, second


def in_hbm(array):
    return pltpu.with_memory_space_constraint(array, pltpu.HBM)


def lane_index(shape):
    return lax.broadcasted_iota(jnp.int32, shape, 1)


def start_copies(pairs, sems):
    copies = [pltpu.make_async_copy(source, target, sems.at[i]) for i, (source, target) in enumerate(pairs)]
    for copy in copies:
        copy.start()
    return copies


def find_rows(list_ref, slot_ref, lon_count, held):
    me = lax.axis_index("lon")
    owners = (me, lax.rem(me + lon_count - 1, lon_count), lax.rem(me + 1, lon_count))
    counts = [jnp.int32(0)] * 3
    places = [[jnp.int32(0)] * PER_OWNER for _ in range(3)]
    rows = [[jnp.int32(0)] * PER_OWNER for _ in range(3)]
    for i in range(list_ref.shape[2]):
        slot = slot_ref[list_ref[0, 0, i]]
        for group, owner in enumerate(owners):
            local = slot - owner * held
            hit = (local >= 0) & (local < held)
            for nth in range(PER_OWNER):
                take = hit & (counts[group] == nth)
                places[group][nth] = jnp.where(take, i, places[group][nth])
                rows[group][nth] = jnp.where(take, local, rows[group][nth])
            counts[group] = counts[group] + hit.astype(jnp.int32)
    return places, rows


def reduce_kernel(
    lon_count,
    held,
    list_hbm,
    slot_hbm,
    feat_hbm,
    in_hbm,
    red_ref,
    pay_a_ref,
    pay_b_ref,
    list_ref,
    slot_ref,
    feat_ref,
    in_ref,
    rows_ref,
    sems,
):
    channels, lat_len, lon_len = feat_ref.shape
    rank = in_ref.shape[0]
    pairs = ((feat_hbm, feat_ref), (slot_hbm, slot_ref), (list_hbm, list_ref), (in_hbm, in_ref))
    for copy in start_copies(pairs, sems):
        copy.wait()
    rows_ref[...] = feat_ref[...].astype(F32).reshape(channels * lat_len, lon_len)
    cells = jnp.concatenate(
        [rows_ref[pl.ds(p, channels, stride=lat_len), :].astype(BF16) for p in range(lat_len)], axis=1
    )
    reduced = jnp.dot(in_ref[...], cells, preferred_element_type=F32)
    red_ref[...] = reduced.astype(BF16)
    _, rows = find_rows(list_ref, slot_ref, lon_count, held)
    even = (lax.axis_index("lon") % 2) == 0
    lane = lane_index((rank, LANES))
    pack = jnp.zeros((rank, LANES), F32)
    for p in range(lat_len):
        turned = pltpu.roll(reduced[:, p * lon_len : (p + 1) * lon_len], EDGE * p + REACH, 1)
        pack = jnp.where(lane // EDGE == p, turned, pack)
    for out_ref, wanted in ((pay_a_ref, even), (pay_b_ref, jnp.logical_not(even))):
        load = pack
        for nth in range(PER_OWNER):
            row = jnp.where(wanted, rows[2][nth], rows[1][nth]).astype(F32)
            load = jnp.where(lane == EDGE * lat_len + nth, row, load)
        out_ref[...] = load.astype(BF16)


def prepare_kernel(
    lon_count,
    lat_len,
    red_hbm,
    list_hbm,
    slot_hbm,
    bank_hbm,
    labels_hbm,
    tap_hbm,
    out_factor_hbm,
    bias_hbm,
    bank_ref,
    own_ref,
    position_ref,
    weights_ref,
    mixer_ref,
    offset_ref,
    list_ref,
    slot_ref,
    labels_ref,
    tap_ref,
    out_factor_ref,
    bias_ref,
    sems,
):
    held = bank_hbm.shape[0]
    small = (
        (list_hbm, list_ref),
        (slot_hbm, slot_ref),
        (labels_hbm, labels_ref),
        (tap_hbm, tap_ref),
        (out_factor_hbm, out_factor_ref),
        (bias_hbm, bias_ref),
    )
    copies = start_copies(small, sems)
    copy = pltpu.make_async_copy(bank_hbm, bank_ref, sems.at[len(small)])
    copy.start()
    for other in copies:
        other.wait()
    places, rows = find_rows(list_ref, slot_ref, lon_count, held)
    even = (lax.axis_index("lon") % 2) == 0
    order = list(places[0])
    order += [jnp.where(even, places[2][nth], places[1][nth]) for nth in range(PER_OWNER)]
    order += [jnp.where(even, places[1][nth], places[2][nth]) for nth in range(PER_OWNER)]
    labels = labels_ref[...]
    position = jnp.zeros(labels.shape, jnp.int32)
    for index, place in enumerate(order):
        position = jnp.where(labels == place, index, position)
    position_ref[...] = position

    rank, out_channels = out_factor_ref.shape
    half = rank // 2
    tap_rank, taps = tap_ref.shape
    shape = (tap_rank * half, taps * half)
    spread = (
        lax.broadcasted_iota(jnp.int32, (shape[0], tap_rank), 0) // half == lane_index((shape[0], tap_rank))
    ).astype(BF16)
    repeat = (
        lax.broadcasted_iota(jnp.int32, (taps, shape[1]), 0) == lane_index((taps, shape[1])) // half
    ).astype(BF16)
    tall = jnp.dot(spread, tap_ref[...], preferred_element_type=F32).astype(BF16)
    wide = jnp.dot(tall, repeat, preferred_element_type=F32)
    same = lax.broadcasted_iota(jnp.int32, shape, 0) % half == lane_index(shape) % half
    weights_ref[...] = jnp.where(same, wide, 0.0).astype(BF16)

    shape = (out_channels * GROUP, rank * GROUP)
    spread = (
        lax.broadcasted_iota(jnp.int32, (shape[0], out_channels), 0) // GROUP
        == lane_index((shape[0], out_channels))
    ).astype(BF16)
    repeat = (
        lax.broadcasted_iota(jnp.int32, (rank, shape[1]), 0) == lane_index((rank, shape[1])) % rank
    ).astype(BF16)
    tall = lax.dot_general(
        spread, out_factor_ref[...], (((1,), (1,)), ((), ())), preferred_element_type=F32
    ).astype(BF16)
    wide = jnp.dot(tall, repeat, preferred_element_type=F32)
    same = lax.broadcasted_iota(jnp.int32, shape, 0) % GROUP == lane_index(shape) // rank
    mixer_ref[...] = jnp.where(same, wide, 0.0).astype(BF16)

    shape = (out_channels * GROUP, out_channels)
    mine = lax.broadcasted_iota(jnp.int32, shape, 0) // GROUP == lane_index(shape)
    offset = jnp.sum(jnp.where(mine, bias_ref[...], 0.0), axis=1, keepdims=True)
    offset_ref[...] = jnp.broadcast_to(offset, offset_ref.shape)
    copy.wait()
    for nth in range(PER_OWNER):
        own_ref[nth] = bank_ref[rows[0][nth]]


def pick_kernel(
    lat_len, got_b_ref, got_a_ref, red_ref, bank_ref, core_b_ref, core_a_ref, edge_ref, row_a_ref, row_b_ref
):
    lon_len = red_ref.shape[1] // lat_len
    rank = red_ref.shape[0]
    lane = lane_index((1, LANES))
    for got_ref, core_ref in ((got_b_ref, core_b_ref), (got_a_ref, core_a_ref)):
        head = got_ref[...].astype(F32)[0:1, :]
        for nth in range(PER_OWNER):
            row = jnp.sum(jnp.where(lane == EDGE * lat_len + nth, head, 0.0)).astype(jnp.int32)
            core_ref[nth] = bank_ref[row]
    even_lon = (lax.axis_index("lon") % 2) == 0
    even_lat = (lax.axis_index("lat") % 2) == 0
    lane = lane_index((rank, LANES))
    got_a = got_a_ref[...].astype(F32)
    got_b = got_b_ref[...].astype(F32)
    from_prev = lane % EDGE < REACH
    edges = jnp.where(from_prev == even_lon, got_b, got_a).astype(BF16)
    edge_ref[...] = edges
    head = red_ref[:, : REACH * lon_len].astype(F32)
    tail = red_ref[:, (lat_len - REACH) * lon_len :].astype(F32)
    row_a_ref[:, : REACH * lon_len] = jnp.where(even_lat, tail, head).astype(BF16)
    row_b_ref[:, : REACH * lon_len] = jnp.where(even_lat, head, tail).astype(BF16)
    row_a_ref[:, REACH * lon_len :] = edges
    row_b_ref[:, REACH * lon_len :] = edges


def stencil_kernel(lat_count, red_ref, edge_ref, row_a_ref, row_b_ref, weights_ref, tapped_ref, stack_ref):
    rank = red_ref.shape[0]
    half = rank // 2
    tap_rank = weights_ref.shape[0] // half
    lon_len = (row_a_ref.shape[1] - LANES) // REACH
    lat_len = red_ref.shape[1] // lon_len
    lat = lax.axis_index("lat")
    even_lat = (lat % 2) == 0
    lane = lane_index((rank, LANES))
    row_a = row_a_ref[...].astype(F32)
    row_b = row_b_ref[...].astype(F32)
    above = jnp.where(lat == 0, 0.0, jnp.where(even_lat, row_b, row_a))
    below = jnp.where(lat == lat_count - 1, 0.0, jnp.where(even_lat, row_a, row_b))
    inner_edges = edge_ref[...].astype(F32)
    for w in range(lat_len + KS - 1):
        p = w - REACH
        if p < 0:
            row = above[:, w * lon_len : (w + 1) * lon_len]
            edges, place = above[:, REACH * lon_len :], lat_len + p
        elif p >= lat_len:
            row = below[:, (p - lat_len) * lon_len : (p - lat_len + 1) * lon_len]
            edges, place = below[:, REACH * lon_len :], p - lat_len
        else:
            row = red_ref[:, p * lon_len : (p + 1) * lon_len].astype(F32)
            edges, place = inner_edges, p
        edges = pltpu.roll(edges, (LANES - REACH - EDGE * place) % LANES, 1)
        for col_off in range(KS):
            shift = REACH - col_off
            if shift > 0:
                moved = pltpu.roll(jnp.where(lane >= lon_len - shift, edges, row), shift, 1)
            elif shift < 0:
                moved = pltpu.roll(jnp.where(lane < -shift, edges, row), lon_len + shift, 1)
            else:
                moved = row
            moved = moved.astype(BF16)
            for row_off in range(KS):
                q = w - row_off
                if 0 <= q < lat_len:
                    k = row_off * KS + col_off
                    for h in range(2):
                        stack_ref[h, k * half : (k + 1) * half, q * lon_len : (q + 1) * lon_len] = moved[
                            h * half : (h + 1) * half
                        ]

    step = 2
    for start in range(0, lat_len, step):
        span = slice(start * lon_len, (start + step) * lon_len)
        parts = [
            jnp.dot(weights_ref[...], stack_ref[h, :, span], preferred_element_type=F32)
            .astype(BF16)
            .reshape(tap_rank, 1, half, step * lon_len)
            for h in range(2)
        ]
        tapped_ref[:, span] = jnp.concatenate(parts, axis=1).reshape(tap_rank * rank, step * lon_len)


def mix_kernel(tapped_ref, core_a_ref, core_b_ref, own_ref, position_ref, mixer_ref, offset_ref, out_ref):
    lat_len, lon_len = position_ref.shape
    rank = own_ref.shape[1]
    cores = jnp.concatenate(
        [ref[...].reshape(PER_OWNER * rank, -1) for ref in (own_ref, core_a_ref, core_b_ref)], axis=0
    )
    step = 2
    blocks = []
    for base in range(0, lat_len, GROUP):
        pieces = []
        for start in range(base, base + GROUP, step):
            span = slice(start * lon_len, (start + step) * lon_len)
            every = jnp.dot(cores, tapped_ref[:, span], preferred_element_type=F32)
            position = jnp.concatenate([position_ref[start + r : start + r + 1, :] for r in range(step)], axis=1)
            hidden = jnp.zeros((rank, step * lon_len), F32)
            for index in range(3 * PER_OWNER):
                hidden = jnp.where(position == index, every[index * rank : (index + 1) * rank], hidden)
            hidden = hidden.astype(BF16)
            pieces += [hidden[:, r * lon_len : (r + 1) * lon_len] for r in range(step)]
        output = jnp.dot(mixer_ref[...], jnp.concatenate(pieces, axis=0), preferred_element_type=F32) + offset_ref[...]
        mixed = output / (1.0 + jnp.exp(-output))
        blocks.append(mixed.reshape(out_ref.shape[0], GROUP, lon_len))
    out_ref[...] = jnp.concatenate(blocks, axis=1).astype(BF16)


def on_device(
    features, labels, tile_regions, bank_slot, kernel_bank, in_factor, tap_factor, out_factor, out_bias
):
    channels, lat_len, lon_len = features.shape
    rank = in_factor.shape[0]
    held, core_rows, core_cols = kernel_bank.shape
    tap_rank, taps = tap_factor.shape
    out_channels = out_factor.shape[0]
    cells = lat_len * lon_len
    lon_count, lat_count = lax.axis_size("lon"), lax.axis_size("lat")
    lon_first, lon_second = swap_pairs(lon_count, True)
    lat_first, lat_second = swap_pairs(lat_count, False)
    edge_shape = jax.ShapeDtypeStruct((rank, LANES), BF16)
    reduced, pay_a, pay_b = pl.pallas_call(
        functools.partial(reduce_kernel, lon_count, held),
        out_shape=(jax.ShapeDtypeStruct((rank, cells), BF16), edge_shape, edge_shape),
        in_specs=[HBM] * 4,
        out_specs=(VMEM,) * 3,
        scratch_shapes=[
            pltpu.SMEM(tile_regions.shape, jnp.int32),
            pltpu.SMEM(bank_slot.shape, jnp.int32),
            pltpu.VMEM(features.shape, BF16),
            pltpu.VMEM(in_factor.shape, BF16),
            pltpu.VMEM((channels * lat_len, lon_len), F32),
            pltpu.SemaphoreType.DMA((4,)),
        ],
        compiler_params=PARAMS,
    )(*(in_hbm(x) for x in (tile_regions, bank_slot, features, in_factor)))
    got_b = lax.ppermute(pay_b, "lon", lon_second)
    got_a = lax.ppermute(pay_a, "lon", lon_first)
    core_shape = jax.ShapeDtypeStruct((PER_OWNER, core_rows, core_cols), BF16)
    bank, own, position, weights, mixer, offset = pl.pallas_call(
        functools.partial(prepare_kernel, lon_count, lat_len),
        out_shape=(
            jax.ShapeDtypeStruct(kernel_bank.shape, BF16),
            core_shape,
            jax.ShapeDtypeStruct(labels.shape, jnp.int32),
            jax.ShapeDtypeStruct((tap_rank * rank // 2, taps * rank // 2), BF16),
            jax.ShapeDtypeStruct((out_channels * GROUP, rank * GROUP), BF16),
            jax.ShapeDtypeStruct((out_channels * GROUP, lon_len), F32),
        ),
        in_specs=[HBM] * 8,
        out_specs=(VMEM,) * 6,
        scratch_shapes=[
            pltpu.SMEM(tile_regions.shape, jnp.int32),
            pltpu.SMEM(bank_slot.shape, jnp.int32),
            pltpu.VMEM(labels.shape, jnp.int32),
            pltpu.VMEM(tap_factor.shape, BF16),
            pltpu.VMEM(out_factor.shape[::-1], BF16),
            pltpu.VMEM((1, out_channels), F32),
            pltpu.SemaphoreType.DMA((7,)),
        ],
        compiler_params=PARAMS,
        cost_estimate=pl.CostEstimate(flops=10**6, bytes_accessed=kernel_bank.size * 4, transcendentals=0),
    )(
        reduced,
        *(
            in_hbm(x)
            for x in (
                tile_regions,
                bank_slot,
                kernel_bank,
                labels,
                tap_factor,
                out_factor.T,
                out_bias.reshape(1, -1),
            )
        ),
    )
    row_shape = jax.ShapeDtypeStruct((rank, REACH * lon_len + LANES), BF16)
    core_b, core_a, edges, row_a, row_b = pl.pallas_call(
        functools.partial(pick_kernel, lat_len),
        out_shape=(core_shape, core_shape, edge_shape, row_shape, row_shape),
        in_specs=[VMEM] * 4,
        out_specs=(VMEM,) * 5,
        compiler_params=PARAMS,
    )(got_b, got_a, reduced, bank)
    core_b = lax.ppermute(core_b, "lon", lon_second)
    core_a = lax.ppermute(core_a, "lon", lon_first)
    row_a = lax.ppermute(row_a, "lat", lat_first)
    row_b = lax.ppermute(row_b, "lat", lat_second)
    tapped = pl.pallas_call(
        functools.partial(stencil_kernel, lat_count),
        out_shape=jax.ShapeDtypeStruct((tap_rank * rank, cells), BF16),
        in_specs=[VMEM] * 5,
        out_specs=VMEM,
        scratch_shapes=[pltpu.VMEM((2, taps * rank // 2, cells), BF16)],
        compiler_params=PARAMS,
        cost_estimate=pl.CostEstimate(
            flops=2 * 16 * taps * tap_rank * rank * cells, bytes_accessed=4 * tap_rank * rank * cells, transcendentals=0
        ),
    )(reduced, edges, row_a, row_b, weights)
    return pl.pallas_call(
        mix_kernel,
        out_shape=jax.ShapeDtypeStruct((out_channels, lat_len, lon_len), BF16),
        in_specs=[VMEM] * 7,
        out_specs=VMEM,
        compiler_params=PARAMS,
    )(tapped, core_a, core_b, own, position, mixer, offset)


def solution(mesh):
    placed = (
        P(None, "lat", "lon"),
        P("lat", "lon"),
        P("lat", "lon", None),
        P(),
        P("lon", None, None),
        P(),
        P(),
        P(),
        P(),
    )
    return jax.shard_map(
        on_device, mesh=mesh, in_specs=placed, out_specs=P(None, "lat", "lon"), check_vma=False
    )
```

```python
import functools

import jax
import jax.numpy as jnp
from jax import lax
from jax.experimental import pallas as pl
from jax.experimental.pallas import tpu as pltpu
from jax.sharding import PartitionSpec as P

KS = 5
REACH = KS // 2
PER_OWNER = 2
LANES = 128
EDGE = 2 * REACH
GROUP = 8
STEP = 2
OUT_COPIES = 4
IN_COPIES = 4
BANK_COPIES = 8
F32 = jnp.float32
BF16 = jnp.bfloat16
VMEM = pl.BlockSpec(memory_space=pltpu.VMEM)
SMEM = pl.BlockSpec(memory_space=pltpu.SMEM)
HBM = pl.BlockSpec(memory_space=pltpu.HBM)
PARAMS = pltpu.CompilerParams(vmem_limit_bytes=24 * 1024 * 1024)


def swap_pairs(count, wrap):
    first = [(i, i ^ 1) for i in range(count)]
    second = [] if wrap else [(0, 0), (count - 1, count - 1)]
    for i in range(1, count if wrap else count - 1, 2):
        second += [(i, (i + 1) % count), ((i + 1) % count, i)]
    return first, second


def in_hbm(array):
    return pltpu.with_memory_space_constraint(array, pltpu.HBM)


def lane_index(shape):
    return lax.broadcasted_iota(jnp.int32, shape, 1)


def start_copies(pairs, sems):
    copies = [pltpu.make_async_copy(source, target, sems.at[i]) for i, (source, target) in enumerate(pairs)]
    for copy in copies:
        copy.start()
    return copies


def in_parts(source, target, count):
    share = target.shape[0] // count
    return tuple((source.at[pl.ds(i * share, share)], target.at[pl.ds(i * share, share)]) for i in range(count))


def find_rows(list_ref, slot_ref, lon_count, held):
    me = lax.axis_index("lon")
    owners = (me, lax.rem(me + lon_count - 1, lon_count), lax.rem(me + 1, lon_count))
    counts = [jnp.int32(0)] * 3
    places = [[jnp.int32(0)] * PER_OWNER for _ in range(3)]
    rows = [[jnp.int32(0)] * PER_OWNER for _ in range(3)]
    for i in range(list_ref.shape[2]):
        slot = slot_ref[list_ref[0, 0, i]]
        for group, owner in enumerate(owners):
            local = slot - owner * held
            hit = (local >= 0) & (local < held)
            for nth in range(PER_OWNER):
                take = hit & (counts[group] == nth)
                places[group][nth] = jnp.where(take, i, places[group][nth])
                rows[group][nth] = jnp.where(take, local, rows[group][nth])
            counts[group] = counts[group] + hit.astype(jnp.int32)
    return places, rows


def reduce_kernel(
    lon_count,
    held,
    list_hbm,
    slot_hbm,
    feat_hbm,
    in_hbm,
    red_ref,
    pay_a_ref,
    pay_b_ref,
    list_ref,
    slot_ref,
    feat_ref,
    in_ref,
    rows_ref,
    sems,
):
    channels, lat_len, lon_len = feat_ref.shape
    rank = in_ref.shape[0]
    pairs = in_parts(feat_hbm, feat_ref, IN_COPIES)
    pairs += ((slot_hbm, slot_ref), (list_hbm, list_ref), (in_hbm, in_ref))
    for copy in start_copies(pairs, sems):
        copy.wait()
    rows_ref[...] = feat_ref[...].astype(F32).reshape(channels * lat_len, lon_len)
    cells = jnp.concatenate(
        [rows_ref[pl.ds(p, channels, stride=lat_len), :].astype(BF16) for p in range(lat_len)], axis=1
    )
    reduced = jnp.dot(in_ref[...], cells, preferred_element_type=F32)
    red_ref[...] = reduced.astype(BF16)
    _, rows = find_rows(list_ref, slot_ref, lon_count, held)
    even = (lax.axis_index("lon") % 2) == 0
    lane = lane_index((rank, LANES))
    pack = jnp.zeros((rank, LANES), F32)
    for p in range(lat_len):
        turned = pltpu.roll(reduced[:, p * lon_len : (p + 1) * lon_len], EDGE * p + REACH, 1)
        pack = jnp.where(lane // EDGE == p, turned, pack)
    for out_ref, wanted in ((pay_a_ref, even), (pay_b_ref, jnp.logical_not(even))):
        load = pack
        for nth in range(PER_OWNER):
            row = jnp.where(wanted, rows[2][nth], rows[1][nth]).astype(F32)
            load = jnp.where(lane == EDGE * lat_len + nth, row, load)
        out_ref[...] = load.astype(BF16)


def prepare_kernel(
    lon_count,
    lat_len,
    red_hbm,
    list_hbm,
    slot_hbm,
    bank_hbm,
    labels_hbm,
    tap_hbm,
    out_factor_hbm,
    bias_hbm,
    bank_ref,
    own_ref,
    position_ref,
    weights_ref,
    mixer_ref,
    offset_ref,
    list_ref,
    slot_ref,
    labels_ref,
    tap_ref,
    out_factor_ref,
    bias_ref,
    sems,
):
    held = bank_hbm.shape[0]
    small = (
        (list_hbm, list_ref),
        (slot_hbm, slot_ref),
        (labels_hbm, labels_ref),
        (tap_hbm, tap_ref),
        (out_factor_hbm, out_factor_ref),
        (bias_hbm, bias_ref),
    )
    copies = start_copies(small + in_parts(bank_hbm, bank_ref, BANK_COPIES), sems)
    for copy in copies[: len(small)]:
        copy.wait()
    places, rows = find_rows(list_ref, slot_ref, lon_count, held)
    even = (lax.axis_index("lon") % 2) == 0
    order = list(places[0])
    order += [jnp.where(even, places[2][nth], places[1][nth]) for nth in range(PER_OWNER)]
    order += [jnp.where(even, places[1][nth], places[2][nth]) for nth in range(PER_OWNER)]
    labels = labels_ref[...]
    position = jnp.zeros(labels.shape, jnp.int32)
    for index, place in enumerate(order):
        position = jnp.where(labels == place, index, position)
    position_ref[...] = position

    rank, out_channels = out_factor_ref.shape
    half = rank // 2
    tap_rank, taps = tap_ref.shape
    shape = (tap_rank * half, taps * half)
    spread = (
        lax.broadcasted_iota(jnp.int32, (shape[0], tap_rank), 0) // half == lane_index((shape[0], tap_rank))
    ).astype(BF16)
    repeat = (
        lax.broadcasted_iota(jnp.int32, (taps, shape[1]), 0) == lane_index((taps, shape[1])) // half
    ).astype(BF16)
    tall = jnp.dot(spread, tap_ref[...], preferred_element_type=F32).astype(BF16)
    wide = jnp.dot(tall, repeat, preferred_element_type=F32)
    same = lax.broadcasted_iota(jnp.int32, shape, 0) % half == lane_index(shape) % half
    weights_ref[...] = jnp.where(same, wide, 0.0).astype(BF16)

    shape = (out_channels * GROUP, rank * GROUP)
    spread = (
        lax.broadcasted_iota(jnp.int32, (shape[0], out_channels), 0) // GROUP
        == lane_index((shape[0], out_channels))
    ).astype(BF16)
    repeat = (
        lax.broadcasted_iota(jnp.int32, (rank, shape[1]), 0) == lane_index((rank, shape[1])) % rank
    ).astype(BF16)
    tall = lax.dot_general(
        spread, out_factor_ref[...], (((1,), (1,)), ((), ())), preferred_element_type=F32
    ).astype(BF16)
    wide = jnp.dot(tall, repeat, preferred_element_type=F32)
    same = lax.broadcasted_iota(jnp.int32, shape, 0) % GROUP == lane_index(shape) // rank
    mixer_ref[...] = jnp.where(same, wide, 0.0).astype(BF16)

    shape = (out_channels * GROUP, out_channels)
    mine = lax.broadcasted_iota(jnp.int32, shape, 0) // GROUP == lane_index(shape)
    offset = jnp.sum(jnp.where(mine, bias_ref[...], 0.0), axis=1, keepdims=True)
    offset_ref[...] = jnp.broadcast_to(offset, offset_ref.shape)
    for copy in copies[len(small) :]:
        copy.wait()
    for nth in range(PER_OWNER):
        own_ref[nth] = bank_ref[rows[0][nth]]


def pick_kernel(lat_len, got_b_ref, got_a_ref, bank_ref, core_b_ref, core_a_ref, edge_ref):
    lane = lane_index((1, LANES))
    for got_ref, core_ref in ((got_b_ref, core_b_ref), (got_a_ref, core_a_ref)):
        head = got_ref[...].astype(F32)[0:1, :]
        for nth in range(PER_OWNER):
            row = jnp.sum(jnp.where(lane == EDGE * lat_len + nth, head, 0.0)).astype(jnp.int32)
            core_ref[nth] = bank_ref[row]
    even = (lax.axis_index("lon") % 2) == 0
    from_prev = lane_index(got_a_ref.shape) % EDGE < REACH
    got_a = got_a_ref[...].astype(F32)
    got_b = got_b_ref[...].astype(F32)
    edge_ref[...] = jnp.where(from_prev == even, got_b, got_a).astype(BF16)


def rows_kernel(lat_len, red_ref, edge_ref, row_a_ref, row_b_ref):
    lon_len = red_ref.shape[1] // lat_len
    even = (lax.axis_index("lat") % 2) == 0
    head = red_ref[:, : REACH * lon_len].astype(F32)
    tail = red_ref[:, (lat_len - REACH) * lon_len :].astype(F32)
    row_a_ref[:, : REACH * lon_len] = jnp.where(even, tail, head).astype(BF16)
    row_b_ref[:, : REACH * lon_len] = jnp.where(even, head, tail).astype(BF16)
    row_a_ref[:, REACH * lon_len :] = edge_ref[...]
    row_b_ref[:, REACH * lon_len :] = edge_ref[...]


def shifted_columns(row, edges, place):
    lane = lane_index(row.shape)
    lon_len = row.shape[1]
    edges = pltpu.roll(edges, (LANES - REACH - EDGE * place) % LANES, 1)
    moved = []
    for col_off in range(KS):
        shift = REACH - col_off
        if shift > 0:
            piece = pltpu.roll(jnp.where(lane >= lon_len - shift, edges, row), shift, 1)
        elif shift < 0:
            piece = pltpu.roll(jnp.where(lane < -shift, edges, row), lon_len + shift, 1)
        else:
            piece = row
        moved.append(piece.astype(BF16))
    return moved


def stack_row(stack_ref, p, moved, slots, lon_len):
    half = moved[0].shape[0] // 2
    for col_off, piece in enumerate(moved):
        for row_off in range(KS):
            slot = slots.get(p + REACH - row_off)
            if slot is not None:
                k = row_off * KS + col_off
                for h in range(2):
                    stack_ref[h, k * half : (k + 1) * half, slot * lon_len : (slot + 1) * lon_len] = piece[
                        h * half : (h + 1) * half
                    ]


def apply_taps(rank, weights_ref, stack_ref, tapped_ref, lon_len):
    half = rank // 2
    tap_rank = tapped_ref.shape[0] // rank
    width = STEP * lon_len
    for start in range(0, tapped_ref.shape[1], width):
        span = slice(start, start + width)
        parts = [
            jnp.dot(weights_ref[...], stack_ref[h, :, span], preferred_element_type=F32)
            .astype(BF16)
            .reshape(tap_rank, 1, half, width)
            for h in range(2)
        ]
        tapped_ref[:, span] = jnp.concatenate(parts, axis=1).reshape(tap_rank * rank, width)


def inner_kernel(lat_len, red_ref, edge_ref, weights_ref, tapped_ref, stack_ref):
    rank = red_ref.shape[0]
    lon_len = red_ref.shape[1] // lat_len
    slots = {p: p - REACH for p in range(REACH, lat_len - REACH)}
    edges = edge_ref[...].astype(F32)
    for p in range(lat_len):
        row = red_ref[:, p * lon_len : (p + 1) * lon_len].astype(F32)
        stack_row(stack_ref, p, shifted_columns(row, edges, p), slots, lon_len)
    apply_taps(rank, weights_ref, stack_ref, tapped_ref, lon_len)


def border_kernel(
    lat_len, lat_count, red_ref, edge_ref, row_a_ref, row_b_ref, weights_ref, tapped_ref, stack_ref
):
    rank = red_ref.shape[0]
    lon_len = red_ref.shape[1] // lat_len
    lat = lax.axis_index("lat")
    even = (lat % 2) == 0
    row_a = row_a_ref[...].astype(F32)
    row_b = row_b_ref[...].astype(F32)
    above = jnp.where(lat == 0, 0.0, jnp.where(even, row_b, row_a))
    below = jnp.where(lat == lat_count - 1, 0.0, jnp.where(even, row_a, row_b))
    slots = {p: p for p in range(REACH)}
    slots.update({lat_len - REACH + p: REACH + p for p in range(REACH)})
    edges = edge_ref[...].astype(F32)
    sources = []
    for p in range(REACH):
        sources.append((p - REACH, above[:, p * lon_len : (p + 1) * lon_len], above, lat_len - REACH + p))
        sources.append((lat_len + p, below[:, p * lon_len : (p + 1) * lon_len], below, p))
    for p in [*range(2 * REACH), *range(lat_len - 2 * REACH, lat_len)]:
        sources.append((p, red_ref[:, p * lon_len : (p + 1) * lon_len].astype(F32), None, p))
    for p, row, holder, place in sources:
        side = edges if holder is None else holder[:, REACH * lon_len :]
        stack_row(stack_ref, p, shifted_columns(row, side, place), slots, lon_len)
    apply_taps(rank, weights_ref, stack_ref, tapped_ref, lon_len)


def mix_kernel(
    inner_ref,
    border_ref,
    core_b_ref,
    core_a_ref,
    own_ref,
    position_ref,
    mixer_ref,
    offset_ref,
    out_hbm,
    stage_ref,
    sems,
):
    lat_len, lon_len = position_ref.shape
    rank = own_ref.shape[1]
    cores = jnp.concatenate(
        [ref[...].reshape(PER_OWNER * rank, -1) for ref in (own_ref, core_a_ref, core_b_ref)], axis=0
    )
    pieces = []
    for start in range(0, lat_len, STEP):
        if start < REACH:
            ref, first = border_ref, start
        elif start < lat_len - REACH:
            ref, first = inner_ref, start - REACH
        else:
            ref, first = border_ref, start - (lat_len - 2 * REACH)
        every = jnp.dot(cores, ref[:, first * lon_len : (first + STEP) * lon_len], preferred_element_type=F32)
        position = jnp.concatenate([position_ref[start + r : start + r + 1, :] for r in range(STEP)], axis=1)
        hidden = jnp.zeros((rank, STEP * lon_len), F32)
        for index in range(3 * PER_OWNER):
            hidden = jnp.where(position == index, every[index * rank : (index + 1) * rank], hidden)
        hidden = hidden.astype(BF16)
        pieces += [hidden[:, r * lon_len : (r + 1) * lon_len] for r in range(STEP)]
    groups = [jnp.concatenate(pieces[g : g + GROUP], axis=0) for g in range(0, lat_len, GROUP)]
    channels = stage_ref.shape[0]
    share = channels // OUT_COPIES
    copies = []
    for part in range(OUT_COPIES):
        span = slice(part * share * GROUP, (part + 1) * share * GROUP)
        blocks = []
        for hidden in groups:
            output = jnp.dot(mixer_ref[span, :], hidden, preferred_element_type=F32) + offset_ref[span, :]
            mixed = output / (1.0 + jnp.exp(-output))
            blocks.append(mixed.reshape(share, GROUP, lon_len))
        held = slice(part * share, (part + 1) * share)
        stage_ref[held] = jnp.concatenate(blocks, axis=1).astype(BF16)
        copy = pltpu.make_async_copy(stage_ref.at[held], out_hbm.at[held], sems.at[part])
        copy.start()
        copies.append(copy)
    for copy in copies:
        copy.wait()


def on_device(
    features, labels, tile_regions, bank_slot, kernel_bank, in_factor, tap_factor, out_factor, out_bias
):
    channels, lat_len, lon_len = features.shape
    rank = in_factor.shape[0]
    held, core_rows, core_cols = kernel_bank.shape
    tap_rank, taps = tap_factor.shape
    out_channels = out_factor.shape[0]
    cells = lat_len * lon_len
    lon_count, lat_count = lax.axis_size("lon"), lax.axis_size("lat")
    lon_first, lon_second = swap_pairs(lon_count, True)
    lat_first, lat_second = swap_pairs(lat_count, False)
    edge_shape = jax.ShapeDtypeStruct((rank, LANES), BF16)
    reduced, pay_a, pay_b = pl.pallas_call(
        functools.partial(reduce_kernel, lon_count, held),
        out_shape=(jax.ShapeDtypeStruct((rank, cells), BF16), edge_shape, edge_shape),
        in_specs=[HBM] * 4,
        out_specs=(VMEM,) * 3,
        scratch_shapes=[
            pltpu.SMEM(tile_regions.shape, jnp.int32),
            pltpu.SMEM(bank_slot.shape, jnp.int32),
            pltpu.VMEM(features.shape, BF16),
            pltpu.VMEM(in_factor.shape, BF16),
            pltpu.VMEM((channels * lat_len, lon_len), F32),
            pltpu.SemaphoreType.DMA((IN_COPIES + 3,)),
        ],
        compiler_params=PARAMS,
    )(*(in_hbm(x) for x in (tile_regions, bank_slot, features, in_factor)))
    got_b = lax.ppermute(pay_b, "lon", lon_second)
    got_a = lax.ppermute(pay_a, "lon", lon_first)
    core_shape = jax.ShapeDtypeStruct((PER_OWNER, core_rows, core_cols), BF16)
    bank, own, position, weights, mixer, offset = pl.pallas_call(
        functools.partial(prepare_kernel, lon_count, lat_len),
        out_shape=(
            jax.ShapeDtypeStruct(kernel_bank.shape, BF16),
            core_shape,
            jax.ShapeDtypeStruct(labels.shape, jnp.int32),
            jax.ShapeDtypeStruct((tap_rank * rank // 2, taps * rank // 2), BF16),
            jax.ShapeDtypeStruct((out_channels * GROUP, rank * GROUP), BF16),
            jax.ShapeDtypeStruct((out_channels * GROUP, lon_len), F32),
        ),
        in_specs=[HBM] * 8,
        out_specs=(VMEM,) * 6,
        scratch_shapes=[
            pltpu.SMEM(tile_regions.shape, jnp.int32),
            pltpu.SMEM(bank_slot.shape, jnp.int32),
            pltpu.VMEM(labels.shape, jnp.int32),
            pltpu.VMEM(tap_factor.shape, BF16),
            pltpu.VMEM(out_factor.shape[::-1], BF16),
            pltpu.VMEM((1, out_channels), F32),
            pltpu.SemaphoreType.DMA((6 + BANK_COPIES,)),
        ],
        compiler_params=PARAMS,
        cost_estimate=pl.CostEstimate(flops=10**6, bytes_accessed=kernel_bank.size * 4, transcendentals=0),
    )(
        reduced,
        *(
            in_hbm(x)
            for x in (
                tile_regions,
                bank_slot,
                kernel_bank,
                labels,
                tap_factor,
                out_factor.T,
                out_bias.reshape(1, -1),
            )
        ),
    )
    row_shape = jax.ShapeDtypeStruct((rank, REACH * lon_len + LANES), BF16)
    core_b, core_a, edges = pl.pallas_call(
        functools.partial(pick_kernel, lat_len),
        out_shape=(core_shape, core_shape, edge_shape),
        in_specs=[VMEM] * 3,
        out_specs=(VMEM,) * 3,
        compiler_params=PARAMS,
    )(got_b, got_a, bank)
    core_b = lax.ppermute(core_b, "lon", lon_second)
    core_a = lax.ppermute(core_a, "lon", lon_first)
    row_a, row_b = pl.pallas_call(
        functools.partial(rows_kernel, lat_len),
        out_shape=(row_shape, row_shape),
        in_specs=[VMEM] * 2,
        out_specs=(VMEM,) * 2,
        compiler_params=PARAMS,
    )(reduced, edges)
    row_a = lax.ppermute(row_a, "lat", lat_first)
    row_b = lax.ppermute(row_b, "lat", lat_second)
    border_cells = 2 * REACH * lon_len
    inner = pl.pallas_call(
        functools.partial(inner_kernel, lat_len),
        out_shape=jax.ShapeDtypeStruct((tap_rank * rank, cells - border_cells), BF16),
        in_specs=[VMEM] * 3,
        out_specs=VMEM,
        scratch_shapes=[pltpu.VMEM((2, taps * rank // 2, cells - border_cells), BF16)],
        compiler_params=PARAMS,
    )(reduced, edges, weights)
    border = pl.pallas_call(
        functools.partial(border_kernel, lat_len, lat_count),
        out_shape=jax.ShapeDtypeStruct((tap_rank * rank, border_cells), BF16),
        in_specs=[VMEM] * 5,
        out_specs=VMEM,
        scratch_shapes=[pltpu.VMEM((2, taps * rank // 2, border_cells), BF16)],
        compiler_params=PARAMS,
    )(reduced, edges, row_a, row_b, weights)
    out_shape = (out_channels, lat_len, lon_len)
    return pl.pallas_call(
        mix_kernel,
        out_shape=jax.ShapeDtypeStruct(out_shape, BF16),
        in_specs=[VMEM] * 8,
        out_specs=HBM,
        scratch_shapes=[pltpu.VMEM(out_shape, BF16), pltpu.SemaphoreType.DMA((OUT_COPIES,))],
        compiler_params=PARAMS,
    )(inner, border, core_b, core_a, own, position, mixer, offset)


def solution(mesh):
    placed = (
        P(None, "lat", "lon"),
        P("lat", "lon"),
        P("lat", "lon", None),
        P(),
        P("lon", None, None),
        P(),
        P(),
        P(),
        P(),
    )
    return jax.shard_map(
        on_device, mesh=mesh, in_specs=placed, out_specs=P(None, "lat", "lon"), check_vma=False
    )
```

```python
import functools

import jax
import jax.numpy as jnp
from jax import lax
from jax.experimental import pallas as pl
from jax.experimental.pallas import tpu as pltpu
from jax.sharding import PartitionSpec as P

KS = 5
REACH = KS // 2
PER_OWNER = 2
LANES = 128
EDGE = 2 * REACH
GROUP = 8
STEP = 2
OUT_COPIES = 4
IN_COPIES = 4
BANK_COPIES = 8
F32 = jnp.float32
BF16 = jnp.bfloat16
VMEM = pl.BlockSpec(memory_space=pltpu.VMEM)
SMEM = pl.BlockSpec(memory_space=pltpu.SMEM)
HBM = pl.BlockSpec(memory_space=pltpu.HBM)
PARAMS = pltpu.CompilerParams(vmem_limit_bytes=24 * 1024 * 1024)


def swap_pairs(count):
    first = [(i, i ^ 1) for i in range(count)]
    second = [(i, (i + 1 if i % 2 else i - 1) % count) for i in range(count)]
    return first, second


def in_hbm(array):
    return pltpu.with_memory_space_constraint(array, pltpu.HBM)


def lane_index(shape):
    return lax.broadcasted_iota(jnp.int32, shape, 1)


def start_copies(pairs, sems):
    copies = [pltpu.make_async_copy(source, target, sems.at[i]) for i, (source, target) in enumerate(pairs)]
    for copy in copies:
        copy.start()
    return copies


def in_parts(source, target, count):
    share = target.shape[0] // count
    return tuple((source.at[pl.ds(i * share, share)], target.at[pl.ds(i * share, share)]) for i in range(count))


def find_rows(list_ref, slot_ref, lon_count, held):
    me = lax.axis_index("lon")
    owners = (me, lax.rem(me + lon_count - 1, lon_count), lax.rem(me + 1, lon_count))
    counts = [jnp.int32(0)] * 3
    places = [[jnp.int32(0)] * PER_OWNER for _ in range(3)]
    rows = [[jnp.int32(0)] * PER_OWNER for _ in range(3)]
    for i in range(list_ref.shape[2]):
        slot = slot_ref[list_ref[0, 0, i]]
        for group, owner in enumerate(owners):
            local = slot - owner * held
            hit = (local >= 0) & (local < held)
            for nth in range(PER_OWNER):
                take = hit & (counts[group] == nth)
                places[group][nth] = jnp.where(take, i, places[group][nth])
                rows[group][nth] = jnp.where(take, local, rows[group][nth])
            counts[group] = counts[group] + hit.astype(jnp.int32)
    return places, rows


def reduce_kernel(
    lon_count,
    held,
    list_hbm,
    slot_hbm,
    feat_hbm,
    in_hbm,
    red_ref,
    pay_a_ref,
    pay_b_ref,
    list_ref,
    slot_ref,
    feat_ref,
    in_ref,
    rows_ref,
    sems,
):
    channels, lat_len, lon_len = feat_ref.shape
    rank = in_ref.shape[0]
    pairs = in_parts(feat_hbm, feat_ref, IN_COPIES)
    pairs += ((slot_hbm, slot_ref), (list_hbm, list_ref), (in_hbm, in_ref))
    for copy in start_copies(pairs, sems):
        copy.wait()
    rows_ref[...] = feat_ref[...].astype(F32).reshape(channels * lat_len, lon_len)
    cells = jnp.concatenate(
        [rows_ref[pl.ds(p, channels, stride=lat_len), :].astype(BF16) for p in range(lat_len)], axis=1
    )
    reduced = jnp.dot(in_ref[...], cells, preferred_element_type=F32)
    red_ref[...] = reduced.astype(BF16)
    _, rows = find_rows(list_ref, slot_ref, lon_count, held)
    even = (lax.axis_index("lon") % 2) == 0
    lane = lane_index((rank, LANES))
    pack = jnp.zeros((rank, LANES), F32)
    for p in range(lat_len):
        turned = pltpu.roll(reduced[:, p * lon_len : (p + 1) * lon_len], EDGE * p + REACH, 1)
        pack = jnp.where(lane // EDGE == p, turned, pack)
    for out_ref, wanted in ((pay_a_ref, even), (pay_b_ref, jnp.logical_not(even))):
        load = pack
        for nth in range(PER_OWNER):
            row = jnp.where(wanted, rows[2][nth], rows[1][nth]).astype(F32)
            load = jnp.where(lane == EDGE * lat_len + nth, row, load)
        out_ref[...] = load.astype(BF16)


def prepare_kernel(
    lon_count,
    lat_len,
    red_hbm,
    list_hbm,
    slot_hbm,
    bank_hbm,
    labels_hbm,
    tap_hbm,
    out_factor_hbm,
    bias_hbm,
    bank_ref,
    own_ref,
    position_ref,
    weights_ref,
    mixer_ref,
    offset_ref,
    list_ref,
    slot_ref,
    labels_ref,
    tap_ref,
    out_factor_ref,
    bias_ref,
    sems,
):
    held = bank_hbm.shape[0]
    small = (
        (list_hbm, list_ref),
        (slot_hbm, slot_ref),
        (labels_hbm, labels_ref),
        (tap_hbm, tap_ref),
        (out_factor_hbm, out_factor_ref),
        (bias_hbm, bias_ref),
    )
    copies = start_copies(small + in_parts(bank_hbm, bank_ref, BANK_COPIES), sems)
    for copy in copies[: len(small)]:
        copy.wait()
    places, rows = find_rows(list_ref, slot_ref, lon_count, held)
    even = (lax.axis_index("lon") % 2) == 0
    order = list(places[0])
    order += [jnp.where(even, places[2][nth], places[1][nth]) for nth in range(PER_OWNER)]
    order += [jnp.where(even, places[1][nth], places[2][nth]) for nth in range(PER_OWNER)]
    labels = labels_ref[...]
    position = jnp.zeros(labels.shape, jnp.int32)
    for index, place in enumerate(order):
        position = jnp.where(labels == place, index, position)
    position_ref[...] = position

    rank, out_channels = out_factor_ref.shape
    half = rank // 2
    tap_rank, taps = tap_ref.shape
    shape = (tap_rank * half, taps * half)
    spread = (
        lax.broadcasted_iota(jnp.int32, (shape[0], tap_rank), 0) // half == lane_index((shape[0], tap_rank))
    ).astype(BF16)
    repeat = (
        lax.broadcasted_iota(jnp.int32, (taps, shape[1]), 0) == lane_index((taps, shape[1])) // half
    ).astype(BF16)
    tall = jnp.dot(spread, tap_ref[...], preferred_element_type=F32).astype(BF16)
    wide = jnp.dot(tall, repeat, preferred_element_type=F32)
    same = lax.broadcasted_iota(jnp.int32, shape, 0) % half == lane_index(shape) % half
    weights_ref[...] = jnp.where(same, wide, 0.0).astype(BF16)

    shape = (out_channels * GROUP, rank * GROUP)
    spread = (
        lax.broadcasted_iota(jnp.int32, (shape[0], out_channels), 0) // GROUP
        == lane_index((shape[0], out_channels))
    ).astype(BF16)
    repeat = (
        lax.broadcasted_iota(jnp.int32, (rank, shape[1]), 0) == lane_index((rank, shape[1])) % rank
    ).astype(BF16)
    tall = lax.dot_general(
        spread, out_factor_ref[...], (((1,), (1,)), ((), ())), preferred_element_type=F32
    ).astype(BF16)
    wide = jnp.dot(tall, repeat, preferred_element_type=F32)
    same = lax.broadcasted_iota(jnp.int32, shape, 0) % GROUP == lane_index(shape) // rank
    mixer_ref[...] = jnp.where(same, wide, 0.0).astype(BF16)

    shape = (out_channels * GROUP, out_channels)
    mine = lax.broadcasted_iota(jnp.int32, shape, 0) // GROUP == lane_index(shape)
    offset = jnp.sum(jnp.where(mine, bias_ref[...], 0.0), axis=1, keepdims=True)
    offset_ref[...] = jnp.broadcast_to(offset, offset_ref.shape)
    for copy in copies[len(small) :]:
        copy.wait()
    for nth in range(PER_OWNER):
        own_ref[nth] = bank_ref[rows[0][nth]]


def pick_kernel(lat_len, got_b_ref, got_a_ref, bank_ref, core_b_ref, core_a_ref, edge_ref):
    lane = lane_index((1, LANES))
    for got_ref, core_ref in ((got_b_ref, core_b_ref), (got_a_ref, core_a_ref)):
        head = got_ref[...].astype(F32)[0:1, :]
        for nth in range(PER_OWNER):
            row = jnp.sum(jnp.where(lane == EDGE * lat_len + nth, head, 0.0)).astype(jnp.int32)
            core_ref[nth] = bank_ref[row]
    even = (lax.axis_index("lon") % 2) == 0
    from_prev = lane_index(got_a_ref.shape) % EDGE < REACH
    got_a = got_a_ref[...].astype(F32)
    got_b = got_b_ref[...].astype(F32)
    edge_ref[...] = jnp.where(from_prev == even, got_b, got_a).astype(BF16)


def rows_kernel(lat_len, red_ref, edge_ref, row_a_ref, row_b_ref):
    lon_len = red_ref.shape[1] // lat_len
    even = (lax.axis_index("lat") % 2) == 0
    head = red_ref[:, : REACH * lon_len].astype(F32)
    tail = red_ref[:, (lat_len - REACH) * lon_len :].astype(F32)
    row_a_ref[:, : REACH * lon_len] = jnp.where(even, tail, head).astype(BF16)
    row_b_ref[:, : REACH * lon_len] = jnp.where(even, head, tail).astype(BF16)
    row_a_ref[:, REACH * lon_len :] = edge_ref[...]
    row_b_ref[:, REACH * lon_len :] = edge_ref[...]


def shifted_columns(row, edges, place):
    lane = lane_index(row.shape)
    lon_len = row.shape[1]
    edges = pltpu.roll(edges, (LANES - REACH - EDGE * place) % LANES, 1)
    moved = []
    for col_off in range(KS):
        shift = REACH - col_off
        if shift > 0:
            piece = pltpu.roll(jnp.where(lane >= lon_len - shift, edges, row), shift, 1)
        elif shift < 0:
            piece = pltpu.roll(jnp.where(lane < -shift, edges, row), lon_len + shift, 1)
        else:
            piece = row
        moved.append(piece.astype(BF16))
    return moved


def stack_row(stack_ref, p, moved, slots, lon_len):
    half = moved[0].shape[0] // 2
    for col_off, piece in enumerate(moved):
        for row_off in range(KS):
            slot = slots.get(p + REACH - row_off)
            if slot is not None:
                k = row_off * KS + col_off
                for h in range(2):
                    stack_ref[h, k * half : (k + 1) * half, slot * lon_len : (slot + 1) * lon_len] = piece[
                        h * half : (h + 1) * half
                    ]


def apply_taps(rank, weights_ref, stack_ref, tapped_ref, lon_len):
    half = rank // 2
    tap_rank = tapped_ref.shape[0] // rank
    width = STEP * lon_len
    for start in range(0, tapped_ref.shape[1], width):
        span = slice(start, start + width)
        parts = [
            jnp.dot(weights_ref[...], stack_ref[h, :, span], preferred_element_type=F32)
            .astype(BF16)
            .reshape(tap_rank, 1, half, width)
            for h in range(2)
        ]
        tapped_ref[:, span] = jnp.concatenate(parts, axis=1).reshape(tap_rank * rank, width)


def inner_kernel(lat_len, red_ref, edge_ref, weights_ref, tapped_ref, stack_ref):
    rank = red_ref.shape[0]
    lon_len = red_ref.shape[1] // lat_len
    slots = {p: p - REACH for p in range(REACH, lat_len - REACH)}
    edges = edge_ref[...].astype(F32)
    for p in range(lat_len):
        row = red_ref[:, p * lon_len : (p + 1) * lon_len].astype(F32)
        stack_row(stack_ref, p, shifted_columns(row, edges, p), slots, lon_len)
    apply_taps(rank, weights_ref, stack_ref, tapped_ref, lon_len)


def border_kernel(
    lat_len, lat_count, red_ref, edge_ref, row_a_ref, row_b_ref, weights_ref, tapped_ref, stack_ref
):
    rank = red_ref.shape[0]
    lon_len = red_ref.shape[1] // lat_len
    lat = lax.axis_index("lat")
    even = (lat % 2) == 0
    row_a = row_a_ref[...].astype(F32)
    row_b = row_b_ref[...].astype(F32)
    above = jnp.where(lat == 0, 0.0, jnp.where(even, row_b, row_a))
    below = jnp.where(lat == lat_count - 1, 0.0, jnp.where(even, row_a, row_b))
    slots = {p: p for p in range(REACH)}
    slots.update({lat_len - REACH + p: REACH + p for p in range(REACH)})
    edges = edge_ref[...].astype(F32)
    sources = []
    for p in range(REACH):
        sources.append((p - REACH, above[:, p * lon_len : (p + 1) * lon_len], above, lat_len - REACH + p))
        sources.append((lat_len + p, below[:, p * lon_len : (p + 1) * lon_len], below, p))
    for p in [*range(2 * REACH), *range(lat_len - 2 * REACH, lat_len)]:
        sources.append((p, red_ref[:, p * lon_len : (p + 1) * lon_len].astype(F32), None, p))
    for p, row, holder, place in sources:
        side = edges if holder is None else holder[:, REACH * lon_len :]
        stack_row(stack_ref, p, shifted_columns(row, side, place), slots, lon_len)
    apply_taps(rank, weights_ref, stack_ref, tapped_ref, lon_len)


def mix_kernel(
    inner_ref,
    border_ref,
    core_b_ref,
    core_a_ref,
    own_ref,
    position_ref,
    mixer_ref,
    offset_ref,
    out_hbm,
    stage_ref,
    sems,
):
    lat_len, lon_len = position_ref.shape
    rank = own_ref.shape[1]
    cores = jnp.concatenate(
        [ref[...].reshape(PER_OWNER * rank, -1) for ref in (own_ref, core_a_ref, core_b_ref)], axis=0
    )
    pieces = []
    for start in range(0, lat_len, STEP):
        if start < REACH:
            ref, first = border_ref, start
        elif start < lat_len - REACH:
            ref, first = inner_ref, start - REACH
        else:
            ref, first = border_ref, start - (lat_len - 2 * REACH)
        every = jnp.dot(cores, ref[:, first * lon_len : (first + STEP) * lon_len], preferred_element_type=F32)
        position = jnp.concatenate([position_ref[start + r : start + r + 1, :] for r in range(STEP)], axis=1)
        hidden = jnp.zeros((rank, STEP * lon_len), F32)
        for index in range(3 * PER_OWNER):
            hidden = jnp.where(position == index, every[index * rank : (index + 1) * rank], hidden)
        hidden = hidden.astype(BF16)
        pieces += [hidden[:, r * lon_len : (r + 1) * lon_len] for r in range(STEP)]
    groups = [jnp.concatenate(pieces[g : g + GROUP], axis=0) for g in range(0, lat_len, GROUP)]
    channels = stage_ref.shape[0]
    share = channels // OUT_COPIES
    copies = []
    for part in range(OUT_COPIES):
        span = slice(part * share * GROUP, (part + 1) * share * GROUP)
        blocks = []
        for hidden in groups:
            output = jnp.dot(mixer_ref[span, :], hidden, preferred_element_type=F32) + offset_ref[span, :]
            mixed = output / (1.0 + jnp.exp(-output))
            blocks.append(mixed.reshape(share, GROUP, lon_len))
        held = slice(part * share, (part + 1) * share)
        stage_ref[held] = jnp.concatenate(blocks, axis=1).astype(BF16)
        copy = pltpu.make_async_copy(stage_ref.at[held], out_hbm.at[held], sems.at[part])
        copy.start()
        copies.append(copy)
    for copy in copies:
        copy.wait()


def on_device(
    features, labels, tile_regions, bank_slot, kernel_bank, in_factor, tap_factor, out_factor, out_bias
):
    channels, lat_len, lon_len = features.shape
    rank = in_factor.shape[0]
    held, core_rows, core_cols = kernel_bank.shape
    tap_rank, taps = tap_factor.shape
    out_channels = out_factor.shape[0]
    cells = lat_len * lon_len
    lon_count, lat_count = lax.axis_size("lon"), lax.axis_size("lat")
    lon_first, lon_second = swap_pairs(lon_count)
    lat_first, lat_second = swap_pairs(lat_count)
    edge_shape = jax.ShapeDtypeStruct((rank, LANES), BF16)
    reduced, pay_a, pay_b = pl.pallas_call(
        functools.partial(reduce_kernel, lon_count, held),
        out_shape=(jax.ShapeDtypeStruct((rank, cells), BF16), edge_shape, edge_shape),
        in_specs=[HBM] * 4,
        out_specs=(VMEM,) * 3,
        scratch_shapes=[
            pltpu.SMEM(tile_regions.shape, jnp.int32),
            pltpu.SMEM(bank_slot.shape, jnp.int32),
            pltpu.VMEM(features.shape, BF16),
            pltpu.VMEM(in_factor.shape, BF16),
            pltpu.VMEM((channels * lat_len, lon_len), F32),
            pltpu.SemaphoreType.DMA((IN_COPIES + 3,)),
        ],
        compiler_params=PARAMS,
    )(*(in_hbm(x) for x in (tile_regions, bank_slot, features, in_factor)))
    got_b = lax.ppermute(pay_b, "lon", lon_second)
    got_a = lax.ppermute(pay_a, "lon", lon_first)
    core_shape = jax.ShapeDtypeStruct((PER_OWNER, core_rows, core_cols), BF16)
    bank, own, position, weights, mixer, offset = pl.pallas_call(
        functools.partial(prepare_kernel, lon_count, lat_len),
        out_shape=(
            jax.ShapeDtypeStruct(kernel_bank.shape, BF16),
            core_shape,
            jax.ShapeDtypeStruct(labels.shape, jnp.int32),
            jax.ShapeDtypeStruct((tap_rank * rank // 2, taps * rank // 2), BF16),
            jax.ShapeDtypeStruct((out_channels * GROUP, rank * GROUP), BF16),
            jax.ShapeDtypeStruct((out_channels * GROUP, lon_len), F32),
        ),
        in_specs=[HBM] * 8,
        out_specs=(VMEM,) * 6,
        scratch_shapes=[
            pltpu.SMEM(tile_regions.shape, jnp.int32),
            pltpu.SMEM(bank_slot.shape, jnp.int32),
            pltpu.VMEM(labels.shape, jnp.int32),
            pltpu.VMEM(tap_factor.shape, BF16),
            pltpu.VMEM(out_factor.shape[::-1], BF16),
            pltpu.VMEM((1, out_channels), F32),
            pltpu.SemaphoreType.DMA((6 + BANK_COPIES,)),
        ],
        compiler_params=PARAMS,
        cost_estimate=pl.CostEstimate(flops=10**6, bytes_accessed=kernel_bank.size * 4, transcendentals=0),
    )(
        reduced,
        *(
            in_hbm(x)
            for x in (
                tile_regions,
                bank_slot,
                kernel_bank,
                labels,
                tap_factor,
                out_factor.T,
                out_bias.reshape(1, -1),
            )
        ),
    )
    row_shape = jax.ShapeDtypeStruct((rank, REACH * lon_len + LANES), BF16)
    core_b, core_a, edges = pl.pallas_call(
        functools.partial(pick_kernel, lat_len),
        out_shape=(core_shape, core_shape, edge_shape),
        in_specs=[VMEM] * 3,
        out_specs=(VMEM,) * 3,
        compiler_params=PARAMS,
    )(got_b, got_a, bank)
    core_b = lax.ppermute(core_b, "lon", lon_second)
    core_a = lax.ppermute(core_a, "lon", lon_first)
    row_a, row_b = pl.pallas_call(
        functools.partial(rows_kernel, lat_len),
        out_shape=(row_shape, row_shape),
        in_specs=[VMEM] * 2,
        out_specs=(VMEM,) * 2,
        compiler_params=PARAMS,
    )(reduced, edges)
    row_a = lax.ppermute(row_a, "lat", lat_first)
    row_b = lax.ppermute(row_b, "lat", lat_second)
    border_cells = 2 * REACH * lon_len
    inner = pl.pallas_call(
        functools.partial(inner_kernel, lat_len),
        out_shape=jax.ShapeDtypeStruct((tap_rank * rank, cells - border_cells), BF16),
        in_specs=[VMEM] * 3,
        out_specs=VMEM,
        scratch_shapes=[pltpu.VMEM((2, taps * rank // 2, cells - border_cells), BF16)],
        compiler_params=PARAMS,
    )(reduced, edges, weights)
    border = pl.pallas_call(
        functools.partial(border_kernel, lat_len, lat_count),
        out_shape=jax.ShapeDtypeStruct((tap_rank * rank, border_cells), BF16),
        in_specs=[VMEM] * 5,
        out_specs=VMEM,
        scratch_shapes=[pltpu.VMEM((2, taps * rank // 2, border_cells), BF16)],
        compiler_params=PARAMS,
    )(reduced, edges, row_a, row_b, weights)
    out_shape = (out_channels, lat_len, lon_len)
    return pl.pallas_call(
        mix_kernel,
        out_shape=jax.ShapeDtypeStruct(out_shape, BF16),
        in_specs=[VMEM] * 8,
        out_specs=HBM,
        scratch_shapes=[pltpu.VMEM(out_shape, BF16), pltpu.SemaphoreType.DMA((OUT_COPIES,))],
        compiler_params=PARAMS,
    )(inner, border, core_b, core_a, own, position, mixer, offset)


def solution(mesh):
    placed = (
        P(None, "lat", "lon"),
        P("lat", "lon"),
        P("lat", "lon", None),
        P(),
        P("lon", None, None),
        P(),
        P(),
        P(),
        P(),
    )
    return jax.shard_map(
        on_device, mesh=mesh, in_specs=placed, out_specs=P(None, "lat", "lon"), check_vma=False
    )
```

```python
import functools

import jax
import jax.numpy as jnp
from jax import lax
from jax.experimental import pallas as pl
from jax.experimental.pallas import tpu as pltpu
from jax.sharding import PartitionSpec as P

KS = 5
REACH = KS // 2
PER_OWNER = 2
LANES = 128
EDGE = 2 * REACH
GROUP = 8
STEP = 2
OUT_COPIES = 4
IN_COPIES = 4
BANK_COPIES = 8
F32 = jnp.float32
BF16 = jnp.bfloat16
VMEM = pl.BlockSpec(memory_space=pltpu.VMEM)
SMEM = pl.BlockSpec(memory_space=pltpu.SMEM)
HBM = pl.BlockSpec(memory_space=pltpu.HBM)
PARAMS = pltpu.CompilerParams(vmem_limit_bytes=24 * 1024 * 1024)


def swap_pairs(count):
    first = [(i, i ^ 1) for i in range(count)]
    second = [(i, (i + 1 if i % 2 else i - 1) % count) for i in range(count)]
    return first, second


def in_hbm(array):
    return pltpu.with_memory_space_constraint(array, pltpu.HBM)


def lane_index(shape):
    return lax.broadcasted_iota(jnp.int32, shape, 1)


def start_copies(pairs, sems):
    copies = [pltpu.make_async_copy(source, target, sems.at[i]) for i, (source, target) in enumerate(pairs)]
    for copy in copies:
        copy.start()
    return copies


def in_parts(source, target, count):
    share = target.shape[0] // count
    return tuple((source.at[pl.ds(i * share, share)], target.at[pl.ds(i * share, share)]) for i in range(count))


def find_rows(list_ref, slot_ref, lon_count, held):
    me = lax.axis_index("lon")
    owners = (me, lax.rem(me + lon_count - 1, lon_count), lax.rem(me + 1, lon_count))
    counts = [jnp.int32(0)] * 3
    places = [[jnp.int32(0)] * PER_OWNER for _ in range(3)]
    rows = [[jnp.int32(0)] * PER_OWNER for _ in range(3)]
    for i in range(list_ref.shape[2]):
        slot = slot_ref[list_ref[0, 0, i]]
        for group, owner in enumerate(owners):
            local = slot - owner * held
            hit = (local >= 0) & (local < held)
            for nth in range(PER_OWNER):
                take = hit & (counts[group] == nth)
                places[group][nth] = jnp.where(take, i, places[group][nth])
                rows[group][nth] = jnp.where(take, local, rows[group][nth])
            counts[group] = counts[group] + hit.astype(jnp.int32)
    return places, rows


def edge_kernel(
    lon_count,
    held,
    list_hbm,
    slot_hbm,
    feat_hbm,
    in_hbm,
    pay_a_ref,
    pay_b_ref,
    list_ref,
    slot_ref,
    feat_ref,
    in_ref,
    turned_ref,
    sems,
):
    channels, lat_len, lon_len = feat_ref.shape
    rank = in_ref.shape[0]
    pairs = in_parts(feat_hbm, feat_ref, IN_COPIES)
    pairs += ((slot_hbm, slot_ref), (list_hbm, list_ref), (in_hbm, in_ref))
    for copy in start_copies(pairs, sems):
        copy.wait()
    lane = lane_index((lat_len, LANES))
    batch = LANES // EDGE
    for first in range(0, channels, batch):
        packed = jnp.zeros((lat_len, LANES), F32)
        for c in range(batch):
            moved = pltpu.roll(feat_ref[first + c].astype(F32), (EDGE * c + REACH) % LANES, 1)
            packed = jnp.where(lane // EDGE == c, moved, packed)
        turned_ref[first * EDGE : (first + batch) * EDGE, :] = jnp.transpose(packed)
    columns = jnp.concatenate(
        [turned_ref[pl.ds(j, channels, stride=EDGE), :].astype(BF16) for j in range(EDGE)], axis=1
    )
    edges = jnp.dot(in_ref[...], columns, preferred_element_type=F32)
    edges = jnp.concatenate([edges, jnp.zeros((rank, LANES - EDGE * lat_len), F32)], axis=1)
    _, rows = find_rows(list_ref, slot_ref, lon_count, held)
    even = (lax.axis_index("lon") % 2) == 0
    lane = lane_index((rank, LANES))
    for out_ref, wanted in ((pay_a_ref, even), (pay_b_ref, jnp.logical_not(even))):
        load = edges
        for nth in range(PER_OWNER):
            row = jnp.where(wanted, rows[2][nth], rows[1][nth]).astype(F32)
            load = jnp.where(lane == EDGE * lat_len + nth, row, load)
        out_ref[...] = load.astype(BF16)


def prepare_kernel(
    lon_count,
    lat_len,
    pay_hbm,
    list_hbm,
    slot_hbm,
    feat_hbm,
    in_hbm,
    bank_hbm,
    labels_hbm,
    tap_hbm,
    out_factor_hbm,
    bias_hbm,
    red_ref,
    bank_ref,
    own_ref,
    position_ref,
    weights_ref,
    mixer_ref,
    offset_ref,
    list_ref,
    slot_ref,
    labels_ref,
    tap_ref,
    out_factor_ref,
    bias_ref,
    feat_ref,
    in_ref,
    rows_ref,
    sems,
):
    held = bank_hbm.shape[0]
    small = (
        (list_hbm, list_ref),
        (slot_hbm, slot_ref),
        (labels_hbm, labels_ref),
        (tap_hbm, tap_ref),
        (out_factor_hbm, out_factor_ref),
        (bias_hbm, bias_ref),
        (in_hbm, in_ref),
        (feat_hbm, feat_ref),
    )
    copies = start_copies(small + in_parts(bank_hbm, bank_ref, BANK_COPIES), sems)
    for copy in copies[: len(small)]:
        copy.wait()
    channels, lon_len = feat_ref.shape[0], feat_ref.shape[2]
    rows_ref[...] = feat_ref[...].astype(F32).reshape(channels * lat_len, lon_len)
    cells = jnp.concatenate(
        [rows_ref[pl.ds(p, channels, stride=lat_len), :].astype(BF16) for p in range(lat_len)], axis=1
    )
    red_ref[...] = jnp.dot(in_ref[...], cells, preferred_element_type=F32).astype(BF16)
    places, rows = find_rows(list_ref, slot_ref, lon_count, held)
    even = (lax.axis_index("lon") % 2) == 0
    order = list(places[0])
    order += [jnp.where(even, places[2][nth], places[1][nth]) for nth in range(PER_OWNER)]
    order += [jnp.where(even, places[1][nth], places[2][nth]) for nth in range(PER_OWNER)]
    labels = labels_ref[...]
    position = jnp.zeros(labels.shape, jnp.int32)
    for index, place in enumerate(order):
        position = jnp.where(labels == place, index, position)
    position_ref[...] = position

    rank, out_channels = out_factor_ref.shape
    half = rank // 2
    tap_rank, taps = tap_ref.shape
    shape = (tap_rank * half, taps * half)
    spread = (
        lax.broadcasted_iota(jnp.int32, (shape[0], tap_rank), 0) // half == lane_index((shape[0], tap_rank))
    ).astype(BF16)
    repeat = (
        lax.broadcasted_iota(jnp.int32, (taps, shape[1]), 0) == lane_index((taps, shape[1])) // half
    ).astype(BF16)
    tall = jnp.dot(spread, tap_ref[...], preferred_element_type=F32).astype(BF16)
    wide = jnp.dot(tall, repeat, preferred_element_type=F32)
    same = lax.broadcasted_iota(jnp.int32, shape, 0) % half == lane_index(shape) % half
    weights_ref[...] = jnp.where(same, wide, 0.0).astype(BF16)

    shape = (out_channels * GROUP, rank * GROUP)
    spread = (
        lax.broadcasted_iota(jnp.int32, (shape[0], out_channels), 0) // GROUP
        == lane_index((shape[0], out_channels))
    ).astype(BF16)
    repeat = (
        lax.broadcasted_iota(jnp.int32, (rank, shape[1]), 0) == lane_index((rank, shape[1])) % rank
    ).astype(BF16)
    tall = lax.dot_general(
        spread, out_factor_ref[...], (((1,), (1,)), ((), ())), preferred_element_type=F32
    ).astype(BF16)
    wide = jnp.dot(tall, repeat, preferred_element_type=F32)
    same = lax.broadcasted_iota(jnp.int32, shape, 0) % GROUP == lane_index(shape) // rank
    mixer_ref[...] = jnp.where(same, wide, 0.0).astype(BF16)

    shape = (out_channels * GROUP, out_channels)
    mine = lax.broadcasted_iota(jnp.int32, shape, 0) // GROUP == lane_index(shape)
    offset = jnp.sum(jnp.where(mine, bias_ref[...], 0.0), axis=1, keepdims=True)
    offset_ref[...] = jnp.broadcast_to(offset, offset_ref.shape)
    for copy in copies[len(small) :]:
        copy.wait()
    for nth in range(PER_OWNER):
        own_ref[nth] = bank_ref[rows[0][nth]]


def pick_kernel(lat_len, got_b_ref, got_a_ref, bank_ref, core_b_ref, core_a_ref):
    lane = lane_index((1, LANES))
    for got_ref, core_ref in ((got_b_ref, core_b_ref), (got_a_ref, core_a_ref)):
        head = got_ref[...].astype(F32)[0:1, :]
        for nth in range(PER_OWNER):
            row = jnp.sum(jnp.where(lane == EDGE * lat_len + nth, head, 0.0)).astype(jnp.int32)
            core_ref[nth] = bank_ref[row]


def rows_kernel(lat_len, got_b_ref, got_a_ref, core_ref, red_ref, edge_ref, row_a_ref, row_b_ref):
    lon_len = red_ref.shape[1] // lat_len
    even = (lax.axis_index("lon") % 2) == 0
    from_prev = lane_index(got_a_ref.shape) < REACH * lat_len
    got = jnp.where(from_prev == even, got_b_ref[...].astype(F32), got_a_ref[...].astype(F32)).astype(BF16)
    source = lax.broadcasted_iota(jnp.int32, (LANES, LANES), 0)
    target = lane_index((LANES, LANES))
    order = (source == (target % EDGE) * lat_len + target // EDGE) & (target < EDGE * lat_len)
    edges = jnp.dot(got, order.astype(BF16), preferred_element_type=F32).astype(BF16)
    edge_ref[...] = edges
    even = (lax.axis_index("lat") % 2) == 0
    head = red_ref[:, : REACH * lon_len].astype(F32)
    tail = red_ref[:, (lat_len - REACH) * lon_len :].astype(F32)
    row_a_ref[:, : REACH * lon_len] = jnp.where(even, tail, head).astype(BF16)
    row_b_ref[:, : REACH * lon_len] = jnp.where(even, head, tail).astype(BF16)
    row_a_ref[:, REACH * lon_len :] = edges
    row_b_ref[:, REACH * lon_len :] = edges


def shifted_columns(row, edges, place):
    lane = lane_index(row.shape)
    lon_len = row.shape[1]
    edges = pltpu.roll(edges, (LANES - REACH - EDGE * place) % LANES, 1)
    moved = []
    for col_off in range(KS):
        shift = REACH - col_off
        if shift > 0:
            piece = pltpu.roll(jnp.where(lane >= lon_len - shift, edges, row), shift, 1)
        elif shift < 0:
            piece = pltpu.roll(jnp.where(lane < -shift, edges, row), lon_len + shift, 1)
        else:
            piece = row
        moved.append(piece.astype(BF16))
    return moved


def stack_row(stack_ref, p, moved, slots, lon_len):
    half = moved[0].shape[0] // 2
    for col_off, piece in enumerate(moved):
        for row_off in range(KS):
            slot = slots.get(p + REACH - row_off)
            if slot is not None:
                k = row_off * KS + col_off
                for h in range(2):
                    stack_ref[h, k * half : (k + 1) * half, slot * lon_len : (slot + 1) * lon_len] = piece[
                        h * half : (h + 1) * half
                    ]


def apply_taps(rank, weights_ref, stacked, tapped_ref, lon_len):
    half = rank // 2
    tap_rank = tapped_ref.shape[0] // rank
    width = STEP * lon_len
    for start in range(0, tapped_ref.shape[1], width):
        parts = [
            jnp.dot(weights_ref[...], stacked(h, start, width), preferred_element_type=F32)
            .astype(BF16)
            .reshape(tap_rank, 1, half, width)
            for h in range(2)
        ]
        tapped_ref[:, start : start + width] = jnp.concatenate(parts, axis=1).reshape(tap_rank * rank, width)


def border_slots(lat_len):
    slots = {p: p for p in range(REACH)}
    slots.update({lat_len - REACH + p: REACH + p for p in range(REACH)})
    return slots


def inner_kernel(lat_len, red_ref, edge_ref, weights_ref, tapped_ref, halo_stack_ref, stack_ref):
    rank = red_ref.shape[0]
    lon_len = red_ref.shape[1] // lat_len
    slots = {p: p - REACH for p in range(REACH, lat_len - REACH)}
    edges = edge_ref[...].astype(F32)
    for p in range(lat_len):
        row = red_ref[:, p * lon_len : (p + 1) * lon_len].astype(F32)
        moved = shifted_columns(row, edges, p)
        stack_row(stack_ref, p, moved, slots, lon_len)
        stack_row(halo_stack_ref, p, moved, border_slots(lat_len), lon_len)
    apply_taps(rank, weights_ref, lambda h, start, width: stack_ref[h, :, start : start + width], tapped_ref, lon_len)


def border_kernel(lat_len, lat_count, row_a_ref, row_b_ref, weights_ref, own_stack_ref, tapped_ref, stack_ref):
    rank = row_a_ref.shape[0]
    lon_len = (row_a_ref.shape[1] - LANES) // REACH
    lat = lax.axis_index("lat")
    even = (lat % 2) == 0
    row_a = row_a_ref[...].astype(F32)
    row_b = row_b_ref[...].astype(F32)
    above = jnp.where(lat == 0, 0.0, jnp.where(even, row_b, row_a))
    below = jnp.where(lat == lat_count - 1, 0.0, jnp.where(even, row_a, row_b))
    slots = border_slots(lat_len)
    for i in range(REACH):
        for p, holder, place in ((i - REACH, above, lat_len - REACH + i), (lat_len + i, below, i)):
            row = holder[:, i * lon_len : (i + 1) * lon_len]
            moved = shifted_columns(row, holder[:, REACH * lon_len :], place)
            stack_row(stack_ref, p, moved, slots, lon_len)
    block = KS * rank // 2
    in_halo = {
        (slot, row_off)
        for p, slot in slots.items()
        for row_off in range(KS)
        if not 0 <= p + row_off - REACH < lat_len
    }

    def stacked(h, start, width):
        columns = []
        for slot in range(start // lon_len, (start + width) // lon_len):
            span = slice(slot * lon_len, (slot + 1) * lon_len)
            pieces = []
            for row_off in range(KS):
                ref = stack_ref if (slot, row_off) in in_halo else own_stack_ref
                pieces.append(ref[h, row_off * block : (row_off + 1) * block, span])
            columns.append(jnp.concatenate(pieces, axis=0))
        return jnp.concatenate(columns, axis=1)

    apply_taps(rank, weights_ref, stacked, tapped_ref, lon_len)


def mix_kernel(
    inner_ref,
    border_ref,
    core_b_ref,
    core_a_ref,
    own_ref,
    position_ref,
    mixer_ref,
    offset_ref,
    out_hbm,
    stage_ref,
    sems,
):
    lat_len, lon_len = position_ref.shape
    rank = own_ref.shape[1]
    cores = jnp.concatenate(
        [ref[...].reshape(PER_OWNER * rank, -1) for ref in (own_ref, core_a_ref, core_b_ref)], axis=0
    )
    pieces = []
    for start in range(0, lat_len, STEP):
        if start < REACH:
            ref, first = border_ref, start
        elif start < lat_len - REACH:
            ref, first = inner_ref, start - REACH
        else:
            ref, first = border_ref, start - (lat_len - 2 * REACH)
        every = jnp.dot(cores, ref[:, first * lon_len : (first + STEP) * lon_len], preferred_element_type=F32)
        position = jnp.concatenate([position_ref[start + r : start + r + 1, :] for r in range(STEP)], axis=1)
        hidden = jnp.zeros((rank, STEP * lon_len), F32)
        for index in range(3 * PER_OWNER):
            hidden = jnp.where(position == index, every[index * rank : (index + 1) * rank], hidden)
        hidden = hidden.astype(BF16)
        pieces += [hidden[:, r * lon_len : (r + 1) * lon_len] for r in range(STEP)]
    groups = [jnp.concatenate(pieces[g : g + GROUP], axis=0) for g in range(0, lat_len, GROUP)]
    channels = stage_ref.shape[0]
    share = channels // OUT_COPIES
    copies = []
    for part in range(OUT_COPIES):
        span = slice(part * share * GROUP, (part + 1) * share * GROUP)
        blocks = []
        for hidden in groups:
            output = jnp.dot(mixer_ref[span, :], hidden, preferred_element_type=F32) + offset_ref[span, :]
            mixed = 0.5 * output * (1.0 + jnp.tanh(0.5 * output))
            blocks.append(mixed.reshape(share, GROUP, lon_len))
        held = slice(part * share, (part + 1) * share)
        stage_ref[held] = jnp.concatenate(blocks, axis=1).astype(BF16)
        copy = pltpu.make_async_copy(stage_ref.at[held], out_hbm.at[held], sems.at[part])
        copy.start()
        copies.append(copy)
    for copy in copies:
        copy.wait()


def on_device(
    features, labels, tile_regions, bank_slot, kernel_bank, in_factor, tap_factor, out_factor, out_bias
):
    channels, lat_len, lon_len = features.shape
    rank = in_factor.shape[0]
    held, core_rows, core_cols = kernel_bank.shape
    tap_rank, taps = tap_factor.shape
    out_channels = out_factor.shape[0]
    cells = lat_len * lon_len
    lon_count, lat_count = lax.axis_size("lon"), lax.axis_size("lat")
    lon_first, lon_second = swap_pairs(lon_count)
    lat_first, lat_second = swap_pairs(lat_count)
    edge_shape = jax.ShapeDtypeStruct((rank, LANES), BF16)
    pay_a, pay_b = pl.pallas_call(
        functools.partial(edge_kernel, lon_count, held),
        out_shape=(edge_shape, edge_shape),
        in_specs=[HBM] * 4,
        out_specs=(VMEM,) * 2,
        scratch_shapes=[
            pltpu.SMEM(tile_regions.shape, jnp.int32),
            pltpu.SMEM(bank_slot.shape, jnp.int32),
            pltpu.VMEM(features.shape, BF16),
            pltpu.VMEM(in_factor.shape, BF16),
            pltpu.VMEM((channels * EDGE, lat_len), F32),
            pltpu.SemaphoreType.DMA((IN_COPIES + 3,)),
        ],
        compiler_params=PARAMS,
    )(*(in_hbm(x) for x in (tile_regions, bank_slot, features, in_factor)))
    got_b = lax.ppermute(pay_b, "lon", lon_second)
    got_a = lax.ppermute(pay_a, "lon", lon_first)
    core_shape = jax.ShapeDtypeStruct((PER_OWNER, core_rows, core_cols), BF16)
    reduced, bank, own, position, weights, mixer, offset = pl.pallas_call(
        functools.partial(prepare_kernel, lon_count, lat_len),
        out_shape=(
            jax.ShapeDtypeStruct((rank, cells), BF16),
            jax.ShapeDtypeStruct(kernel_bank.shape, BF16),
            core_shape,
            jax.ShapeDtypeStruct(labels.shape, jnp.int32),
            jax.ShapeDtypeStruct((tap_rank * rank // 2, taps * rank // 2), BF16),
            jax.ShapeDtypeStruct((out_channels * GROUP, rank * GROUP), BF16),
            jax.ShapeDtypeStruct((out_channels * GROUP, lon_len), F32),
        ),
        in_specs=[HBM] * 10,
        out_specs=(VMEM,) * 7,
        scratch_shapes=[
            pltpu.SMEM(tile_regions.shape, jnp.int32),
            pltpu.SMEM(bank_slot.shape, jnp.int32),
            pltpu.VMEM(labels.shape, jnp.int32),
            pltpu.VMEM(tap_factor.shape, BF16),
            pltpu.VMEM(out_factor.shape[::-1], BF16),
            pltpu.VMEM((1, out_channels), F32),
            pltpu.VMEM(features.shape, BF16),
            pltpu.VMEM(in_factor.shape, BF16),
            pltpu.VMEM((channels * lat_len, lon_len), F32),
            pltpu.SemaphoreType.DMA((8 + BANK_COPIES,)),
        ],
        compiler_params=PARAMS,
        cost_estimate=pl.CostEstimate(flops=10**6, bytes_accessed=kernel_bank.size * 4, transcendentals=0),
    )(
        pay_a,
        *(
            in_hbm(x)
            for x in (
                tile_regions,
                bank_slot,
                features,
                in_factor,
                kernel_bank,
                labels,
                tap_factor,
                out_factor.T,
                out_bias.reshape(1, -1),
            )
        ),
    )
    row_shape = jax.ShapeDtypeStruct((rank, REACH * lon_len + LANES), BF16)
    core_b, core_a = pl.pallas_call(
        functools.partial(pick_kernel, lat_len),
        out_shape=(core_shape, core_shape),
        in_specs=[VMEM] * 3,
        out_specs=(VMEM,) * 2,
        compiler_params=PARAMS,
    )(got_b, got_a, bank)
    edges, row_a, row_b = pl.pallas_call(
        functools.partial(rows_kernel, lat_len),
        out_shape=(edge_shape, row_shape, row_shape),
        in_specs=[VMEM, VMEM, HBM, VMEM],
        out_specs=(VMEM,) * 3,
        compiler_params=PARAMS,
    )(got_b, got_a, core_a, reduced)
    core_b = lax.ppermute(core_b, "lon", lon_second)
    core_a = lax.ppermute(core_a, "lon", lon_first)
    row_a = lax.ppermute(row_a, "lat", lat_first)
    row_b = lax.ppermute(row_b, "lat", lat_second)
    border_cells = 2 * REACH * lon_len
    stack_rows = taps * rank // 2
    halo_stack_shape = jax.ShapeDtypeStruct((2, stack_rows, border_cells), BF16)
    inner, halo_stack = pl.pallas_call(
        functools.partial(inner_kernel, lat_len),
        out_shape=(jax.ShapeDtypeStruct((tap_rank * rank, cells - border_cells), BF16), halo_stack_shape),
        in_specs=[VMEM] * 3,
        out_specs=(VMEM,) * 2,
        scratch_shapes=[pltpu.VMEM((2, stack_rows, cells - border_cells), BF16)],
        compiler_params=PARAMS,
    )(reduced, edges, weights)
    border = pl.pallas_call(
        functools.partial(border_kernel, lat_len, lat_count),
        out_shape=jax.ShapeDtypeStruct((tap_rank * rank, border_cells), BF16),
        in_specs=[VMEM] * 4,
        out_specs=VMEM,
        scratch_shapes=[pltpu.VMEM(halo_stack_shape.shape, BF16)],
        compiler_params=PARAMS,
    )(row_a, row_b, weights, halo_stack)
    out_shape = (out_channels, lat_len, lon_len)
    return pl.pallas_call(
        mix_kernel,
        out_shape=jax.ShapeDtypeStruct(out_shape, BF16),
        in_specs=[VMEM] * 8,
        out_specs=HBM,
        scratch_shapes=[pltpu.VMEM(out_shape, BF16), pltpu.SemaphoreType.DMA((OUT_COPIES,))],
        compiler_params=PARAMS,
    )(inner, border, core_b, core_a, own, position, mixer, offset)


def solution(mesh):
    placed = (
        P(None, "lat", "lon"),
        P("lat", "lon"),
        P("lat", "lon", None),
        P(),
        P("lon", None, None),
        P(),
        P(),
        P(),
        P(),
    )
    return jax.shard_map(
        on_device, mesh=mesh, in_specs=placed, out_specs=P(None, "lat", "lon"), check_vma=False
    )
```

```python
import functools

import jax
import jax.numpy as jnp
from jax import lax
from jax.experimental import pallas as pl
from jax.experimental.pallas import tpu as pltpu
from jax.sharding import PartitionSpec as P

KS = 5
REACH = KS // 2
PER_OWNER = 2
LANES = 128
EDGE = 2 * REACH
GROUP = 8
STEP = 2
OUT_COPIES = 4
BANK_COPIES = 8
F32 = jnp.float32
BF16 = jnp.bfloat16
VMEM = pl.BlockSpec(memory_space=pltpu.VMEM)
SMEM = pl.BlockSpec(memory_space=pltpu.SMEM)
HBM = pl.BlockSpec(memory_space=pltpu.HBM)
PARAMS = pltpu.CompilerParams(vmem_limit_bytes=24 * 1024 * 1024)


def swap_pairs(count):
    first = [(i, i ^ 1) for i in range(count)]
    second = [(i, (i + 1 if i % 2 else i - 1) % count) for i in range(count)]
    return first, second


def in_hbm(array):
    return pltpu.with_memory_space_constraint(array, pltpu.HBM)


def lane_index(shape):
    return lax.broadcasted_iota(jnp.int32, shape, 1)


def start_copies(pairs, sems):
    copies = [pltpu.make_async_copy(source, target, sems.at[i]) for i, (source, target) in enumerate(pairs)]
    for copy in copies:
        copy.start()
    return copies


def in_parts(source, target, count):
    share = target.shape[0] // count
    return tuple((source.at[pl.ds(i * share, share)], target.at[pl.ds(i * share, share)]) for i in range(count))


def find_rows(list_ref, slot_ref, lon_count, held):
    me = lax.axis_index("lon")
    owners = (me, lax.rem(me + lon_count - 1, lon_count), lax.rem(me + 1, lon_count))
    counts = [jnp.int32(0)] * 3
    places = [[jnp.int32(0)] * PER_OWNER for _ in range(3)]
    rows = [[jnp.int32(0)] * PER_OWNER for _ in range(3)]
    for i in range(list_ref.shape[2]):
        slot = slot_ref[list_ref[0, 0, i]]
        for group, owner in enumerate(owners):
            local = slot - owner * held
            hit = (local >= 0) & (local < held)
            for nth in range(PER_OWNER):
                take = hit & (counts[group] == nth)
                places[group][nth] = jnp.where(take, i, places[group][nth])
                rows[group][nth] = jnp.where(take, local, rows[group][nth])
            counts[group] = counts[group] + hit.astype(jnp.int32)
    return places, rows


def edge_kernel(
    lon_count,
    held,
    list_hbm,
    slot_hbm,
    feat_hbm,
    in_hbm,
    pay_a_ref,
    pay_b_ref,
    list_ref,
    slot_ref,
    feat_ref,
    in_ref,
    turned_ref,
    sems,
):
    channels, lat_len, lon_len = feat_ref.shape
    rank = in_ref.shape[0]
    batch = LANES // EDGE
    parts = channels // batch
    pairs = ((slot_hbm, slot_ref), (list_hbm, list_ref)) + in_parts(feat_hbm, feat_ref, parts) + ((in_hbm, in_ref),)
    copies = start_copies(pairs, sems)
    for copy in copies[:2]:
        copy.wait()
    _, rows = find_rows(list_ref, slot_ref, lon_count, held)
    even = (lax.axis_index("lon") % 2) == 0
    asked = []
    for wanted in (even, jnp.logical_not(even)):
        asked.append([jnp.where(wanted, rows[2][nth], rows[1][nth]).astype(F32) for nth in range(PER_OWNER)])
    lane = lane_index((lat_len, LANES))
    for part in range(parts):
        copies[2 + part].wait()
        packed = jnp.zeros((lat_len, LANES), F32)
        for c in range(batch):
            moved = pltpu.roll(feat_ref[part * batch + c].astype(F32), (EDGE * c + REACH) % LANES, 1)
            packed = jnp.where(lane // EDGE == c, moved, packed)
        turned_ref[part * LANES : (part + 1) * LANES, :] = jnp.transpose(packed)
    columns = jnp.concatenate(
        [turned_ref[pl.ds(j, channels, stride=EDGE), :].astype(BF16) for j in range(EDGE)], axis=1
    )
    copies[2 + parts].wait()
    edges = jnp.dot(in_ref[...], columns, preferred_element_type=F32)
    edges = jnp.concatenate([edges, jnp.zeros((rank, LANES - EDGE * lat_len), F32)], axis=1)
    lane = lane_index((rank, LANES))
    for out_ref, ask in ((pay_a_ref, asked[0]), (pay_b_ref, asked[1])):
        load = edges
        for nth in range(PER_OWNER):
            load = jnp.where(lane == EDGE * lat_len + nth, ask[nth], load)
        out_ref[...] = load.astype(BF16)


def prepare_kernel(
    lon_count,
    lat_len,
    pay_hbm,
    list_hbm,
    slot_hbm,
    feat_hbm,
    in_hbm,
    bank_hbm,
    labels_hbm,
    tap_hbm,
    out_factor_hbm,
    bias_hbm,
    red_ref,
    bank_ref,
    own_ref,
    position_ref,
    weights_ref,
    mixer_ref,
    offset_ref,
    list_ref,
    slot_ref,
    labels_ref,
    tap_ref,
    out_factor_ref,
    bias_ref,
    feat_ref,
    in_ref,
    rows_ref,
    sems,
):
    held = bank_hbm.shape[0]
    small = (
        (list_hbm, list_ref),
        (slot_hbm, slot_ref),
        (labels_hbm, labels_ref),
        (tap_hbm, tap_ref),
        (out_factor_hbm, out_factor_ref),
        (bias_hbm, bias_ref),
        (in_hbm, in_ref),
        (feat_hbm, feat_ref),
    )
    copies = start_copies(small + in_parts(bank_hbm, bank_ref, BANK_COPIES), sems)
    for copy in copies[: len(small)]:
        copy.wait()
    channels, lon_len = feat_ref.shape[0], feat_ref.shape[2]
    rows_ref[...] = feat_ref[...].astype(F32).reshape(channels * lat_len, lon_len)
    cells = jnp.concatenate(
        [rows_ref[pl.ds(p, channels, stride=lat_len), :].astype(BF16) for p in range(lat_len)], axis=1
    )
    red_ref[...] = jnp.dot(in_ref[...], cells, preferred_element_type=F32).astype(BF16)
    places, rows = find_rows(list_ref, slot_ref, lon_count, held)
    even = (lax.axis_index("lon") % 2) == 0
    order = list(places[0])
    order += [jnp.where(even, places[2][nth], places[1][nth]) for nth in range(PER_OWNER)]
    order += [jnp.where(even, places[1][nth], places[2][nth]) for nth in range(PER_OWNER)]
    labels = labels_ref[...]
    position = jnp.zeros(labels.shape, jnp.int32)
    for index, place in enumerate(order):
        position = jnp.where(labels == place, index, position)
    position_ref[...] = position

    rank, out_channels = out_factor_ref.shape
    half = rank // 2
    tap_rank, taps = tap_ref.shape
    shape = (tap_rank * half, taps * half)
    spread = (
        lax.broadcasted_iota(jnp.int32, (shape[0], tap_rank), 0) // half == lane_index((shape[0], tap_rank))
    ).astype(BF16)
    repeat = (
        lax.broadcasted_iota(jnp.int32, (taps, shape[1]), 0) == lane_index((taps, shape[1])) // half
    ).astype(BF16)
    tall = jnp.dot(spread, tap_ref[...], preferred_element_type=F32).astype(BF16)
    wide = jnp.dot(tall, repeat, preferred_element_type=F32)
    same = lax.broadcasted_iota(jnp.int32, shape, 0) % half == lane_index(shape) % half
    weights_ref[...] = jnp.where(same, wide, 0.0).astype(BF16)

    shape = (out_channels * GROUP, rank * GROUP)
    spread = (
        lax.broadcasted_iota(jnp.int32, (shape[0], out_channels), 0) // GROUP
        == lane_index((shape[0], out_channels))
    ).astype(BF16)
    repeat = (
        lax.broadcasted_iota(jnp.int32, (rank, shape[1]), 0) == lane_index((rank, shape[1])) % rank
    ).astype(BF16)
    tall = lax.dot_general(
        spread, out_factor_ref[...], (((1,), (1,)), ((), ())), preferred_element_type=F32
    ).astype(BF16)
    wide = jnp.dot(tall, repeat, preferred_element_type=F32)
    same = lax.broadcasted_iota(jnp.int32, shape, 0) % GROUP == lane_index(shape) // rank
    mixer_ref[...] = jnp.where(same, wide, 0.0).astype(BF16)

    shape = (out_channels * GROUP, out_channels)
    mine = lax.broadcasted_iota(jnp.int32, shape, 0) // GROUP == lane_index(shape)
    offset = jnp.sum(jnp.where(mine, bias_ref[...], 0.0), axis=1, keepdims=True)
    offset_ref[...] = jnp.broadcast_to(offset, offset_ref.shape)
    for copy in copies[len(small) :]:
        copy.wait()
    for nth in range(PER_OWNER):
        own_ref[nth] = bank_ref[rows[0][nth]]


def pick_kernel(lat_len, got_b_ref, got_a_ref, bank_ref, core_b_ref, core_a_ref):
    lane = lane_index((1, LANES))
    for got_ref, core_ref in ((got_b_ref, core_b_ref), (got_a_ref, core_a_ref)):
        head = got_ref[...].astype(F32)[0:1, :]
        for nth in range(PER_OWNER):
            row = jnp.sum(jnp.where(lane == EDGE * lat_len + nth, head, 0.0)).astype(jnp.int32)
            core_ref[nth] = bank_ref[row]


def rows_kernel(lat_len, got_b_ref, got_a_ref, core_ref, red_ref, edge_ref, row_a_ref, row_b_ref):
    lon_len = red_ref.shape[1] // lat_len
    even = (lax.axis_index("lon") % 2) == 0
    from_prev = lane_index(got_a_ref.shape) < REACH * lat_len
    got = jnp.where(from_prev == even, got_b_ref[...].astype(F32), got_a_ref[...].astype(F32)).astype(BF16)
    source = lax.broadcasted_iota(jnp.int32, (LANES, LANES), 0)
    target = lane_index((LANES, LANES))
    order = (source == (target % EDGE) * lat_len + target // EDGE) & (target < EDGE * lat_len)
    edges = jnp.dot(got, order.astype(BF16), preferred_element_type=F32).astype(BF16)
    edge_ref[...] = edges
    even = (lax.axis_index("lat") % 2) == 0
    head = red_ref[:, : REACH * lon_len].astype(F32)
    tail = red_ref[:, (lat_len - REACH) * lon_len :].astype(F32)
    row_a_ref[:, : REACH * lon_len] = jnp.where(even, tail, head).astype(BF16)
    row_b_ref[:, : REACH * lon_len] = jnp.where(even, head, tail).astype(BF16)
    row_a_ref[:, REACH * lon_len :] = edges
    row_b_ref[:, REACH * lon_len :] = edges


def shifted_columns(row, edges, place):
    lane = lane_index(row.shape)
    lon_len = row.shape[1]
    edges = pltpu.roll(edges, (LANES - REACH - EDGE * place) % LANES, 1)
    moved = []
    for col_off in range(KS):
        shift = REACH - col_off
        if shift > 0:
            piece = pltpu.roll(jnp.where(lane >= lon_len - shift, edges, row), shift, 1)
        elif shift < 0:
            piece = pltpu.roll(jnp.where(lane < -shift, edges, row), lon_len + shift, 1)
        else:
            piece = row
        moved.append(piece.astype(BF16))
    return moved


def stack_row(stack_ref, p, moved, slots, lon_len):
    half = moved[0].shape[0] // 2
    for col_off, piece in enumerate(moved):
        for row_off in range(KS):
            slot = slots.get(p + REACH - row_off)
            if slot is not None:
                k = row_off * KS + col_off
                for h in range(2):
                    stack_ref[h, k * half : (k + 1) * half, slot * lon_len : (slot + 1) * lon_len] = piece[
                        h * half : (h + 1) * half
                    ]


def apply_taps(rank, weights_ref, stacked, tapped_ref, lon_len, then=None):
    half = rank // 2
    tap_rank = tapped_ref.shape[0] // rank
    width = STEP * lon_len
    for start in range(0, tapped_ref.shape[1], width):
        parts = [
            jnp.dot(weights_ref[...], stacked(h, start, width), preferred_element_type=F32)
            .astype(BF16)
            .reshape(tap_rank, 1, half, width)
            for h in range(2)
        ]
        tapped = jnp.concatenate(parts, axis=1).reshape(tap_rank * rank, width)
        tapped_ref[:, start : start + width] = tapped
        if then is not None:
            then(start, width, tapped)


def pick_cores(cores, first, hidden, tapped, position):
    rank = hidden.shape[0]
    every = jnp.dot(cores, tapped, preferred_element_type=F32)
    for index in range(cores.shape[0] // rank):
        hidden = jnp.where(position == first + index, every[index * rank : (index + 1) * rank], hidden)
    return hidden


def border_slots(lat_len):
    slots = {p: p for p in range(REACH)}
    slots.update({lat_len - REACH + p: REACH + p for p in range(REACH)})
    return slots


def flat_cores(*refs):
    return jnp.concatenate([ref[...].reshape(-1, ref.shape[2]) for ref in refs], axis=0)


def row_positions(position_ref, start):
    return jnp.concatenate([position_ref[start + r : start + r + 1, :] for r in range(STEP)], axis=1)


def inner_kernel(
    lat_len,
    red_ref,
    edge_ref,
    weights_ref,
    own_ref,
    position_ref,
    tapped_ref,
    halo_stack_ref,
    hidden_ref,
    stack_ref,
):
    rank = red_ref.shape[0]
    own = flat_cores(own_ref)
    lon_len = red_ref.shape[1] // lat_len
    slots = {p: p - REACH for p in range(REACH, lat_len - REACH)}
    edges = edge_ref[...].astype(F32)
    for p in range(lat_len):
        row = red_ref[:, p * lon_len : (p + 1) * lon_len].astype(F32)
        moved = shifted_columns(row, edges, p)
        stack_row(stack_ref, p, moved, slots, lon_len)
        stack_row(halo_stack_ref, p, moved, border_slots(lat_len), lon_len)

    def stacked(h, start, width):
        return stack_ref[h, :, start : start + width]

    def add_own(start, width, tapped):
        position = row_positions(position_ref, start // lon_len + REACH)
        hidden = jnp.zeros((rank, width), F32)
        hidden_ref[:, start : start + width] = pick_cores(own, 0, hidden, tapped, position)

    apply_taps(rank, weights_ref, stacked, tapped_ref, lon_len, add_own)


def border_kernel(lat_len, lat_count, row_b_ref, row_a_ref, weights_ref, own_stack_ref, tapped_ref, stack_ref):
    rank = row_a_ref.shape[0]
    lon_len = (row_a_ref.shape[1] - LANES) // REACH
    lat = lax.axis_index("lat")
    even = (lat % 2) == 0
    row_a = row_a_ref[...].astype(F32)
    row_b = row_b_ref[...].astype(F32)
    above = jnp.where(lat == 0, 0.0, jnp.where(even, row_b, row_a))
    below = jnp.where(lat == lat_count - 1, 0.0, jnp.where(even, row_a, row_b))
    slots = border_slots(lat_len)
    for i in range(REACH):
        for p, holder, place in ((i - REACH, above, lat_len - REACH + i), (lat_len + i, below, i)):
            row = holder[:, i * lon_len : (i + 1) * lon_len]
            moved = shifted_columns(row, holder[:, REACH * lon_len :], place)
            stack_row(stack_ref, p, moved, slots, lon_len)
    block = KS * rank // 2
    in_halo = {
        (slot, row_off)
        for p, slot in slots.items()
        for row_off in range(KS)
        if not 0 <= p + row_off - REACH < lat_len
    }

    def stacked(h, start, width):
        columns = []
        for slot in range(start // lon_len, (start + width) // lon_len):
            span = slice(slot * lon_len, (slot + 1) * lon_len)
            pieces = []
            for row_off in range(KS):
                ref = stack_ref if (slot, row_off) in in_halo else own_stack_ref
                pieces.append(ref[h, row_off * block : (row_off + 1) * block, span])
            columns.append(jnp.concatenate(pieces, axis=0))
        return jnp.concatenate(columns, axis=1)

    apply_taps(rank, weights_ref, stacked, tapped_ref, lon_len)


def mix_kernel(
    inner_ref,
    border_ref,
    core_b_ref,
    core_a_ref,
    own_ref,
    hidden_ref,
    position_ref,
    mixer_ref,
    offset_ref,
    out_hbm,
    stage_ref,
    sems,
):
    lat_len, lon_len = position_ref.shape
    rank = own_ref.shape[1]
    some = flat_cores(core_a_ref, core_b_ref)
    every = flat_cores(own_ref, core_a_ref, core_b_ref)
    pieces = []
    for start in range(0, lat_len, STEP):
        position = row_positions(position_ref, start)
        if REACH <= start < lat_len - REACH:
            span = slice((start - REACH) * lon_len, (start - REACH + STEP) * lon_len)
            hidden = pick_cores(some, PER_OWNER, hidden_ref[:, span], inner_ref[:, span], position)
        else:
            first = start if start < REACH else start - (lat_len - 2 * REACH)
            span = slice(first * lon_len, (first + STEP) * lon_len)
            hidden = jnp.zeros((rank, STEP * lon_len), F32)
            hidden = pick_cores(every, 0, hidden, border_ref[:, span], position)
        hidden = hidden.astype(BF16)
        pieces += [hidden[:, r * lon_len : (r + 1) * lon_len] for r in range(STEP)]
    groups = [jnp.concatenate(pieces[g : g + GROUP], axis=0) for g in range(0, lat_len, GROUP)]
    channels = stage_ref.shape[0]
    share = channels // OUT_COPIES
    copies = []
    for part in range(OUT_COPIES):
        span = slice(part * share * GROUP, (part + 1) * share * GROUP)
        blocks = []
        for hidden in groups:
            output = jnp.dot(mixer_ref[span, :], hidden, preferred_element_type=F32) + offset_ref[span, :]
            mixed = 0.5 * output * (1.0 + jnp.tanh(0.5 * output))
            blocks.append(mixed.reshape(share, GROUP, lon_len))
        held = slice(part * share, (part + 1) * share)
        stage_ref[held] = jnp.concatenate(blocks, axis=1).astype(BF16)
        copy = pltpu.make_async_copy(stage_ref.at[held], out_hbm.at[held], sems.at[part])
        copy.start()
        copies.append(copy)
    for copy in copies:
        copy.wait()


def on_device(
    features, labels, tile_regions, bank_slot, kernel_bank, in_factor, tap_factor, out_factor, out_bias
):
    channels, lat_len, lon_len = features.shape
    rank = in_factor.shape[0]
    held, core_rows, core_cols = kernel_bank.shape
    tap_rank, taps = tap_factor.shape
    out_channels = out_factor.shape[0]
    cells = lat_len * lon_len
    lon_count, lat_count = lax.axis_size("lon"), lax.axis_size("lat")
    lon_first, lon_second = swap_pairs(lon_count)
    lat_first, lat_second = swap_pairs(lat_count)
    edge_shape = jax.ShapeDtypeStruct((rank, LANES), BF16)
    pay_a, pay_b = pl.pallas_call(
        functools.partial(edge_kernel, lon_count, held),
        out_shape=(edge_shape, edge_shape),
        in_specs=[HBM] * 4,
        out_specs=(VMEM,) * 2,
        scratch_shapes=[
            pltpu.SMEM(tile_regions.shape, jnp.int32),
            pltpu.SMEM(bank_slot.shape, jnp.int32),
            pltpu.VMEM(features.shape, BF16),
            pltpu.VMEM(in_factor.shape, BF16),
            pltpu.VMEM((channels * EDGE, lat_len), F32),
            pltpu.SemaphoreType.DMA((channels * EDGE // LANES + 3,)),
        ],
        compiler_params=PARAMS,
    )(*(in_hbm(x) for x in (tile_regions, bank_slot, features, in_factor)))
    got_b = lax.ppermute(pay_b, "lon", lon_second)
    got_a = lax.ppermute(pay_a, "lon", lon_first)
    core_shape = jax.ShapeDtypeStruct((PER_OWNER, core_rows, core_cols), BF16)
    reduced, bank, own, position, weights, mixer, offset = pl.pallas_call(
        functools.partial(prepare_kernel, lon_count, lat_len),
        out_shape=(
            jax.ShapeDtypeStruct((rank, cells), BF16),
            jax.ShapeDtypeStruct(kernel_bank.shape, BF16),
            core_shape,
            jax.ShapeDtypeStruct(labels.shape, jnp.int32),
            jax.ShapeDtypeStruct((tap_rank * rank // 2, taps * rank // 2), BF16),
            jax.ShapeDtypeStruct((out_channels * GROUP, rank * GROUP), BF16),
            jax.ShapeDtypeStruct((out_channels * GROUP, lon_len), F32),
        ),
        in_specs=[HBM] * 10,
        out_specs=(VMEM,) * 7,
        scratch_shapes=[
            pltpu.SMEM(tile_regions.shape, jnp.int32),
            pltpu.SMEM(bank_slot.shape, jnp.int32),
            pltpu.VMEM(labels.shape, jnp.int32),
            pltpu.VMEM(tap_factor.shape, BF16),
            pltpu.VMEM(out_factor.shape[::-1], BF16),
            pltpu.VMEM((1, out_channels), F32),
            pltpu.VMEM(features.shape, BF16),
            pltpu.VMEM(in_factor.shape, BF16),
            pltpu.VMEM((channels * lat_len, lon_len), F32),
            pltpu.SemaphoreType.DMA((8 + BANK_COPIES,)),
        ],
        compiler_params=PARAMS,
        cost_estimate=pl.CostEstimate(flops=10**6, bytes_accessed=kernel_bank.size * 4, transcendentals=0),
    )(
        pay_a,
        *(
            in_hbm(x)
            for x in (
                tile_regions,
                bank_slot,
                features,
                in_factor,
                kernel_bank,
                labels,
                tap_factor,
                out_factor.T,
                out_bias.reshape(1, -1),
            )
        ),
    )
    row_shape = jax.ShapeDtypeStruct((rank, REACH * lon_len + LANES), BF16)
    core_b, core_a = pl.pallas_call(
        functools.partial(pick_kernel, lat_len),
        out_shape=(core_shape, core_shape),
        in_specs=[VMEM] * 3,
        out_specs=(VMEM,) * 2,
        compiler_params=PARAMS,
    )(got_b, got_a, bank)
    edges, row_a, row_b = pl.pallas_call(
        functools.partial(rows_kernel, lat_len),
        out_shape=(edge_shape, row_shape, row_shape),
        in_specs=[VMEM, VMEM, HBM, VMEM],
        out_specs=(VMEM,) * 3,
        compiler_params=PARAMS,
    )(got_b, got_a, core_a, reduced)
    core_b = lax.ppermute(core_b, "lon", lon_second)
    core_a = lax.ppermute(core_a, "lon", lon_first)
    row_a = lax.ppermute(row_a, "lat", lat_first)
    row_b = lax.ppermute(row_b, "lat", lat_second)
    border_cells = 2 * REACH * lon_len
    stack_rows = taps * rank // 2
    halo_stack_shape = jax.ShapeDtypeStruct((2, stack_rows, border_cells), BF16)
    inner, halo_stack, hidden = pl.pallas_call(
        functools.partial(inner_kernel, lat_len),
        out_shape=(
            jax.ShapeDtypeStruct((tap_rank * rank, cells - border_cells), BF16),
            halo_stack_shape,
            jax.ShapeDtypeStruct((rank, cells - border_cells), F32),
        ),
        in_specs=[VMEM] * 5,
        out_specs=(VMEM,) * 3,
        scratch_shapes=[pltpu.VMEM((2, stack_rows, cells - border_cells), BF16)],
        compiler_params=PARAMS,
    )(reduced, edges, weights, own, position)
    border = pl.pallas_call(
        functools.partial(border_kernel, lat_len, lat_count),
        out_shape=jax.ShapeDtypeStruct((tap_rank * rank, border_cells), BF16),
        in_specs=[VMEM] * 4,
        out_specs=VMEM,
        scratch_shapes=[pltpu.VMEM(halo_stack_shape.shape, BF16)],
        compiler_params=PARAMS,
    )(row_b, row_a, weights, halo_stack)
    out_shape = (out_channels, lat_len, lon_len)
    return pl.pallas_call(
        mix_kernel,
        out_shape=jax.ShapeDtypeStruct(out_shape, BF16),
        in_specs=[VMEM] * 9,
        out_specs=HBM,
        scratch_shapes=[pltpu.VMEM(out_shape, BF16), pltpu.SemaphoreType.DMA((OUT_COPIES,))],
        compiler_params=PARAMS,
    )(inner, border, core_b, core_a, own, hidden, position, mixer, offset)


def solution(mesh):
    placed = (
        P(None, "lat", "lon"),
        P("lat", "lon"),
        P("lat", "lon", None),
        P(),
        P("lon", None, None),
        P(),
        P(),
        P(),
        P(),
    )
    return jax.shard_map(
        on_device, mesh=mesh, in_specs=placed, out_specs=P(None, "lat", "lon"), check_vma=False
    )
```

```python
import functools

import jax
import jax.numpy as jnp
from jax import lax
from jax.experimental import pallas as pl
from jax.experimental.pallas import tpu as pltpu
from jax.sharding import PartitionSpec as P

KS = 5
REACH = KS // 2
PER_OWNER = 2
LANES = 128
EDGE = 2 * REACH
GROUP = 8
STEP = 4
OUT_COPIES = 4
IN_COPIES = 4
BANK_COPIES = 8
F32 = jnp.float32
BF16 = jnp.bfloat16
VMEM = pl.BlockSpec(memory_space=pltpu.VMEM)
SMEM = pl.BlockSpec(memory_space=pltpu.SMEM)
HBM = pl.BlockSpec(memory_space=pltpu.HBM)
PARAMS = pltpu.CompilerParams(vmem_limit_bytes=24 * 1024 * 1024)


def swap_pairs(count):
    first = [(i, i ^ 1) for i in range(count)]
    second = [(i, (i + 1 if i % 2 else i - 1) % count) for i in range(count)]
    return first, second


def in_hbm(array):
    return pltpu.with_memory_space_constraint(array, pltpu.HBM)


def lane_index(shape):
    return lax.broadcasted_iota(jnp.int32, shape, 1)


def start_copies(pairs, sems):
    copies = [pltpu.make_async_copy(source, target, sems.at[i]) for i, (source, target) in enumerate(pairs)]
    for copy in copies:
        copy.start()
    return copies


def in_parts(source, target, count):
    share = target.shape[0] // count
    return tuple((source.at[pl.ds(i * share, share)], target.at[pl.ds(i * share, share)]) for i in range(count))


def find_rows(list_ref, slot_ref, lon_count, held):
    me = lax.axis_index("lon")
    owners = (me, lax.rem(me + lon_count - 1, lon_count), lax.rem(me + 1, lon_count))
    counts = [jnp.int32(0)] * 3
    places = [[jnp.int32(0)] * PER_OWNER for _ in range(3)]
    rows = [[jnp.int32(0)] * PER_OWNER for _ in range(3)]
    for i in range(list_ref.shape[2]):
        slot = slot_ref[list_ref[0, 0, i]]
        for group, owner in enumerate(owners):
            local = slot - owner * held
            hit = (local >= 0) & (local < held)
            for nth in range(PER_OWNER):
                take = hit & (counts[group] == nth)
                places[group][nth] = jnp.where(take, i, places[group][nth])
                rows[group][nth] = jnp.where(take, local, rows[group][nth])
            counts[group] = counts[group] + hit.astype(jnp.int32)
    return places, rows


def edge_kernel(
    lon_count,
    held,
    list_hbm,
    slot_hbm,
    feat_hbm,
    in_hbm,
    pay_a_ref,
    pay_b_ref,
    list_ref,
    slot_ref,
    feat_ref,
    in_ref,
    turned_ref,
    sems,
):
    channels, lat_len, lon_len = feat_ref.shape
    rank = in_ref.shape[0]
    pairs = in_parts(feat_hbm, feat_ref, IN_COPIES)
    pairs += ((slot_hbm, slot_ref), (list_hbm, list_ref), (in_hbm, in_ref))
    for copy in start_copies(pairs, sems):
        copy.wait()
    lane = lane_index((lat_len, LANES))
    batch = LANES // EDGE
    for first in range(0, channels, batch):
        packed = jnp.zeros((lat_len, LANES), F32)
        for c in range(batch):
            moved = pltpu.roll(feat_ref[first + c].astype(F32), (EDGE * c + REACH) % LANES, 1)
            packed = jnp.where(lane // EDGE == c, moved, packed)
        turned_ref[first * EDGE : (first + batch) * EDGE, :] = jnp.transpose(packed)
    columns = jnp.concatenate(
        [turned_ref[pl.ds(j, channels, stride=EDGE), :].astype(BF16) for j in range(EDGE)], axis=1
    )
    edges = jnp.dot(in_ref[...], columns, preferred_element_type=F32)
    edges = jnp.concatenate([edges, jnp.zeros((rank, LANES - EDGE * lat_len), F32)], axis=1)
    _, rows = find_rows(list_ref, slot_ref, lon_count, held)
    even = (lax.axis_index("lon") % 2) == 0
    lane = lane_index((rank, LANES))
    for out_ref, wanted in ((pay_a_ref, even), (pay_b_ref, jnp.logical_not(even))):
        load = edges
        for nth in range(PER_OWNER):
            row = jnp.where(wanted, rows[2][nth], rows[1][nth]).astype(F32)
            load = jnp.where(lane == EDGE * lat_len + nth, row, load)
        out_ref[...] = load.astype(BF16)


def prepare_kernel(
    lon_count,
    lat_len,
    pay_hbm,
    list_hbm,
    slot_hbm,
    feat_hbm,
    in_hbm,
    bank_hbm,
    labels_hbm,
    tap_hbm,
    out_factor_hbm,
    bias_hbm,
    red_ref,
    bank_ref,
    own_ref,
    position_ref,
    weights_ref,
    mixer_ref,
    offset_ref,
    list_ref,
    slot_ref,
    labels_ref,
    tap_ref,
    out_factor_ref,
    bias_ref,
    feat_ref,
    in_ref,
    rows_ref,
    sems,
):
    held = bank_hbm.shape[0]
    small = (
        (list_hbm, list_ref),
        (slot_hbm, slot_ref),
        (labels_hbm, labels_ref),
        (tap_hbm, tap_ref),
        (out_factor_hbm, out_factor_ref),
        (bias_hbm, bias_ref),
        (in_hbm, in_ref),
        (feat_hbm, feat_ref),
    )
    copies = start_copies(small + in_parts(bank_hbm, bank_ref, BANK_COPIES), sems)
    for copy in copies[: len(small)]:
        copy.wait()
    channels, lon_len = feat_ref.shape[0], feat_ref.shape[2]
    rows_ref[...] = feat_ref[...].astype(F32).reshape(channels * lat_len, lon_len)
    cells = jnp.concatenate(
        [rows_ref[pl.ds(p, channels, stride=lat_len), :].astype(BF16) for p in range(lat_len)], axis=1
    )
    red_ref[...] = jnp.dot(in_ref[...], cells, preferred_element_type=F32).astype(BF16)
    places, rows = find_rows(list_ref, slot_ref, lon_count, held)
    even = (lax.axis_index("lon") % 2) == 0
    order = list(places[0])
    order += [jnp.where(even, places[2][nth], places[1][nth]) for nth in range(PER_OWNER)]
    order += [jnp.where(even, places[1][nth], places[2][nth]) for nth in range(PER_OWNER)]
    labels = labels_ref[...]
    position = jnp.zeros(labels.shape, jnp.int32)
    for index, place in enumerate(order):
        position = jnp.where(labels == place, index, position)
    position_ref[...] = position

    rank, out_channels = out_factor_ref.shape
    half = rank // 2
    tap_rank, taps = tap_ref.shape
    shape = (tap_rank * half, taps * half)
    spread = (
        lax.broadcasted_iota(jnp.int32, (shape[0], tap_rank), 0) // half == lane_index((shape[0], tap_rank))
    ).astype(BF16)
    repeat = (
        lax.broadcasted_iota(jnp.int32, (taps, shape[1]), 0) == lane_index((taps, shape[1])) // half
    ).astype(BF16)
    tall = jnp.dot(spread, tap_ref[...], preferred_element_type=F32).astype(BF16)
    wide = jnp.dot(tall, repeat, preferred_element_type=F32)
    same = lax.broadcasted_iota(jnp.int32, shape, 0) % half == lane_index(shape) % half
    weights_ref[...] = jnp.where(same, wide, 0.0).astype(BF16)

    shape = (out_channels * GROUP, rank * GROUP)
    spread = (
        lax.broadcasted_iota(jnp.int32, (shape[0], out_channels), 0) // GROUP
        == lane_index((shape[0], out_channels))
    ).astype(BF16)
    repeat = (
        lax.broadcasted_iota(jnp.int32, (rank, shape[1]), 0) == lane_index((rank, shape[1])) % rank
    ).astype(BF16)
    tall = lax.dot_general(
        spread, out_factor_ref[...], (((1,), (1,)), ((), ())), preferred_element_type=F32
    ).astype(BF16)
    wide = jnp.dot(tall, repeat, preferred_element_type=F32)
    same = lax.broadcasted_iota(jnp.int32, shape, 0) % GROUP == lane_index(shape) // rank
    mixer_ref[...] = jnp.where(same, wide, 0.0).astype(BF16)

    shape = (out_channels * GROUP, out_channels)
    mine = lax.broadcasted_iota(jnp.int32, shape, 0) // GROUP == lane_index(shape)
    offset = jnp.sum(jnp.where(mine, bias_ref[...], 0.0), axis=1, keepdims=True)
    offset_ref[...] = jnp.broadcast_to(offset, offset_ref.shape)
    for copy in copies[len(small) :]:
        copy.wait()
    for nth in range(PER_OWNER):
        own_ref[nth] = bank_ref[rows[0][nth]]


def pick_kernel(lat_len, got_b_ref, got_a_ref, bank_ref, core_b_ref, core_a_ref):
    lane = lane_index((1, LANES))
    for got_ref, core_ref in ((got_b_ref, core_b_ref), (got_a_ref, core_a_ref)):
        head = got_ref[...].astype(F32)[0:1, :]
        for nth in range(PER_OWNER):
            row = jnp.sum(jnp.where(lane == EDGE * lat_len + nth, head, 0.0)).astype(jnp.int32)
            core_ref[nth] = bank_ref[row]


def rows_kernel(lat_len, got_b_ref, got_a_ref, core_ref, red_ref, edge_ref, row_a_ref, row_b_ref):
    lon_len = red_ref.shape[1] // lat_len
    even = (lax.axis_index("lon") % 2) == 0
    from_prev = lane_index(got_a_ref.shape) < REACH * lat_len
    got = jnp.where(from_prev == even, got_b_ref[...].astype(F32), got_a_ref[...].astype(F32)).astype(BF16)
    source = lax.broadcasted_iota(jnp.int32, (LANES, LANES), 0)
    target = lane_index((LANES, LANES))
    order = (source == (target % EDGE) * lat_len + target // EDGE) & (target < EDGE * lat_len)
    edges = jnp.dot(got, order.astype(BF16), preferred_element_type=F32).astype(BF16)
    edge_ref[...] = edges
    even = (lax.axis_index("lat") % 2) == 0
    head = red_ref[:, : REACH * lon_len].astype(F32)
    tail = red_ref[:, (lat_len - REACH) * lon_len :].astype(F32)
    row_a_ref[:, : REACH * lon_len] = jnp.where(even, tail, head).astype(BF16)
    row_b_ref[:, : REACH * lon_len] = jnp.where(even, head, tail).astype(BF16)
    row_a_ref[:, REACH * lon_len :] = edges
    row_b_ref[:, REACH * lon_len :] = edges


def shifted_columns(row, edges, place):
    lane = lane_index(row.shape)
    lon_len = row.shape[1]
    edges = pltpu.roll(edges, (LANES - REACH - EDGE * place) % LANES, 1)
    moved = []
    for col_off in range(KS):
        shift = REACH - col_off
        if shift > 0:
            piece = pltpu.roll(jnp.where(lane >= lon_len - shift, edges, row), shift, 1)
        elif shift < 0:
            piece = pltpu.roll(jnp.where(lane < -shift, edges, row), lon_len + shift, 1)
        else:
            piece = row
        moved.append(piece.astype(BF16))
    return moved


def stack_row(stack_ref, p, moved, slots, lon_len):
    half = moved[0].shape[0] // 2
    for col_off, piece in enumerate(moved):
        for row_off in range(KS):
            slot = slots.get(p + REACH - row_off)
            if slot is not None:
                k = row_off * KS + col_off
                for h in range(2):
                    stack_ref[h, k * half : (k + 1) * half, slot * lon_len : (slot + 1) * lon_len] = piece[
                        h * half : (h + 1) * half
                    ]


def apply_taps(rank, weights_ref, stacked, tapped_ref, lon_len):
    half = rank // 2
    tap_rank = tapped_ref.shape[0] // rank
    width = STEP * lon_len
    for start in range(0, tapped_ref.shape[1], width):
        parts = [
            jnp.dot(weights_ref[...], stacked(h, start, width), preferred_element_type=F32)
            .astype(BF16)
            .reshape(tap_rank, 1, half, width)
            for h in range(2)
        ]
        tapped_ref[:, start : start + width] = jnp.concatenate(parts, axis=1).reshape(tap_rank * rank, width)


def border_slots(lat_len):
    slots = {p: p for p in range(REACH)}
    slots.update({lat_len - REACH + p: REACH + p for p in range(REACH)})
    return slots


def inner_kernel(lat_len, red_ref, edge_ref, weights_ref, tapped_ref, halo_stack_ref, stack_ref):
    rank = red_ref.shape[0]
    lon_len = red_ref.shape[1] // lat_len
    slots = {p: p - REACH for p in range(REACH, lat_len - REACH)}
    edges = edge_ref[...].astype(F32)
    for p in range(lat_len):
        row = red_ref[:, p * lon_len : (p + 1) * lon_len].astype(F32)
        moved = shifted_columns(row, edges, p)
        stack_row(stack_ref, p, moved, slots, lon_len)
        stack_row(halo_stack_ref, p, moved, border_slots(lat_len), lon_len)
    apply_taps(rank, weights_ref, lambda h, start, width: stack_ref[h, :, start : start + width], tapped_ref, lon_len)


def border_kernel(lat_len, lat_count, row_b_ref, row_a_ref, weights_ref, own_stack_ref, tapped_ref, stack_ref):
    rank = row_a_ref.shape[0]
    lon_len = (row_a_ref.shape[1] - LANES) // REACH
    lat = lax.axis_index("lat")
    even = (lat % 2) == 0
    row_a = row_a_ref[...].astype(F32)
    row_b = row_b_ref[...].astype(F32)
    above = jnp.where(lat == 0, 0.0, jnp.where(even, row_b, row_a))
    below = jnp.where(lat == lat_count - 1, 0.0, jnp.where(even, row_a, row_b))
    slots = border_slots(lat_len)
    for i in range(REACH):
        for p, holder, place in ((i - REACH, above, lat_len - REACH + i), (lat_len + i, below, i)):
            row = holder[:, i * lon_len : (i + 1) * lon_len]
            moved = shifted_columns(row, holder[:, REACH * lon_len :], place)
            stack_row(stack_ref, p, moved, slots, lon_len)
    block = KS * rank // 2
    in_halo = {
        (slot, row_off)
        for p, slot in slots.items()
        for row_off in range(KS)
        if not 0 <= p + row_off - REACH < lat_len
    }

    def stacked(h, start, width):
        columns = []
        for slot in range(start // lon_len, (start + width) // lon_len):
            span = slice(slot * lon_len, (slot + 1) * lon_len)
            pieces = []
            for row_off in range(KS):
                ref = stack_ref if (slot, row_off) in in_halo else own_stack_ref
                pieces.append(ref[h, row_off * block : (row_off + 1) * block, span])
            columns.append(jnp.concatenate(pieces, axis=0))
        return jnp.concatenate(columns, axis=1)

    apply_taps(rank, weights_ref, stacked, tapped_ref, lon_len)


def mix_kernel(
    inner_ref,
    border_ref,
    core_b_ref,
    core_a_ref,
    own_ref,
    position_ref,
    mixer_ref,
    offset_ref,
    out_hbm,
    stage_ref,
    sems,
):
    lat_len, lon_len = position_ref.shape
    rank = own_ref.shape[1]
    cores = jnp.concatenate(
        [ref[...].reshape(PER_OWNER * rank, -1) for ref in (own_ref, core_a_ref, core_b_ref)], axis=0
    )
    chunks = [(border_ref, 0, [*range(REACH), *range(lat_len - REACH, lat_len)])]
    for start in range(REACH, lat_len - REACH, STEP):
        chunks.append((inner_ref, start - REACH, [*range(start, start + STEP)]))
    by_row = {}
    for ref, first, rows in chunks:
        width = len(rows) * lon_len
        every = jnp.dot(cores, ref[:, first * lon_len : first * lon_len + width], preferred_element_type=F32)
        position = jnp.concatenate([position_ref[r : r + 1, :] for r in rows], axis=1)
        hidden = jnp.zeros((rank, width), F32)
        for index in range(3 * PER_OWNER):
            hidden = jnp.where(position == index, every[index * rank : (index + 1) * rank], hidden)
        hidden = hidden.astype(BF16)
        for i, r in enumerate(rows):
            by_row[r] = hidden[:, i * lon_len : (i + 1) * lon_len]
    pieces = [by_row[r] for r in range(lat_len)]
    groups = [jnp.concatenate(pieces[g : g + GROUP], axis=0) for g in range(0, lat_len, GROUP)]
    channels = stage_ref.shape[0]
    share = channels // OUT_COPIES
    copies = []
    for part in range(OUT_COPIES):
        span = slice(part * share * GROUP, (part + 1) * share * GROUP)
        blocks = []
        for hidden in groups:
            output = jnp.dot(mixer_ref[span, :], hidden, preferred_element_type=F32) + offset_ref[span, :]
            mixed = 0.5 * output * (1.0 + jnp.tanh(0.5 * output))
            blocks.append(mixed.reshape(share, GROUP, lon_len))
        held = slice(part * share, (part + 1) * share)
        stage_ref[held] = jnp.concatenate(blocks, axis=1).astype(BF16)
        copy = pltpu.make_async_copy(stage_ref.at[held], out_hbm.at[held], sems.at[part])
        copy.start()
        copies.append(copy)
    for copy in copies:
        copy.wait()


def on_device(
    features, labels, tile_regions, bank_slot, kernel_bank, in_factor, tap_factor, out_factor, out_bias
):
    channels, lat_len, lon_len = features.shape
    rank = in_factor.shape[0]
    held, core_rows, core_cols = kernel_bank.shape
    tap_rank, taps = tap_factor.shape
    out_channels = out_factor.shape[0]
    cells = lat_len * lon_len
    lon_count, lat_count = lax.axis_size("lon"), lax.axis_size("lat")
    lon_first, lon_second = swap_pairs(lon_count)
    lat_first, lat_second = swap_pairs(lat_count)
    edge_shape = jax.ShapeDtypeStruct((rank, LANES), BF16)
    pay_a, pay_b = pl.pallas_call(
        functools.partial(edge_kernel, lon_count, held),
        out_shape=(edge_shape, edge_shape),
        in_specs=[HBM] * 4,
        out_specs=(VMEM,) * 2,
        scratch_shapes=[
            pltpu.SMEM(tile_regions.shape, jnp.int32),
            pltpu.SMEM(bank_slot.shape, jnp.int32),
            pltpu.VMEM(features.shape, BF16),
            pltpu.VMEM(in_factor.shape, BF16),
            pltpu.VMEM((channels * EDGE, lat_len), F32),
            pltpu.SemaphoreType.DMA((IN_COPIES + 3,)),
        ],
        compiler_params=PARAMS,
    )(*(in_hbm(x) for x in (tile_regions, bank_slot, features, in_factor)))
    got_b = lax.ppermute(pay_b, "lon", lon_second)
    got_a = lax.ppermute(pay_a, "lon", lon_first)
    core_shape = jax.ShapeDtypeStruct((PER_OWNER, core_rows, core_cols), BF16)
    reduced, bank, own, position, weights, mixer, offset = pl.pallas_call(
        functools.partial(prepare_kernel, lon_count, lat_len),
        out_shape=(
            jax.ShapeDtypeStruct((rank, cells), BF16),
            jax.ShapeDtypeStruct(kernel_bank.shape, BF16),
            core_shape,
            jax.ShapeDtypeStruct(labels.shape, jnp.int32),
            jax.ShapeDtypeStruct((tap_rank * rank // 2, taps * rank // 2), BF16),
            jax.ShapeDtypeStruct((out_channels * GROUP, rank * GROUP), BF16),
            jax.ShapeDtypeStruct((out_channels * GROUP, lon_len), F32),
        ),
        in_specs=[HBM] * 10,
        out_specs=(VMEM,) * 7,
        scratch_shapes=[
            pltpu.SMEM(tile_regions.shape, jnp.int32),
            pltpu.SMEM(bank_slot.shape, jnp.int32),
            pltpu.VMEM(labels.shape, jnp.int32),
            pltpu.VMEM(tap_factor.shape, BF16),
            pltpu.VMEM(out_factor.shape[::-1], BF16),
            pltpu.VMEM((1, out_channels), F32),
            pltpu.VMEM(features.shape, BF16),
            pltpu.VMEM(in_factor.shape, BF16),
            pltpu.VMEM((channels * lat_len, lon_len), F32),
            pltpu.SemaphoreType.DMA((8 + BANK_COPIES,)),
        ],
        compiler_params=PARAMS,
        cost_estimate=pl.CostEstimate(flops=10**6, bytes_accessed=kernel_bank.size * 4, transcendentals=0),
    )(
        pay_a,
        *(
            in_hbm(x)
            for x in (
                tile_regions,
                bank_slot,
                features,
                in_factor,
                kernel_bank,
                labels,
                tap_factor,
                out_factor.T,
                out_bias.reshape(1, -1),
            )
        ),
    )
    row_shape = jax.ShapeDtypeStruct((rank, REACH * lon_len + LANES), BF16)
    core_b, core_a = pl.pallas_call(
        functools.partial(pick_kernel, lat_len),
        out_shape=(core_shape, core_shape),
        in_specs=[VMEM] * 3,
        out_specs=(VMEM,) * 2,
        compiler_params=PARAMS,
    )(got_b, got_a, bank)
    edges, row_a, row_b = pl.pallas_call(
        functools.partial(rows_kernel, lat_len),
        out_shape=(edge_shape, row_shape, row_shape),
        in_specs=[VMEM, VMEM, HBM, VMEM],
        out_specs=(VMEM,) * 3,
        compiler_params=PARAMS,
    )(got_b, got_a, core_a, reduced)
    core_b = lax.ppermute(core_b, "lon", lon_second)
    core_a = lax.ppermute(core_a, "lon", lon_first)
    row_a = lax.ppermute(row_a, "lat", lat_first)
    row_b = lax.ppermute(row_b, "lat", lat_second)
    border_cells = 2 * REACH * lon_len
    stack_rows = taps * rank // 2
    halo_stack_shape = jax.ShapeDtypeStruct((2, stack_rows, border_cells), BF16)
    inner, halo_stack = pl.pallas_call(
        functools.partial(inner_kernel, lat_len),
        out_shape=(jax.ShapeDtypeStruct((tap_rank * rank, cells - border_cells), BF16), halo_stack_shape),
        in_specs=[VMEM] * 3,
        out_specs=(VMEM,) * 2,
        scratch_shapes=[pltpu.VMEM((2, stack_rows, cells - border_cells), BF16)],
        compiler_params=PARAMS,
    )(reduced, edges, weights)
    border = pl.pallas_call(
        functools.partial(border_kernel, lat_len, lat_count),
        out_shape=jax.ShapeDtypeStruct((tap_rank * rank, border_cells), BF16),
        in_specs=[VMEM] * 4,
        out_specs=VMEM,
        scratch_shapes=[pltpu.VMEM(halo_stack_shape.shape, BF16)],
        compiler_params=PARAMS,
    )(row_b, row_a, weights, halo_stack)
    out_shape = (out_channels, lat_len, lon_len)
    return pl.pallas_call(
        mix_kernel,
        out_shape=jax.ShapeDtypeStruct(out_shape, BF16),
        in_specs=[VMEM] * 8,
        out_specs=HBM,
        scratch_shapes=[pltpu.VMEM(out_shape, BF16), pltpu.SemaphoreType.DMA((OUT_COPIES,))],
        compiler_params=PARAMS,
    )(inner, border, core_b, core_a, own, position, mixer, offset)


def solution(mesh):
    placed = (
        P(None, "lat", "lon"),
        P("lat", "lon"),
        P("lat", "lon", None),
        P(),
        P("lon", None, None),
        P(),
        P(),
        P(),
        P(),
    )
    return jax.shard_map(
        on_device, mesh=mesh, in_specs=placed, out_specs=P(None, "lat", "lon"), check_vma=False
    )
```

```python
import functools

import jax
import jax.numpy as jnp
from jax import lax
from jax.experimental import pallas as pl
from jax.experimental.pallas import tpu as pltpu
from jax.sharding import PartitionSpec as P

KS = 5
REACH = KS // 2
PER_OWNER = 2
LANES = 128
EDGE = 2 * REACH
GROUP = 8
STEP = 4
OUT_COPIES = 4
IN_COPIES = 4
BANK_COPIES = 4
F32 = jnp.float32
BF16 = jnp.bfloat16
VMEM = pl.BlockSpec(memory_space=pltpu.VMEM)
SMEM = pl.BlockSpec(memory_space=pltpu.SMEM)
HBM = pl.BlockSpec(memory_space=pltpu.HBM)
PARAMS = pltpu.CompilerParams(vmem_limit_bytes=24 * 1024 * 1024)


def swap_pairs(count):
    first = [(i, i ^ 1) for i in range(count)]
    second = [(i, (i + 1 if i % 2 else i - 1) % count) for i in range(count)]
    return first, second


def in_hbm(array):
    return pltpu.with_memory_space_constraint(array, pltpu.HBM)


def lane_index(shape):
    return lax.broadcasted_iota(jnp.int32, shape, 1)


def start_copies(pairs, sems):
    copies = [pltpu.make_async_copy(source, target, sems.at[i]) for i, (source, target) in enumerate(pairs)]
    for copy in copies:
        copy.start()
    return copies


def in_parts(source, target, count):
    share = target.shape[0] // count
    return tuple((source.at[pl.ds(i * share, share)], target.at[pl.ds(i * share, share)]) for i in range(count))


def find_rows(list_ref, slot_ref, lon_count, held):
    me = lax.axis_index("lon")
    owners = (me, lax.rem(me + lon_count - 1, lon_count), lax.rem(me + 1, lon_count))
    counts = [jnp.int32(0)] * 3
    places = [[jnp.int32(0)] * PER_OWNER for _ in range(3)]
    rows = [[jnp.int32(0)] * PER_OWNER for _ in range(3)]
    for i in range(list_ref.shape[2]):
        slot = slot_ref[list_ref[0, 0, i]]
        for group, owner in enumerate(owners):
            local = slot - owner * held
            hit = (local >= 0) & (local < held)
            for nth in range(PER_OWNER):
                take = hit & (counts[group] == nth)
                places[group][nth] = jnp.where(take, i, places[group][nth])
                rows[group][nth] = jnp.where(take, local, rows[group][nth])
            counts[group] = counts[group] + hit.astype(jnp.int32)
    return places, rows


def edge_kernel(
    lon_count,
    held,
    list_hbm,
    slot_hbm,
    feat_hbm,
    in_hbm,
    bank_hbm,
    pay_a_ref,
    pay_b_ref,
    low_ref,
    list_ref,
    slot_ref,
    feat_ref,
    in_ref,
    turned_ref,
    sems,
):
    channels, lat_len, lon_len = feat_ref.shape
    rank = in_ref.shape[0]
    pairs = in_parts(feat_hbm, feat_ref, IN_COPIES)
    pairs += ((slot_hbm, slot_ref), (list_hbm, list_ref), (in_hbm, in_ref))
    bank_low = bank_hbm.at[pl.ds(0, low_ref.shape[0])]
    copies = start_copies(pairs + in_parts(bank_low, low_ref, BANK_COPIES), sems)
    for copy in copies[: len(pairs)]:
        copy.wait()
    lane = lane_index((lat_len, LANES))
    batch = LANES // EDGE
    for first in range(0, channels, batch):
        packed = jnp.zeros((lat_len, LANES), F32)
        for c in range(batch):
            moved = pltpu.roll(feat_ref[first + c].astype(F32), (EDGE * c + REACH) % LANES, 1)
            packed = jnp.where(lane // EDGE == c, moved, packed)
        turned_ref[first * EDGE : (first + batch) * EDGE, :] = jnp.transpose(packed)
    columns = jnp.concatenate(
        [turned_ref[pl.ds(j, channels, stride=EDGE), :].astype(BF16) for j in range(EDGE)], axis=1
    )
    edges = jnp.dot(in_ref[...], columns, preferred_element_type=F32)
    edges = jnp.concatenate([edges, jnp.zeros((rank, LANES - EDGE * lat_len), F32)], axis=1)
    _, rows = find_rows(list_ref, slot_ref, lon_count, held)
    even = (lax.axis_index("lon") % 2) == 0
    lane = lane_index((rank, LANES))
    for out_ref, wanted in ((pay_a_ref, even), (pay_b_ref, jnp.logical_not(even))):
        load = edges
        for nth in range(PER_OWNER):
            row = jnp.where(wanted, rows[2][nth], rows[1][nth]).astype(F32)
            load = jnp.where(lane == EDGE * lat_len + nth, row, load)
        out_ref[...] = load.astype(BF16)
    for copy in copies[len(pairs) :]:
        copy.wait()


def bank_row(low_ref, high_ref, row):
    low = low_ref.shape[0]
    return jnp.where(row < low, low_ref[jnp.minimum(row, low - 1)], high_ref[jnp.maximum(row - low, 0)])


def prepare_kernel(
    lon_count,
    lat_len,
    low_ref,
    list_hbm,
    slot_hbm,
    feat_hbm,
    in_hbm,
    bank_hbm,
    labels_hbm,
    tap_hbm,
    red_ref,
    high_ref,
    own_ref,
    position_ref,
    weights_ref,
    list_ref,
    slot_ref,
    labels_ref,
    tap_ref,
    feat_ref,
    in_ref,
    rows_ref,
    sems,
):
    held, low = bank_hbm.shape[0], low_ref.shape[0]
    pairs = (
        (feat_hbm, feat_ref),
        (in_hbm, in_ref),
        (tap_hbm, tap_ref),
        (list_hbm, list_ref),
        (slot_hbm, slot_ref),
        (labels_hbm, labels_ref),
    )
    bank_high = bank_hbm.at[pl.ds(low, held - low)]
    copies = start_copies(pairs + in_parts(bank_high, high_ref, BANK_COPIES), sems)
    for copy in copies[: len(pairs)]:
        copy.wait()
    channels, lon_len = feat_ref.shape[0], feat_ref.shape[2]
    rows_ref[...] = feat_ref[...].astype(F32).reshape(channels * lat_len, lon_len)
    cells = jnp.concatenate(
        [rows_ref[pl.ds(p, channels, stride=lat_len), :].astype(BF16) for p in range(lat_len)], axis=1
    )
    red_ref[...] = jnp.dot(in_ref[...], cells, preferred_element_type=F32).astype(BF16)
    places, rows = find_rows(list_ref, slot_ref, lon_count, held)
    even = (lax.axis_index("lon") % 2) == 0
    order = list(places[0])
    order += [jnp.where(even, places[2][nth], places[1][nth]) for nth in range(PER_OWNER)]
    order += [jnp.where(even, places[1][nth], places[2][nth]) for nth in range(PER_OWNER)]
    labels = labels_ref[...]
    position = jnp.zeros(labels.shape, jnp.int32)
    for index, place in enumerate(order):
        position = jnp.where(labels == place, index, position)
    position_ref[...] = position

    half = in_ref.shape[0] // 2
    tap_rank, taps = tap_ref.shape
    shape = (tap_rank * half, taps * half)
    spread = (
        lax.broadcasted_iota(jnp.int32, (shape[0], tap_rank), 0) // half == lane_index((shape[0], tap_rank))
    ).astype(BF16)
    repeat = (
        lax.broadcasted_iota(jnp.int32, (taps, shape[1]), 0) == lane_index((taps, shape[1])) // half
    ).astype(BF16)
    tall = jnp.dot(spread, tap_ref[...], preferred_element_type=F32).astype(BF16)
    wide = jnp.dot(tall, repeat, preferred_element_type=F32)
    same = lax.broadcasted_iota(jnp.int32, shape, 0) % half == lane_index(shape) % half
    weights_ref[...] = jnp.where(same, wide, 0.0).astype(BF16)
    for copy in copies[len(pairs) :]:
        copy.wait()
    for nth in range(PER_OWNER):
        own_ref[nth] = bank_row(low_ref, high_ref, rows[0][nth])


def spread_mixer(out_factor_ref, bias_ref, mixer_ref, offset_ref):
    rank, out_channels = out_factor_ref.shape
    shape = (out_channels * GROUP, rank * GROUP)
    spread = (
        lax.broadcasted_iota(jnp.int32, (shape[0], out_channels), 0) // GROUP
        == lane_index((shape[0], out_channels))
    ).astype(BF16)
    repeat = (
        lax.broadcasted_iota(jnp.int32, (rank, shape[1]), 0) == lane_index((rank, shape[1])) % rank
    ).astype(BF16)
    tall = lax.dot_general(
        spread, out_factor_ref[...], (((1,), (1,)), ((), ())), preferred_element_type=F32
    ).astype(BF16)
    wide = jnp.dot(tall, repeat, preferred_element_type=F32)
    same = lax.broadcasted_iota(jnp.int32, shape, 0) % GROUP == lane_index(shape) // rank
    mixer_ref[...] = jnp.where(same, wide, 0.0).astype(BF16)
    shape = (out_channels * GROUP, out_channels)
    mine = lax.broadcasted_iota(jnp.int32, shape, 0) // GROUP == lane_index(shape)
    offset = jnp.sum(jnp.where(mine, bias_ref[...], 0.0), axis=1, keepdims=True)
    offset_ref[...] = jnp.broadcast_to(offset, offset_ref.shape)


def pick_kernel(lat_len, got_b_ref, got_a_ref, low_ref, high_ref, core_a_ref, core_b_ref):
    lane = lane_index((1, LANES))
    for got_ref, core_ref in ((got_b_ref, core_b_ref), (got_a_ref, core_a_ref)):
        head = got_ref[...].astype(F32)[0:1, :]
        for nth in range(PER_OWNER):
            row = jnp.sum(jnp.where(lane == EDGE * lat_len + nth, head, 0.0)).astype(jnp.int32)
            core_ref[nth] = bank_row(low_ref, high_ref, row)


def rows_kernel(lat_len, got_b_ref, got_a_ref, core_ref, red_ref, edge_ref, row_a_ref, row_b_ref):
    lon_len = red_ref.shape[1] // lat_len
    even = (lax.axis_index("lon") % 2) == 0
    from_prev = lane_index(got_a_ref.shape) < REACH * lat_len
    got = jnp.where(from_prev == even, got_b_ref[...].astype(F32), got_a_ref[...].astype(F32)).astype(BF16)
    source = lax.broadcasted_iota(jnp.int32, (LANES, LANES), 0)
    target = lane_index((LANES, LANES))
    order = (source == (target % EDGE) * lat_len + target // EDGE) & (target < EDGE * lat_len)
    edges = jnp.dot(got, order.astype(BF16), preferred_element_type=F32).astype(BF16)
    edge_ref[...] = edges
    even = (lax.axis_index("lat") % 2) == 0
    head = red_ref[:, : REACH * lon_len].astype(F32)
    tail = red_ref[:, (lat_len - REACH) * lon_len :].astype(F32)
    row_a_ref[:, : REACH * lon_len] = jnp.where(even, tail, head).astype(BF16)
    row_b_ref[:, : REACH * lon_len] = jnp.where(even, head, tail).astype(BF16)
    row_a_ref[:, REACH * lon_len :] = edges
    row_b_ref[:, REACH * lon_len :] = edges


def shifted_columns(row, edges, place):
    lane = lane_index(row.shape)
    lon_len = row.shape[1]
    edges = pltpu.roll(edges, (LANES - REACH - EDGE * place) % LANES, 1)
    moved = []
    for col_off in range(KS):
        shift = REACH - col_off
        if shift > 0:
            piece = pltpu.roll(jnp.where(lane >= lon_len - shift, edges, row), shift, 1)
        elif shift < 0:
            piece = pltpu.roll(jnp.where(lane < -shift, edges, row), lon_len + shift, 1)
        else:
            piece = row
        moved.append(piece.astype(BF16))
    return moved


def stack_row(stack_ref, p, moved, slots, lon_len):
    half = moved[0].shape[0] // 2
    for col_off, piece in enumerate(moved):
        for row_off in range(KS):
            slot = slots.get(p + REACH - row_off)
            if slot is not None:
                k = row_off * KS + col_off
                for h in range(2):
                    stack_ref[h, k * half : (k + 1) * half, slot * lon_len : (slot + 1) * lon_len] = piece[
                        h * half : (h + 1) * half
                    ]


def apply_taps(rank, weights_ref, stacked, tapped_ref, lon_len):
    half = rank // 2
    tap_rank = tapped_ref.shape[0] // rank
    width = STEP * lon_len
    for start in range(0, tapped_ref.shape[1], width):
        parts = [
            jnp.dot(weights_ref[...], stacked(h, start, width), preferred_element_type=F32)
            .astype(BF16)
            .reshape(tap_rank, 1, half, width)
            for h in range(2)
        ]
        tapped_ref[:, start : start + width] = jnp.concatenate(parts, axis=1).reshape(tap_rank * rank, width)


def border_slots(lat_len):
    slots = {p: p for p in range(REACH)}
    slots.update({lat_len - REACH + p: REACH + p for p in range(REACH)})
    return slots


def inner_kernel(
    lat_len,
    red_ref,
    edge_ref,
    weights_ref,
    out_factor_hbm,
    bias_hbm,
    tapped_ref,
    halo_stack_ref,
    mixer_ref,
    offset_ref,
    stack_ref,
    out_factor_ref,
    bias_ref,
    sems,
):
    rank = red_ref.shape[0]
    copies = start_copies(((out_factor_hbm, out_factor_ref), (bias_hbm, bias_ref)), sems)
    lon_len = red_ref.shape[1] // lat_len
    slots = {p: p - REACH for p in range(REACH, lat_len - REACH)}
    edges = edge_ref[...].astype(F32)
    for p in range(lat_len):
        row = red_ref[:, p * lon_len : (p + 1) * lon_len].astype(F32)
        moved = shifted_columns(row, edges, p)
        stack_row(stack_ref, p, moved, slots, lon_len)
        stack_row(halo_stack_ref, p, moved, border_slots(lat_len), lon_len)
    for copy in copies:
        copy.wait()
    spread_mixer(out_factor_ref, bias_ref, mixer_ref, offset_ref)
    apply_taps(rank, weights_ref, lambda h, start, width: stack_ref[h, :, start : start + width], tapped_ref, lon_len)


def border_kernel(lat_len, lat_count, row_b_ref, row_a_ref, weights_ref, own_stack_ref, tapped_ref, stack_ref):
    rank = row_a_ref.shape[0]
    lon_len = (row_a_ref.shape[1] - LANES) // REACH
    lat = lax.axis_index("lat")
    even = (lat % 2) == 0
    row_a = row_a_ref[...].astype(F32)
    row_b = row_b_ref[...].astype(F32)
    above = jnp.where(lat == 0, 0.0, jnp.where(even, row_b, row_a))
    below = jnp.where(lat == lat_count - 1, 0.0, jnp.where(even, row_a, row_b))
    slots = border_slots(lat_len)
    for i in range(REACH):
        for p, holder, place in ((i - REACH, above, lat_len - REACH + i), (lat_len + i, below, i)):
            row = holder[:, i * lon_len : (i + 1) * lon_len]
            moved = shifted_columns(row, holder[:, REACH * lon_len :], place)
            stack_row(stack_ref, p, moved, slots, lon_len)
    block = KS * rank // 2
    in_halo = {
        (slot, row_off)
        for p, slot in slots.items()
        for row_off in range(KS)
        if not 0 <= p + row_off - REACH < lat_len
    }

    def stacked(h, start, width):
        columns = []
        for slot in range(start // lon_len, (start + width) // lon_len):
            span = slice(slot * lon_len, (slot + 1) * lon_len)
            pieces = []
            for row_off in range(KS):
                ref = stack_ref if (slot, row_off) in in_halo else own_stack_ref
                pieces.append(ref[h, row_off * block : (row_off + 1) * block, span])
            columns.append(jnp.concatenate(pieces, axis=0))
        return jnp.concatenate(columns, axis=1)

    apply_taps(rank, weights_ref, stacked, tapped_ref, lon_len)


def mix_kernel(
    inner_ref,
    border_ref,
    core_a_ref,
    core_b_ref,
    own_ref,
    position_ref,
    mixer_ref,
    offset_ref,
    out_hbm,
    stage_ref,
    sems,
):
    lat_len, lon_len = position_ref.shape
    rank = own_ref.shape[1]
    cores = jnp.concatenate(
        [ref[...].reshape(PER_OWNER * rank, -1) for ref in (own_ref, core_a_ref, core_b_ref)], axis=0
    )
    chunks = [(border_ref, 0, [*range(REACH), *range(lat_len - REACH, lat_len)])]
    for start in range(REACH, lat_len - REACH, STEP):
        chunks.append((inner_ref, start - REACH, [*range(start, start + STEP)]))
    by_row = {}
    for ref, first, rows in chunks:
        width = len(rows) * lon_len
        every = jnp.dot(cores, ref[:, first * lon_len : first * lon_len + width], preferred_element_type=F32)
        position = jnp.concatenate([position_ref[r : r + 1, :] for r in rows], axis=1)
        hidden = jnp.zeros((rank, width), F32)
        for index in range(3 * PER_OWNER):
            hidden = jnp.where(position == index, every[index * rank : (index + 1) * rank], hidden)
        hidden = hidden.astype(BF16)
        for i, r in enumerate(rows):
            by_row[r] = hidden[:, i * lon_len : (i + 1) * lon_len]
    pieces = [by_row[r] for r in range(lat_len)]
    groups = [jnp.concatenate(pieces[g : g + GROUP], axis=0) for g in range(0, lat_len, GROUP)]
    channels = stage_ref.shape[0]
    share = channels // OUT_COPIES
    copies = []
    for part in range(OUT_COPIES):
        span = slice(part * share * GROUP, (part + 1) * share * GROUP)
        blocks = []
        for hidden in groups:
            output = jnp.dot(mixer_ref[span, :], hidden, preferred_element_type=F32) + offset_ref[span, :]
            mixed = 0.5 * output * (1.0 + jnp.tanh(0.5 * output))
            blocks.append(mixed.reshape(share, GROUP, lon_len))
        held = slice(part * share, (part + 1) * share)
        stage_ref[held] = jnp.concatenate(blocks, axis=1).astype(BF16)
        copy = pltpu.make_async_copy(stage_ref.at[held], out_hbm.at[held], sems.at[part])
        copy.start()
        copies.append(copy)
    for copy in copies:
        copy.wait()


def on_device(
    features, labels, tile_regions, bank_slot, kernel_bank, in_factor, tap_factor, out_factor, out_bias
):
    channels, lat_len, lon_len = features.shape
    rank = in_factor.shape[0]
    held, core_rows, core_cols = kernel_bank.shape
    tap_rank, taps = tap_factor.shape
    out_channels = out_factor.shape[0]
    cells = lat_len * lon_len
    lon_count, lat_count = lax.axis_size("lon"), lax.axis_size("lat")
    lon_first, lon_second = swap_pairs(lon_count)
    lat_first, lat_second = swap_pairs(lat_count)
    edge_shape = jax.ShapeDtypeStruct((rank, LANES), BF16)
    low = held // 2
    core_shape = jax.ShapeDtypeStruct((PER_OWNER, core_rows, core_cols), BF16)
    pay_a, pay_b, bank_low = pl.pallas_call(
        functools.partial(edge_kernel, lon_count, held),
        out_shape=(edge_shape, edge_shape, jax.ShapeDtypeStruct((low, core_rows, core_cols), BF16)),
        in_specs=[HBM] * 5,
        out_specs=(VMEM,) * 3,
        scratch_shapes=[
            pltpu.SMEM(tile_regions.shape, jnp.int32),
            pltpu.SMEM(bank_slot.shape, jnp.int32),
            pltpu.VMEM(features.shape, BF16),
            pltpu.VMEM(in_factor.shape, BF16),
            pltpu.VMEM((channels * EDGE, lat_len), F32),
            pltpu.SemaphoreType.DMA((IN_COPIES + 3 + BANK_COPIES,)),
        ],
        compiler_params=PARAMS,
    )(*(in_hbm(x) for x in (tile_regions, bank_slot, features, in_factor, kernel_bank)))
    got_b = lax.ppermute(pay_b, "lon", lon_second)
    got_a = lax.ppermute(pay_a, "lon", lon_first)
    reduced, bank_high, own, position, weights = pl.pallas_call(
        functools.partial(prepare_kernel, lon_count, lat_len),
        out_shape=(
            jax.ShapeDtypeStruct((rank, cells), BF16),
            jax.ShapeDtypeStruct((held - low, core_rows, core_cols), BF16),
            core_shape,
            jax.ShapeDtypeStruct(labels.shape, jnp.int32),
            jax.ShapeDtypeStruct((tap_rank * rank // 2, taps * rank // 2), BF16),
        ),
        in_specs=[VMEM] + [HBM] * 7,
        out_specs=(VMEM,) * 5,
        scratch_shapes=[
            pltpu.SMEM(tile_regions.shape, jnp.int32),
            pltpu.SMEM(bank_slot.shape, jnp.int32),
            pltpu.VMEM(labels.shape, jnp.int32),
            pltpu.VMEM(tap_factor.shape, BF16),
            pltpu.VMEM(features.shape, BF16),
            pltpu.VMEM(in_factor.shape, BF16),
            pltpu.VMEM((channels * lat_len, lon_len), F32),
            pltpu.SemaphoreType.DMA((6 + BANK_COPIES,)),
        ],
        compiler_params=PARAMS,
        cost_estimate=pl.CostEstimate(flops=10**6, bytes_accessed=kernel_bank.size * 4, transcendentals=0),
    )(
        bank_low,
        *(
            in_hbm(x)
            for x in (tile_regions, bank_slot, features, in_factor, kernel_bank, labels, tap_factor)
        ),
    )
    row_shape = jax.ShapeDtypeStruct((rank, REACH * lon_len + LANES), BF16)
    core_a, core_b = pl.pallas_call(
        functools.partial(pick_kernel, lat_len),
        out_shape=(core_shape, core_shape),
        in_specs=[VMEM] * 4,
        out_specs=(VMEM,) * 2,
        compiler_params=PARAMS,
    )(got_b, got_a, bank_low, bank_high)
    edges, row_a, row_b = pl.pallas_call(
        functools.partial(rows_kernel, lat_len),
        out_shape=(edge_shape, row_shape, row_shape),
        in_specs=[VMEM, VMEM, HBM, VMEM],
        out_specs=(VMEM,) * 3,
        compiler_params=PARAMS,
    )(got_b, got_a, core_b, reduced)
    core_b = lax.ppermute(core_b, "lon", lon_second)
    core_a = lax.ppermute(core_a, "lon", lon_first)
    row_a = lax.ppermute(row_a, "lat", lat_first)
    row_b = lax.ppermute(row_b, "lat", lat_second)
    border_cells = 2 * REACH * lon_len
    stack_rows = taps * rank // 2
    halo_stack_shape = jax.ShapeDtypeStruct((2, stack_rows, border_cells), BF16)
    inner, halo_stack, mixer, offset = pl.pallas_call(
        functools.partial(inner_kernel, lat_len),
        out_shape=(
            jax.ShapeDtypeStruct((tap_rank * rank, cells - border_cells), BF16),
            halo_stack_shape,
            jax.ShapeDtypeStruct((out_channels * GROUP, rank * GROUP), BF16),
            jax.ShapeDtypeStruct((out_channels * GROUP, lon_len), F32),
        ),
        in_specs=[VMEM] * 3 + [HBM] * 2,
        out_specs=(VMEM,) * 4,
        scratch_shapes=[
            pltpu.VMEM((2, stack_rows, cells - border_cells), BF16),
            pltpu.VMEM((rank, out_channels), BF16),
            pltpu.VMEM((1, out_channels), F32),
            pltpu.SemaphoreType.DMA((2,)),
        ],
        compiler_params=PARAMS,
    )(reduced, edges, weights, in_hbm(out_factor.T), in_hbm(out_bias.reshape(1, -1)))
    border = pl.pallas_call(
        functools.partial(border_kernel, lat_len, lat_count),
        out_shape=jax.ShapeDtypeStruct((tap_rank * rank, border_cells), BF16),
        in_specs=[VMEM] * 4,
        out_specs=VMEM,
        scratch_shapes=[pltpu.VMEM(halo_stack_shape.shape, BF16)],
        compiler_params=PARAMS,
    )(row_b, row_a, weights, halo_stack)
    out_shape = (out_channels, lat_len, lon_len)
    return pl.pallas_call(
        mix_kernel,
        out_shape=jax.ShapeDtypeStruct(out_shape, BF16),
        in_specs=[VMEM] * 8,
        out_specs=HBM,
        scratch_shapes=[pltpu.VMEM(out_shape, BF16), pltpu.SemaphoreType.DMA((OUT_COPIES,))],
        compiler_params=PARAMS,
    )(inner, border, core_a, core_b, own, position, mixer, offset)


def solution(mesh):
    placed = (
        P(None, "lat", "lon"),
        P("lat", "lon"),
        P("lat", "lon", None),
        P(),
        P("lon", None, None),
        P(),
        P(),
        P(),
        P(),
    )
    return jax.shard_map(
        on_device, mesh=mesh, in_specs=placed, out_specs=P(None, "lat", "lon"), check_vma=False
    )
```

```python
import functools

import jax
import jax.numpy as jnp
from jax import lax
from jax.experimental import pallas as pl
from jax.experimental.pallas import tpu as pltpu
from jax.sharding import PartitionSpec as P

KS = 5
REACH = KS // 2
PER_OWNER = 2
LANES = 128
EDGE = 2 * REACH
GROUP = 8
STEP = 4
OUT_COPIES = 4
IN_COPIES = 4
BANK_COPIES = 8
F32 = jnp.float32
BF16 = jnp.bfloat16
VMEM = pl.BlockSpec(memory_space=pltpu.VMEM)
SMEM = pl.BlockSpec(memory_space=pltpu.SMEM)
HBM = pl.BlockSpec(memory_space=pltpu.HBM)
PARAMS = pltpu.CompilerParams(vmem_limit_bytes=24 * 1024 * 1024)


def swap_pairs(count):
    first = [(i, i ^ 1) for i in range(count)]
    second = [(i, (i + 1 if i % 2 else i - 1) % count) for i in range(count)]
    return first, second


def in_hbm(array):
    return pltpu.with_memory_space_constraint(array, pltpu.HBM)


def lane_index(shape):
    return lax.broadcasted_iota(jnp.int32, shape, 1)


def start_copies(pairs, sems):
    copies = [pltpu.make_async_copy(source, target, sems.at[i]) for i, (source, target) in enumerate(pairs)]
    for copy in copies:
        copy.start()
    return copies


def in_parts(source, target, count):
    share = target.shape[0] // count
    return tuple((source.at[pl.ds(i * share, share)], target.at[pl.ds(i * share, share)]) for i in range(count))


def find_rows(list_ref, slot_ref, lon_count, held):
    me = lax.axis_index("lon")
    owners = (me, lax.rem(me + lon_count - 1, lon_count), lax.rem(me + 1, lon_count))
    counts = [jnp.int32(0)] * 3
    places = [[jnp.int32(0)] * PER_OWNER for _ in range(3)]
    rows = [[jnp.int32(0)] * PER_OWNER for _ in range(3)]
    for i in range(list_ref.shape[2]):
        slot = slot_ref[list_ref[0, 0, i]]
        for group, owner in enumerate(owners):
            local = slot - owner * held
            hit = (local >= 0) & (local < held)
            for nth in range(PER_OWNER):
                take = hit & (counts[group] == nth)
                places[group][nth] = jnp.where(take, i, places[group][nth])
                rows[group][nth] = jnp.where(take, local, rows[group][nth])
            counts[group] = counts[group] + hit.astype(jnp.int32)
    return places, rows


def edge_kernel(
    lon_count,
    held,
    list_hbm,
    slot_hbm,
    feat_hbm,
    in_hbm,
    pay_a_ref,
    pay_b_ref,
    list_ref,
    slot_ref,
    feat_ref,
    in_ref,
    turned_ref,
    sems,
):
    channels, lat_len, lon_len = feat_ref.shape
    rank = in_ref.shape[0]
    pairs = in_parts(feat_hbm, feat_ref, IN_COPIES)
    pairs += ((slot_hbm, slot_ref), (list_hbm, list_ref), (in_hbm, in_ref))
    for copy in start_copies(pairs, sems):
        copy.wait()
    lane = lane_index((lat_len, LANES))
    batch = LANES // EDGE
    for first in range(0, channels, batch):
        packed = jnp.zeros((lat_len, LANES), F32)
        for c in range(batch):
            moved = pltpu.roll(feat_ref[first + c].astype(F32), (EDGE * c + REACH) % LANES, 1)
            packed = jnp.where(lane // EDGE == c, moved, packed)
        turned_ref[first * EDGE : (first + batch) * EDGE, :] = jnp.transpose(packed)
    columns = jnp.concatenate(
        [turned_ref[pl.ds(j, channels, stride=EDGE), :].astype(BF16) for j in range(EDGE)], axis=1
    )
    edges = jnp.dot(in_ref[...], columns, preferred_element_type=F32)
    edges = jnp.concatenate([edges, jnp.zeros((rank, LANES - EDGE * lat_len), F32)], axis=1)
    _, rows = find_rows(list_ref, slot_ref, lon_count, held)
    even = (lax.axis_index("lon") % 2) == 0
    lane = lane_index((rank, LANES))
    for out_ref, wanted in ((pay_a_ref, even), (pay_b_ref, jnp.logical_not(even))):
        load = edges
        for nth in range(PER_OWNER):
            row = jnp.where(wanted, rows[2][nth], rows[1][nth]).astype(F32)
            load = jnp.where(lane == EDGE * lat_len + nth, row, load)
        out_ref[...] = load.astype(BF16)


def prepare_kernel(
    lon_count,
    lat_len,
    pay_hbm,
    list_hbm,
    slot_hbm,
    feat_hbm,
    in_hbm,
    bank_hbm,
    labels_hbm,
    tap_hbm,
    red_ref,
    bank_ref,
    own_ref,
    position_ref,
    weights_ref,
    list_ref,
    slot_ref,
    labels_ref,
    tap_ref,
    feat_ref,
    in_ref,
    rows_ref,
    sems,
):
    held = bank_hbm.shape[0]
    pairs = (
        (feat_hbm, feat_ref),
        (in_hbm, in_ref),
        (tap_hbm, tap_ref),
        (list_hbm, list_ref),
        (slot_hbm, slot_ref),
        (labels_hbm, labels_ref),
    )
    copies = start_copies(pairs + in_parts(bank_hbm, bank_ref, BANK_COPIES), sems)
    for copy in copies[: len(pairs)]:
        copy.wait()
    channels, lon_len = feat_ref.shape[0], feat_ref.shape[2]
    rows_ref[...] = feat_ref[...].astype(F32).reshape(channels * lat_len, lon_len)
    cells = jnp.concatenate(
        [rows_ref[pl.ds(p, channels, stride=lat_len), :].astype(BF16) for p in range(lat_len)], axis=1
    )
    red_ref[...] = jnp.dot(in_ref[...], cells, preferred_element_type=F32).astype(BF16)
    places, rows = find_rows(list_ref, slot_ref, lon_count, held)
    even = (lax.axis_index("lon") % 2) == 0
    order = list(places[0])
    order += [jnp.where(even, places[2][nth], places[1][nth]) for nth in range(PER_OWNER)]
    order += [jnp.where(even, places[1][nth], places[2][nth]) for nth in range(PER_OWNER)]
    labels = labels_ref[...]
    position = jnp.zeros(labels.shape, jnp.int32)
    for index, place in enumerate(order):
        position = jnp.where(labels == place, index, position)
    position_ref[...] = position

    half = in_ref.shape[0] // 2
    tap_rank, taps = tap_ref.shape
    shape = (tap_rank * half, taps * half)
    spread = (
        lax.broadcasted_iota(jnp.int32, (shape[0], tap_rank), 0) // half == lane_index((shape[0], tap_rank))
    ).astype(BF16)
    repeat = (
        lax.broadcasted_iota(jnp.int32, (taps, shape[1]), 0) == lane_index((taps, shape[1])) // half
    ).astype(BF16)
    tall = jnp.dot(spread, tap_ref[...], preferred_element_type=F32).astype(BF16)
    wide = jnp.dot(tall, repeat, preferred_element_type=F32)
    same = lax.broadcasted_iota(jnp.int32, shape, 0) % half == lane_index(shape) % half
    weights_ref[...] = jnp.where(same, wide, 0.0).astype(BF16)
    for copy in copies[len(pairs) :]:
        copy.wait()
    for nth in range(PER_OWNER):
        own_ref[nth] = bank_ref[rows[0][nth]]


def spread_mixer(out_factor_ref, mixer_ref):
    rank, out_channels = out_factor_ref.shape
    shape = (out_channels * GROUP, rank * GROUP)
    spread = (
        lax.broadcasted_iota(jnp.int32, (shape[0], out_channels), 0) // GROUP
        == lane_index((shape[0], out_channels))
    ).astype(BF16)
    repeat = (
        lax.broadcasted_iota(jnp.int32, (rank, shape[1]), 0) == lane_index((rank, shape[1])) % rank
    ).astype(BF16)
    tall = lax.dot_general(
        spread, out_factor_ref[...], (((1,), (1,)), ((), ())), preferred_element_type=F32
    ).astype(BF16)
    wide = jnp.dot(tall, repeat, preferred_element_type=F32)
    same = lax.broadcasted_iota(jnp.int32, shape, 0) % GROUP == lane_index(shape) // rank
    mixer_ref[...] = jnp.where(same, wide, 0.0).astype(BF16)


def pick_kernel(lat_len, got_b_ref, got_a_ref, bank_ref, core_a_ref, core_b_ref):
    lane = lane_index((1, LANES))
    for got_ref, core_ref in ((got_b_ref, core_b_ref), (got_a_ref, core_a_ref)):
        head = got_ref[...].astype(F32)[0:1, :]
        for nth in range(PER_OWNER):
            row = jnp.sum(jnp.where(lane == EDGE * lat_len + nth, head, 0.0)).astype(jnp.int32)
            core_ref[nth] = bank_ref[row]


def rows_kernel(lat_len, got_b_ref, got_a_ref, core_ref, red_ref, edge_ref, row_a_ref, row_b_ref):
    lon_len = red_ref.shape[1] // lat_len
    even = (lax.axis_index("lon") % 2) == 0
    from_prev = lane_index(got_a_ref.shape) < REACH * lat_len
    got = jnp.where(from_prev == even, got_b_ref[...].astype(F32), got_a_ref[...].astype(F32)).astype(BF16)
    source = lax.broadcasted_iota(jnp.int32, (LANES, LANES), 0)
    target = lane_index((LANES, LANES))
    order = (source == (target % EDGE) * lat_len + target // EDGE) & (target < EDGE * lat_len)
    edges = jnp.dot(got, order.astype(BF16), preferred_element_type=F32).astype(BF16)
    edge_ref[...] = edges
    even = (lax.axis_index("lat") % 2) == 0
    head = red_ref[:, : REACH * lon_len].astype(F32)
    tail = red_ref[:, (lat_len - REACH) * lon_len :].astype(F32)
    row_a_ref[:, : REACH * lon_len] = jnp.where(even, tail, head).astype(BF16)
    row_b_ref[:, : REACH * lon_len] = jnp.where(even, head, tail).astype(BF16)
    row_a_ref[:, REACH * lon_len :] = edges
    row_b_ref[:, REACH * lon_len :] = edges


def shifted_columns(row, edges, place):
    lane = lane_index(row.shape)
    lon_len = row.shape[1]
    edges = pltpu.roll(edges, (LANES - REACH - EDGE * place) % LANES, 1)
    moved = []
    for col_off in range(KS):
        shift = REACH - col_off
        if shift > 0:
            piece = pltpu.roll(jnp.where(lane >= lon_len - shift, edges, row), shift, 1)
        elif shift < 0:
            piece = pltpu.roll(jnp.where(lane < -shift, edges, row), lon_len + shift, 1)
        else:
            piece = row
        moved.append(piece.astype(BF16))
    return moved


def stack_row(stack_ref, p, moved, slots, lon_len):
    half = moved[0].shape[0] // 2
    for col_off, piece in enumerate(moved):
        for row_off in range(KS):
            slot = slots.get(p + REACH - row_off)
            if slot is not None:
                k = row_off * KS + col_off
                for h in range(2):
                    stack_ref[h, k * half : (k + 1) * half, slot * lon_len : (slot + 1) * lon_len] = piece[
                        h * half : (h + 1) * half
                    ]


def apply_taps(rank, weights_ref, stacked, tapped_ref, lon_len):
    half = rank // 2
    tap_rank = tapped_ref.shape[0] // rank
    width = STEP * lon_len
    for start in range(0, tapped_ref.shape[1], width):
        parts = [
            jnp.dot(weights_ref[...], stacked(h, start, width), preferred_element_type=F32)
            .astype(BF16)
            .reshape(tap_rank, 1, half, width)
            for h in range(2)
        ]
        tapped_ref[:, start : start + width] = jnp.concatenate(parts, axis=1).reshape(tap_rank * rank, width)


def border_slots(lat_len):
    slots = {p: p for p in range(REACH)}
    slots.update({lat_len - REACH + p: REACH + p for p in range(REACH)})
    return slots


def inner_kernel(
    lat_len,
    red_ref,
    edge_ref,
    weights_ref,
    out_factor_hbm,
    tapped_ref,
    halo_stack_ref,
    mixer_ref,
    stack_ref,
    out_factor_ref,
    sem,
):
    rank = red_ref.shape[0]
    copy = pltpu.make_async_copy(out_factor_hbm, out_factor_ref, sem)
    copy.start()
    lon_len = red_ref.shape[1] // lat_len
    slots = {p: p - REACH for p in range(REACH, lat_len - REACH)}
    edges = edge_ref[...].astype(F32)
    for p in range(lat_len):
        row = red_ref[:, p * lon_len : (p + 1) * lon_len].astype(F32)
        moved = shifted_columns(row, edges, p)
        stack_row(stack_ref, p, moved, slots, lon_len)
        stack_row(halo_stack_ref, p, moved, border_slots(lat_len), lon_len)
    copy.wait()
    spread_mixer(out_factor_ref, mixer_ref)
    apply_taps(rank, weights_ref, lambda h, start, width: stack_ref[h, :, start : start + width], tapped_ref, lon_len)


def border_kernel(lat_len, lat_count, row_b_ref, row_a_ref, weights_ref, own_stack_ref, tapped_ref, stack_ref):
    rank = row_a_ref.shape[0]
    lon_len = (row_a_ref.shape[1] - LANES) // REACH
    lat = lax.axis_index("lat")
    even = (lat % 2) == 0
    row_a = row_a_ref[...].astype(F32)
    row_b = row_b_ref[...].astype(F32)
    above = jnp.where(lat == 0, 0.0, jnp.where(even, row_b, row_a))
    below = jnp.where(lat == lat_count - 1, 0.0, jnp.where(even, row_a, row_b))
    slots = border_slots(lat_len)
    for i in range(REACH):
        for p, holder, place in ((i - REACH, above, lat_len - REACH + i), (lat_len + i, below, i)):
            row = holder[:, i * lon_len : (i + 1) * lon_len]
            moved = shifted_columns(row, holder[:, REACH * lon_len :], place)
            stack_row(stack_ref, p, moved, slots, lon_len)
    block = KS * rank // 2
    in_halo = {
        (slot, row_off)
        for p, slot in slots.items()
        for row_off in range(KS)
        if not 0 <= p + row_off - REACH < lat_len
    }

    def stacked(h, start, width):
        columns = []
        for slot in range(start // lon_len, (start + width) // lon_len):
            span = slice(slot * lon_len, (slot + 1) * lon_len)
            pieces = []
            for row_off in range(KS):
                ref = stack_ref if (slot, row_off) in in_halo else own_stack_ref
                pieces.append(ref[h, row_off * block : (row_off + 1) * block, span])
            columns.append(jnp.concatenate(pieces, axis=0))
        return jnp.concatenate(columns, axis=1)

    apply_taps(rank, weights_ref, stacked, tapped_ref, lon_len)


def mix_kernel(
    inner_ref,
    border_ref,
    core_a_ref,
    core_b_ref,
    own_ref,
    position_ref,
    mixer_ref,
    bias_hbm,
    out_hbm,
    stage_ref,
    bias_ref,
    sems,
    bias_sem,
):
    bias_copy = pltpu.make_async_copy(bias_hbm, bias_ref, bias_sem)
    bias_copy.start()
    lat_len, lon_len = position_ref.shape
    rank = own_ref.shape[1]
    cores = jnp.concatenate(
        [ref[...].reshape(PER_OWNER * rank, -1) for ref in (own_ref, core_a_ref, core_b_ref)], axis=0
    )
    chunks = [(border_ref, 0, [*range(REACH), *range(lat_len - REACH, lat_len)])]
    for start in range(REACH, lat_len - REACH, STEP):
        chunks.append((inner_ref, start - REACH, [*range(start, start + STEP)]))
    by_row = {}
    for ref, first, rows in chunks:
        width = len(rows) * lon_len
        every = jnp.dot(cores, ref[:, first * lon_len : first * lon_len + width], preferred_element_type=F32)
        position = jnp.concatenate([position_ref[r : r + 1, :] for r in rows], axis=1)
        hidden = jnp.zeros((rank, width), F32)
        for index in range(3 * PER_OWNER):
            hidden = jnp.where(position == index, every[index * rank : (index + 1) * rank], hidden)
        hidden = hidden.astype(BF16)
        for i, r in enumerate(rows):
            by_row[r] = hidden[:, i * lon_len : (i + 1) * lon_len]
    pieces = [by_row[r] for r in range(lat_len)]
    groups = [jnp.concatenate(pieces[g : g + GROUP], axis=0) for g in range(0, lat_len, GROUP)]
    channels = stage_ref.shape[0]
    share = channels // OUT_COPIES
    copies = []
    bias_copy.wait()
    for part in range(OUT_COPIES):
        span = slice(part * share * GROUP, (part + 1) * share * GROUP)
        blocks = []
        for hidden in groups:
            output = jnp.dot(mixer_ref[span, :], hidden, preferred_element_type=F32)
            output = jnp.stack(
                [output[i * GROUP : (i + 1) * GROUP] + bias_ref[part * share + i] for i in range(share)]
            )
            blocks.append(0.5 * output * (1.0 + jnp.tanh(0.5 * output)))
        held = slice(part * share, (part + 1) * share)
        stage_ref[held] = jnp.concatenate(blocks, axis=1).astype(BF16)
        copy = pltpu.make_async_copy(stage_ref.at[held], out_hbm.at[held], sems.at[part])
        copy.start()
        copies.append(copy)
    for copy in copies:
        copy.wait()


def on_device(
    features, labels, tile_regions, bank_slot, kernel_bank, in_factor, tap_factor, out_factor, out_bias
):
    channels, lat_len, lon_len = features.shape
    rank = in_factor.shape[0]
    held, core_rows, core_cols = kernel_bank.shape
    tap_rank, taps = tap_factor.shape
    out_channels = out_factor.shape[0]
    cells = lat_len * lon_len
    lon_count, lat_count = lax.axis_size("lon"), lax.axis_size("lat")
    lon_first, lon_second = swap_pairs(lon_count)
    lat_first, lat_second = swap_pairs(lat_count)
    edge_shape = jax.ShapeDtypeStruct((rank, LANES), BF16)
    core_shape = jax.ShapeDtypeStruct((PER_OWNER, core_rows, core_cols), BF16)
    pay_a, pay_b = pl.pallas_call(
        functools.partial(edge_kernel, lon_count, held),
        out_shape=(edge_shape, edge_shape),
        in_specs=[HBM] * 4,
        out_specs=(VMEM,) * 2,
        scratch_shapes=[
            pltpu.SMEM(tile_regions.shape, jnp.int32),
            pltpu.SMEM(bank_slot.shape, jnp.int32),
            pltpu.VMEM(features.shape, BF16),
            pltpu.VMEM(in_factor.shape, BF16),
            pltpu.VMEM((channels * EDGE, lat_len), F32),
            pltpu.SemaphoreType.DMA((IN_COPIES + 3,)),
        ],
        compiler_params=PARAMS,
    )(*(in_hbm(x) for x in (tile_regions, bank_slot, features, in_factor)))
    got_b = lax.ppermute(pay_b, "lon", lon_second)
    got_a = lax.ppermute(pay_a, "lon", lon_first)
    reduced, bank, own, position, weights = pl.pallas_call(
        functools.partial(prepare_kernel, lon_count, lat_len),
        out_shape=(
            jax.ShapeDtypeStruct((rank, cells), BF16),
            jax.ShapeDtypeStruct(kernel_bank.shape, BF16),
            core_shape,
            jax.ShapeDtypeStruct(labels.shape, jnp.int32),
            jax.ShapeDtypeStruct((tap_rank * rank // 2, taps * rank // 2), BF16),
        ),
        in_specs=[HBM] * 8,
        out_specs=(VMEM,) * 5,
        scratch_shapes=[
            pltpu.SMEM(tile_regions.shape, jnp.int32),
            pltpu.SMEM(bank_slot.shape, jnp.int32),
            pltpu.VMEM(labels.shape, jnp.int32),
            pltpu.VMEM(tap_factor.shape, BF16),
            pltpu.VMEM(features.shape, BF16),
            pltpu.VMEM(in_factor.shape, BF16),
            pltpu.VMEM((channels * lat_len, lon_len), F32),
            pltpu.SemaphoreType.DMA((6 + BANK_COPIES,)),
        ],
        compiler_params=PARAMS,
        cost_estimate=pl.CostEstimate(flops=10**6, bytes_accessed=kernel_bank.size * 4, transcendentals=0),
    )(
        pay_a,
        *(
            in_hbm(x)
            for x in (tile_regions, bank_slot, features, in_factor, kernel_bank, labels, tap_factor)
        ),
    )
    row_shape = jax.ShapeDtypeStruct((rank, REACH * lon_len + LANES), BF16)
    core_a, core_b = pl.pallas_call(
        functools.partial(pick_kernel, lat_len),
        out_shape=(core_shape, core_shape),
        in_specs=[VMEM] * 3,
        out_specs=(VMEM,) * 2,
        compiler_params=PARAMS,
    )(got_b, got_a, bank)
    edges, row_a, row_b = pl.pallas_call(
        functools.partial(rows_kernel, lat_len),
        out_shape=(edge_shape, row_shape, row_shape),
        in_specs=[VMEM, VMEM, HBM, VMEM],
        out_specs=(VMEM,) * 3,
        compiler_params=PARAMS,
    )(got_b, got_a, core_b, reduced)
    core_b = lax.ppermute(core_b, "lon", lon_second)
    core_a = lax.ppermute(core_a, "lon", lon_first)
    row_a = lax.ppermute(row_a, "lat", lat_first)
    row_b = lax.ppermute(row_b, "lat", lat_second)
    border_cells = 2 * REACH * lon_len
    stack_rows = taps * rank // 2
    halo_stack_shape = jax.ShapeDtypeStruct((2, stack_rows, border_cells), BF16)
    inner, halo_stack, mixer = pl.pallas_call(
        functools.partial(inner_kernel, lat_len),
        out_shape=(
            jax.ShapeDtypeStruct((tap_rank * rank, cells - border_cells), BF16),
            halo_stack_shape,
            jax.ShapeDtypeStruct((out_channels * GROUP, rank * GROUP), BF16),
        ),
        in_specs=[VMEM] * 3 + [HBM],
        out_specs=(VMEM,) * 3,
        scratch_shapes=[
            pltpu.VMEM((2, stack_rows, cells - border_cells), BF16),
            pltpu.VMEM((rank, out_channels), BF16),
            pltpu.SemaphoreType.DMA,
        ],
        compiler_params=PARAMS,
    )(reduced, edges, weights, in_hbm(out_factor.T))
    border = pl.pallas_call(
        functools.partial(border_kernel, lat_len, lat_count),
        out_shape=jax.ShapeDtypeStruct((tap_rank * rank, border_cells), BF16),
        in_specs=[VMEM] * 4,
        out_specs=VMEM,
        scratch_shapes=[pltpu.VMEM(halo_stack_shape.shape, BF16)],
        compiler_params=PARAMS,
    )(row_b, row_a, weights, halo_stack)
    out_shape = (out_channels, lat_len, lon_len)
    return pl.pallas_call(
        mix_kernel,
        out_shape=jax.ShapeDtypeStruct(out_shape, BF16),
        in_specs=[VMEM] * 7 + [HBM],
        out_specs=HBM,
        scratch_shapes=[
            pltpu.VMEM(out_shape, BF16),
            pltpu.SMEM(out_bias.shape, F32),
            pltpu.SemaphoreType.DMA((OUT_COPIES,)),
            pltpu.SemaphoreType.DMA,
        ],
        compiler_params=PARAMS,
    )(inner, border, core_a, core_b, own, position, mixer, in_hbm(out_bias))


def solution(mesh):
    placed = (
        P(None, "lat", "lon"),
        P("lat", "lon"),
        P("lat", "lon", None),
        P(),
        P("lon", None, None),
        P(),
        P(),
        P(),
        P(),
    )
    return jax.shard_map(
        on_device, mesh=mesh, in_specs=placed, out_specs=P(None, "lat", "lon"), check_vma=False
    )
```

```python
import functools

import jax
import jax.numpy as jnp
from jax import lax
from jax.experimental import pallas as pl
from jax.experimental.pallas import tpu as pltpu
from jax.sharding import PartitionSpec as P

KS = 5
REACH = KS // 2
PER_OWNER = 2
LANES = 128
EDGE = 2 * REACH
GROUP = 8
STEP = 4
OUT_COPIES = 4
IN_COPIES = 4
BANK_COPIES = 8
F32 = jnp.float32
BF16 = jnp.bfloat16
VMEM = pl.BlockSpec(memory_space=pltpu.VMEM)
SMEM = pl.BlockSpec(memory_space=pltpu.SMEM)
HBM = pl.BlockSpec(memory_space=pltpu.HBM)
PARAMS = pltpu.CompilerParams(vmem_limit_bytes=24 * 1024 * 1024)


def swap_pairs(count):
    first = [(i, i ^ 1) for i in range(count)]
    second = [(i, (i + 1 if i % 2 else i - 1) % count) for i in range(count)]
    return first, second


def in_hbm(array):
    return pltpu.with_memory_space_constraint(array, pltpu.HBM)


def lane_index(shape):
    return lax.broadcasted_iota(jnp.int32, shape, 1)


def start_copies(pairs, sems):
    copies = [pltpu.make_async_copy(source, target, sems.at[i]) for i, (source, target) in enumerate(pairs)]
    for copy in copies:
        copy.start()
    return copies


def in_parts(source, target, count):
    share = target.shape[0] // count
    return tuple((source.at[pl.ds(i * share, share)], target.at[pl.ds(i * share, share)]) for i in range(count))


def find_rows(list_ref, slot_ref, lon_count, held):
    me = lax.axis_index("lon")
    owners = (me, lax.rem(me + lon_count - 1, lon_count), lax.rem(me + 1, lon_count))
    slots = [slot_ref[list_ref[0, 0, i]] for i in range(list_ref.shape[2])]
    places, rows = [], []
    for owner in owners:
        least, greatest = jnp.int32(held), jnp.int32(-1)
        first, last = jnp.int32(0), jnp.int32(0)
        for i, slot in enumerate(slots):
            local = slot - owner * held
            hit = (local >= 0) & (local < held)
            first = jnp.where(hit & (local < least), i, first)
            last = jnp.where(hit & (local > greatest), i, last)
            least = jnp.where(hit, jnp.minimum(local, least), least)
            greatest = jnp.where(hit, jnp.maximum(local, greatest), greatest)
        places.append([first, last])
        rows.append([jnp.minimum(least, held - 1), jnp.maximum(greatest, 0)])
    return places, rows


class Held:
    names = ("bank", "own", "position", "weights", "mixer", "offset")
    sources = ("labels", "tap", "out_factor", "bias")

    def __init__(self, refs):
        self.__dict__.update(zip(self.names, refs))


def start_sources(sources, targets, bank_hbm, bank_ref, sems):
    pairs = tuple(zip(sources, targets))
    return start_copies(pairs + in_parts(bank_hbm, bank_ref, BANK_COPIES), sems)


def build_held(lon_count, list_ref, slot_ref, targets, copies, held):
    labels_ref, tap_ref, out_factor_ref, bias_ref = targets
    for copy in copies[: len(targets)]:
        copy.wait()
    places, rows = find_rows(list_ref, slot_ref, lon_count, held.bank.shape[0])
    even = (lax.axis_index("lon") % 2) == 0
    order = list(places[0])
    order += [jnp.where(even, places[2][nth], places[1][nth]) for nth in range(PER_OWNER)]
    order += [jnp.where(even, places[1][nth], places[2][nth]) for nth in range(PER_OWNER)]
    labels = labels_ref[...]
    position = jnp.zeros(labels.shape, jnp.int32)
    for index, place in enumerate(order):
        position = jnp.where(labels == place, index, position)
    held.position[...] = position

    rank, out_channels = out_factor_ref.shape
    half = rank // 2
    tap_rank, taps = tap_ref.shape
    shape = (tap_rank * half, taps * half)
    spread = (
        lax.broadcasted_iota(jnp.int32, (shape[0], tap_rank), 0) // half == lane_index((shape[0], tap_rank))
    ).astype(BF16)
    repeat = (
        lax.broadcasted_iota(jnp.int32, (taps, shape[1]), 0) == lane_index((taps, shape[1])) // half
    ).astype(BF16)
    tall = jnp.dot(spread, tap_ref[...], preferred_element_type=F32).astype(BF16)
    wide = jnp.dot(tall, repeat, preferred_element_type=F32)
    same = lax.broadcasted_iota(jnp.int32, shape, 0) % half == lane_index(shape) % half
    held.weights[...] = jnp.where(same, wide, 0.0).astype(BF16)

    shape = (out_channels * GROUP, rank * GROUP)
    spread = (
        lax.broadcasted_iota(jnp.int32, (shape[0], out_channels), 0) // GROUP
        == lane_index((shape[0], out_channels))
    ).astype(BF16)
    repeat = (
        lax.broadcasted_iota(jnp.int32, (rank, shape[1]), 0) == lane_index((rank, shape[1])) % rank
    ).astype(BF16)
    tall = lax.dot_general(
        spread, out_factor_ref[...], (((1,), (1,)), ((), ())), preferred_element_type=F32
    ).astype(BF16)
    wide = jnp.dot(tall, repeat, preferred_element_type=F32)
    same = lax.broadcasted_iota(jnp.int32, shape, 0) % GROUP == lane_index(shape) // rank
    held.mixer[...] = jnp.where(same, wide, 0.0).astype(BF16)

    shape = (out_channels * GROUP, out_channels)
    mine = lax.broadcasted_iota(jnp.int32, shape, 0) // GROUP == lane_index(shape)
    offset = jnp.sum(jnp.where(mine, bias_ref[...], 0.0), axis=1, keepdims=True)
    held.offset[...] = jnp.broadcast_to(offset, held.offset.shape)
    for copy in copies[len(targets) :]:
        copy.wait()
    for nth in range(PER_OWNER):
        held.own[nth] = held.bank[rows[0][nth]]


def edge_kernel(lon_count, *refs):
    list_hbm, slot_hbm, feat_hbm, in_hbm, bank_hbm = refs[:5]
    sources, (pay_a_ref, pay_b_ref), held_refs = refs[5:9], refs[9:11], refs[11:17]
    list_ref, slot_ref, feat_ref, in_ref, turned_ref = refs[17:22]
    targets, sems, held_sems = refs[22:26], refs[26], refs[27]
    held = Held(held_refs)
    channels, lat_len, lon_len = feat_ref.shape
    rank = in_ref.shape[0]
    early = lax.axis_index("lon") != lon_count - 1
    pairs = in_parts(feat_hbm, feat_ref, IN_COPIES)
    pairs += ((slot_hbm, slot_ref), (list_hbm, list_ref), (in_hbm, in_ref))
    copies = start_copies(pairs, sems)

    @pl.when(early)
    def _():
        start_sources(sources, targets, bank_hbm, held.bank, held_sems)

    for copy in copies:
        copy.wait()
    lane = lane_index((lat_len, LANES))
    batch = LANES // EDGE
    for first in range(0, channels, batch):
        packed = jnp.zeros((lat_len, LANES), F32)
        for c in range(batch):
            moved = pltpu.roll(feat_ref[first + c].astype(F32), (EDGE * c + REACH) % LANES, 1)
            packed = jnp.where(lane // EDGE == c, moved, packed)
        turned_ref[first * EDGE : (first + batch) * EDGE, :] = jnp.transpose(packed)
    columns = jnp.concatenate(
        [turned_ref[pl.ds(j, channels, stride=EDGE), :].astype(BF16) for j in range(EDGE)], axis=1
    )
    edges = jnp.dot(in_ref[...], columns, preferred_element_type=F32)
    edges = jnp.concatenate([edges, jnp.zeros((rank, LANES - EDGE * lat_len), F32)], axis=1)
    _, rows = find_rows(list_ref, slot_ref, lon_count, held.bank.shape[0])
    even = (lax.axis_index("lon") % 2) == 0
    lane = lane_index((rank, LANES))
    for out_ref, wanted in ((pay_a_ref, even), (pay_b_ref, jnp.logical_not(even))):
        load = edges
        for nth in range(PER_OWNER):
            row = jnp.where(wanted, rows[2][nth], rows[1][nth]).astype(F32)
            load = jnp.where(lane == EDGE * lat_len + nth, row, load)
        out_ref[...] = load.astype(BF16)

    @pl.when(early)
    def _():
        pairs = tuple(zip(sources, targets)) + in_parts(bank_hbm, held.bank, BANK_COPIES)
        waits = [pltpu.make_async_copy(source, target, held_sems.at[i]) for i, (source, target) in enumerate(pairs)]
        build_held(lon_count, list_ref, slot_ref, targets, waits, held)


def prepare_kernel(lon_count, lat_len, *refs):
    list_hbm, slot_hbm, feat_hbm, in_hbm, bank_hbm = refs[:5]
    sources, given = refs[5:9], Held((None, *refs[9:14]))
    red_ref, held = refs[14], Held(refs[15:21])
    list_ref, slot_ref, feat_ref, in_ref, rows_ref = refs[21:26]
    targets, sems, held_sems = refs[26:30], refs[30], refs[31]
    early = lax.axis_index("lon") != lon_count - 1
    pairs = in_parts(feat_hbm, feat_ref, IN_COPIES) + ((in_hbm, in_ref),)
    copies = start_copies(pairs, sems)
    late_pairs = ((slot_hbm, slot_ref), (list_hbm, list_ref))
    late_pairs += tuple(zip(sources, targets)) + in_parts(bank_hbm, held.bank, BANK_COPIES)

    @pl.when(jnp.logical_not(early))
    def _():
        start_copies(late_pairs, held_sems)

    @pl.when(early)
    def _():
        for name in held.names[1:]:
            getattr(held, name)[...] = getattr(given, name)[...]

    for copy in copies:
        copy.wait()
    channels, lon_len = feat_ref.shape[0], feat_ref.shape[2]
    rows_ref[...] = feat_ref[...].astype(F32).reshape(channels * lat_len, lon_len)
    cells = jnp.concatenate(
        [rows_ref[pl.ds(p, channels, stride=lat_len), :].astype(BF16) for p in range(lat_len)], axis=1
    )
    red_ref[...] = jnp.dot(in_ref[...], cells, preferred_element_type=F32).astype(BF16)

    @pl.when(jnp.logical_not(early))
    def _():
        waits = [
            pltpu.make_async_copy(source, target, held_sems.at[i]) for i, (source, target) in enumerate(late_pairs)
        ]
        for copy in waits[:2]:
            copy.wait()
        build_held(lon_count, list_ref, slot_ref, targets, waits[2:], held)


def pick_kernel(lon_count, lat_len, got_b_ref, got_a_ref, early_bank_ref, late_bank_ref, core_a_ref, core_b_ref):
    early = lax.axis_index("lon") != lon_count - 1
    lane = lane_index((1, LANES))
    for got_ref, core_ref in ((got_b_ref, core_b_ref), (got_a_ref, core_a_ref)):
        head = got_ref[...].astype(F32)[0:1, :]
        for nth in range(PER_OWNER):
            row = jnp.sum(jnp.where(lane == EDGE * lat_len + nth, head, 0.0)).astype(jnp.int32)
            core_ref[nth] = jnp.where(early, early_bank_ref[row], late_bank_ref[row])


def rows_kernel(lat_len, got_b_ref, got_a_ref, core_ref, red_ref, edge_ref, row_a_ref, row_b_ref):
    lon_len = red_ref.shape[1] // lat_len
    even = (lax.axis_index("lon") % 2) == 0
    from_prev = lane_index(got_a_ref.shape) < REACH * lat_len
    got = jnp.where(from_prev == even, got_b_ref[...].astype(F32), got_a_ref[...].astype(F32)).astype(BF16)
    source = lax.broadcasted_iota(jnp.int32, (LANES, LANES), 0)
    target = lane_index((LANES, LANES))
    order = (source == (target % EDGE) * lat_len + target // EDGE) & (target < EDGE * lat_len)
    edges = jnp.dot(got, order.astype(BF16), preferred_element_type=F32).astype(BF16)
    edge_ref[...] = edges
    even = (lax.axis_index("lat") % 2) == 0
    head = red_ref[:, : REACH * lon_len].astype(F32)
    tail = red_ref[:, (lat_len - REACH) * lon_len :].astype(F32)
    row_a_ref[:, : REACH * lon_len] = jnp.where(even, tail, head).astype(BF16)
    row_b_ref[:, : REACH * lon_len] = jnp.where(even, head, tail).astype(BF16)
    row_a_ref[:, REACH * lon_len :] = edges
    row_b_ref[:, REACH * lon_len :] = edges


def shifted_columns(row, edges, place):
    lane = lane_index(row.shape)
    lon_len = row.shape[1]
    edges = pltpu.roll(edges, (LANES - REACH - EDGE * place) % LANES, 1)
    moved = []
    for col_off in range(KS):
        shift = REACH - col_off
        if shift > 0:
            piece = pltpu.roll(jnp.where(lane >= lon_len - shift, edges, row), shift, 1)
        elif shift < 0:
            piece = pltpu.roll(jnp.where(lane < -shift, edges, row), lon_len + shift, 1)
        else:
            piece = row
        moved.append(piece.astype(BF16))
    return moved


def stack_row(stack_ref, p, moved, slots, lon_len):
    half = moved[0].shape[0] // 2
    for col_off, piece in enumerate(moved):
        for row_off in range(KS):
            slot = slots.get(p + REACH - row_off)
            if slot is not None:
                k = row_off * KS + col_off
                for h in range(2):
                    stack_ref[h, k * half : (k + 1) * half, slot * lon_len : (slot + 1) * lon_len] = piece[
                        h * half : (h + 1) * half
                    ]


def apply_taps(rank, weights_ref, stacked, tapped_ref, lon_len):
    half = rank // 2
    tap_rank = tapped_ref.shape[0] // rank
    width = STEP * lon_len
    for start in range(0, tapped_ref.shape[1], width):
        parts = [
            jnp.dot(weights_ref[...], stacked(h, start, width), preferred_element_type=F32)
            .astype(BF16)
            .reshape(tap_rank, 1, half, width)
            for h in range(2)
        ]
        tapped_ref[:, start : start + width] = jnp.concatenate(parts, axis=1).reshape(tap_rank * rank, width)


def border_slots(lat_len):
    slots = {p: p for p in range(REACH)}
    slots.update({lat_len - REACH + p: REACH + p for p in range(REACH)})
    return slots


def inner_kernel(lat_len, red_ref, edge_ref, weights_ref, tapped_ref, halo_stack_ref, stack_ref):
    rank = red_ref.shape[0]
    lon_len = red_ref.shape[1] // lat_len
    slots = {p: p - REACH for p in range(REACH, lat_len - REACH)}
    edges = edge_ref[...].astype(F32)
    for p in range(lat_len):
        row = red_ref[:, p * lon_len : (p + 1) * lon_len].astype(F32)
        moved = shifted_columns(row, edges, p)
        stack_row(stack_ref, p, moved, slots, lon_len)
        stack_row(halo_stack_ref, p, moved, border_slots(lat_len), lon_len)
    apply_taps(rank, weights_ref, lambda h, start, width: stack_ref[h, :, start : start + width], tapped_ref, lon_len)


def border_kernel(lat_len, lat_count, row_b_ref, row_a_ref, weights_ref, own_stack_ref, tapped_ref, stack_ref):
    rank = row_a_ref.shape[0]
    lon_len = (row_a_ref.shape[1] - LANES) // REACH
    lat = lax.axis_index("lat")
    even = (lat % 2) == 0
    row_a = row_a_ref[...].astype(F32)
    row_b = row_b_ref[...].astype(F32)
    above = jnp.where(lat == 0, 0.0, jnp.where(even, row_b, row_a))
    below = jnp.where(lat == lat_count - 1, 0.0, jnp.where(even, row_a, row_b))
    slots = border_slots(lat_len)
    for i in range(REACH):
        for p, holder, place in ((i - REACH, above, lat_len - REACH + i), (lat_len + i, below, i)):
            row = holder[:, i * lon_len : (i + 1) * lon_len]
            moved = shifted_columns(row, holder[:, REACH * lon_len :], place)
            stack_row(stack_ref, p, moved, slots, lon_len)
    block = KS * rank // 2
    in_halo = {
        (slot, row_off)
        for p, slot in slots.items()
        for row_off in range(KS)
        if not 0 <= p + row_off - REACH < lat_len
    }

    def stacked(h, start, width):
        columns = []
        for slot in range(start // lon_len, (start + width) // lon_len):
            span = slice(slot * lon_len, (slot + 1) * lon_len)
            pieces = []
            for row_off in range(KS):
                ref = stack_ref if (slot, row_off) in in_halo else own_stack_ref
                pieces.append(ref[h, row_off * block : (row_off + 1) * block, span])
            columns.append(jnp.concatenate(pieces, axis=0))
        return jnp.concatenate(columns, axis=1)

    apply_taps(rank, weights_ref, stacked, tapped_ref, lon_len)


def mix_kernel(
    inner_ref,
    border_ref,
    core_a_ref,
    core_b_ref,
    own_ref,
    position_ref,
    mixer_ref,
    offset_ref,
    out_hbm,
    stage_ref,
    sems,
):
    lat_len, lon_len = position_ref.shape
    rank = own_ref.shape[1]
    cores = jnp.concatenate(
        [ref[...].reshape(PER_OWNER * rank, -1) for ref in (own_ref, core_a_ref, core_b_ref)], axis=0
    )
    chunks = [(border_ref, 0, [*range(REACH), *range(lat_len - REACH, lat_len)])]
    for start in range(REACH, lat_len - REACH, STEP):
        chunks.append((inner_ref, start - REACH, [*range(start, start + STEP)]))
    by_row = {}
    for ref, first, rows in chunks:
        width = len(rows) * lon_len
        every = jnp.dot(cores, ref[:, first * lon_len : first * lon_len + width], preferred_element_type=F32)
        position = jnp.concatenate([position_ref[r : r + 1, :] for r in rows], axis=1)
        hidden = jnp.zeros((rank, width), F32)
        for index in range(3 * PER_OWNER):
            hidden = jnp.where(position == index, every[index * rank : (index + 1) * rank], hidden)
        hidden = hidden.astype(BF16)
        for i, r in enumerate(rows):
            by_row[r] = hidden[:, i * lon_len : (i + 1) * lon_len]
    pieces = [by_row[r] for r in range(lat_len)]
    groups = [jnp.concatenate(pieces[g : g + GROUP], axis=0) for g in range(0, lat_len, GROUP)]
    channels = stage_ref.shape[0]
    share = channels // OUT_COPIES
    copies = []
    for part in range(OUT_COPIES):
        span = slice(part * share * GROUP, (part + 1) * share * GROUP)
        blocks = []
        for hidden in groups:
            output = jnp.dot(mixer_ref[span, :], hidden, preferred_element_type=F32) + offset_ref[span, :]
            mixed = 0.5 * output * (1.0 + jnp.tanh(0.5 * output))
            blocks.append(mixed.reshape(share, GROUP, lon_len))
        held = slice(part * share, (part + 1) * share)
        stage_ref[held] = jnp.concatenate(blocks, axis=1).astype(BF16)
        copy = pltpu.make_async_copy(stage_ref.at[held], out_hbm.at[held], sems.at[part])
        copy.start()
        copies.append(copy)
    for copy in copies:
        copy.wait()


def on_device(
    features, labels, tile_regions, bank_slot, kernel_bank, in_factor, tap_factor, out_factor, out_bias
):
    channels, lat_len, lon_len = features.shape
    rank = in_factor.shape[0]
    held, core_rows, core_cols = kernel_bank.shape
    tap_rank, taps = tap_factor.shape
    out_channels = out_factor.shape[0]
    cells = lat_len * lon_len
    lon_count, lat_count = lax.axis_size("lon"), lax.axis_size("lat")
    lon_first, lon_second = swap_pairs(lon_count)
    lat_first, lat_second = swap_pairs(lat_count)
    edge_shape = jax.ShapeDtypeStruct((rank, LANES), BF16)
    core_shape = jax.ShapeDtypeStruct((PER_OWNER, core_rows, core_cols), BF16)
    held_shapes = (
        jax.ShapeDtypeStruct(kernel_bank.shape, BF16),
        core_shape,
        jax.ShapeDtypeStruct(labels.shape, jnp.int32),
        jax.ShapeDtypeStruct((tap_rank * rank // 2, taps * rank // 2), BF16),
        jax.ShapeDtypeStruct((out_channels * GROUP, rank * GROUP), BF16),
        jax.ShapeDtypeStruct((out_channels * GROUP, lon_len), F32),
    )
    lists = [
        pltpu.SMEM(tile_regions.shape, jnp.int32),
        pltpu.SMEM(bank_slot.shape, jnp.int32),
        pltpu.VMEM(features.shape, BF16),
        pltpu.VMEM(in_factor.shape, BF16),
    ]
    targets = [
        pltpu.VMEM(labels.shape, jnp.int32),
        pltpu.VMEM(tap_factor.shape, BF16),
        pltpu.VMEM(out_factor.shape[::-1], BF16),
        pltpu.VMEM((1, out_channels), F32),
    ]
    sources = tuple(
        in_hbm(x)
        for x in (
            tile_regions,
            bank_slot,
            features,
            in_factor,
            kernel_bank,
            labels,
            tap_factor,
            out_factor.T,
            out_bias.reshape(1, -1),
        )
    )
    pay_a, pay_b, early_bank, *given = pl.pallas_call(
        functools.partial(edge_kernel, lon_count),
        out_shape=(edge_shape, edge_shape, *held_shapes),
        in_specs=[HBM] * 9,
        out_specs=(VMEM,) * 8,
        scratch_shapes=[
            *lists,
            pltpu.VMEM((channels * EDGE, lat_len), F32),
            *targets,
            pltpu.SemaphoreType.DMA((IN_COPIES + 3,)),
            pltpu.SemaphoreType.DMA((4 + BANK_COPIES,)),
        ],
        compiler_params=PARAMS,
    )(*sources)
    got_b = lax.ppermute(pay_b, "lon", lon_second)
    got_a = lax.ppermute(pay_a, "lon", lon_first)
    reduced, late_bank, own, position, weights, mixer, offset = pl.pallas_call(
        functools.partial(prepare_kernel, lon_count, lat_len),
        out_shape=(jax.ShapeDtypeStruct((rank, cells), BF16), *held_shapes),
        in_specs=[HBM] * 9 + [VMEM] * 5,
        out_specs=(VMEM,) * 7,
        scratch_shapes=[
            *lists,
            pltpu.VMEM((channels * lat_len, lon_len), F32),
            *targets,
            pltpu.SemaphoreType.DMA((IN_COPIES + 1,)),
            pltpu.SemaphoreType.DMA((6 + BANK_COPIES,)),
        ],
        compiler_params=PARAMS,
        cost_estimate=pl.CostEstimate(flops=10**6, bytes_accessed=kernel_bank.size * 4, transcendentals=0),
    )(*sources, *given)
    row_shape = jax.ShapeDtypeStruct((rank, REACH * lon_len + LANES), BF16)
    core_a, core_b = pl.pallas_call(
        functools.partial(pick_kernel, lon_count, lat_len),
        out_shape=(core_shape, core_shape),
        in_specs=[VMEM] * 4,
        out_specs=(VMEM,) * 2,
        compiler_params=PARAMS,
    )(got_b, got_a, early_bank, late_bank)
    edges, row_a, row_b = pl.pallas_call(
        functools.partial(rows_kernel, lat_len),
        out_shape=(edge_shape, row_shape, row_shape),
        in_specs=[VMEM, VMEM, HBM, VMEM],
        out_specs=(VMEM,) * 3,
        compiler_params=PARAMS,
    )(got_b, got_a, core_b, reduced)
    core_b = lax.ppermute(core_b, "lon", lon_second)
    core_a = lax.ppermute(core_a, "lon", lon_first)
    row_a = lax.ppermute(row_a, "lat", lat_first)
    row_b = lax.ppermute(row_b, "lat", lat_second)
    border_cells = 2 * REACH * lon_len
    stack_rows = taps * rank // 2
    halo_stack_shape = jax.ShapeDtypeStruct((2, stack_rows, border_cells), BF16)
    inner, halo_stack = pl.pallas_call(
        functools.partial(inner_kernel, lat_len),
        out_shape=(jax.ShapeDtypeStruct((tap_rank * rank, cells - border_cells), BF16), halo_stack_shape),
        in_specs=[VMEM] * 3,
        out_specs=(VMEM,) * 2,
        scratch_shapes=[pltpu.VMEM((2, stack_rows, cells - border_cells), BF16)],
        compiler_params=PARAMS,
    )(reduced, edges, weights)
    border = pl.pallas_call(
        functools.partial(border_kernel, lat_len, lat_count),
        out_shape=jax.ShapeDtypeStruct((tap_rank * rank, border_cells), BF16),
        in_specs=[VMEM] * 4,
        out_specs=VMEM,
        scratch_shapes=[pltpu.VMEM(halo_stack_shape.shape, BF16)],
        compiler_params=PARAMS,
    )(row_b, row_a, weights, halo_stack)
    out_shape = (out_channels, lat_len, lon_len)
    return pl.pallas_call(
        mix_kernel,
        out_shape=jax.ShapeDtypeStruct(out_shape, BF16),
        in_specs=[VMEM] * 8,
        out_specs=HBM,
        scratch_shapes=[pltpu.VMEM(out_shape, BF16), pltpu.SemaphoreType.DMA((OUT_COPIES,))],
        compiler_params=PARAMS,
    )(inner, border, core_a, core_b, own, position, mixer, offset)


def solution(mesh):
    placed = (
        P(None, "lat", "lon"),
        P("lat", "lon"),
        P("lat", "lon", None),
        P(),
        P("lon", None, None),
        P(),
        P(),
        P(),
        P(),
    )
    return jax.shard_map(
        on_device, mesh=mesh, in_specs=placed, out_specs=P(None, "lat", "lon"), check_vma=False
    )
```

```python
import functools

import jax
import jax.numpy as jnp
from jax import lax
from jax.experimental import pallas as pl
from jax.experimental.pallas import tpu as pltpu
from jax.sharding import PartitionSpec as P

KS = 5
REACH = KS // 2
PER_OWNER = 2
LANES = 128
EDGE = 2 * REACH
GROUP = 8
STEP = 4
OUT_COPIES = 4
IN_COPIES = 4
BANK_COPIES = 8
EARLY = 2
F32 = jnp.float32
BF16 = jnp.bfloat16
VMEM = pl.BlockSpec(memory_space=pltpu.VMEM)
SMEM = pl.BlockSpec(memory_space=pltpu.SMEM)
HBM = pl.BlockSpec(memory_space=pltpu.HBM)
PARAMS = pltpu.CompilerParams(vmem_limit_bytes=24 * 1024 * 1024)


def swap_pairs(count):
    first = [(i, i ^ 1) for i in range(count)]
    second = [(i, (i + 1 if i % 2 else i - 1) % count) for i in range(count)]
    return first, second


def in_hbm(array):
    return pltpu.with_memory_space_constraint(array, pltpu.HBM)


def lane_index(shape):
    return lax.broadcasted_iota(jnp.int32, shape, 1)


def start_copies(pairs, sems):
    copies = [pltpu.make_async_copy(source, target, sems.at[i]) for i, (source, target) in enumerate(pairs)]
    for copy in copies:
        copy.start()
    return copies


def in_parts(source, target, count):
    share = target.shape[0] // count
    return tuple((source.at[pl.ds(i * share, share)], target.at[pl.ds(i * share, share)]) for i in range(count))


def find_rows(list_ref, slot_ref, lon_count, held):
    me = lax.axis_index("lon")
    owners = (me, lax.rem(me + lon_count - 1, lon_count), lax.rem(me + 1, lon_count))
    slots = [slot_ref[list_ref[0, 0, i]] for i in range(list_ref.shape[2])]
    places, rows = [], []
    for owner in owners:
        least, greatest = jnp.int32(held), jnp.int32(-1)
        first, last = jnp.int32(0), jnp.int32(0)
        for i, slot in enumerate(slots):
            local = slot - owner * held
            hit = (local >= 0) & (local < held)
            first = jnp.where(hit & (local < least), i, first)
            last = jnp.where(hit & (local > greatest), i, last)
            least = jnp.where(hit, jnp.minimum(local, least), least)
            greatest = jnp.where(hit, jnp.maximum(local, greatest), greatest)
        places.append([first, last])
        rows.append([jnp.minimum(least, held - 1), jnp.maximum(greatest, 0)])
    return places, rows


def is_early():
    return lax.axis_index("lon") < EARLY


class Held:
    names = ("bank", "own", "position", "weights", "mixer", "offset")
    sources = ("labels", "tap", "out_factor", "bias")

    def __init__(self, refs):
        self.__dict__.update(zip(self.names, refs))


def start_sources(sources, targets, bank_hbm, bank_ref, sems):
    pairs = tuple(zip(sources, targets))
    return start_copies(pairs + in_parts(bank_hbm, bank_ref, BANK_COPIES), sems)


def build_held(lon_count, list_ref, slot_ref, targets, copies, held):
    labels_ref, tap_ref, out_factor_ref, bias_ref = targets
    for copy in copies[: len(targets)]:
        copy.wait()
    places, rows = find_rows(list_ref, slot_ref, lon_count, held.bank.shape[0])
    even = (lax.axis_index("lon") % 2) == 0
    order = list(places[0])
    order += [jnp.where(even, places[2][nth], places[1][nth]) for nth in range(PER_OWNER)]
    order += [jnp.where(even, places[1][nth], places[2][nth]) for nth in range(PER_OWNER)]
    labels = labels_ref[...]
    position = jnp.zeros(labels.shape, jnp.int32)
    for index, place in enumerate(order):
        position = jnp.where(labels == place, index, position)
    held.position[...] = position

    rank, out_channels = out_factor_ref.shape
    half = rank // 2
    tap_rank, taps = tap_ref.shape
    shape = (tap_rank * half, taps * half)
    spread = (
        lax.broadcasted_iota(jnp.int32, (shape[0], tap_rank), 0) // half == lane_index((shape[0], tap_rank))
    ).astype(BF16)
    repeat = (
        lax.broadcasted_iota(jnp.int32, (taps, shape[1]), 0) == lane_index((taps, shape[1])) // half
    ).astype(BF16)
    tall = jnp.dot(spread, tap_ref[...], preferred_element_type=F32).astype(BF16)
    wide = jnp.dot(tall, repeat, preferred_element_type=F32)
    same = lax.broadcasted_iota(jnp.int32, shape, 0) % half == lane_index(shape) % half
    held.weights[...] = jnp.where(same, wide, 0.0).astype(BF16)

    shape = (out_channels * GROUP, rank * GROUP)
    spread = (
        lax.broadcasted_iota(jnp.int32, (shape[0], out_channels), 0) // GROUP
        == lane_index((shape[0], out_channels))
    ).astype(BF16)
    repeat = (
        lax.broadcasted_iota(jnp.int32, (rank, shape[1]), 0) == lane_index((rank, shape[1])) % rank
    ).astype(BF16)
    tall = lax.dot_general(
        spread, out_factor_ref[...], (((1,), (1,)), ((), ())), preferred_element_type=F32
    ).astype(BF16)
    wide = jnp.dot(tall, repeat, preferred_element_type=F32)
    same = lax.broadcasted_iota(jnp.int32, shape, 0) % GROUP == lane_index(shape) // rank
    held.mixer[...] = jnp.where(same, wide, 0.0).astype(BF16)

    shape = (out_channels * GROUP, out_channels)
    mine = lax.broadcasted_iota(jnp.int32, shape, 0) // GROUP == lane_index(shape)
    offset = jnp.sum(jnp.where(mine, bias_ref[...], 0.0), axis=1, keepdims=True)
    held.offset[...] = jnp.broadcast_to(offset, held.offset.shape)
    for copy in copies[len(targets) :]:
        copy.wait()
    for nth in range(PER_OWNER):
        held.own[nth] = held.bank[rows[0][nth]]


def edge_kernel(lon_count, *refs):
    list_hbm, slot_hbm, feat_hbm, in_hbm, bank_hbm = refs[:5]
    sources, (pay_a_ref, pay_b_ref), held_refs = refs[5:9], refs[9:11], refs[11:17]
    list_ref, slot_ref, feat_ref, in_ref, turned_ref = refs[17:22]
    targets, sems, held_sems = refs[22:26], refs[26], refs[27]
    held = Held(held_refs)
    channels, lat_len, lon_len = feat_ref.shape
    rank = in_ref.shape[0]
    pairs = in_parts(feat_hbm, feat_ref, IN_COPIES)
    pairs += ((slot_hbm, slot_ref), (list_hbm, list_ref), (in_hbm, in_ref))
    for copy in start_copies(pairs, sems):
        copy.wait()
    lane = lane_index((lat_len, LANES))
    batch = LANES // EDGE
    for first in range(0, channels, batch):
        packed = jnp.zeros((lat_len, LANES), F32)
        for c in range(batch):
            moved = pltpu.roll(feat_ref[first + c].astype(F32), (EDGE * c + REACH) % LANES, 1)
            packed = jnp.where(lane // EDGE == c, moved, packed)
        turned_ref[first * EDGE : (first + batch) * EDGE, :] = jnp.transpose(packed)
    columns = jnp.concatenate(
        [turned_ref[pl.ds(j, channels, stride=EDGE), :].astype(BF16) for j in range(EDGE)], axis=1
    )
    edges = jnp.dot(in_ref[...], columns, preferred_element_type=F32)
    edges = jnp.concatenate([edges, jnp.zeros((rank, LANES - EDGE * lat_len), F32)], axis=1)
    _, rows = find_rows(list_ref, slot_ref, lon_count, held.bank.shape[0])
    even = (lax.axis_index("lon") % 2) == 0
    lane = lane_index((rank, LANES))
    for out_ref, wanted in ((pay_a_ref, even), (pay_b_ref, jnp.logical_not(even))):
        load = edges
        for nth in range(PER_OWNER):
            row = jnp.where(wanted, rows[2][nth], rows[1][nth]).astype(F32)
            load = jnp.where(lane == EDGE * lat_len + nth, row, load)
        out_ref[...] = load.astype(BF16)

    @pl.when(is_early())
    def _():
        copies = start_sources(sources, targets, bank_hbm, held.bank, held_sems)
        build_held(lon_count, list_ref, slot_ref, targets, copies, held)


def prepare_kernel(lon_count, lat_len, *refs):
    list_hbm, slot_hbm, feat_hbm, in_hbm, bank_hbm = refs[:5]
    sources, given = refs[5:9], Held((None, *refs[9:14]))
    red_ref, held = refs[14], Held(refs[15:21])
    list_ref, slot_ref, feat_ref, in_ref, rows_ref = refs[21:26]
    targets, sems, held_sems = refs[26:30], refs[30], refs[31]
    early = is_early()
    pairs = in_parts(feat_hbm, feat_ref, IN_COPIES) + ((in_hbm, in_ref),)
    copies = start_copies(pairs, sems)
    late_pairs = ((slot_hbm, slot_ref), (list_hbm, list_ref))
    late_pairs += tuple(zip(sources, targets)) + in_parts(bank_hbm, held.bank, BANK_COPIES)

    @pl.when(jnp.logical_not(early))
    def _():
        start_copies(late_pairs, held_sems)

    @pl.when(early)
    def _():
        for name in held.names[1:]:
            getattr(held, name)[...] = getattr(given, name)[...]

    for copy in copies:
        copy.wait()
    channels, lon_len = feat_ref.shape[0], feat_ref.shape[2]
    rows_ref[...] = feat_ref[...].astype(F32).reshape(channels * lat_len, lon_len)
    cells = jnp.concatenate(
        [rows_ref[pl.ds(p, channels, stride=lat_len), :].astype(BF16) for p in range(lat_len)], axis=1
    )
    red_ref[...] = jnp.dot(in_ref[...], cells, preferred_element_type=F32).astype(BF16)

    @pl.when(jnp.logical_not(early))
    def _():
        waits = [
            pltpu.make_async_copy(source, target, held_sems.at[i]) for i, (source, target) in enumerate(late_pairs)
        ]
        for copy in waits[:2]:
            copy.wait()
        build_held(lon_count, list_ref, slot_ref, targets, waits[2:], held)


def pick_kernel(lat_len, got_b_ref, got_a_ref, early_bank_ref, late_bank_ref, core_a_ref, core_b_ref):
    early = is_early()
    lane = lane_index((1, LANES))
    for got_ref, core_ref in ((got_b_ref, core_b_ref), (got_a_ref, core_a_ref)):
        head = got_ref[...].astype(F32)[0:1, :]
        for nth in range(PER_OWNER):
            row = jnp.sum(jnp.where(lane == EDGE * lat_len + nth, head, 0.0)).astype(jnp.int32)
            core_ref[nth] = jnp.where(early, early_bank_ref[row], late_bank_ref[row])


def rows_kernel(lat_len, got_b_ref, got_a_ref, core_ref, red_ref, edge_ref, row_a_ref, row_b_ref):
    lon_len = red_ref.shape[1] // lat_len
    even = (lax.axis_index("lon") % 2) == 0
    from_prev = lane_index(got_a_ref.shape) < REACH * lat_len
    got = jnp.where(from_prev == even, got_b_ref[...].astype(F32), got_a_ref[...].astype(F32)).astype(BF16)
    source = lax.broadcasted_iota(jnp.int32, (LANES, LANES), 0)
    target = lane_index((LANES, LANES))
    order = (source == (target % EDGE) * lat_len + target // EDGE) & (target < EDGE * lat_len)
    edges = jnp.dot(got, order.astype(BF16), preferred_element_type=F32).astype(BF16)
    edge_ref[...] = edges
    even = (lax.axis_index("lat") % 2) == 0
    head = red_ref[:, : REACH * lon_len].astype(F32)
    tail = red_ref[:, (lat_len - REACH) * lon_len :].astype(F32)
    row_a_ref[:, : REACH * lon_len] = jnp.where(even, tail, head).astype(BF16)
    row_b_ref[:, : REACH * lon_len] = jnp.where(even, head, tail).astype(BF16)
    row_a_ref[:, REACH * lon_len :] = edges
    row_b_ref[:, REACH * lon_len :] = edges


def shifted_columns(row, edges, place):
    lane = lane_index(row.shape)
    lon_len = row.shape[1]
    edges = pltpu.roll(edges, (LANES - REACH - EDGE * place) % LANES, 1)
    moved = []
    for col_off in range(KS):
        shift = REACH - col_off
        if shift > 0:
            piece = pltpu.roll(jnp.where(lane >= lon_len - shift, edges, row), shift, 1)
        elif shift < 0:
            piece = pltpu.roll(jnp.where(lane < -shift, edges, row), lon_len + shift, 1)
        else:
            piece = row
        moved.append(piece.astype(BF16))
    return moved


def stack_row(stack_ref, p, moved, slots, lon_len):
    half = moved[0].shape[0] // 2
    for col_off, piece in enumerate(moved):
        for row_off in range(KS):
            slot = slots.get(p + REACH - row_off)
            if slot is not None:
                k = row_off * KS + col_off
                for h in range(2):
                    stack_ref[h, k * half : (k + 1) * half, slot * lon_len : (slot + 1) * lon_len] = piece[
                        h * half : (h + 1) * half
                    ]


def apply_taps(rank, weights_ref, stacked, tapped_ref, lon_len):
    half = rank // 2
    tap_rank = tapped_ref.shape[0] // rank
    width = STEP * lon_len
    for start in range(0, tapped_ref.shape[1], width):
        parts = [
            jnp.dot(weights_ref[...], stacked(h, start, width), preferred_element_type=F32)
            .astype(BF16)
            .reshape(tap_rank, 1, half, width)
            for h in range(2)
        ]
        tapped_ref[:, start : start + width] = jnp.concatenate(parts, axis=1).reshape(tap_rank * rank, width)


def border_slots(lat_len):
    slots = {p: p for p in range(REACH)}
    slots.update({lat_len - REACH + p: REACH + p for p in range(REACH)})
    return slots


def inner_kernel(lat_len, red_ref, edge_ref, weights_ref, tapped_ref, halo_stack_ref, stack_ref):
    rank = red_ref.shape[0]
    lon_len = red_ref.shape[1] // lat_len
    slots = {p: p - REACH for p in range(REACH, lat_len - REACH)}
    edges = edge_ref[...].astype(F32)
    for p in range(lat_len):
        row = red_ref[:, p * lon_len : (p + 1) * lon_len].astype(F32)
        moved = shifted_columns(row, edges, p)
        stack_row(stack_ref, p, moved, slots, lon_len)
        stack_row(halo_stack_ref, p, moved, border_slots(lat_len), lon_len)
    apply_taps(rank, weights_ref, lambda h, start, width: stack_ref[h, :, start : start + width], tapped_ref, lon_len)


def border_kernel(lat_len, lat_count, row_b_ref, row_a_ref, weights_ref, own_stack_ref, tapped_ref, stack_ref):
    rank = row_a_ref.shape[0]
    lon_len = (row_a_ref.shape[1] - LANES) // REACH
    lat = lax.axis_index("lat")
    even = (lat % 2) == 0
    row_a = row_a_ref[...].astype(F32)
    row_b = row_b_ref[...].astype(F32)
    above = jnp.where(lat == 0, 0.0, jnp.where(even, row_b, row_a))
    below = jnp.where(lat == lat_count - 1, 0.0, jnp.where(even, row_a, row_b))
    slots = border_slots(lat_len)
    for i in range(REACH):
        for p, holder, place in ((i - REACH, above, lat_len - REACH + i), (lat_len + i, below, i)):
            row = holder[:, i * lon_len : (i + 1) * lon_len]
            moved = shifted_columns(row, holder[:, REACH * lon_len :], place)
            stack_row(stack_ref, p, moved, slots, lon_len)
    block = KS * rank // 2
    in_halo = {
        (slot, row_off)
        for p, slot in slots.items()
        for row_off in range(KS)
        if not 0 <= p + row_off - REACH < lat_len
    }

    def stacked(h, start, width):
        columns = []
        for slot in range(start // lon_len, (start + width) // lon_len):
            span = slice(slot * lon_len, (slot + 1) * lon_len)
            pieces = []
            for row_off in range(KS):
                ref = stack_ref if (slot, row_off) in in_halo else own_stack_ref
                pieces.append(ref[h, row_off * block : (row_off + 1) * block, span])
            columns.append(jnp.concatenate(pieces, axis=0))
        return jnp.concatenate(columns, axis=1)

    apply_taps(rank, weights_ref, stacked, tapped_ref, lon_len)


def mix_kernel(
    inner_ref,
    border_ref,
    core_a_ref,
    core_b_ref,
    own_ref,
    position_ref,
    mixer_ref,
    offset_ref,
    out_hbm,
    stage_ref,
    sems,
):
    lat_len, lon_len = position_ref.shape
    rank = own_ref.shape[1]
    cores = jnp.concatenate(
        [ref[...].reshape(PER_OWNER * rank, -1) for ref in (own_ref, core_a_ref, core_b_ref)], axis=0
    )
    chunks = [(border_ref, 0, [*range(REACH), *range(lat_len - REACH, lat_len)])]
    for start in range(REACH, lat_len - REACH, STEP):
        chunks.append((inner_ref, start - REACH, [*range(start, start + STEP)]))
    by_row = {}
    for ref, first, rows in chunks:
        width = len(rows) * lon_len
        every = jnp.dot(cores, ref[:, first * lon_len : first * lon_len + width], preferred_element_type=F32)
        position = jnp.concatenate([position_ref[r : r + 1, :] for r in rows], axis=1)
        hidden = jnp.zeros((rank, width), F32)
        for index in range(3 * PER_OWNER):
            hidden = jnp.where(position == index, every[index * rank : (index + 1) * rank], hidden)
        hidden = hidden.astype(BF16)
        for i, r in enumerate(rows):
            by_row[r] = hidden[:, i * lon_len : (i + 1) * lon_len]
    pieces = [by_row[r] for r in range(lat_len)]
    groups = [jnp.concatenate(pieces[g : g + GROUP], axis=0) for g in range(0, lat_len, GROUP)]
    channels = stage_ref.shape[0]
    share = channels // OUT_COPIES
    copies = []
    for part in range(OUT_COPIES):
        span = slice(part * share * GROUP, (part + 1) * share * GROUP)
        blocks = []
        for hidden in groups:
            output = jnp.dot(mixer_ref[span, :], hidden, preferred_element_type=F32) + offset_ref[span, :]
            mixed = 0.5 * output * (1.0 + jnp.tanh(0.5 * output))
            blocks.append(mixed.reshape(share, GROUP, lon_len))
        held = slice(part * share, (part + 1) * share)
        stage_ref[held] = jnp.concatenate(blocks, axis=1).astype(BF16)
        copy = pltpu.make_async_copy(stage_ref.at[held], out_hbm.at[held], sems.at[part])
        copy.start()
        copies.append(copy)
    for copy in copies:
        copy.wait()


def on_device(
    features, labels, tile_regions, bank_slot, kernel_bank, in_factor, tap_factor, out_factor, out_bias
):
    channels, lat_len, lon_len = features.shape
    rank = in_factor.shape[0]
    held, core_rows, core_cols = kernel_bank.shape
    tap_rank, taps = tap_factor.shape
    out_channels = out_factor.shape[0]
    cells = lat_len * lon_len
    lon_count, lat_count = lax.axis_size("lon"), lax.axis_size("lat")
    lon_first, lon_second = swap_pairs(lon_count)
    lat_first, lat_second = swap_pairs(lat_count)
    edge_shape = jax.ShapeDtypeStruct((rank, LANES), BF16)
    core_shape = jax.ShapeDtypeStruct((PER_OWNER, core_rows, core_cols), BF16)
    held_shapes = (
        jax.ShapeDtypeStruct(kernel_bank.shape, BF16),
        core_shape,
        jax.ShapeDtypeStruct(labels.shape, jnp.int32),
        jax.ShapeDtypeStruct((tap_rank * rank // 2, taps * rank // 2), BF16),
        jax.ShapeDtypeStruct((out_channels * GROUP, rank * GROUP), BF16),
        jax.ShapeDtypeStruct((out_channels * GROUP, lon_len), F32),
    )
    lists = [
        pltpu.SMEM(tile_regions.shape, jnp.int32),
        pltpu.SMEM(bank_slot.shape, jnp.int32),
        pltpu.VMEM(features.shape, BF16),
        pltpu.VMEM(in_factor.shape, BF16),
    ]
    targets = [
        pltpu.VMEM(labels.shape, jnp.int32),
        pltpu.VMEM(tap_factor.shape, BF16),
        pltpu.VMEM(out_factor.shape[::-1], BF16),
        pltpu.VMEM((1, out_channels), F32),
    ]
    sources = tuple(
        in_hbm(x)
        for x in (
            tile_regions,
            bank_slot,
            features,
            in_factor,
            kernel_bank,
            labels,
            tap_factor,
            out_factor.T,
            out_bias.reshape(1, -1),
        )
    )
    pay_a, pay_b, early_bank, *given = pl.pallas_call(
        functools.partial(edge_kernel, lon_count),
        out_shape=(edge_shape, edge_shape, *held_shapes),
        in_specs=[HBM] * 9,
        out_specs=(VMEM,) * 8,
        scratch_shapes=[
            *lists,
            pltpu.VMEM((channels * EDGE, lat_len), F32),
            *targets,
            pltpu.SemaphoreType.DMA((IN_COPIES + 3,)),
            pltpu.SemaphoreType.DMA((4 + BANK_COPIES,)),
        ],
        compiler_params=PARAMS,
    )(*sources)
    got_b = lax.ppermute(pay_b, "lon", lon_second)
    got_a = lax.ppermute(pay_a, "lon", lon_first)
    reduced, late_bank, own, position, weights, mixer, offset = pl.pallas_call(
        functools.partial(prepare_kernel, lon_count, lat_len),
        out_shape=(jax.ShapeDtypeStruct((rank, cells), BF16), *held_shapes),
        in_specs=[HBM] * 9 + [VMEM] * 5,
        out_specs=(VMEM,) * 7,
        scratch_shapes=[
            *lists,
            pltpu.VMEM((channels * lat_len, lon_len), F32),
            *targets,
            pltpu.SemaphoreType.DMA((IN_COPIES + 1,)),
            pltpu.SemaphoreType.DMA((6 + BANK_COPIES,)),
        ],
        compiler_params=PARAMS,
        cost_estimate=pl.CostEstimate(flops=10**6, bytes_accessed=kernel_bank.size * 4, transcendentals=0),
    )(*sources, *given)
    row_shape = jax.ShapeDtypeStruct((rank, REACH * lon_len + LANES), BF16)
    core_a, core_b = pl.pallas_call(
        functools.partial(pick_kernel, lat_len),
        out_shape=(core_shape, core_shape),
        in_specs=[VMEM] * 4,
        out_specs=(VMEM,) * 2,
        compiler_params=PARAMS,
    )(got_b, got_a, early_bank, late_bank)
    edges, row_a, row_b = pl.pallas_call(
        functools.partial(rows_kernel, lat_len),
        out_shape=(edge_shape, row_shape, row_shape),
        in_specs=[VMEM, VMEM, HBM, VMEM],
        out_specs=(VMEM,) * 3,
        compiler_params=PARAMS,
    )(got_b, got_a, core_b, reduced)
    core_b = lax.ppermute(core_b, "lon", lon_second)
    core_a = lax.ppermute(core_a, "lon", lon_first)
    row_a = lax.ppermute(row_a, "lat", lat_first)
    row_b = lax.ppermute(row_b, "lat", lat_second)
    border_cells = 2 * REACH * lon_len
    stack_rows = taps * rank // 2
    halo_stack_shape = jax.ShapeDtypeStruct((2, stack_rows, border_cells), BF16)
    inner, halo_stack = pl.pallas_call(
        functools.partial(inner_kernel, lat_len),
        out_shape=(jax.ShapeDtypeStruct((tap_rank * rank, cells - border_cells), BF16), halo_stack_shape),
        in_specs=[VMEM] * 3,
        out_specs=(VMEM,) * 2,
        scratch_shapes=[pltpu.VMEM((2, stack_rows, cells - border_cells), BF16)],
        compiler_params=PARAMS,
    )(reduced, edges, weights)
    border = pl.pallas_call(
        functools.partial(border_kernel, lat_len, lat_count),
        out_shape=jax.ShapeDtypeStruct((tap_rank * rank, border_cells), BF16),
        in_specs=[VMEM] * 4,
        out_specs=VMEM,
        scratch_shapes=[pltpu.VMEM(halo_stack_shape.shape, BF16)],
        compiler_params=PARAMS,
    )(row_b, row_a, weights, halo_stack)
    out_shape = (out_channels, lat_len, lon_len)
    return pl.pallas_call(
        mix_kernel,
        out_shape=jax.ShapeDtypeStruct(out_shape, BF16),
        in_specs=[VMEM] * 8,
        out_specs=HBM,
        scratch_shapes=[pltpu.VMEM(out_shape, BF16), pltpu.SemaphoreType.DMA((OUT_COPIES,))],
        compiler_params=PARAMS,
    )(inner, border, core_a, core_b, own, position, mixer, offset)


def solution(mesh):
    placed = (
        P(None, "lat", "lon"),
        P("lat", "lon"),
        P("lat", "lon", None),
        P(),
        P("lon", None, None),
        P(),
        P(),
        P(),
        P(),
    )
    return jax.shard_map(
        on_device, mesh=mesh, in_specs=placed, out_specs=P(None, "lat", "lon"), check_vma=False
    )
```

```python
import functools

import jax
import jax.numpy as jnp
from jax import lax
from jax.experimental import pallas as pl
from jax.experimental.pallas import tpu as pltpu
from jax.sharding import PartitionSpec as P

KS = 5
REACH = KS // 2
PER_OWNER = 2
LANES = 128
EDGE = 2 * REACH
GROUP = 8
STEP = 4
OUT_COPIES = 4
IN_COPIES = 4
BANK_COPIES = 8
EARLY = 1
F32 = jnp.float32
BF16 = jnp.bfloat16
VMEM = pl.BlockSpec(memory_space=pltpu.VMEM)
SMEM = pl.BlockSpec(memory_space=pltpu.SMEM)
HBM = pl.BlockSpec(memory_space=pltpu.HBM)
PARAMS = pltpu.CompilerParams(vmem_limit_bytes=24 * 1024 * 1024)


def swap_pairs(count):
    first = [(i, i ^ 1) for i in range(count)]
    second = [(i, (i + 1 if i % 2 else i - 1) % count) for i in range(count)]
    return first, second


def in_hbm(array):
    return pltpu.with_memory_space_constraint(array, pltpu.HBM)


def lane_index(shape):
    return lax.broadcasted_iota(jnp.int32, shape, 1)


def start_copies(pairs, sems):
    copies = [pltpu.make_async_copy(source, target, sems.at[i]) for i, (source, target) in enumerate(pairs)]
    for copy in copies:
        copy.start()
    return copies


def in_parts(source, target, count):
    share = target.shape[0] // count
    return tuple((source.at[pl.ds(i * share, share)], target.at[pl.ds(i * share, share)]) for i in range(count))


def find_rows(list_ref, slot_ref, lon_count, held):
    me = lax.axis_index("lon")
    owners = (me, lax.rem(me + lon_count - 1, lon_count), lax.rem(me + 1, lon_count))
    slots = [slot_ref[list_ref[0, 0, i]] for i in range(list_ref.shape[2])]
    places, rows = [], []
    for owner in owners:
        least, greatest = jnp.int32(held), jnp.int32(-1)
        first, last = jnp.int32(0), jnp.int32(0)
        for i, slot in enumerate(slots):
            local = slot - owner * held
            hit = (local >= 0) & (local < held)
            first = jnp.where(hit & (local < least), i, first)
            last = jnp.where(hit & (local > greatest), i, last)
            least = jnp.where(hit, jnp.minimum(local, least), least)
            greatest = jnp.where(hit, jnp.maximum(local, greatest), greatest)
        places.append([first, last])
        rows.append([jnp.minimum(least, held - 1), jnp.maximum(greatest, 0)])
    return places, rows


def is_early():
    return lax.axis_index("lon") == EARLY


class Held:
    names = ("bank", "own", "position", "weights", "mixer", "offset")
    sources = ("labels", "tap", "out_factor", "bias")

    def __init__(self, refs):
        self.__dict__.update(zip(self.names, refs))


def start_sources(sources, targets, bank_hbm, bank_ref, sems):
    pairs = tuple(zip(sources, targets))
    return start_copies(pairs + in_parts(bank_hbm, bank_ref, BANK_COPIES), sems)


def build_held(lon_count, list_ref, slot_ref, targets, copies, held):
    labels_ref, tap_ref, out_factor_ref, bias_ref = targets
    places, rows = find_rows(list_ref, slot_ref, lon_count, held.bank.shape[0])
    even = (lax.axis_index("lon") % 2) == 0
    order = list(places[0])
    order += [jnp.where(even, places[2][nth], places[1][nth]) for nth in range(PER_OWNER)]
    order += [jnp.where(even, places[1][nth], places[2][nth]) for nth in range(PER_OWNER)]
    labels = labels_ref[...]
    position = jnp.zeros(labels.shape, jnp.int32)
    for index, place in enumerate(order):
        position = jnp.where(labels == place, index, position)
    held.position[...] = position

    rank, out_channels = out_factor_ref.shape
    half = rank // 2
    tap_rank, taps = tap_ref.shape
    shape = (tap_rank * half, taps * half)
    spread = (
        lax.broadcasted_iota(jnp.int32, (shape[0], tap_rank), 0) // half == lane_index((shape[0], tap_rank))
    ).astype(BF16)
    repeat = (
        lax.broadcasted_iota(jnp.int32, (taps, shape[1]), 0) == lane_index((taps, shape[1])) // half
    ).astype(BF16)
    tall = jnp.dot(spread, tap_ref[...], preferred_element_type=F32).astype(BF16)
    wide = jnp.dot(tall, repeat, preferred_element_type=F32)
    same = lax.broadcasted_iota(jnp.int32, shape, 0) % half == lane_index(shape) % half
    held.weights[...] = jnp.where(same, wide, 0.0).astype(BF16)

    shape = (out_channels * GROUP, rank * GROUP)
    spread = (
        lax.broadcasted_iota(jnp.int32, (shape[0], out_channels), 0) // GROUP
        == lane_index((shape[0], out_channels))
    ).astype(BF16)
    repeat = (
        lax.broadcasted_iota(jnp.int32, (rank, shape[1]), 0) == lane_index((rank, shape[1])) % rank
    ).astype(BF16)
    tall = lax.dot_general(
        spread, out_factor_ref[...], (((1,), (1,)), ((), ())), preferred_element_type=F32
    ).astype(BF16)
    wide = jnp.dot(tall, repeat, preferred_element_type=F32)
    same = lax.broadcasted_iota(jnp.int32, shape, 0) % GROUP == lane_index(shape) // rank
    held.mixer[...] = jnp.where(same, wide, 0.0).astype(BF16)

    shape = (out_channels * GROUP, out_channels)
    mine = lax.broadcasted_iota(jnp.int32, shape, 0) // GROUP == lane_index(shape)
    offset = jnp.sum(jnp.where(mine, bias_ref[...], 0.0), axis=1, keepdims=True)
    held.offset[...] = jnp.broadcast_to(offset, held.offset.shape)
    for copy in copies:
        copy.wait()
    for nth in range(PER_OWNER):
        held.own[nth] = held.bank[rows[0][nth]]


def edge_kernel(lon_count, *refs):
    list_hbm, slot_hbm, feat_hbm, in_hbm, bank_hbm = refs[:5]
    sources, (pay_a_ref, pay_b_ref), held_refs = refs[5:9], refs[9:11], refs[11:17]
    list_ref, slot_ref, feat_ref, in_ref, turned_ref = refs[17:22]
    targets, sems, held_sems = refs[22:26], refs[26], refs[27]
    held = Held(held_refs)
    channels, lat_len, lon_len = feat_ref.shape
    rank = in_ref.shape[0]
    pairs = in_parts(feat_hbm, feat_ref, IN_COPIES)
    pairs += ((slot_hbm, slot_ref), (list_hbm, list_ref), (in_hbm, in_ref))
    for copy in start_copies(pairs, sems):
        copy.wait()
    lane = lane_index((lat_len, LANES))
    batch = LANES // EDGE
    for first in range(0, channels, batch):
        packed = jnp.zeros((lat_len, LANES), F32)
        for c in range(batch):
            moved = pltpu.roll(feat_ref[first + c].astype(F32), (EDGE * c + REACH) % LANES, 1)
            packed = jnp.where(lane // EDGE == c, moved, packed)
        turned_ref[first * EDGE : (first + batch) * EDGE, :] = jnp.transpose(packed)
    columns = jnp.concatenate(
        [turned_ref[pl.ds(j, channels, stride=EDGE), :].astype(BF16) for j in range(EDGE)], axis=1
    )
    edges = jnp.dot(in_ref[...], columns, preferred_element_type=F32)
    edges = jnp.concatenate([edges, jnp.zeros((rank, LANES - EDGE * lat_len), F32)], axis=1)
    _, rows = find_rows(list_ref, slot_ref, lon_count, held.bank.shape[0])
    even = (lax.axis_index("lon") % 2) == 0
    lane = lane_index((rank, LANES))
    for out_ref, wanted in ((pay_a_ref, even), (pay_b_ref, jnp.logical_not(even))):
        load = edges
        for nth in range(PER_OWNER):
            row = jnp.where(wanted, rows[2][nth], rows[1][nth]).astype(F32)
            load = jnp.where(lane == EDGE * lat_len + nth, row, load)
        out_ref[...] = load.astype(BF16)

    @pl.when(is_early())
    def _():
        copies = start_sources(sources, targets, bank_hbm, held.bank, held_sems)
        for copy in copies[: len(targets)]:
            copy.wait()
        build_held(lon_count, list_ref, slot_ref, targets, copies[len(targets) :], held)


def reduce_tile(lat_len, feat_ref, in_ref, rows_ref, red_ref):
    channels, lon_len = feat_ref.shape[0], feat_ref.shape[2]
    rows_ref[...] = feat_ref[...].astype(F32).reshape(channels * lat_len, lon_len)
    cells = jnp.concatenate(
        [rows_ref[pl.ds(p, channels, stride=lat_len), :].astype(BF16) for p in range(lat_len)], axis=1
    )
    red_ref[...] = jnp.dot(in_ref[...], cells, preferred_element_type=F32).astype(BF16)


def prepare_kernel(lon_count, lat_len, *refs):
    list_hbm, slot_hbm, feat_hbm, in_hbm, bank_hbm = refs[:5]
    sources, given = refs[5:9], Held((None, *refs[9:14]))
    red_ref, held = refs[14], Held(refs[15:21])
    list_ref, slot_ref, feat_ref, in_ref, rows_ref = refs[21:26]
    targets, sems, held_sems = refs[26:30], refs[30], refs[31]
    early = is_early()
    shared = in_parts(feat_hbm, feat_ref, IN_COPIES) + ((in_hbm, in_ref),)
    lists = ((slot_hbm, slot_ref), (list_hbm, list_ref))

    @pl.when(early)
    def _():
        copies = start_copies(shared, sems)
        for name in held.names[1:]:
            getattr(held, name)[...] = getattr(given, name)[...]
        for copy in copies:
            copy.wait()
        reduce_tile(lat_len, feat_ref, in_ref, rows_ref, red_ref)

    @pl.when(jnp.logical_not(early))
    def _():
        copies = start_copies(shared + lists, sems)
        others = start_sources(sources, targets, bank_hbm, held.bank, held_sems)
        for copy in copies + others[: len(targets)]:
            copy.wait()
        reduce_tile(lat_len, feat_ref, in_ref, rows_ref, red_ref)
        build_held(lon_count, list_ref, slot_ref, targets, others[len(targets) :], held)


def pick_kernel(lat_len, got_b_ref, got_a_ref, early_bank_ref, late_bank_ref, core_a_ref, core_b_ref):
    early = is_early()
    lane = lane_index((1, LANES))
    for got_ref, core_ref in ((got_b_ref, core_b_ref), (got_a_ref, core_a_ref)):
        head = got_ref[...].astype(F32)[0:1, :]
        for nth in range(PER_OWNER):
            row = jnp.sum(jnp.where(lane == EDGE * lat_len + nth, head, 0.0)).astype(jnp.int32)
            core_ref[nth] = jnp.where(early, early_bank_ref[row], late_bank_ref[row])


def rows_kernel(lat_len, got_b_ref, got_a_ref, core_ref, red_ref, edge_ref, row_a_ref, row_b_ref):
    lon_len = red_ref.shape[1] // lat_len
    even = (lax.axis_index("lon") % 2) == 0
    from_prev = lane_index(got_a_ref.shape) < REACH * lat_len
    got = jnp.where(from_prev == even, got_b_ref[...].astype(F32), got_a_ref[...].astype(F32)).astype(BF16)
    source = lax.broadcasted_iota(jnp.int32, (LANES, LANES), 0)
    target = lane_index((LANES, LANES))
    order = (source == (target % EDGE) * lat_len + target // EDGE) & (target < EDGE * lat_len)
    edges = jnp.dot(got, order.astype(BF16), preferred_element_type=F32).astype(BF16)
    edge_ref[...] = edges
    even = (lax.axis_index("lat") % 2) == 0
    head = red_ref[:, : REACH * lon_len].astype(F32)
    tail = red_ref[:, (lat_len - REACH) * lon_len :].astype(F32)
    row_a_ref[:, : REACH * lon_len] = jnp.where(even, tail, head).astype(BF16)
    row_b_ref[:, : REACH * lon_len] = jnp.where(even, head, tail).astype(BF16)
    row_a_ref[:, REACH * lon_len :] = edges
    row_b_ref[:, REACH * lon_len :] = edges


def shifted_columns(row, edges, place):
    lane = lane_index(row.shape)
    lon_len = row.shape[1]
    edges = pltpu.roll(edges, (LANES - REACH - EDGE * place) % LANES, 1)
    moved = []
    for col_off in range(KS):
        shift = REACH - col_off
        if shift > 0:
            piece = pltpu.roll(jnp.where(lane >= lon_len - shift, edges, row), shift, 1)
        elif shift < 0:
            piece = pltpu.roll(jnp.where(lane < -shift, edges, row), lon_len + shift, 1)
        else:
            piece = row
        moved.append(piece.astype(BF16))
    return moved


def stack_row(stack_ref, p, moved, slots, lon_len):
    half = moved[0].shape[0] // 2
    for col_off, piece in enumerate(moved):
        for row_off in range(KS):
            slot = slots.get(p + REACH - row_off)
            if slot is not None:
                k = row_off * KS + col_off
                for h in range(2):
                    stack_ref[h, k * half : (k + 1) * half, slot * lon_len : (slot + 1) * lon_len] = piece[
                        h * half : (h + 1) * half
                    ]


def apply_taps(rank, weights_ref, stacked, tapped_ref, lon_len):
    half = rank // 2
    tap_rank = tapped_ref.shape[0] // rank
    width = STEP * lon_len
    for start in range(0, tapped_ref.shape[1], width):
        parts = [
            jnp.dot(weights_ref[...], stacked(h, start, width), preferred_element_type=F32)
            .astype(BF16)
            .reshape(tap_rank, 1, half, width)
            for h in range(2)
        ]
        tapped_ref[:, start : start + width] = jnp.concatenate(parts, axis=1).reshape(tap_rank * rank, width)


def border_slots(lat_len):
    slots = {p: p for p in range(REACH)}
    slots.update({lat_len - REACH + p: REACH + p for p in range(REACH)})
    return slots


def inner_kernel(lat_len, red_ref, edge_ref, weights_ref, tapped_ref, halo_stack_ref, stack_ref):
    rank = red_ref.shape[0]
    lon_len = red_ref.shape[1] // lat_len
    slots = {p: p - REACH for p in range(REACH, lat_len - REACH)}
    edges = edge_ref[...].astype(F32)
    for p in range(lat_len):
        row = red_ref[:, p * lon_len : (p + 1) * lon_len].astype(F32)
        moved = shifted_columns(row, edges, p)
        stack_row(stack_ref, p, moved, slots, lon_len)
        stack_row(halo_stack_ref, p, moved, border_slots(lat_len), lon_len)
    apply_taps(rank, weights_ref, lambda h, start, width: stack_ref[h, :, start : start + width], tapped_ref, lon_len)


def border_kernel(lat_len, lat_count, row_b_ref, row_a_ref, weights_ref, own_stack_ref, tapped_ref, stack_ref):
    rank = row_a_ref.shape[0]
    lon_len = (row_a_ref.shape[1] - LANES) // REACH
    lat = lax.axis_index("lat")
    even = (lat % 2) == 0
    row_a = row_a_ref[...].astype(F32)
    row_b = row_b_ref[...].astype(F32)
    above = jnp.where(lat == 0, 0.0, jnp.where(even, row_b, row_a))
    below = jnp.where(lat == lat_count - 1, 0.0, jnp.where(even, row_a, row_b))
    slots = border_slots(lat_len)
    for i in range(REACH):
        for p, holder, place in ((i - REACH, above, lat_len - REACH + i), (lat_len + i, below, i)):
            row = holder[:, i * lon_len : (i + 1) * lon_len]
            moved = shifted_columns(row, holder[:, REACH * lon_len :], place)
            stack_row(stack_ref, p, moved, slots, lon_len)
    block = KS * rank // 2
    in_halo = {
        (slot, row_off)
        for p, slot in slots.items()
        for row_off in range(KS)
        if not 0 <= p + row_off - REACH < lat_len
    }

    def stacked(h, start, width):
        columns = []
        for slot in range(start // lon_len, (start + width) // lon_len):
            span = slice(slot * lon_len, (slot + 1) * lon_len)
            pieces = []
            for row_off in range(KS):
                ref = stack_ref if (slot, row_off) in in_halo else own_stack_ref
                pieces.append(ref[h, row_off * block : (row_off + 1) * block, span])
            columns.append(jnp.concatenate(pieces, axis=0))
        return jnp.concatenate(columns, axis=1)

    apply_taps(rank, weights_ref, stacked, tapped_ref, lon_len)


def mix_kernel(
    inner_ref,
    border_ref,
    core_a_ref,
    core_b_ref,
    own_ref,
    position_ref,
    mixer_ref,
    offset_ref,
    out_hbm,
    stage_ref,
    sems,
):
    lat_len, lon_len = position_ref.shape
    rank = own_ref.shape[1]
    cores = jnp.concatenate(
        [ref[...].reshape(PER_OWNER * rank, -1) for ref in (own_ref, core_a_ref, core_b_ref)], axis=0
    )
    chunks = [(border_ref, 0, [*range(REACH), *range(lat_len - REACH, lat_len)])]
    for start in range(REACH, lat_len - REACH, STEP):
        chunks.append((inner_ref, start - REACH, [*range(start, start + STEP)]))
    by_row = {}
    for ref, first, rows in chunks:
        width = len(rows) * lon_len
        every = jnp.dot(cores, ref[:, first * lon_len : first * lon_len + width], preferred_element_type=F32)
        position = jnp.concatenate([position_ref[r : r + 1, :] for r in rows], axis=1)
        hidden = jnp.zeros((rank, width), F32)
        for index in range(3 * PER_OWNER):
            hidden = jnp.where(position == index, every[index * rank : (index + 1) * rank], hidden)
        hidden = hidden.astype(BF16)
        for i, r in enumerate(rows):
            by_row[r] = hidden[:, i * lon_len : (i + 1) * lon_len]
    pieces = [by_row[r] for r in range(lat_len)]
    groups = [jnp.concatenate(pieces[g : g + GROUP], axis=0) for g in range(0, lat_len, GROUP)]
    channels = stage_ref.shape[0]
    share = channels // OUT_COPIES
    copies = []
    for part in range(OUT_COPIES):
        span = slice(part * share * GROUP, (part + 1) * share * GROUP)
        blocks = []
        for hidden in groups:
            output = jnp.dot(mixer_ref[span, :], hidden, preferred_element_type=F32) + offset_ref[span, :]
            mixed = 0.5 * output * (1.0 + jnp.tanh(0.5 * output))
            blocks.append(mixed.reshape(share, GROUP, lon_len))
        held = slice(part * share, (part + 1) * share)
        stage_ref[held] = jnp.concatenate(blocks, axis=1).astype(BF16)
        copy = pltpu.make_async_copy(stage_ref.at[held], out_hbm.at[held], sems.at[part])
        copy.start()
        copies.append(copy)
    for copy in copies:
        copy.wait()


def on_device(
    features, labels, tile_regions, bank_slot, kernel_bank, in_factor, tap_factor, out_factor, out_bias
):
    channels, lat_len, lon_len = features.shape
    rank = in_factor.shape[0]
    held, core_rows, core_cols = kernel_bank.shape
    tap_rank, taps = tap_factor.shape
    out_channels = out_factor.shape[0]
    cells = lat_len * lon_len
    lon_count, lat_count = lax.axis_size("lon"), lax.axis_size("lat")
    lon_first, lon_second = swap_pairs(lon_count)
    lat_first, lat_second = swap_pairs(lat_count)
    edge_shape = jax.ShapeDtypeStruct((rank, LANES), BF16)
    core_shape = jax.ShapeDtypeStruct((PER_OWNER, core_rows, core_cols), BF16)
    held_shapes = (
        jax.ShapeDtypeStruct(kernel_bank.shape, BF16),
        core_shape,
        jax.ShapeDtypeStruct(labels.shape, jnp.int32),
        jax.ShapeDtypeStruct((tap_rank * rank // 2, taps * rank // 2), BF16),
        jax.ShapeDtypeStruct((out_channels * GROUP, rank * GROUP), BF16),
        jax.ShapeDtypeStruct((out_channels * GROUP, lon_len), F32),
    )
    lists = [
        pltpu.SMEM(tile_regions.shape, jnp.int32),
        pltpu.SMEM(bank_slot.shape, jnp.int32),
        pltpu.VMEM(features.shape, BF16),
        pltpu.VMEM(in_factor.shape, BF16),
    ]
    targets = [
        pltpu.VMEM(labels.shape, jnp.int32),
        pltpu.VMEM(tap_factor.shape, BF16),
        pltpu.VMEM(out_factor.shape[::-1], BF16),
        pltpu.VMEM((1, out_channels), F32),
    ]
    sources = tuple(
        in_hbm(x)
        for x in (
            tile_regions,
            bank_slot,
            features,
            in_factor,
            kernel_bank,
            labels,
            tap_factor,
            out_factor.T,
            out_bias.reshape(1, -1),
        )
    )
    pay_a, pay_b, early_bank, *given = pl.pallas_call(
        functools.partial(edge_kernel, lon_count),
        out_shape=(edge_shape, edge_shape, *held_shapes),
        in_specs=[HBM] * 9,
        out_specs=(VMEM,) * 8,
        scratch_shapes=[
            *lists,
            pltpu.VMEM((channels * EDGE, lat_len), F32),
            *targets,
            pltpu.SemaphoreType.DMA((IN_COPIES + 3,)),
            pltpu.SemaphoreType.DMA((4 + BANK_COPIES,)),
        ],
        compiler_params=PARAMS,
    )(*sources)
    got_b = lax.ppermute(pay_b, "lon", lon_second)
    got_a = lax.ppermute(pay_a, "lon", lon_first)
    reduced, late_bank, own, position, weights, mixer, offset = pl.pallas_call(
        functools.partial(prepare_kernel, lon_count, lat_len),
        out_shape=(jax.ShapeDtypeStruct((rank, cells), BF16), *held_shapes),
        in_specs=[HBM] * 9 + [VMEM] * 5,
        out_specs=(VMEM,) * 7,
        scratch_shapes=[
            *lists,
            pltpu.VMEM((channels * lat_len, lon_len), F32),
            *targets,
            pltpu.SemaphoreType.DMA((IN_COPIES + 3,)),
            pltpu.SemaphoreType.DMA((4 + BANK_COPIES,)),
        ],
        compiler_params=PARAMS,
        cost_estimate=pl.CostEstimate(flops=10**6, bytes_accessed=kernel_bank.size * 4, transcendentals=0),
    )(*sources, *given)
    row_shape = jax.ShapeDtypeStruct((rank, REACH * lon_len + LANES), BF16)
    core_a, core_b = pl.pallas_call(
        functools.partial(pick_kernel, lat_len),
        out_shape=(core_shape, core_shape),
        in_specs=[VMEM] * 4,
        out_specs=(VMEM,) * 2,
        compiler_params=PARAMS,
    )(got_b, got_a, early_bank, late_bank)
    edges, row_a, row_b = pl.pallas_call(
        functools.partial(rows_kernel, lat_len),
        out_shape=(edge_shape, row_shape, row_shape),
        in_specs=[VMEM, VMEM, HBM, VMEM],
        out_specs=(VMEM,) * 3,
        compiler_params=PARAMS,
    )(got_b, got_a, core_b, reduced)
    core_b = lax.ppermute(core_b, "lon", lon_second)
    core_a = lax.ppermute(core_a, "lon", lon_first)
    row_a = lax.ppermute(row_a, "lat", lat_first)
    row_b = lax.ppermute(row_b, "lat", lat_second)
    border_cells = 2 * REACH * lon_len
    stack_rows = taps * rank // 2
    halo_stack_shape = jax.ShapeDtypeStruct((2, stack_rows, border_cells), BF16)
    inner, halo_stack = pl.pallas_call(
        functools.partial(inner_kernel, lat_len),
        out_shape=(jax.ShapeDtypeStruct((tap_rank * rank, cells - border_cells), BF16), halo_stack_shape),
        in_specs=[VMEM] * 3,
        out_specs=(VMEM,) * 2,
        scratch_shapes=[pltpu.VMEM((2, stack_rows, cells - border_cells), BF16)],
        compiler_params=PARAMS,
    )(reduced, edges, weights)
    border = pl.pallas_call(
        functools.partial(border_kernel, lat_len, lat_count),
        out_shape=jax.ShapeDtypeStruct((tap_rank * rank, border_cells), BF16),
        in_specs=[VMEM] * 4,
        out_specs=VMEM,
        scratch_shapes=[pltpu.VMEM(halo_stack_shape.shape, BF16)],
        compiler_params=PARAMS,
    )(row_b, row_a, weights, halo_stack)
    out_shape = (out_channels, lat_len, lon_len)
    return pl.pallas_call(
        mix_kernel,
        out_shape=jax.ShapeDtypeStruct(out_shape, BF16),
        in_specs=[VMEM] * 8,
        out_specs=HBM,
        scratch_shapes=[pltpu.VMEM(out_shape, BF16), pltpu.SemaphoreType.DMA((OUT_COPIES,))],
        compiler_params=PARAMS,
    )(inner, border, core_a, core_b, own, position, mixer, offset)


def solution(mesh):
    placed = (
        P(None, "lat", "lon"),
        P("lat", "lon"),
        P("lat", "lon", None),
        P(),
        P("lon", None, None),
        P(),
        P(),
        P(),
        P(),
    )
    return jax.shard_map(
        on_device, mesh=mesh, in_specs=placed, out_specs=P(None, "lat", "lon"), check_vma=False
    )
```

```python
import functools

import jax
import jax.numpy as jnp
from jax import lax
from jax.experimental import pallas as pl
from jax.experimental.pallas import tpu as pltpu
from jax.sharding import PartitionSpec as P

KS = 5
REACH = KS // 2
PER_OWNER = 2
LANES = 128
EDGE = 2 * REACH
GROUP = 8
STEP = 4
OUT_COPIES = 4
IN_COPIES = 4
BANK_COPIES = 8
EARLY = 1
F32 = jnp.float32
BF16 = jnp.bfloat16
VMEM = pl.BlockSpec(memory_space=pltpu.VMEM)
SMEM = pl.BlockSpec(memory_space=pltpu.SMEM)
HBM = pl.BlockSpec(memory_space=pltpu.HBM)
PARAMS = pltpu.CompilerParams(vmem_limit_bytes=24 * 1024 * 1024)


def swap_pairs(count):
    first = [(i, i ^ 1) for i in range(count)]
    second = [(i, (i + 1 if i % 2 else i - 1) % count) for i in range(count)]
    return first, second


def in_hbm(array):
    return pltpu.with_memory_space_constraint(array, pltpu.HBM)


def lane_index(shape):
    return lax.broadcasted_iota(jnp.int32, shape, 1)


def start_copies(pairs, sems):
    copies = [pltpu.make_async_copy(source, target, sems.at[i]) for i, (source, target) in enumerate(pairs)]
    for copy in copies:
        copy.start()
    return copies


def in_parts(source, target, count):
    share = target.shape[0] // count
    return tuple((source.at[pl.ds(i * share, share)], target.at[pl.ds(i * share, share)]) for i in range(count))


def find_rows(list_ref, slot_ref, lon_count, held):
    me = lax.axis_index("lon")
    owners = (me, lax.rem(me + lon_count - 1, lon_count), lax.rem(me + 1, lon_count))
    slots = [slot_ref[list_ref[0, 0, i]] for i in range(list_ref.shape[2])]
    places, rows = [], []
    for owner in owners:
        least, greatest = jnp.int32(held), jnp.int32(-1)
        first, last = jnp.int32(0), jnp.int32(0)
        for i, slot in enumerate(slots):
            local = slot - owner * held
            hit = (local >= 0) & (local < held)
            first = jnp.where(hit & (local < least), i, first)
            last = jnp.where(hit & (local > greatest), i, last)
            least = jnp.where(hit, jnp.minimum(local, least), least)
            greatest = jnp.where(hit, jnp.maximum(local, greatest), greatest)
        places.append([first, last])
        rows.append([jnp.minimum(least, held - 1), jnp.maximum(greatest, 0)])
    return places, rows


def is_early():
    return lax.axis_index("lon") == EARLY


class Held:
    names = ("bank", "own", "position", "weights", "mixer", "offset")
    sources = ("labels", "tap", "out_factor", "bias")

    def __init__(self, refs):
        self.__dict__.update(zip(self.names, refs))


def start_sources(sources, targets, bank_hbm, bank_ref, sems):
    pairs = tuple(zip(sources, targets))
    return start_copies(pairs + in_parts(bank_hbm, bank_ref, BANK_COPIES), sems)


def build_held(lon_count, list_ref, slot_ref, targets, copies, held):
    labels_ref, tap_ref, out_factor_ref, bias_ref = targets
    places, rows = find_rows(list_ref, slot_ref, lon_count, held.bank.shape[0])
    even = (lax.axis_index("lon") % 2) == 0
    order = list(places[0])
    order += [jnp.where(even, places[2][nth], places[1][nth]) for nth in range(PER_OWNER)]
    order += [jnp.where(even, places[1][nth], places[2][nth]) for nth in range(PER_OWNER)]
    labels = labels_ref[...]
    position = jnp.zeros(labels.shape, jnp.int32)
    for index, place in enumerate(order):
        position = jnp.where(labels == place, index, position)
    held.position[...] = position

    rank, out_channels = out_factor_ref.shape
    half = rank // 2
    tap_rank, taps = tap_ref.shape
    shape = (tap_rank * half, taps * half)
    spread = (
        lax.broadcasted_iota(jnp.int32, (shape[0], tap_rank), 0) // half == lane_index((shape[0], tap_rank))
    ).astype(BF16)
    repeat = (
        lax.broadcasted_iota(jnp.int32, (taps, shape[1]), 0) == lane_index((taps, shape[1])) // half
    ).astype(BF16)
    tall = jnp.dot(spread, tap_ref[...], preferred_element_type=F32).astype(BF16)
    wide = jnp.dot(tall, repeat, preferred_element_type=F32)
    same = lax.broadcasted_iota(jnp.int32, shape, 0) % half == lane_index(shape) % half
    held.weights[...] = jnp.where(same, wide, 0.0).astype(BF16)

    shape = (out_channels * GROUP, rank * GROUP)
    spread = (
        lax.broadcasted_iota(jnp.int32, (shape[0], out_channels), 0) // GROUP
        == lane_index((shape[0], out_channels))
    ).astype(BF16)
    repeat = (
        lax.broadcasted_iota(jnp.int32, (rank, shape[1]), 0) == lane_index((rank, shape[1])) % rank
    ).astype(BF16)
    tall = lax.dot_general(
        spread, out_factor_ref[...], (((1,), (1,)), ((), ())), preferred_element_type=F32
    ).astype(BF16)
    wide = jnp.dot(tall, repeat, preferred_element_type=F32)
    same = lax.broadcasted_iota(jnp.int32, shape, 0) % GROUP == lane_index(shape) // rank
    held.mixer[...] = jnp.where(same, wide, 0.0).astype(BF16)

    shape = (out_channels * GROUP, out_channels)
    mine = lax.broadcasted_iota(jnp.int32, shape, 0) // GROUP == lane_index(shape)
    offset = jnp.sum(jnp.where(mine, bias_ref[...], 0.0), axis=1, keepdims=True)
    held.offset[...] = jnp.broadcast_to(offset, held.offset.shape)
    for copy in copies:
        copy.wait()
    for nth in range(PER_OWNER):
        held.own[nth] = held.bank[rows[0][nth]]


def asked_rows(list_ref, slot_ref, owner, held):
    lane = lane_index((1, LANES))
    count = list_ref.shape[2]
    hits = []
    for i in range(count):
        region = list_ref[0, 0, i]
        row = slot_ref[pl.ds(region // LANES, 1), :]
        hits.append(jnp.where(lane == region % LANES, row - owner * held, -1))
    local = jnp.max(jnp.concatenate(hits, axis=0), axis=1, keepdims=True)
    hit = (local >= 0) & (local < held)
    least = jnp.min(jnp.where(hit, local, held - 1), axis=0, keepdims=True)
    greatest = jnp.max(jnp.where(hit, local, 0), axis=0, keepdims=True)
    return least, greatest


def edge_kernel(lon_count, held_rows, *refs):
    list_hbm, slot_hbm, feat_hbm, in_hbm, pay_a_ref, pay_b_ref = refs[:6]
    list_ref, slot_ref, feat_ref, in_ref, turned_ref, sems = refs[6:]
    channels, lat_len, lon_len = feat_ref.shape
    rank = in_ref.shape[0]
    pairs = in_parts(feat_hbm, feat_ref, IN_COPIES)
    pairs += ((slot_hbm, slot_ref), (list_hbm, list_ref), (in_hbm, in_ref))
    for copy in start_copies(pairs, sems):
        copy.wait()
    lane = lane_index((lat_len, LANES))
    batch = LANES // EDGE
    for first in range(0, channels, batch):
        packed = jnp.zeros((lat_len, LANES), F32)
        for c in range(batch):
            moved = pltpu.roll(feat_ref[first + c].astype(F32), (EDGE * c + REACH) % LANES, 1)
            packed = jnp.where(lane // EDGE == c, moved, packed)
        turned_ref[first * EDGE : (first + batch) * EDGE, :] = jnp.transpose(packed)
    columns = jnp.concatenate(
        [turned_ref[pl.ds(j, channels, stride=EDGE), :].astype(BF16) for j in range(EDGE)], axis=1
    )
    edges = jnp.dot(in_ref[...], columns, preferred_element_type=F32)
    edges = jnp.concatenate([edges, jnp.zeros((rank, LANES - EDGE * lat_len), F32)], axis=1)
    me = lax.axis_index("lon")
    even = (me % 2) == 0
    prev, following = lax.rem(me + lon_count - 1, lon_count), lax.rem(me + 1, lon_count)
    lane = lane_index((rank, LANES))
    for out_ref, owner in (
        (pay_a_ref, jnp.where(even, following, prev)),
        (pay_b_ref, jnp.where(even, prev, following)),
    ):
        load = edges
        for nth, row in enumerate(asked_rows(list_ref, slot_ref, owner, held_rows)):
            load = jnp.where(lane == EDGE * lat_len + nth, row.astype(F32), load)
        out_ref[...] = load.astype(BF16)


def early_kernel(lon_count, *refs):
    pay_ref, list_hbm, slot_hbm, bank_hbm, sources = *refs[:4], refs[4:8]
    passed_ref, held = refs[8], Held(refs[9:15])
    list_ref, slot_ref, targets, sems, held_sems = *refs[15:17], refs[17:21], *refs[21:]
    passed_ref[...] = pay_ref[...]

    @pl.when(is_early())
    def _():
        lists = start_copies(((list_hbm, list_ref), (slot_hbm, slot_ref)), sems)
        copies = start_sources(sources, targets, bank_hbm, held.bank, held_sems)
        for copy in lists + copies[: len(targets)]:
            copy.wait()
        build_held(lon_count, list_ref, slot_ref, targets, copies[len(targets) :], held)


def reduce_tile(lat_len, feat_ref, in_ref, rows_ref, red_ref):
    channels, lon_len = feat_ref.shape[0], feat_ref.shape[2]
    rows_ref[...] = feat_ref[...].astype(F32).reshape(channels * lat_len, lon_len)
    cells = jnp.concatenate(
        [rows_ref[pl.ds(p, channels, stride=lat_len), :].astype(BF16) for p in range(lat_len)], axis=1
    )
    red_ref[...] = jnp.dot(in_ref[...], cells, preferred_element_type=F32).astype(BF16)


def prepare_kernel(lon_count, lat_len, *refs):
    list_hbm, slot_hbm, feat_hbm, in_hbm, bank_hbm = refs[:5]
    sources, given = refs[5:9], Held((None, *refs[9:14]))
    red_ref, held = refs[14], Held(refs[15:21])
    list_ref, slot_ref, feat_ref, in_ref, rows_ref = refs[21:26]
    targets, sems, held_sems = refs[26:30], refs[30], refs[31]
    early = is_early()
    shared = in_parts(feat_hbm, feat_ref, IN_COPIES) + ((in_hbm, in_ref),)
    lists = ((slot_hbm, slot_ref), (list_hbm, list_ref))

    @pl.when(early)
    def _():
        copies = start_copies(shared, sems)
        for name in held.names[1:]:
            getattr(held, name)[...] = getattr(given, name)[...]
        for copy in copies:
            copy.wait()
        reduce_tile(lat_len, feat_ref, in_ref, rows_ref, red_ref)

    @pl.when(jnp.logical_not(early))
    def _():
        copies = start_copies(shared + lists, sems)
        others = start_sources(sources, targets, bank_hbm, held.bank, held_sems)
        for copy in copies + others[: len(targets)]:
            copy.wait()
        reduce_tile(lat_len, feat_ref, in_ref, rows_ref, red_ref)
        build_held(lon_count, list_ref, slot_ref, targets, others[len(targets) :], held)


def pick_kernel(lat_len, got_b_ref, got_a_ref, early_bank_ref, late_bank_ref, core_a_ref, core_b_ref):
    early = is_early()
    lane = lane_index((1, LANES))
    for got_ref, core_ref in ((got_b_ref, core_b_ref), (got_a_ref, core_a_ref)):
        head = got_ref[...].astype(F32)[0:1, :]
        for nth in range(PER_OWNER):
            row = jnp.sum(jnp.where(lane == EDGE * lat_len + nth, head, 0.0)).astype(jnp.int32)
            core_ref[nth] = jnp.where(early, early_bank_ref[row], late_bank_ref[row])


def rows_kernel(lat_len, got_b_ref, got_a_ref, core_ref, red_ref, edge_ref, row_a_ref, row_b_ref):
    lon_len = red_ref.shape[1] // lat_len
    even = (lax.axis_index("lon") % 2) == 0
    from_prev = lane_index(got_a_ref.shape) < REACH * lat_len
    got = jnp.where(from_prev == even, got_b_ref[...].astype(F32), got_a_ref[...].astype(F32)).astype(BF16)
    source = lax.broadcasted_iota(jnp.int32, (LANES, LANES), 0)
    target = lane_index((LANES, LANES))
    order = (source == (target % EDGE) * lat_len + target // EDGE) & (target < EDGE * lat_len)
    edges = jnp.dot(got, order.astype(BF16), preferred_element_type=F32).astype(BF16)
    edge_ref[...] = edges
    even = (lax.axis_index("lat") % 2) == 0
    head = red_ref[:, : REACH * lon_len].astype(F32)
    tail = red_ref[:, (lat_len - REACH) * lon_len :].astype(F32)
    row_a_ref[:, : REACH * lon_len] = jnp.where(even, tail, head).astype(BF16)
    row_b_ref[:, : REACH * lon_len] = jnp.where(even, head, tail).astype(BF16)
    row_a_ref[:, REACH * lon_len :] = edges
    row_b_ref[:, REACH * lon_len :] = edges


def shifted_columns(row, edges, place):
    lane = lane_index(row.shape)
    lon_len = row.shape[1]
    edges = pltpu.roll(edges, (LANES - REACH - EDGE * place) % LANES, 1)
    moved = []
    for col_off in range(KS):
        shift = REACH - col_off
        if shift > 0:
            piece = pltpu.roll(jnp.where(lane >= lon_len - shift, edges, row), shift, 1)
        elif shift < 0:
            piece = pltpu.roll(jnp.where(lane < -shift, edges, row), lon_len + shift, 1)
        else:
            piece = row
        moved.append(piece.astype(BF16))
    return moved


def stack_row(stack_ref, p, moved, slots, lon_len):
    half = moved[0].shape[0] // 2
    for col_off, piece in enumerate(moved):
        for row_off in range(KS):
            slot = slots.get(p + REACH - row_off)
            if slot is not None:
                k = row_off * KS + col_off
                for h in range(2):
                    stack_ref[h, k * half : (k + 1) * half, slot * lon_len : (slot + 1) * lon_len] = piece[
                        h * half : (h + 1) * half
                    ]


def apply_taps(rank, weights_ref, stacked, tapped_ref, lon_len):
    half = rank // 2
    tap_rank = tapped_ref.shape[0] // rank
    width = STEP * lon_len
    for start in range(0, tapped_ref.shape[1], width):
        parts = [
            jnp.dot(weights_ref[...], stacked(h, start, width), preferred_element_type=F32)
            .astype(BF16)
            .reshape(tap_rank, 1, half, width)
            for h in range(2)
        ]
        tapped_ref[:, start : start + width] = jnp.concatenate(parts, axis=1).reshape(tap_rank * rank, width)


def border_slots(lat_len):
    slots = {p: p for p in range(REACH)}
    slots.update({lat_len - REACH + p: REACH + p for p in range(REACH)})
    return slots


def inner_kernel(lat_len, red_ref, edge_ref, weights_ref, tapped_ref, halo_stack_ref, stack_ref):
    rank = red_ref.shape[0]
    lon_len = red_ref.shape[1] // lat_len
    slots = {p: p - REACH for p in range(REACH, lat_len - REACH)}
    edges = edge_ref[...].astype(F32)
    for p in range(lat_len):
        row = red_ref[:, p * lon_len : (p + 1) * lon_len].astype(F32)
        moved = shifted_columns(row, edges, p)
        stack_row(stack_ref, p, moved, slots, lon_len)
        stack_row(halo_stack_ref, p, moved, border_slots(lat_len), lon_len)
    apply_taps(rank, weights_ref, lambda h, start, width: stack_ref[h, :, start : start + width], tapped_ref, lon_len)


def border_kernel(lat_len, lat_count, row_b_ref, row_a_ref, weights_ref, own_stack_ref, tapped_ref, stack_ref):
    rank = row_a_ref.shape[0]
    lon_len = (row_a_ref.shape[1] - LANES) // REACH
    lat = lax.axis_index("lat")
    even = (lat % 2) == 0
    row_a = row_a_ref[...].astype(F32)
    row_b = row_b_ref[...].astype(F32)
    above = jnp.where(lat == 0, 0.0, jnp.where(even, row_b, row_a))
    below = jnp.where(lat == lat_count - 1, 0.0, jnp.where(even, row_a, row_b))
    slots = border_slots(lat_len)
    for i in range(REACH):
        for p, holder, place in ((i - REACH, above, lat_len - REACH + i), (lat_len + i, below, i)):
            row = holder[:, i * lon_len : (i + 1) * lon_len]
            moved = shifted_columns(row, holder[:, REACH * lon_len :], place)
            stack_row(stack_ref, p, moved, slots, lon_len)
    block = KS * rank // 2
    in_halo = {
        (slot, row_off)
        for p, slot in slots.items()
        for row_off in range(KS)
        if not 0 <= p + row_off - REACH < lat_len
    }

    def stacked(h, start, width):
        columns = []
        for slot in range(start // lon_len, (start + width) // lon_len):
            span = slice(slot * lon_len, (slot + 1) * lon_len)
            pieces = []
            for row_off in range(KS):
                ref = stack_ref if (slot, row_off) in in_halo else own_stack_ref
                pieces.append(ref[h, row_off * block : (row_off + 1) * block, span])
            columns.append(jnp.concatenate(pieces, axis=0))
        return jnp.concatenate(columns, axis=1)

    apply_taps(rank, weights_ref, stacked, tapped_ref, lon_len)


def mix_kernel(
    inner_ref,
    border_ref,
    core_a_ref,
    core_b_ref,
    own_ref,
    position_ref,
    mixer_ref,
    offset_ref,
    out_hbm,
    stage_ref,
    sems,
):
    lat_len, lon_len = position_ref.shape
    rank = own_ref.shape[1]
    cores = jnp.concatenate(
        [ref[...].reshape(PER_OWNER * rank, -1) for ref in (own_ref, core_a_ref, core_b_ref)], axis=0
    )
    chunks = [(border_ref, 0, [*range(REACH), *range(lat_len - REACH, lat_len)])]
    for start in range(REACH, lat_len - REACH, STEP):
        chunks.append((inner_ref, start - REACH, [*range(start, start + STEP)]))
    by_row = {}
    for ref, first, rows in chunks:
        width = len(rows) * lon_len
        every = jnp.dot(cores, ref[:, first * lon_len : first * lon_len + width], preferred_element_type=F32)
        position = jnp.concatenate([position_ref[r : r + 1, :] for r in rows], axis=1)
        hidden = jnp.zeros((rank, width), F32)
        for index in range(3 * PER_OWNER):
            hidden = jnp.where(position == index, every[index * rank : (index + 1) * rank], hidden)
        hidden = hidden.astype(BF16)
        for i, r in enumerate(rows):
            by_row[r] = hidden[:, i * lon_len : (i + 1) * lon_len]
    pieces = [by_row[r] for r in range(lat_len)]
    groups = [jnp.concatenate(pieces[g : g + GROUP], axis=0) for g in range(0, lat_len, GROUP)]
    channels = stage_ref.shape[0]
    share = channels // OUT_COPIES
    copies = []
    for part in range(OUT_COPIES):
        span = slice(part * share * GROUP, (part + 1) * share * GROUP)
        blocks = []
        for hidden in groups:
            output = jnp.dot(mixer_ref[span, :], hidden, preferred_element_type=F32) + offset_ref[span, :]
            mixed = 0.5 * output * (1.0 + jnp.tanh(0.5 * output))
            blocks.append(mixed.reshape(share, GROUP, lon_len))
        held = slice(part * share, (part + 1) * share)
        stage_ref[held] = jnp.concatenate(blocks, axis=1).astype(BF16)
        copy = pltpu.make_async_copy(stage_ref.at[held], out_hbm.at[held], sems.at[part])
        copy.start()
        copies.append(copy)
    for copy in copies:
        copy.wait()


def on_device(
    features, labels, tile_regions, bank_slot, kernel_bank, in_factor, tap_factor, out_factor, out_bias
):
    channels, lat_len, lon_len = features.shape
    rank = in_factor.shape[0]
    held, core_rows, core_cols = kernel_bank.shape
    tap_rank, taps = tap_factor.shape
    out_channels = out_factor.shape[0]
    cells = lat_len * lon_len
    lon_count, lat_count = lax.axis_size("lon"), lax.axis_size("lat")
    lon_first, lon_second = swap_pairs(lon_count)
    lat_first, lat_second = swap_pairs(lat_count)
    edge_shape = jax.ShapeDtypeStruct((rank, LANES), BF16)
    core_shape = jax.ShapeDtypeStruct((PER_OWNER, core_rows, core_cols), BF16)
    held_shapes = (
        jax.ShapeDtypeStruct(kernel_bank.shape, BF16),
        core_shape,
        jax.ShapeDtypeStruct(labels.shape, jnp.int32),
        jax.ShapeDtypeStruct((tap_rank * rank // 2, taps * rank // 2), BF16),
        jax.ShapeDtypeStruct((out_channels * GROUP, rank * GROUP), BF16),
        jax.ShapeDtypeStruct((out_channels * GROUP, lon_len), F32),
    )
    lists = [
        pltpu.SMEM(tile_regions.shape, jnp.int32),
        pltpu.SMEM(bank_slot.shape, jnp.int32),
        pltpu.VMEM(features.shape, BF16),
        pltpu.VMEM(in_factor.shape, BF16),
    ]
    targets = [
        pltpu.VMEM(labels.shape, jnp.int32),
        pltpu.VMEM(tap_factor.shape, BF16),
        pltpu.VMEM(out_factor.shape[::-1], BF16),
        pltpu.VMEM((1, out_channels), F32),
    ]
    sources = tuple(
        in_hbm(x)
        for x in (
            tile_regions,
            bank_slot,
            features,
            in_factor,
            kernel_bank,
            labels,
            tap_factor,
            out_factor.T,
            out_bias.reshape(1, -1),
        )
    )
    pay_a, pay_b = pl.pallas_call(
        functools.partial(edge_kernel, lon_count, held),
        out_shape=(edge_shape, edge_shape),
        in_specs=[HBM] * 4,
        out_specs=(VMEM,) * 2,
        scratch_shapes=[
            lists[0],
            pltpu.VMEM((bank_slot.shape[0] // LANES, LANES), jnp.int32),
            *lists[2:],
            pltpu.VMEM((channels * EDGE, lat_len), F32),
            pltpu.SemaphoreType.DMA((IN_COPIES + 3,)),
        ],
        compiler_params=PARAMS,
    )(sources[0], in_hbm(bank_slot.reshape(-1, LANES)), *sources[2:4])
    got_b = lax.ppermute(pay_b, "lon", lon_second)
    pay_a, early_bank, *given = pl.pallas_call(
        functools.partial(early_kernel, lon_count),
        out_shape=(edge_shape, *held_shapes),
        in_specs=[VMEM] + [HBM] * 7,
        out_specs=(VMEM,) * 7,
        scratch_shapes=[
            *lists[:2],
            *targets,
            pltpu.SemaphoreType.DMA((2,)),
            pltpu.SemaphoreType.DMA((4 + BANK_COPIES,)),
        ],
        compiler_params=PARAMS,
    )(pay_a, *sources[:2], *sources[4:])
    got_a = lax.ppermute(pay_a, "lon", lon_first)
    reduced, late_bank, own, position, weights, mixer, offset = pl.pallas_call(
        functools.partial(prepare_kernel, lon_count, lat_len),
        out_shape=(jax.ShapeDtypeStruct((rank, cells), BF16), *held_shapes),
        in_specs=[HBM] * 9 + [VMEM] * 5,
        out_specs=(VMEM,) * 7,
        scratch_shapes=[
            *lists,
            pltpu.VMEM((channels * lat_len, lon_len), F32),
            *targets,
            pltpu.SemaphoreType.DMA((IN_COPIES + 3,)),
            pltpu.SemaphoreType.DMA((4 + BANK_COPIES,)),
        ],
        compiler_params=PARAMS,
        cost_estimate=pl.CostEstimate(flops=10**6, bytes_accessed=kernel_bank.size * 4, transcendentals=0),
    )(*sources, *given)
    row_shape = jax.ShapeDtypeStruct((rank, REACH * lon_len + LANES), BF16)
    core_a, core_b = pl.pallas_call(
        functools.partial(pick_kernel, lat_len),
        out_shape=(core_shape, core_shape),
        in_specs=[VMEM] * 4,
        out_specs=(VMEM,) * 2,
        compiler_params=PARAMS,
    )(got_b, got_a, early_bank, late_bank)
    edges, row_a, row_b = pl.pallas_call(
        functools.partial(rows_kernel, lat_len),
        out_shape=(edge_shape, row_shape, row_shape),
        in_specs=[VMEM, VMEM, HBM, VMEM],
        out_specs=(VMEM,) * 3,
        compiler_params=PARAMS,
    )(got_b, got_a, core_b, reduced)
    core_b = lax.ppermute(core_b, "lon", lon_second)
    core_a = lax.ppermute(core_a, "lon", lon_first)
    row_a = lax.ppermute(row_a, "lat", lat_first)
    row_b = lax.ppermute(row_b, "lat", lat_second)
    border_cells = 2 * REACH * lon_len
    stack_rows = taps * rank // 2
    halo_stack_shape = jax.ShapeDtypeStruct((2, stack_rows, border_cells), BF16)
    inner, halo_stack = pl.pallas_call(
        functools.partial(inner_kernel, lat_len),
        out_shape=(jax.ShapeDtypeStruct((tap_rank * rank, cells - border_cells), BF16), halo_stack_shape),
        in_specs=[VMEM] * 3,
        out_specs=(VMEM,) * 2,
        scratch_shapes=[pltpu.VMEM((2, stack_rows, cells - border_cells), BF16)],
        compiler_params=PARAMS,
    )(reduced, edges, weights)
    border = pl.pallas_call(
        functools.partial(border_kernel, lat_len, lat_count),
        out_shape=jax.ShapeDtypeStruct((tap_rank * rank, border_cells), BF16),
        in_specs=[VMEM] * 4,
        out_specs=VMEM,
        scratch_shapes=[pltpu.VMEM(halo_stack_shape.shape, BF16)],
        compiler_params=PARAMS,
    )(row_b, row_a, weights, halo_stack)
    out_shape = (out_channels, lat_len, lon_len)
    return pl.pallas_call(
        mix_kernel,
        out_shape=jax.ShapeDtypeStruct(out_shape, BF16),
        in_specs=[VMEM] * 8,
        out_specs=HBM,
        scratch_shapes=[pltpu.VMEM(out_shape, BF16), pltpu.SemaphoreType.DMA((OUT_COPIES,))],
        compiler_params=PARAMS,
    )(inner, border, core_a, core_b, own, position, mixer, offset)


def solution(mesh):
    placed = (
        P(None, "lat", "lon"),
        P("lat", "lon"),
        P("lat", "lon", None),
        P(),
        P("lon", None, None),
        P(),
        P(),
        P(),
        P(),
    )
    return jax.shard_map(
        on_device, mesh=mesh, in_specs=placed, out_specs=P(None, "lat", "lon"), check_vma=False
    )
```

```python
import functools

import jax
import jax.numpy as jnp
from jax import lax
from jax.experimental import pallas as pl
from jax.experimental.pallas import tpu as pltpu
from jax.sharding import PartitionSpec as P

KS = 5
REACH = KS // 2
PER_OWNER = 2
LANES = 128
EDGE = 2 * REACH
GROUP = 8
STEP = 4
OUT_COPIES = 4
IN_COPIES = 4
BANK_COPIES = 8
EARLY = 1
F32 = jnp.float32
BF16 = jnp.bfloat16
VMEM = pl.BlockSpec(memory_space=pltpu.VMEM)
SMEM = pl.BlockSpec(memory_space=pltpu.SMEM)
HBM = pl.BlockSpec(memory_space=pltpu.HBM)
PARAMS = pltpu.CompilerParams(vmem_limit_bytes=24 * 1024 * 1024)


def swap_pairs(count):
    first = [(i, i ^ 1) for i in range(count)]
    second = [(i, (i + 1 if i % 2 else i - 1) % count) for i in range(count)]
    return first, second


def in_hbm(array):
    return pltpu.with_memory_space_constraint(array, pltpu.HBM)


def lane_index(shape):
    return lax.broadcasted_iota(jnp.int32, shape, 1)


def start_copies(pairs, sems):
    copies = [pltpu.make_async_copy(source, target, sems.at[i]) for i, (source, target) in enumerate(pairs)]
    for copy in copies:
        copy.start()
    return copies


def in_parts(source, target, count):
    share = target.shape[0] // count
    return tuple((source.at[pl.ds(i * share, share)], target.at[pl.ds(i * share, share)]) for i in range(count))


def find_rows(list_ref, slot_ref, lon_count, held):
    me = lax.axis_index("lon")
    owners = (me, lax.rem(me + lon_count - 1, lon_count), lax.rem(me + 1, lon_count))
    slots = [slot_ref[list_ref[0, 0, i]] for i in range(list_ref.shape[2])]
    places, rows = [], []
    for owner in owners:
        least, greatest = jnp.int32(held), jnp.int32(-1)
        first, last = jnp.int32(0), jnp.int32(0)
        for i, slot in enumerate(slots):
            local = slot - owner * held
            hit = (local >= 0) & (local < held)
            first = jnp.where(hit & (local < least), i, first)
            last = jnp.where(hit & (local > greatest), i, last)
            least = jnp.where(hit, jnp.minimum(local, least), least)
            greatest = jnp.where(hit, jnp.maximum(local, greatest), greatest)
        places.append([first, last])
        rows.append([jnp.minimum(least, held - 1), jnp.maximum(greatest, 0)])
    return places, rows


def is_early():
    return lax.axis_index("lon") == EARLY


class Held:
    names = ("bank", "own", "position", "weights", "mixer", "offset")
    sources = ("labels", "tap", "out_factor", "bias")

    def __init__(self, refs):
        self.__dict__.update(zip(self.names, refs))


def start_sources(sources, targets, bank_hbm, bank_ref, sems):
    pairs = tuple(zip(sources, targets))
    return start_copies(pairs + in_parts(bank_hbm, bank_ref, BANK_COPIES), sems)


def build_held(lon_count, list_ref, slot_ref, targets, copies, held):
    labels_ref, tap_ref, out_factor_ref, bias_ref = targets
    places, rows = find_rows(list_ref, slot_ref, lon_count, held.bank.shape[0])
    even = (lax.axis_index("lon") % 2) == 0
    order = list(places[0])
    order += [jnp.where(even, places[2][nth], places[1][nth]) for nth in range(PER_OWNER)]
    order += [jnp.where(even, places[1][nth], places[2][nth]) for nth in range(PER_OWNER)]
    labels = labels_ref[...]
    position = jnp.zeros(labels.shape, jnp.int32)
    for index, place in enumerate(order):
        position = jnp.where(labels == place, index, position)
    held.position[...] = position

    rank, out_channels = out_factor_ref.shape
    half = rank // 2
    tap_rank, taps = tap_ref.shape
    shape = (tap_rank * half, taps * half)
    spread = (
        lax.broadcasted_iota(jnp.int32, (shape[0], tap_rank), 0) // half == lane_index((shape[0], tap_rank))
    ).astype(BF16)
    repeat = (
        lax.broadcasted_iota(jnp.int32, (taps, shape[1]), 0) == lane_index((taps, shape[1])) // half
    ).astype(BF16)
    tall = jnp.dot(spread, tap_ref[...], preferred_element_type=F32).astype(BF16)
    wide = jnp.dot(tall, repeat, preferred_element_type=F32)
    same = lax.broadcasted_iota(jnp.int32, shape, 0) % half == lane_index(shape) % half
    held.weights[...] = jnp.where(same, wide, 0.0).astype(BF16)

    shape = (out_channels * GROUP, rank * GROUP)
    spread = (
        lax.broadcasted_iota(jnp.int32, (shape[0], out_channels), 0) // GROUP
        == lane_index((shape[0], out_channels))
    ).astype(BF16)
    repeat = (
        lax.broadcasted_iota(jnp.int32, (rank, shape[1]), 0) == lane_index((rank, shape[1])) % rank
    ).astype(BF16)
    tall = lax.dot_general(
        spread, out_factor_ref[...], (((1,), (1,)), ((), ())), preferred_element_type=F32
    ).astype(BF16)
    wide = jnp.dot(tall, repeat, preferred_element_type=F32)
    same = lax.broadcasted_iota(jnp.int32, shape, 0) % GROUP == lane_index(shape) // rank
    held.mixer[...] = jnp.where(same, wide, 0.0).astype(BF16)

    shape = (out_channels * GROUP, out_channels)
    mine = lax.broadcasted_iota(jnp.int32, shape, 0) // GROUP == lane_index(shape)
    offset = jnp.sum(jnp.where(mine, bias_ref[...], 0.0), axis=1, keepdims=True)
    held.offset[...] = jnp.broadcast_to(offset, held.offset.shape)
    for copy in copies:
        copy.wait()
    for nth in range(PER_OWNER):
        held.own[nth] = held.bank[rows[0][nth]]


def asked_rows(list_ref, slots_ref, owner, held):
    lane = lane_index((1, LANES))
    found = []
    for i in range(list_ref.shape[2]):
        region = list_ref[0, 0, i]
        row = slots_ref[pl.ds(region // LANES, 1), :]
        found.append(jnp.where(lane == region % LANES, row - owner * held, -1))
    local = jnp.max(jnp.concatenate(found, axis=0), axis=1, keepdims=True)
    hit = (local >= 0) & (local < held)
    least = jnp.min(jnp.where(hit, local, held - 1), axis=0, keepdims=True)
    greatest = jnp.max(jnp.where(hit, local, 0), axis=0, keepdims=True)
    return least, greatest


def edge_kernel(lon_count, *refs):
    list_hbm, slot_hbm, feat_hbm, in_hbm, bank_hbm = refs[:5]
    sources, slots_hbm, (pay_a_ref, pay_b_ref), held_refs = refs[5:9], refs[9], refs[10:12], refs[12:18]
    list_ref, slot_ref, feat_ref, in_ref, turned_ref, slots_ref = refs[18:24]
    targets, sems, held_sems = refs[24:28], refs[28], refs[29]
    held = Held(held_refs)
    channels, lat_len, lon_len = feat_ref.shape
    rank = in_ref.shape[0]
    batch = LANES // EDGE
    parts = channels // batch
    pairs = in_parts(feat_hbm, feat_ref, IN_COPIES)
    pairs += ((slots_hbm, slots_ref), (list_hbm, list_ref), (in_hbm, in_ref))
    copies = start_copies(pairs, sems)
    lane = lane_index((lat_len, LANES))
    for part in range(parts):
        for copy in copies[part * IN_COPIES // parts : (part + 1) * IN_COPIES // parts]:
            copy.wait()
        packed = jnp.zeros((lat_len, LANES), BF16)
        for c in range(batch):
            moved = pltpu.roll(feat_ref[part * batch + c], (EDGE * c + REACH) % LANES, 1)
            packed = jnp.where(lane // EDGE == c, moved, packed)
        turned_ref[part * LANES : (part + 1) * LANES, :] = jnp.transpose(packed.astype(F32))
    for copy in copies[IN_COPIES:]:
        copy.wait()
    columns = jnp.concatenate(
        [turned_ref[pl.ds(j, channels, stride=EDGE), :].astype(BF16) for j in range(EDGE)], axis=1
    )
    edges = jnp.dot(in_ref[...], columns, preferred_element_type=F32)
    edges = jnp.concatenate([edges, jnp.zeros((rank, LANES - EDGE * lat_len), F32)], axis=1)
    me = lax.axis_index("lon")
    even = (me % 2) == 0
    prev, following = lax.rem(me + lon_count - 1, lon_count), lax.rem(me + 1, lon_count)
    lane = lane_index((rank, LANES))
    for out_ref, owner in (
        (pay_a_ref, jnp.where(even, following, prev)),
        (pay_b_ref, jnp.where(even, prev, following)),
    ):
        load = edges
        for nth, row in enumerate(asked_rows(list_ref, slots_ref, owner, held.bank.shape[0])):
            load = jnp.where(lane == EDGE * lat_len + nth, row.astype(F32), load)
        out_ref[...] = load.astype(BF16)

    @pl.when(is_early())
    def _():
        copies = start_sources(sources, targets, bank_hbm, held.bank, held_sems)
        scalars = pltpu.make_async_copy(slot_hbm, slot_ref, sems.at[0])
        scalars.start()
        for copy in [scalars, *copies[: len(targets)]]:
            copy.wait()
        build_held(lon_count, list_ref, slot_ref, targets, copies[len(targets) :], held)


def reduce_tile(lat_len, feat_ref, in_ref, rows_ref, red_ref):
    channels, lon_len = feat_ref.shape[0], feat_ref.shape[2]
    rows_ref[...] = feat_ref[...].astype(F32).reshape(channels * lat_len, lon_len)
    cells = jnp.concatenate(
        [rows_ref[pl.ds(p, channels, stride=lat_len), :].astype(BF16) for p in range(lat_len)], axis=1
    )
    red_ref[...] = jnp.dot(in_ref[...], cells, preferred_element_type=F32).astype(BF16)


def prepare_kernel(lon_count, lat_len, *refs):
    list_hbm, slot_hbm, feat_hbm, in_hbm, bank_hbm = refs[:5]
    sources, given = refs[5:9], Held((None, *refs[9:14]))
    red_ref, held = refs[14], Held(refs[15:21])
    list_ref, slot_ref, feat_ref, in_ref, rows_ref = refs[21:26]
    targets, sems, held_sems = refs[26:30], refs[30], refs[31]
    early = is_early()
    shared = in_parts(feat_hbm, feat_ref, IN_COPIES) + ((in_hbm, in_ref),)
    lists = ((slot_hbm, slot_ref), (list_hbm, list_ref))

    @pl.when(early)
    def _():
        copies = start_copies(shared, sems)
        for name in held.names[1:]:
            getattr(held, name)[...] = getattr(given, name)[...]
        for copy in copies:
            copy.wait()
        reduce_tile(lat_len, feat_ref, in_ref, rows_ref, red_ref)

    @pl.when(jnp.logical_not(early))
    def _():
        copies = start_copies(shared + lists, sems)
        others = start_sources(sources, targets, bank_hbm, held.bank, held_sems)
        for copy in copies + others[: len(targets)]:
            copy.wait()
        reduce_tile(lat_len, feat_ref, in_ref, rows_ref, red_ref)
        build_held(lon_count, list_ref, slot_ref, targets, others[len(targets) :], held)


def pick_kernel(lat_len, got_b_ref, got_a_ref, early_bank_ref, late_bank_ref, core_a_ref, core_b_ref):
    early = is_early()
    lane = lane_index((1, LANES))
    for got_ref, core_ref in ((got_b_ref, core_b_ref), (got_a_ref, core_a_ref)):
        head = got_ref[...].astype(F32)[0:1, :]
        for nth in range(PER_OWNER):
            row = jnp.sum(jnp.where(lane == EDGE * lat_len + nth, head, 0.0)).astype(jnp.int32)
            core_ref[nth] = jnp.where(early, early_bank_ref[row], late_bank_ref[row])


def rows_kernel(lat_len, got_b_ref, got_a_ref, core_ref, red_ref, edge_ref, row_a_ref, row_b_ref):
    lon_len = red_ref.shape[1] // lat_len
    even = (lax.axis_index("lon") % 2) == 0
    from_prev = lane_index(got_a_ref.shape) < REACH * lat_len
    got = jnp.where(from_prev == even, got_b_ref[...].astype(F32), got_a_ref[...].astype(F32)).astype(BF16)
    source = lax.broadcasted_iota(jnp.int32, (LANES, LANES), 0)
    target = lane_index((LANES, LANES))
    order = (source == (target % EDGE) * lat_len + target // EDGE) & (target < EDGE * lat_len)
    edges = jnp.dot(got, order.astype(BF16), preferred_element_type=F32).astype(BF16)
    edge_ref[...] = edges
    even = (lax.axis_index("lat") % 2) == 0
    head = red_ref[:, : REACH * lon_len].astype(F32)
    tail = red_ref[:, (lat_len - REACH) * lon_len :].astype(F32)
    row_a_ref[:, : REACH * lon_len] = jnp.where(even, tail, head).astype(BF16)
    row_b_ref[:, : REACH * lon_len] = jnp.where(even, head, tail).astype(BF16)
    row_a_ref[:, REACH * lon_len :] = edges
    row_b_ref[:, REACH * lon_len :] = edges


def shifted_columns(row, edges, place):
    lane = lane_index(row.shape)
    lon_len = row.shape[1]
    edges = pltpu.roll(edges, (LANES - REACH - EDGE * place) % LANES, 1)
    moved = []
    for col_off in range(KS):
        shift = REACH - col_off
        if shift > 0:
            piece = pltpu.roll(jnp.where(lane >= lon_len - shift, edges, row), shift, 1)
        elif shift < 0:
            piece = pltpu.roll(jnp.where(lane < -shift, edges, row), lon_len + shift, 1)
        else:
            piece = row
        moved.append(piece.astype(BF16))
    return moved


def stack_row(stack_ref, p, moved, slots, lon_len):
    half = moved[0].shape[0] // 2
    for col_off, piece in enumerate(moved):
        for row_off in range(KS):
            slot = slots.get(p + REACH - row_off)
            if slot is not None:
                k = row_off * KS + col_off
                for h in range(2):
                    stack_ref[h, k * half : (k + 1) * half, slot * lon_len : (slot + 1) * lon_len] = piece[
                        h * half : (h + 1) * half
                    ]


def apply_taps(rank, weights_ref, stacked, tapped_ref, lon_len):
    half = rank // 2
    tap_rank = tapped_ref.shape[0] // rank
    width = STEP * lon_len
    for start in range(0, tapped_ref.shape[1], width):
        parts = [
            jnp.dot(weights_ref[...], stacked(h, start, width), preferred_element_type=F32)
            .astype(BF16)
            .reshape(tap_rank, 1, half, width)
            for h in range(2)
        ]
        tapped_ref[:, start : start + width] = jnp.concatenate(parts, axis=1).reshape(tap_rank * rank, width)


def border_slots(lat_len):
    slots = {p: p for p in range(REACH)}
    slots.update({lat_len - REACH + p: REACH + p for p in range(REACH)})
    return slots


def inner_kernel(lat_len, red_ref, edge_ref, weights_ref, tapped_ref, halo_stack_ref, stack_ref):
    rank = red_ref.shape[0]
    lon_len = red_ref.shape[1] // lat_len
    slots = {p: p - REACH for p in range(REACH, lat_len - REACH)}
    edges = edge_ref[...].astype(F32)
    for p in range(lat_len):
        row = red_ref[:, p * lon_len : (p + 1) * lon_len].astype(F32)
        moved = shifted_columns(row, edges, p)
        stack_row(stack_ref, p, moved, slots, lon_len)
        stack_row(halo_stack_ref, p, moved, border_slots(lat_len), lon_len)
    apply_taps(rank, weights_ref, lambda h, start, width: stack_ref[h, :, start : start + width], tapped_ref, lon_len)


def border_kernel(lat_len, lat_count, row_b_ref, row_a_ref, weights_ref, own_stack_ref, tapped_ref, stack_ref):
    rank = row_a_ref.shape[0]
    lon_len = (row_a_ref.shape[1] - LANES) // REACH
    lat = lax.axis_index("lat")
    even = (lat % 2) == 0
    row_a = row_a_ref[...].astype(F32)
    row_b = row_b_ref[...].astype(F32)
    above = jnp.where(lat == 0, 0.0, jnp.where(even, row_b, row_a))
    below = jnp.where(lat == lat_count - 1, 0.0, jnp.where(even, row_a, row_b))
    slots = border_slots(lat_len)
    for i in range(REACH):
        for p, holder, place in ((i - REACH, above, lat_len - REACH + i), (lat_len + i, below, i)):
            row = holder[:, i * lon_len : (i + 1) * lon_len]
            moved = shifted_columns(row, holder[:, REACH * lon_len :], place)
            stack_row(stack_ref, p, moved, slots, lon_len)
    block = KS * rank // 2
    in_halo = {
        (slot, row_off)
        for p, slot in slots.items()
        for row_off in range(KS)
        if not 0 <= p + row_off - REACH < lat_len
    }

    def stacked(h, start, width):
        columns = []
        for slot in range(start // lon_len, (start + width) // lon_len):
            span = slice(slot * lon_len, (slot + 1) * lon_len)
            pieces = []
            for row_off in range(KS):
                ref = stack_ref if (slot, row_off) in in_halo else own_stack_ref
                pieces.append(ref[h, row_off * block : (row_off + 1) * block, span])
            columns.append(jnp.concatenate(pieces, axis=0))
        return jnp.concatenate(columns, axis=1)

    apply_taps(rank, weights_ref, stacked, tapped_ref, lon_len)


def mix_kernel(
    inner_ref,
    border_ref,
    core_a_ref,
    core_b_ref,
    own_ref,
    position_ref,
    mixer_ref,
    offset_ref,
    out_hbm,
    stage_ref,
    sems,
):
    lat_len, lon_len = position_ref.shape
    rank = own_ref.shape[1]
    cores = jnp.concatenate(
        [ref[...].reshape(PER_OWNER * rank, -1) for ref in (own_ref, core_a_ref, core_b_ref)], axis=0
    )
    chunks = [(border_ref, 0, [*range(REACH), *range(lat_len - REACH, lat_len)])]
    for start in range(REACH, lat_len - REACH, STEP):
        chunks.append((inner_ref, start - REACH, [*range(start, start + STEP)]))
    by_row = {}
    for ref, first, rows in chunks:
        width = len(rows) * lon_len
        every = jnp.dot(cores, ref[:, first * lon_len : first * lon_len + width], preferred_element_type=F32)
        position = jnp.concatenate([position_ref[r : r + 1, :] for r in rows], axis=1)
        hidden = jnp.zeros((rank, width), F32)
        for index in range(3 * PER_OWNER):
            hidden = jnp.where(position == index, every[index * rank : (index + 1) * rank], hidden)
        hidden = hidden.astype(BF16)
        for i, r in enumerate(rows):
            by_row[r] = hidden[:, i * lon_len : (i + 1) * lon_len]
    pieces = [by_row[r] for r in range(lat_len)]
    groups = [jnp.concatenate(pieces[g : g + GROUP], axis=0) for g in range(0, lat_len, GROUP)]
    channels = stage_ref.shape[0]
    share = channels // OUT_COPIES
    copies = []
    for part in range(OUT_COPIES):
        span = slice(part * share * GROUP, (part + 1) * share * GROUP)
        blocks = []
        for hidden in groups:
            output = jnp.dot(mixer_ref[span, :], hidden, preferred_element_type=F32) + offset_ref[span, :]
            mixed = 0.5 * output * (1.0 + jnp.tanh(0.5 * output))
            blocks.append(mixed.reshape(share, GROUP, lon_len))
        held = slice(part * share, (part + 1) * share)
        stage_ref[held] = jnp.concatenate(blocks, axis=1).astype(BF16)
        copy = pltpu.make_async_copy(stage_ref.at[held], out_hbm.at[held], sems.at[part])
        copy.start()
        copies.append(copy)
    for copy in copies:
        copy.wait()


def on_device(
    features, labels, tile_regions, bank_slot, kernel_bank, in_factor, tap_factor, out_factor, out_bias
):
    channels, lat_len, lon_len = features.shape
    rank = in_factor.shape[0]
    held, core_rows, core_cols = kernel_bank.shape
    tap_rank, taps = tap_factor.shape
    out_channels = out_factor.shape[0]
    cells = lat_len * lon_len
    lon_count, lat_count = lax.axis_size("lon"), lax.axis_size("lat")
    lon_first, lon_second = swap_pairs(lon_count)
    lat_first, lat_second = swap_pairs(lat_count)
    edge_shape = jax.ShapeDtypeStruct((rank, LANES), BF16)
    core_shape = jax.ShapeDtypeStruct((PER_OWNER, core_rows, core_cols), BF16)
    held_shapes = (
        jax.ShapeDtypeStruct(kernel_bank.shape, BF16),
        core_shape,
        jax.ShapeDtypeStruct(labels.shape, jnp.int32),
        jax.ShapeDtypeStruct((tap_rank * rank // 2, taps * rank // 2), BF16),
        jax.ShapeDtypeStruct((out_channels * GROUP, rank * GROUP), BF16),
        jax.ShapeDtypeStruct((out_channels * GROUP, lon_len), F32),
    )
    lists = [
        pltpu.SMEM(tile_regions.shape, jnp.int32),
        pltpu.SMEM(bank_slot.shape, jnp.int32),
        pltpu.VMEM(features.shape, BF16),
        pltpu.VMEM(in_factor.shape, BF16),
    ]
    targets = [
        pltpu.VMEM(labels.shape, jnp.int32),
        pltpu.VMEM(tap_factor.shape, BF16),
        pltpu.VMEM(out_factor.shape[::-1], BF16),
        pltpu.VMEM((1, out_channels), F32),
    ]
    sources = tuple(
        in_hbm(x)
        for x in (
            tile_regions,
            bank_slot,
            features,
            in_factor,
            kernel_bank,
            labels,
            tap_factor,
            out_factor.T,
            out_bias.reshape(1, -1),
        )
    )
    pay_a, pay_b, early_bank, *given = pl.pallas_call(
        functools.partial(edge_kernel, lon_count),
        out_shape=(edge_shape, edge_shape, *held_shapes),
        in_specs=[HBM] * 10,
        out_specs=(VMEM,) * 8,
        scratch_shapes=[
            *lists,
            pltpu.VMEM((channels * EDGE, lat_len), F32),
            pltpu.VMEM((bank_slot.shape[0] // LANES, LANES), jnp.int32),
            *targets,
            pltpu.SemaphoreType.DMA((IN_COPIES + 3,)),
            pltpu.SemaphoreType.DMA((4 + BANK_COPIES,)),
        ],
        compiler_params=PARAMS,
    )(*sources, in_hbm(bank_slot.reshape(-1, LANES)))
    got_b = lax.ppermute(pay_b, "lon", lon_second)
    got_a = lax.ppermute(pay_a, "lon", lon_first)
    reduced, late_bank, own, position, weights, mixer, offset = pl.pallas_call(
        functools.partial(prepare_kernel, lon_count, lat_len),
        out_shape=(jax.ShapeDtypeStruct((rank, cells), BF16), *held_shapes),
        in_specs=[HBM] * 9 + [VMEM] * 5,
        out_specs=(VMEM,) * 7,
        scratch_shapes=[
            *lists,
            pltpu.VMEM((channels * lat_len, lon_len), F32),
            *targets,
            pltpu.SemaphoreType.DMA((IN_COPIES + 3,)),
            pltpu.SemaphoreType.DMA((4 + BANK_COPIES,)),
        ],
        compiler_params=PARAMS,
        cost_estimate=pl.CostEstimate(flops=10**6, bytes_accessed=kernel_bank.size * 4, transcendentals=0),
    )(*sources, *given)
    row_shape = jax.ShapeDtypeStruct((rank, REACH * lon_len + LANES), BF16)
    core_a, core_b = pl.pallas_call(
        functools.partial(pick_kernel, lat_len),
        out_shape=(core_shape, core_shape),
        in_specs=[VMEM] * 4,
        out_specs=(VMEM,) * 2,
        compiler_params=PARAMS,
    )(got_b, got_a, early_bank, late_bank)
    edges, row_a, row_b = pl.pallas_call(
        functools.partial(rows_kernel, lat_len),
        out_shape=(edge_shape, row_shape, row_shape),
        in_specs=[VMEM, VMEM, HBM, VMEM],
        out_specs=(VMEM,) * 3,
        compiler_params=PARAMS,
    )(got_b, got_a, core_b, reduced)
    core_b = lax.ppermute(core_b, "lon", lon_second)
    core_a = lax.ppermute(core_a, "lon", lon_first)
    row_a = lax.ppermute(row_a, "lat", lat_first)
    row_b = lax.ppermute(row_b, "lat", lat_second)
    border_cells = 2 * REACH * lon_len
    stack_rows = taps * rank // 2
    halo_stack_shape = jax.ShapeDtypeStruct((2, stack_rows, border_cells), BF16)
    inner, halo_stack = pl.pallas_call(
        functools.partial(inner_kernel, lat_len),
        out_shape=(jax.ShapeDtypeStruct((tap_rank * rank, cells - border_cells), BF16), halo_stack_shape),
        in_specs=[VMEM] * 3,
        out_specs=(VMEM,) * 2,
        scratch_shapes=[pltpu.VMEM((2, stack_rows, cells - border_cells), BF16)],
        compiler_params=PARAMS,
    )(reduced, edges, weights)
    border = pl.pallas_call(
        functools.partial(border_kernel, lat_len, lat_count),
        out_shape=jax.ShapeDtypeStruct((tap_rank * rank, border_cells), BF16),
        in_specs=[VMEM] * 4,
        out_specs=VMEM,
        scratch_shapes=[pltpu.VMEM(halo_stack_shape.shape, BF16)],
        compiler_params=PARAMS,
    )(row_b, row_a, weights, halo_stack)
    out_shape = (out_channels, lat_len, lon_len)
    return pl.pallas_call(
        mix_kernel,
        out_shape=jax.ShapeDtypeStruct(out_shape, BF16),
        in_specs=[VMEM] * 8,
        out_specs=HBM,
        scratch_shapes=[pltpu.VMEM(out_shape, BF16), pltpu.SemaphoreType.DMA((OUT_COPIES,))],
        compiler_params=PARAMS,
    )(inner, border, core_a, core_b, own, position, mixer, offset)


def solution(mesh):
    placed = (
        P(None, "lat", "lon"),
        P("lat", "lon"),
        P("lat", "lon", None),
        P(),
        P("lon", None, None),
        P(),
        P(),
        P(),
        P(),
    )
    return jax.shard_map(
        on_device, mesh=mesh, in_specs=placed, out_specs=P(None, "lat", "lon"), check_vma=False
    )
```

```python
import functools

import jax
import jax.numpy as jnp
from jax import lax
from jax.experimental import pallas as pl
from jax.experimental.pallas import tpu as pltpu
from jax.sharding import PartitionSpec as P

KS = 5
REACH = KS // 2
PER_OWNER = 2
LANES = 128
EDGE = 2 * REACH
GROUP = 8
STEP = 4
OUT_COPIES = 4
IN_COPIES = 4
BANK_COPIES = 8
EARLY = 1
F32 = jnp.float32
BF16 = jnp.bfloat16
VMEM = pl.BlockSpec(memory_space=pltpu.VMEM)
SMEM = pl.BlockSpec(memory_space=pltpu.SMEM)
HBM = pl.BlockSpec(memory_space=pltpu.HBM)
PARAMS = pltpu.CompilerParams(vmem_limit_bytes=24 * 1024 * 1024)


def swap_pairs(count):
    first = [(i, i ^ 1) for i in range(count)]
    second = [(i, (i + 1 if i % 2 else i - 1) % count) for i in range(count)]
    return first, second


def in_hbm(array):
    return pltpu.with_memory_space_constraint(array, pltpu.HBM)


def lane_index(shape):
    return lax.broadcasted_iota(jnp.int32, shape, 1)


def start_copies(pairs, sems):
    copies = [pltpu.make_async_copy(source, target, sems.at[i]) for i, (source, target) in enumerate(pairs)]
    for copy in copies:
        copy.start()
    return copies


def in_parts(source, target, count):
    share = target.shape[0] // count
    return tuple((source.at[pl.ds(i * share, share)], target.at[pl.ds(i * share, share)]) for i in range(count))


def find_rows(list_ref, slot_ref, lon_count, held):
    me = lax.axis_index("lon")
    owners = (me, lax.rem(me + lon_count - 1, lon_count), lax.rem(me + 1, lon_count))
    slots = [slot_ref[list_ref[0, 0, i]] for i in range(list_ref.shape[2])]
    places, rows = [], []
    for owner in owners:
        least, greatest = jnp.int32(held), jnp.int32(-1)
        first, last = jnp.int32(0), jnp.int32(0)
        for i, slot in enumerate(slots):
            local = slot - owner * held
            hit = (local >= 0) & (local < held)
            first = jnp.where(hit & (local < least), i, first)
            last = jnp.where(hit & (local > greatest), i, last)
            least = jnp.where(hit, jnp.minimum(local, least), least)
            greatest = jnp.where(hit, jnp.maximum(local, greatest), greatest)
        places.append([first, last])
        rows.append([jnp.minimum(least, held - 1), jnp.maximum(greatest, 0)])
    return places, rows


def is_early():
    return lax.axis_index("lon") == EARLY


class Held:
    names = ("bank", "own", "position", "weights", "mixer", "offset")
    sources = ("labels", "tap", "out_factor", "bias")

    def __init__(self, refs):
        self.__dict__.update(zip(self.names, refs))


def start_sources(sources, targets, bank_hbm, bank_ref, sems):
    pairs = tuple(zip(sources, targets))
    return start_copies(pairs + in_parts(bank_hbm, bank_ref, BANK_COPIES), sems)


def build_held(lon_count, list_ref, slot_ref, targets, copies, held):
    labels_ref, tap_ref, out_factor_ref, bias_ref = targets
    places, rows = find_rows(list_ref, slot_ref, lon_count, held.bank.shape[0])
    even = (lax.axis_index("lon") % 2) == 0
    order = list(places[0])
    order += [jnp.where(even, places[2][nth], places[1][nth]) for nth in range(PER_OWNER)]
    order += [jnp.where(even, places[1][nth], places[2][nth]) for nth in range(PER_OWNER)]
    labels = labels_ref[...]
    position = jnp.zeros(labels.shape, jnp.int32)
    for index, place in enumerate(order):
        position = jnp.where(labels == place, index, position)
    held.position[...] = position

    rank, out_channels = out_factor_ref.shape
    half = rank // 2
    tap_rank, taps = tap_ref.shape
    shape = (tap_rank * half, taps * half)
    spread = (
        lax.broadcasted_iota(jnp.int32, (shape[0], tap_rank), 0) // half == lane_index((shape[0], tap_rank))
    ).astype(BF16)
    repeat = (
        lax.broadcasted_iota(jnp.int32, (taps, shape[1]), 0) == lane_index((taps, shape[1])) // half
    ).astype(BF16)
    tall = jnp.dot(spread, tap_ref[...], preferred_element_type=F32).astype(BF16)
    wide = jnp.dot(tall, repeat, preferred_element_type=F32)
    same = lax.broadcasted_iota(jnp.int32, shape, 0) % half == lane_index(shape) % half
    held.weights[...] = jnp.where(same, wide, 0.0).astype(BF16)

    shape = (out_channels * GROUP, rank * GROUP)
    spread = (
        lax.broadcasted_iota(jnp.int32, (shape[0], out_channels), 0) // GROUP
        == lane_index((shape[0], out_channels))
    ).astype(BF16)
    repeat = (
        lax.broadcasted_iota(jnp.int32, (rank, shape[1]), 0) == lane_index((rank, shape[1])) % rank
    ).astype(BF16)
    tall = lax.dot_general(
        spread, out_factor_ref[...], (((1,), (1,)), ((), ())), preferred_element_type=F32
    ).astype(BF16)
    wide = jnp.dot(tall, repeat, preferred_element_type=F32)
    same = lax.broadcasted_iota(jnp.int32, shape, 0) % GROUP == lane_index(shape) // rank
    held.mixer[...] = jnp.where(same, wide, 0.0).astype(BF16)

    shape = (out_channels * GROUP, out_channels)
    mine = lax.broadcasted_iota(jnp.int32, shape, 0) // GROUP == lane_index(shape)
    offset = jnp.sum(jnp.where(mine, bias_ref[...], 0.0), axis=1, keepdims=True)
    held.offset[...] = jnp.broadcast_to(offset, held.offset.shape)
    for copy in copies:
        copy.wait()
    for nth in range(PER_OWNER):
        held.own[nth] = held.bank[rows[0][nth]]


def edge_kernel(lon_count, *refs):
    list_hbm, slot_hbm, feat_hbm, in_hbm, bank_hbm = refs[:5]
    sources, (pay_a_ref, pay_b_ref), held_refs = refs[5:9], refs[9:11], refs[11:17]
    list_ref, slot_ref, feat_ref, in_ref, turned_ref = refs[17:22]
    targets, sems, held_sems = refs[22:26], refs[26], refs[27]
    held = Held(held_refs)
    channels, lat_len, lon_len = feat_ref.shape
    rank = in_ref.shape[0]
    pairs = in_parts(feat_hbm, feat_ref, IN_COPIES)
    pairs += ((slot_hbm, slot_ref), (list_hbm, list_ref), (in_hbm, in_ref))
    for copy in start_copies(pairs, sems):
        copy.wait()
    lane = lane_index((lat_len, LANES))
    batch = LANES // EDGE
    for first in range(0, channels, batch):
        packed = jnp.zeros((lat_len, LANES), F32)
        for c in range(batch):
            moved = pltpu.roll(feat_ref[first + c].astype(F32), (EDGE * c + REACH) % LANES, 1)
            packed = jnp.where(lane // EDGE == c, moved, packed)
        turned_ref[first * EDGE : (first + batch) * EDGE, :] = jnp.transpose(packed)
    columns = jnp.concatenate(
        [turned_ref[pl.ds(j, channels, stride=EDGE), :].astype(BF16) for j in range(EDGE)], axis=1
    )
    edges = jnp.dot(in_ref[...], columns, preferred_element_type=F32)
    edges = jnp.concatenate([edges, jnp.zeros((rank, LANES - EDGE * lat_len), F32)], axis=1)
    _, rows = find_rows(list_ref, slot_ref, lon_count, held.bank.shape[0])
    even = (lax.axis_index("lon") % 2) == 0
    lane = lane_index((rank, LANES))
    for out_ref, wanted in ((pay_a_ref, even), (pay_b_ref, jnp.logical_not(even))):
        load = edges
        for nth in range(PER_OWNER):
            row = jnp.where(wanted, rows[2][nth], rows[1][nth]).astype(F32)
            load = jnp.where(lane == EDGE * lat_len + nth, row, load)
        out_ref[...] = load.astype(BF16)

    @pl.when(is_early())
    def _():
        copies = start_sources(sources, targets, bank_hbm, held.bank, held_sems)
        for copy in copies[: len(targets)]:
            copy.wait()
        build_held(lon_count, list_ref, slot_ref, targets, copies[len(targets) :], held)


def reduce_tile(lat_len, feat_ref, in_ref, rows_ref, red_ref):
    channels, lon_len = feat_ref.shape[0], feat_ref.shape[2]
    rows_ref[...] = feat_ref[...].astype(F32).reshape(channels * lat_len, lon_len)
    cells = jnp.concatenate(
        [rows_ref[pl.ds(p, channels, stride=lat_len), :].astype(BF16) for p in range(lat_len)], axis=1
    )
    red_ref[...] = jnp.dot(in_ref[...], cells, preferred_element_type=F32).astype(BF16)


def prepare_kernel(lon_count, lat_len, *refs):
    list_hbm, slot_hbm, feat_hbm, in_hbm, bank_hbm = refs[:5]
    sources, given = refs[5:9], Held((None, *refs[9:14]))
    red_ref, held = refs[14], Held(refs[15:21])
    list_ref, slot_ref, feat_ref, in_ref, rows_ref = refs[21:26]
    targets, sems, held_sems = refs[26:30], refs[30], refs[31]
    early = is_early()
    shared = in_parts(feat_hbm, feat_ref, IN_COPIES) + ((in_hbm, in_ref),)
    lists = ((slot_hbm, slot_ref), (list_hbm, list_ref))

    @pl.when(early)
    def _():
        copies = start_copies(shared, sems)
        for name in held.names[1:]:
            getattr(held, name)[...] = getattr(given, name)[...]
        for copy in copies:
            copy.wait()
        reduce_tile(lat_len, feat_ref, in_ref, rows_ref, red_ref)

    @pl.when(jnp.logical_not(early))
    def _():
        copies = start_copies(shared + lists, sems)
        others = start_sources(sources, targets, bank_hbm, held.bank, held_sems)
        for copy in copies + others[: len(targets)]:
            copy.wait()
        reduce_tile(lat_len, feat_ref, in_ref, rows_ref, red_ref)
        build_held(lon_count, list_ref, slot_ref, targets, others[len(targets) :], held)


def pick_kernel(lat_len, got_b_ref, got_a_ref, early_bank_ref, late_bank_ref, core_a_ref, core_b_ref):
    early = is_early()
    lane = lane_index((1, LANES))
    for got_ref, core_ref in ((got_b_ref, core_b_ref), (got_a_ref, core_a_ref)):
        head = got_ref[...].astype(F32)[0:1, :]
        for nth in range(PER_OWNER):
            row = jnp.sum(jnp.where(lane == EDGE * lat_len + nth, head, 0.0)).astype(jnp.int32)
            core_ref[nth] = jnp.where(early, early_bank_ref[row], late_bank_ref[row])


def rows_kernel(lat_len, got_b_ref, got_a_ref, core_ref, red_ref, edge_ref, row_a_ref, row_b_ref):
    lon_len = red_ref.shape[1] // lat_len
    even = (lax.axis_index("lon") % 2) == 0
    from_prev = lane_index(got_a_ref.shape) < REACH * lat_len
    got = jnp.where(from_prev == even, got_b_ref[...].astype(F32), got_a_ref[...].astype(F32)).astype(BF16)
    source = lax.broadcasted_iota(jnp.int32, (LANES, LANES), 0)
    target = lane_index((LANES, LANES))
    order = (source == (target % EDGE) * lat_len + target // EDGE) & (target < EDGE * lat_len)
    edges = jnp.dot(got, order.astype(BF16), preferred_element_type=F32).astype(BF16)
    edge_ref[...] = edges
    even = (lax.axis_index("lat") % 2) == 0
    head = red_ref[:, : REACH * lon_len].astype(F32)
    tail = red_ref[:, (lat_len - REACH) * lon_len :].astype(F32)
    row_a_ref[:, : REACH * lon_len] = jnp.where(even, tail, head).astype(BF16)
    row_b_ref[:, : REACH * lon_len] = jnp.where(even, head, tail).astype(BF16)
    row_a_ref[:, REACH * lon_len :] = edges
    row_b_ref[:, REACH * lon_len :] = edges


def shifted_columns(row, edges, place):
    lane = lane_index(row.shape)
    lon_len = row.shape[1]
    edges = pltpu.roll(edges, (LANES - REACH - EDGE * place) % LANES, 1)
    moved = []
    for col_off in range(KS):
        shift = REACH - col_off
        if shift > 0:
            piece = pltpu.roll(jnp.where(lane >= lon_len - shift, edges, row), shift, 1)
        elif shift < 0:
            piece = pltpu.roll(jnp.where(lane < -shift, edges, row), lon_len + shift, 1)
        else:
            piece = row
        moved.append(piece.astype(BF16))
    return moved


def stack_row(stack_ref, p, moved, slots, lon_len):
    half = moved[0].shape[0] // 2
    for col_off, piece in enumerate(moved):
        for row_off in range(KS):
            slot = slots.get(p + REACH - row_off)
            if slot is not None:
                k = row_off * KS + col_off
                for h in range(2):
                    stack_ref[h, k * half : (k + 1) * half, slot * lon_len : (slot + 1) * lon_len] = piece[
                        h * half : (h + 1) * half
                    ]


def apply_taps(rank, weights_ref, stacked, tapped_ref, lon_len):
    half = rank // 2
    tap_rank = tapped_ref.shape[0] // rank
    width = STEP * lon_len
    for start in range(0, tapped_ref.shape[1], width):
        parts = [
            jnp.dot(weights_ref[...], stacked(h, start, width), preferred_element_type=F32)
            .astype(BF16)
            .reshape(tap_rank, 1, half, width)
            for h in range(2)
        ]
        tapped_ref[:, start : start + width] = jnp.concatenate(parts, axis=1).reshape(tap_rank * rank, width)


def border_slots(lat_len):
    slots = {p: p for p in range(REACH)}
    slots.update({lat_len - REACH + p: REACH + p for p in range(REACH)})
    return slots


def inner_kernel(lat_len, red_ref, edge_ref, weights_ref, tapped_ref, halo_stack_ref, stack_ref):
    rank = red_ref.shape[0]
    lon_len = red_ref.shape[1] // lat_len
    slots = {p: p - REACH for p in range(REACH, lat_len - REACH)}
    edges = edge_ref[...].astype(F32)
    for p in range(lat_len):
        row = red_ref[:, p * lon_len : (p + 1) * lon_len].astype(F32)
        moved = shifted_columns(row, edges, p)
        stack_row(stack_ref, p, moved, slots, lon_len)
        stack_row(halo_stack_ref, p, moved, border_slots(lat_len), lon_len)
    apply_taps(rank, weights_ref, lambda h, start, width: stack_ref[h, :, start : start + width], tapped_ref, lon_len)


def border_kernel(lat_len, lat_count, row_b_ref, row_a_ref, weights_ref, own_stack_ref, tapped_ref, stack_ref):
    rank = row_a_ref.shape[0]
    lon_len = (row_a_ref.shape[1] - LANES) // REACH
    lat = lax.axis_index("lat")
    even = (lat % 2) == 0
    row_a = row_a_ref[...].astype(F32)
    row_b = row_b_ref[...].astype(F32)
    above = jnp.where(lat == 0, 0.0, jnp.where(even, row_b, row_a))
    below = jnp.where(lat == lat_count - 1, 0.0, jnp.where(even, row_a, row_b))
    slots = border_slots(lat_len)
    for i in range(REACH):
        for p, holder, place in ((i - REACH, above, lat_len - REACH + i), (lat_len + i, below, i)):
            row = holder[:, i * lon_len : (i + 1) * lon_len]
            moved = shifted_columns(row, holder[:, REACH * lon_len :], place)
            stack_row(stack_ref, p, moved, slots, lon_len)
    block = KS * rank // 2
    in_halo = {
        (slot, row_off)
        for p, slot in slots.items()
        for row_off in range(KS)
        if not 0 <= p + row_off - REACH < lat_len
    }

    def stacked(h, start, width):
        columns = []
        for slot in range(start // lon_len, (start + width) // lon_len):
            span = slice(slot * lon_len, (slot + 1) * lon_len)
            pieces = []
            for row_off in range(KS):
                ref = stack_ref if (slot, row_off) in in_halo else own_stack_ref
                pieces.append(ref[h, row_off * block : (row_off + 1) * block, span])
            columns.append(jnp.concatenate(pieces, axis=0))
        return jnp.concatenate(columns, axis=1)

    apply_taps(rank, weights_ref, stacked, tapped_ref, lon_len)


def mix_kernel(
    inner_ref,
    border_ref,
    core_a_ref,
    core_b_ref,
    own_ref,
    position_ref,
    mixer_ref,
    offset_ref,
    out_hbm,
    stage_ref,
    sems,
):
    lat_len, lon_len = position_ref.shape
    rank = own_ref.shape[1]
    cores = jnp.concatenate(
        [ref[...].reshape(PER_OWNER * rank, -1) for ref in (own_ref, core_a_ref, core_b_ref)], axis=0
    )
    chunks = [(border_ref, 0, [*range(REACH), *range(lat_len - REACH, lat_len)])]
    for start in range(REACH, lat_len - REACH, STEP):
        chunks.append((inner_ref, start - REACH, [*range(start, start + STEP)]))
    by_row = {}
    for ref, first, rows in chunks:
        width = len(rows) * lon_len
        every = jnp.dot(cores, ref[:, first * lon_len : first * lon_len + width], preferred_element_type=F32)
        position = jnp.concatenate([position_ref[r : r + 1, :] for r in rows], axis=1)
        hidden = jnp.zeros((rank, width), F32)
        for index in range(3 * PER_OWNER):
            hidden = jnp.where(position == index, every[index * rank : (index + 1) * rank], hidden)
        hidden = hidden.astype(BF16)
        for i, r in enumerate(rows):
            by_row[r] = hidden[:, i * lon_len : (i + 1) * lon_len]
    pieces = [by_row[r] for r in range(lat_len)]
    groups = [jnp.concatenate(pieces[g : g + GROUP], axis=0) for g in range(0, lat_len, GROUP)]
    channels = stage_ref.shape[0]
    share = channels // OUT_COPIES
    outputs = [jnp.dot(mixer_ref[...], hidden, preferred_element_type=F32) for hidden in groups]
    copies = []
    for part in range(OUT_COPIES):
        span = slice(part * share * GROUP, (part + 1) * share * GROUP)
        blocks = []
        for output in outputs:
            output = output[span] + offset_ref[span, :]
            mixed = 0.5 * output * (1.0 + jnp.tanh(0.5 * output))
            blocks.append(mixed.reshape(share, GROUP, lon_len))
        held = slice(part * share, (part + 1) * share)
        stage_ref[held] = jnp.concatenate(blocks, axis=1).astype(BF16)
        copy = pltpu.make_async_copy(stage_ref.at[held], out_hbm.at[held], sems.at[part])
        copy.start()
        copies.append(copy)
    for copy in copies:
        copy.wait()


def on_device(
    features, labels, tile_regions, bank_slot, kernel_bank, in_factor, tap_factor, out_factor, out_bias
):
    channels, lat_len, lon_len = features.shape
    rank = in_factor.shape[0]
    held, core_rows, core_cols = kernel_bank.shape
    tap_rank, taps = tap_factor.shape
    out_channels = out_factor.shape[0]
    cells = lat_len * lon_len
    lon_count, lat_count = lax.axis_size("lon"), lax.axis_size("lat")
    lon_first, lon_second = swap_pairs(lon_count)
    lat_first, lat_second = swap_pairs(lat_count)
    edge_shape = jax.ShapeDtypeStruct((rank, LANES), BF16)
    core_shape = jax.ShapeDtypeStruct((PER_OWNER, core_rows, core_cols), BF16)
    held_shapes = (
        jax.ShapeDtypeStruct(kernel_bank.shape, BF16),
        core_shape,
        jax.ShapeDtypeStruct(labels.shape, jnp.int32),
        jax.ShapeDtypeStruct((tap_rank * rank // 2, taps * rank // 2), BF16),
        jax.ShapeDtypeStruct((out_channels * GROUP, rank * GROUP), BF16),
        jax.ShapeDtypeStruct((out_channels * GROUP, lon_len), F32),
    )
    lists = [
        pltpu.SMEM(tile_regions.shape, jnp.int32),
        pltpu.SMEM(bank_slot.shape, jnp.int32),
        pltpu.VMEM(features.shape, BF16),
        pltpu.VMEM(in_factor.shape, BF16),
    ]
    targets = [
        pltpu.VMEM(labels.shape, jnp.int32),
        pltpu.VMEM(tap_factor.shape, BF16),
        pltpu.VMEM(out_factor.shape[::-1], BF16),
        pltpu.VMEM((1, out_channels), F32),
    ]
    sources = tuple(
        in_hbm(x)
        for x in (
            tile_regions,
            bank_slot,
            features,
            in_factor,
            kernel_bank,
            labels,
            tap_factor,
            out_factor.T,
            out_bias.reshape(1, -1),
        )
    )
    pay_a, pay_b, early_bank, *given = pl.pallas_call(
        functools.partial(edge_kernel, lon_count),
        out_shape=(edge_shape, edge_shape, *held_shapes),
        in_specs=[HBM] * 9,
        out_specs=(VMEM,) * 8,
        scratch_shapes=[
            *lists,
            pltpu.VMEM((channels * EDGE, lat_len), F32),
            *targets,
            pltpu.SemaphoreType.DMA((IN_COPIES + 3,)),
            pltpu.SemaphoreType.DMA((4 + BANK_COPIES,)),
        ],
        compiler_params=PARAMS,
    )(*sources)
    got_b = lax.ppermute(pay_b, "lon", lon_second)
    got_a = lax.ppermute(pay_a, "lon", lon_first)
    reduced, late_bank, own, position, weights, mixer, offset = pl.pallas_call(
        functools.partial(prepare_kernel, lon_count, lat_len),
        out_shape=(jax.ShapeDtypeStruct((rank, cells), BF16), *held_shapes),
        in_specs=[HBM] * 9 + [VMEM] * 5,
        out_specs=(VMEM,) * 7,
        scratch_shapes=[
            *lists,
            pltpu.VMEM((channels * lat_len, lon_len), F32),
            *targets,
            pltpu.SemaphoreType.DMA((IN_COPIES + 3,)),
            pltpu.SemaphoreType.DMA((4 + BANK_COPIES,)),
        ],
        compiler_params=PARAMS,
        cost_estimate=pl.CostEstimate(flops=10**6, bytes_accessed=kernel_bank.size * 4, transcendentals=0),
    )(*sources, *given)
    row_shape = jax.ShapeDtypeStruct((rank, REACH * lon_len + LANES), BF16)
    core_a, core_b = pl.pallas_call(
        functools.partial(pick_kernel, lat_len),
        out_shape=(core_shape, core_shape),
        in_specs=[VMEM] * 4,
        out_specs=(VMEM,) * 2,
        compiler_params=PARAMS,
    )(got_b, got_a, early_bank, late_bank)
    edges, row_a, row_b = pl.pallas_call(
        functools.partial(rows_kernel, lat_len),
        out_shape=(edge_shape, row_shape, row_shape),
        in_specs=[VMEM, VMEM, HBM, VMEM],
        out_specs=(VMEM,) * 3,
        compiler_params=PARAMS,
    )(got_b, got_a, core_b, reduced)
    core_b = lax.ppermute(core_b, "lon", lon_second)
    core_a = lax.ppermute(core_a, "lon", lon_first)
    row_a = lax.ppermute(row_a, "lat", lat_first)
    row_b = lax.ppermute(row_b, "lat", lat_second)
    border_cells = 2 * REACH * lon_len
    stack_rows = taps * rank // 2
    halo_stack_shape = jax.ShapeDtypeStruct((2, stack_rows, border_cells), BF16)
    inner, halo_stack = pl.pallas_call(
        functools.partial(inner_kernel, lat_len),
        out_shape=(jax.ShapeDtypeStruct((tap_rank * rank, cells - border_cells), BF16), halo_stack_shape),
        in_specs=[VMEM] * 3,
        out_specs=(VMEM,) * 2,
        scratch_shapes=[pltpu.VMEM((2, stack_rows, cells - border_cells), BF16)],
        compiler_params=PARAMS,
    )(reduced, edges, weights)
    border = pl.pallas_call(
        functools.partial(border_kernel, lat_len, lat_count),
        out_shape=jax.ShapeDtypeStruct((tap_rank * rank, border_cells), BF16),
        in_specs=[VMEM] * 4,
        out_specs=VMEM,
        scratch_shapes=[pltpu.VMEM(halo_stack_shape.shape, BF16)],
        compiler_params=PARAMS,
    )(row_b, row_a, weights, halo_stack)
    out_shape = (out_channels, lat_len, lon_len)
    return pl.pallas_call(
        mix_kernel,
        out_shape=jax.ShapeDtypeStruct(out_shape, BF16),
        in_specs=[VMEM] * 8,
        out_specs=HBM,
        scratch_shapes=[pltpu.VMEM(out_shape, BF16), pltpu.SemaphoreType.DMA((OUT_COPIES,))],
        compiler_params=PARAMS,
    )(inner, border, core_a, core_b, own, position, mixer, offset)


def solution(mesh):
    placed = (
        P(None, "lat", "lon"),
        P("lat", "lon"),
        P("lat", "lon", None),
        P(),
        P("lon", None, None),
        P(),
        P(),
        P(),
        P(),
    )
    return jax.shard_map(
        on_device, mesh=mesh, in_specs=placed, out_specs=P(None, "lat", "lon"), check_vma=False
    )
```

```python
import functools

import jax
import jax.numpy as jnp
from jax import lax
from jax.experimental import pallas as pl
from jax.experimental.pallas import tpu as pltpu
from jax.sharding import PartitionSpec as P

KS = 5
REACH = KS // 2
PER_OWNER = 2
LANES = 128
EDGE = 2 * REACH
GROUP = 8
STEP = 4
OUT_COPIES = 4
IN_COPIES = 4
BANK_COPIES = 8
EARLY = 1
F32 = jnp.float32
BF16 = jnp.bfloat16
VMEM = pl.BlockSpec(memory_space=pltpu.VMEM)
SMEM = pl.BlockSpec(memory_space=pltpu.SMEM)
HBM = pl.BlockSpec(memory_space=pltpu.HBM)
PARAMS = pltpu.CompilerParams(vmem_limit_bytes=24 * 1024 * 1024)


def swap_pairs(count):
    first = [(i, i ^ 1) for i in range(count)]
    second = [(i, (i + 1 if i % 2 else i - 1) % count) for i in range(count)]
    return first, second


def in_hbm(array):
    return pltpu.with_memory_space_constraint(array, pltpu.HBM)


def lane_index(shape):
    return lax.broadcasted_iota(jnp.int32, shape, 1)


def start_copies(pairs, sems):
    copies = [pltpu.make_async_copy(source, target, sems.at[i]) for i, (source, target) in enumerate(pairs)]
    for copy in copies:
        copy.start()
    return copies


def in_parts(source, target, count):
    share = target.shape[0] // count
    return tuple((source.at[pl.ds(i * share, share)], target.at[pl.ds(i * share, share)]) for i in range(count))


def find_rows(list_ref, slot_ref, lon_count, held):
    me = lax.axis_index("lon")
    owners = (me, lax.rem(me + lon_count - 1, lon_count), lax.rem(me + 1, lon_count))
    slots = [slot_ref[list_ref[0, 0, i]] for i in range(list_ref.shape[2])]
    places, rows = [], []
    for owner in owners:
        least, greatest = jnp.int32(held), jnp.int32(-1)
        first, last = jnp.int32(0), jnp.int32(0)
        for i, slot in enumerate(slots):
            local = slot - owner * held
            hit = (local >= 0) & (local < held)
            first = jnp.where(hit & (local < least), i, first)
            last = jnp.where(hit & (local > greatest), i, last)
            least = jnp.where(hit, jnp.minimum(local, least), least)
            greatest = jnp.where(hit, jnp.maximum(local, greatest), greatest)
        places.append([first, last])
        rows.append([jnp.minimum(least, held - 1), jnp.maximum(greatest, 0)])
    return places, rows


def is_early():
    return lax.axis_index("lon") == EARLY


class Held:
    names = ("bank", "own", "position", "weights", "mixer", "offset")
    sources = ("labels", "tap", "out_factor", "bias")

    def __init__(self, refs):
        self.__dict__.update(zip(self.names, refs))


def start_sources(sources, targets, bank_hbm, bank_ref, sems):
    pairs = tuple(zip(sources, targets))
    return start_copies(pairs + in_parts(bank_hbm, bank_ref, BANK_COPIES), sems)


def build_held(lon_count, list_ref, slot_ref, targets, copies, held):
    labels_ref, tap_ref, out_factor_ref, bias_ref = targets
    places, rows = find_rows(list_ref, slot_ref, lon_count, held.bank.shape[0])
    even = (lax.axis_index("lon") % 2) == 0
    order = list(places[0])
    order += [jnp.where(even, places[2][nth], places[1][nth]) for nth in range(PER_OWNER)]
    order += [jnp.where(even, places[1][nth], places[2][nth]) for nth in range(PER_OWNER)]
    labels = labels_ref[...]
    position = jnp.zeros(labels.shape, jnp.int32)
    for index, place in enumerate(order):
        position = jnp.where(labels == place, index, position)
    held.position[...] = position

    rank, out_channels = out_factor_ref.shape
    half = rank // 2
    tap_rank, taps = tap_ref.shape
    shape = (tap_rank * half, taps * half)
    spread = (
        lax.broadcasted_iota(jnp.int32, (shape[0], tap_rank), 0) // half == lane_index((shape[0], tap_rank))
    ).astype(BF16)
    repeat = (
        lax.broadcasted_iota(jnp.int32, (taps, shape[1]), 0) == lane_index((taps, shape[1])) // half
    ).astype(BF16)
    tall = jnp.dot(spread, tap_ref[...], preferred_element_type=F32).astype(BF16)
    wide = jnp.dot(tall, repeat, preferred_element_type=F32)
    same = lax.broadcasted_iota(jnp.int32, shape, 0) % half == lane_index(shape) % half
    held.weights[...] = jnp.where(same, wide, 0.0).astype(BF16)

    shape = (out_channels * GROUP, rank * GROUP)
    spread = (
        lax.broadcasted_iota(jnp.int32, (shape[0], out_channels), 0) // GROUP
        == lane_index((shape[0], out_channels))
    ).astype(BF16)
    repeat = (
        lax.broadcasted_iota(jnp.int32, (rank, shape[1]), 0) == lane_index((rank, shape[1])) % rank
    ).astype(BF16)
    tall = lax.dot_general(
        spread, out_factor_ref[...], (((1,), (1,)), ((), ())), preferred_element_type=F32
    ).astype(BF16)
    wide = jnp.dot(tall, repeat, preferred_element_type=F32)
    same = lax.broadcasted_iota(jnp.int32, shape, 0) % GROUP == lane_index(shape) // rank
    held.mixer[...] = jnp.where(same, wide, 0.0).astype(BF16)

    shape = (out_channels * GROUP, out_channels)
    mine = lax.broadcasted_iota(jnp.int32, shape, 0) // GROUP == lane_index(shape)
    offset = jnp.sum(jnp.where(mine, bias_ref[...], 0.0), axis=1, keepdims=True)
    held.offset[...] = jnp.broadcast_to(offset, held.offset.shape)
    for copy in copies:
        copy.wait()
    for nth in range(PER_OWNER):
        held.own[nth] = held.bank[rows[0][nth]]


def asked_rows(list_ref, slots_ref, owner, held):
    lane = lane_index((1, LANES))
    found = []
    for i in range(list_ref.shape[2]):
        region = list_ref[0, 0, i]
        row = slots_ref[pl.ds(region // LANES, 1), :]
        found.append(jnp.where(lane == region % LANES, row - owner * held, -1))
    local = jnp.max(jnp.concatenate(found, axis=0), axis=1, keepdims=True)
    hit = (local >= 0) & (local < held)
    least = jnp.min(jnp.where(hit, local, held - 1), axis=0, keepdims=True)
    greatest = jnp.max(jnp.where(hit, local, 0), axis=0, keepdims=True)
    return least, greatest


def edge_kernel(lon_count, *refs):
    list_hbm, slot_hbm, feat_hbm, in_hbm, bank_hbm = refs[:5]
    sources, slots_hbm, (pay_a_ref, pay_b_ref), held_refs = refs[5:9], refs[9], refs[10:12], refs[12:18]
    list_ref, slot_ref, feat_ref, in_ref, turned_ref, slots_ref = refs[18:24]
    targets, sems, held_sems = refs[24:28], refs[28], refs[29]
    held = Held(held_refs)
    channels, lat_len, lon_len = feat_ref.shape
    rank = in_ref.shape[0]
    batch = LANES // EDGE
    pairs = in_parts(feat_hbm, feat_ref, IN_COPIES)
    pairs += ((slots_hbm, slots_ref), (list_hbm, list_ref), (in_hbm, in_ref))
    copies = start_copies(pairs, sems)
    for copy in copies:
        copy.wait()
    lane = lane_index((lat_len, LANES))
    for part in range(channels // batch):
        packed = jnp.zeros((lat_len, LANES), F32)
        for c in range(batch):
            moved = pltpu.roll(feat_ref[part * batch + c].astype(F32), (EDGE * c + REACH) % LANES, 1)
            packed = jnp.where(lane // EDGE == c, moved, packed)
        turned_ref[part * LANES : (part + 1) * LANES, :] = jnp.transpose(packed)
    columns = jnp.concatenate(
        [turned_ref[pl.ds(j, channels, stride=EDGE), :].astype(BF16) for j in range(EDGE)], axis=1
    )
    edges = jnp.dot(in_ref[...], columns, preferred_element_type=F32)
    edges = jnp.concatenate([edges, jnp.zeros((rank, LANES - EDGE * lat_len), F32)], axis=1)
    me = lax.axis_index("lon")
    even = (me % 2) == 0
    prev, following = lax.rem(me + lon_count - 1, lon_count), lax.rem(me + 1, lon_count)
    lane = lane_index((rank, LANES))
    for out_ref, owner in (
        (pay_a_ref, jnp.where(even, following, prev)),
        (pay_b_ref, jnp.where(even, prev, following)),
    ):
        load = edges
        for nth, row in enumerate(asked_rows(list_ref, slots_ref, owner, held.bank.shape[0])):
            load = jnp.where(lane == EDGE * lat_len + nth, row.astype(F32), load)
        out_ref[...] = load.astype(BF16)

    @pl.when(is_early())
    def _():
        copies = start_sources(sources, targets, bank_hbm, held.bank, held_sems)
        scalars = pltpu.make_async_copy(slot_hbm, slot_ref, sems.at[0])
        scalars.start()
        for copy in [scalars, *copies[: len(targets)]]:
            copy.wait()
        build_held(lon_count, list_ref, slot_ref, targets, copies[len(targets) :], held)


def reduce_tile(lat_len, feat_ref, in_ref, rows_ref, red_ref):
    channels, lon_len = feat_ref.shape[0], feat_ref.shape[2]
    rows_ref[...] = feat_ref[...].astype(F32).reshape(channels * lat_len, lon_len)
    cells = jnp.concatenate(
        [rows_ref[pl.ds(p, channels, stride=lat_len), :].astype(BF16) for p in range(lat_len)], axis=1
    )
    red_ref[...] = jnp.dot(in_ref[...], cells, preferred_element_type=F32).astype(BF16)


def prepare_kernel(lon_count, lat_len, *refs):
    list_hbm, slot_hbm, feat_hbm, in_hbm, bank_hbm = refs[:5]
    sources, given = refs[5:9], Held((None, *refs[9:14]))
    red_ref, held = refs[14], Held(refs[15:21])
    list_ref, slot_ref, feat_ref, in_ref, rows_ref = refs[21:26]
    targets, sems, held_sems = refs[26:30], refs[30], refs[31]
    early = is_early()
    shared = in_parts(feat_hbm, feat_ref, IN_COPIES) + ((in_hbm, in_ref),)
    lists = ((slot_hbm, slot_ref), (list_hbm, list_ref))

    @pl.when(early)
    def _():
        copies = start_copies(shared, sems)
        for name in held.names[1:]:
            getattr(held, name)[...] = getattr(given, name)[...]
        for copy in copies:
            copy.wait()
        reduce_tile(lat_len, feat_ref, in_ref, rows_ref, red_ref)

    @pl.when(jnp.logical_not(early))
    def _():
        copies = start_copies(shared + lists, sems)
        others = start_sources(sources, targets, bank_hbm, held.bank, held_sems)
        for copy in copies + others[: len(targets)]:
            copy.wait()
        reduce_tile(lat_len, feat_ref, in_ref, rows_ref, red_ref)
        build_held(lon_count, list_ref, slot_ref, targets, others[len(targets) :], held)


def pick_kernel(lat_len, got_b_ref, got_a_ref, early_bank_ref, late_bank_ref, core_a_ref, core_b_ref):
    early = is_early()
    lane = lane_index((1, LANES))
    for got_ref, core_ref in ((got_b_ref, core_b_ref), (got_a_ref, core_a_ref)):
        head = got_ref[...].astype(F32)[0:1, :]
        for nth in range(PER_OWNER):
            row = jnp.sum(jnp.where(lane == EDGE * lat_len + nth, head, 0.0)).astype(jnp.int32)
            core_ref[nth] = jnp.where(early, early_bank_ref[row], late_bank_ref[row])


def rows_kernel(lat_len, got_b_ref, got_a_ref, core_ref, red_ref, edge_ref, row_a_ref, row_b_ref):
    lon_len = red_ref.shape[1] // lat_len
    even = (lax.axis_index("lon") % 2) == 0
    from_prev = lane_index(got_a_ref.shape) < REACH * lat_len
    got = jnp.where(from_prev == even, got_b_ref[...].astype(F32), got_a_ref[...].astype(F32)).astype(BF16)
    source = lax.broadcasted_iota(jnp.int32, (LANES, LANES), 0)
    target = lane_index((LANES, LANES))
    order = (source == (target % EDGE) * lat_len + target // EDGE) & (target < EDGE * lat_len)
    edges = jnp.dot(got, order.astype(BF16), preferred_element_type=F32).astype(BF16)
    edge_ref[...] = edges
    even = (lax.axis_index("lat") % 2) == 0
    head = red_ref[:, : REACH * lon_len].astype(F32)
    tail = red_ref[:, (lat_len - REACH) * lon_len :].astype(F32)
    row_a_ref[:, : REACH * lon_len] = jnp.where(even, tail, head).astype(BF16)
    row_b_ref[:, : REACH * lon_len] = jnp.where(even, head, tail).astype(BF16)
    row_a_ref[:, REACH * lon_len :] = edges
    row_b_ref[:, REACH * lon_len :] = edges


def shifted_columns(row, edges, place):
    lane = lane_index(row.shape)
    lon_len = row.shape[1]
    edges = pltpu.roll(edges, (LANES - REACH - EDGE * place) % LANES, 1)
    moved = []
    for col_off in range(KS):
        shift = REACH - col_off
        if shift > 0:
            piece = pltpu.roll(jnp.where(lane >= lon_len - shift, edges, row), shift, 1)
        elif shift < 0:
            piece = pltpu.roll(jnp.where(lane < -shift, edges, row), lon_len + shift, 1)
        else:
            piece = row
        moved.append(piece.astype(BF16))
    return moved


def stack_row(stack_ref, p, moved, slots, lon_len):
    half = moved[0].shape[0] // 2
    for col_off, piece in enumerate(moved):
        for row_off in range(KS):
            slot = slots.get(p + REACH - row_off)
            if slot is not None:
                k = row_off * KS + col_off
                for h in range(2):
                    stack_ref[h, k * half : (k + 1) * half, slot * lon_len : (slot + 1) * lon_len] = piece[
                        h * half : (h + 1) * half
                    ]


def apply_taps(rank, weights_ref, stacked, tapped_ref, lon_len):
    half = rank // 2
    tap_rank = tapped_ref.shape[0] // rank
    width = STEP * lon_len
    for start in range(0, tapped_ref.shape[1], width):
        parts = [
            jnp.dot(weights_ref[...], stacked(h, start, width), preferred_element_type=F32)
            .astype(BF16)
            .reshape(tap_rank, 1, half, width)
            for h in range(2)
        ]
        tapped_ref[:, start : start + width] = jnp.concatenate(parts, axis=1).reshape(tap_rank * rank, width)


def border_slots(lat_len):
    slots = {p: p for p in range(REACH)}
    slots.update({lat_len - REACH + p: REACH + p for p in range(REACH)})
    return slots


def inner_kernel(lat_len, red_ref, edge_ref, weights_ref, tapped_ref, halo_stack_ref, stack_ref):
    rank = red_ref.shape[0]
    lon_len = red_ref.shape[1] // lat_len
    slots = {p: p - REACH for p in range(REACH, lat_len - REACH)}
    edges = edge_ref[...].astype(F32)
    for p in range(lat_len):
        row = red_ref[:, p * lon_len : (p + 1) * lon_len].astype(F32)
        moved = shifted_columns(row, edges, p)
        stack_row(stack_ref, p, moved, slots, lon_len)
        stack_row(halo_stack_ref, p, moved, border_slots(lat_len), lon_len)
    apply_taps(rank, weights_ref, lambda h, start, width: stack_ref[h, :, start : start + width], tapped_ref, lon_len)


def border_kernel(lat_len, lat_count, row_b_ref, row_a_ref, weights_ref, own_stack_ref, tapped_ref, stack_ref):
    rank = row_a_ref.shape[0]
    lon_len = (row_a_ref.shape[1] - LANES) // REACH
    lat = lax.axis_index("lat")
    even = (lat % 2) == 0
    row_a = row_a_ref[...].astype(F32)
    row_b = row_b_ref[...].astype(F32)
    above = jnp.where(lat == 0, 0.0, jnp.where(even, row_b, row_a))
    below = jnp.where(lat == lat_count - 1, 0.0, jnp.where(even, row_a, row_b))
    slots = border_slots(lat_len)
    for i in range(REACH):
        for p, holder, place in ((i - REACH, above, lat_len - REACH + i), (lat_len + i, below, i)):
            row = holder[:, i * lon_len : (i + 1) * lon_len]
            moved = shifted_columns(row, holder[:, REACH * lon_len :], place)
            stack_row(stack_ref, p, moved, slots, lon_len)
    block = KS * rank // 2
    in_halo = {
        (slot, row_off)
        for p, slot in slots.items()
        for row_off in range(KS)
        if not 0 <= p + row_off - REACH < lat_len
    }

    def stacked(h, start, width):
        columns = []
        for slot in range(start // lon_len, (start + width) // lon_len):
            span = slice(slot * lon_len, (slot + 1) * lon_len)
            pieces = []
            for row_off in range(KS):
                ref = stack_ref if (slot, row_off) in in_halo else own_stack_ref
                pieces.append(ref[h, row_off * block : (row_off + 1) * block, span])
            columns.append(jnp.concatenate(pieces, axis=0))
        return jnp.concatenate(columns, axis=1)

    apply_taps(rank, weights_ref, stacked, tapped_ref, lon_len)


def mix_kernel(
    inner_ref,
    border_ref,
    core_a_ref,
    core_b_ref,
    own_ref,
    position_ref,
    mixer_ref,
    offset_ref,
    out_hbm,
    stage_ref,
    sems,
):
    lat_len, lon_len = position_ref.shape
    rank = own_ref.shape[1]
    cores = jnp.concatenate(
        [ref[...].reshape(PER_OWNER * rank, -1) for ref in (own_ref, core_a_ref, core_b_ref)], axis=0
    )
    chunks = [(border_ref, 0, [*range(REACH), *range(lat_len - REACH, lat_len)])]
    for start in range(REACH, lat_len - REACH, STEP):
        chunks.append((inner_ref, start - REACH, [*range(start, start + STEP)]))
    by_row = {}
    for ref, first, rows in chunks:
        width = len(rows) * lon_len
        every = jnp.dot(cores, ref[:, first * lon_len : first * lon_len + width], preferred_element_type=F32)
        position = jnp.concatenate([position_ref[r : r + 1, :] for r in rows], axis=1)
        hidden = jnp.zeros((rank, width), F32)
        for index in range(3 * PER_OWNER):
            hidden = jnp.where(position == index, every[index * rank : (index + 1) * rank], hidden)
        hidden = hidden.astype(BF16)
        for i, r in enumerate(rows):
            by_row[r] = hidden[:, i * lon_len : (i + 1) * lon_len]
    pieces = [by_row[r] for r in range(lat_len)]
    groups = [jnp.concatenate(pieces[g : g + GROUP], axis=0) for g in range(0, lat_len, GROUP)]
    channels = stage_ref.shape[0]
    share = channels // OUT_COPIES
    outputs = [jnp.dot(mixer_ref[...], hidden, preferred_element_type=F32) for hidden in groups]
    copies = []
    for part in range(OUT_COPIES):
        span = slice(part * share * GROUP, (part + 1) * share * GROUP)
        blocks = []
        for output in outputs:
            output = output[span] + offset_ref[span, :]
            mixed = 0.5 * output * (1.0 + jnp.tanh(0.5 * output))
            blocks.append(mixed.reshape(share, GROUP, lon_len))
        held = slice(part * share, (part + 1) * share)
        stage_ref[held] = jnp.concatenate(blocks, axis=1).astype(BF16)
        copy = pltpu.make_async_copy(stage_ref.at[held], out_hbm.at[held], sems.at[part])
        copy.start()
        copies.append(copy)
    for copy in copies:
        copy.wait()


def on_device(
    features, labels, tile_regions, bank_slot, kernel_bank, in_factor, tap_factor, out_factor, out_bias
):
    channels, lat_len, lon_len = features.shape
    rank = in_factor.shape[0]
    held, core_rows, core_cols = kernel_bank.shape
    tap_rank, taps = tap_factor.shape
    out_channels = out_factor.shape[0]
    cells = lat_len * lon_len
    lon_count, lat_count = lax.axis_size("lon"), lax.axis_size("lat")
    lon_first, lon_second = swap_pairs(lon_count)
    lat_first, lat_second = swap_pairs(lat_count)
    edge_shape = jax.ShapeDtypeStruct((rank, LANES), BF16)
    core_shape = jax.ShapeDtypeStruct((PER_OWNER, core_rows, core_cols), BF16)
    held_shapes = (
        jax.ShapeDtypeStruct(kernel_bank.shape, BF16),
        core_shape,
        jax.ShapeDtypeStruct(labels.shape, jnp.int32),
        jax.ShapeDtypeStruct((tap_rank * rank // 2, taps * rank // 2), BF16),
        jax.ShapeDtypeStruct((out_channels * GROUP, rank * GROUP), BF16),
        jax.ShapeDtypeStruct((out_channels * GROUP, lon_len), F32),
    )
    lists = [
        pltpu.SMEM(tile_regions.shape, jnp.int32),
        pltpu.SMEM(bank_slot.shape, jnp.int32),
        pltpu.VMEM(features.shape, BF16),
        pltpu.VMEM(in_factor.shape, BF16),
    ]
    targets = [
        pltpu.VMEM(labels.shape, jnp.int32),
        pltpu.VMEM(tap_factor.shape, BF16),
        pltpu.VMEM(out_factor.shape[::-1], BF16),
        pltpu.VMEM((1, out_channels), F32),
    ]
    sources = tuple(
        in_hbm(x)
        for x in (
            tile_regions,
            bank_slot,
            features,
            in_factor,
            kernel_bank,
            labels,
            tap_factor,
            out_factor.T,
            out_bias.reshape(1, -1),
        )
    )
    pay_a, pay_b, early_bank, *given = pl.pallas_call(
        functools.partial(edge_kernel, lon_count),
        out_shape=(edge_shape, edge_shape, *held_shapes),
        in_specs=[HBM] * 10,
        out_specs=(VMEM,) * 8,
        scratch_shapes=[
            *lists,
            pltpu.VMEM((channels * EDGE, lat_len), F32),
            pltpu.VMEM((bank_slot.shape[0] // LANES, LANES), jnp.int32),
            *targets,
            pltpu.SemaphoreType.DMA((IN_COPIES + 3,)),
            pltpu.SemaphoreType.DMA((4 + BANK_COPIES,)),
        ],
        compiler_params=PARAMS,
    )(*sources, in_hbm(bank_slot.reshape(-1, LANES)))
    got_b = lax.ppermute(pay_b, "lon", lon_second)
    got_a = lax.ppermute(pay_a, "lon", lon_first)
    reduced, late_bank, own, position, weights, mixer, offset = pl.pallas_call(
        functools.partial(prepare_kernel, lon_count, lat_len),
        out_shape=(jax.ShapeDtypeStruct((rank, cells), BF16), *held_shapes),
        in_specs=[HBM] * 9 + [VMEM] * 5,
        out_specs=(VMEM,) * 7,
        scratch_shapes=[
            *lists,
            pltpu.VMEM((channels * lat_len, lon_len), F32),
            *targets,
            pltpu.SemaphoreType.DMA((IN_COPIES + 3,)),
            pltpu.SemaphoreType.DMA((4 + BANK_COPIES,)),
        ],
        compiler_params=PARAMS,
        cost_estimate=pl.CostEstimate(flops=10**6, bytes_accessed=kernel_bank.size * 4, transcendentals=0),
    )(*sources, *given)
    row_shape = jax.ShapeDtypeStruct((rank, REACH * lon_len + LANES), BF16)
    core_a, core_b = pl.pallas_call(
        functools.partial(pick_kernel, lat_len),
        out_shape=(core_shape, core_shape),
        in_specs=[VMEM] * 4,
        out_specs=(VMEM,) * 2,
        compiler_params=PARAMS,
    )(got_b, got_a, early_bank, late_bank)
    edges, row_a, row_b = pl.pallas_call(
        functools.partial(rows_kernel, lat_len),
        out_shape=(edge_shape, row_shape, row_shape),
        in_specs=[VMEM, VMEM, HBM, VMEM],
        out_specs=(VMEM,) * 3,
        compiler_params=PARAMS,
    )(got_b, got_a, core_b, reduced)
    core_b = lax.ppermute(core_b, "lon", lon_second)
    core_a = lax.ppermute(core_a, "lon", lon_first)
    row_a = lax.ppermute(row_a, "lat", lat_first)
    row_b = lax.ppermute(row_b, "lat", lat_second)
    border_cells = 2 * REACH * lon_len
    stack_rows = taps * rank // 2
    halo_stack_shape = jax.ShapeDtypeStruct((2, stack_rows, border_cells), BF16)
    inner, halo_stack = pl.pallas_call(
        functools.partial(inner_kernel, lat_len),
        out_shape=(jax.ShapeDtypeStruct((tap_rank * rank, cells - border_cells), BF16), halo_stack_shape),
        in_specs=[VMEM] * 3,
        out_specs=(VMEM,) * 2,
        scratch_shapes=[pltpu.VMEM((2, stack_rows, cells - border_cells), BF16)],
        compiler_params=PARAMS,
    )(reduced, edges, weights)
    border = pl.pallas_call(
        functools.partial(border_kernel, lat_len, lat_count),
        out_shape=jax.ShapeDtypeStruct((tap_rank * rank, border_cells), BF16),
        in_specs=[VMEM] * 4,
        out_specs=VMEM,
        scratch_shapes=[pltpu.VMEM(halo_stack_shape.shape, BF16)],
        compiler_params=PARAMS,
    )(row_b, row_a, weights, halo_stack)
    out_shape = (out_channels, lat_len, lon_len)
    return pl.pallas_call(
        mix_kernel,
        out_shape=jax.ShapeDtypeStruct(out_shape, BF16),
        in_specs=[VMEM] * 8,
        out_specs=HBM,
        scratch_shapes=[pltpu.VMEM(out_shape, BF16), pltpu.SemaphoreType.DMA((OUT_COPIES,))],
        compiler_params=PARAMS,
    )(inner, border, core_a, core_b, own, position, mixer, offset)


def solution(mesh):
    placed = (
        P(None, "lat", "lon"),
        P("lat", "lon"),
        P("lat", "lon", None),
        P(),
        P("lon", None, None),
        P(),
        P(),
        P(),
        P(),
    )
    return jax.shard_map(
        on_device, mesh=mesh, in_specs=placed, out_specs=P(None, "lat", "lon"), check_vma=False
    )
```

```python
import functools

import jax
import jax.numpy as jnp
from jax import lax
from jax.experimental import pallas as pl
from jax.experimental.pallas import tpu as pltpu
from jax.sharding import PartitionSpec as P

KS = 5
REACH = KS // 2
PER_OWNER = 2
LANES = 128
EDGE = 2 * REACH
GROUP = 8
STEP = 4
OUT_COPIES = 4
IN_COPIES = 4
BANK_COPIES = 8
EARLY = 1
F32 = jnp.float32
BF16 = jnp.bfloat16
VMEM = pl.BlockSpec(memory_space=pltpu.VMEM)
SMEM = pl.BlockSpec(memory_space=pltpu.SMEM)
HBM = pl.BlockSpec(memory_space=pltpu.HBM)
PARAMS = pltpu.CompilerParams(vmem_limit_bytes=24 * 1024 * 1024)


def swap_pairs(count):
    first = [(i, i ^ 1) for i in range(count)]
    second = [(i, (i + 1 if i % 2 else i - 1) % count) for i in range(count)]
    return first, second


def in_hbm(array):
    return pltpu.with_memory_space_constraint(array, pltpu.HBM)


def lane_index(shape):
    return lax.broadcasted_iota(jnp.int32, shape, 1)


def start_copies(pairs, sems):
    copies = [pltpu.make_async_copy(source, target, sems.at[i]) for i, (source, target) in enumerate(pairs)]
    for copy in copies:
        copy.start()
    return copies


def in_parts(source, target, count):
    share = target.shape[0] // count
    return tuple((source.at[pl.ds(i * share, share)], target.at[pl.ds(i * share, share)]) for i in range(count))


def find_rows(list_ref, slot_ref, lon_count, held):
    me = lax.axis_index("lon")
    owners = (me, lax.rem(me + lon_count - 1, lon_count), lax.rem(me + 1, lon_count))
    slots = [slot_ref[list_ref[0, 0, i]] for i in range(list_ref.shape[2])]
    places, rows = [], []
    for owner in owners:
        least, greatest = jnp.int32(held), jnp.int32(-1)
        first, last = jnp.int32(0), jnp.int32(0)
        for i, slot in enumerate(slots):
            local = slot - owner * held
            hit = (local >= 0) & (local < held)
            first = jnp.where(hit & (local < least), i, first)
            last = jnp.where(hit & (local > greatest), i, last)
            least = jnp.where(hit, jnp.minimum(local, least), least)
            greatest = jnp.where(hit, jnp.maximum(local, greatest), greatest)
        places.append([first, last])
        rows.append([jnp.minimum(least, held - 1), jnp.maximum(greatest, 0)])
    return places, rows


def is_early():
    return lax.axis_index("lon") == EARLY


class Held:
    names = ("bank", "own", "position", "weights", "mixer", "offset")
    sources = ("labels", "tap", "out_factor", "bias")

    def __init__(self, refs):
        self.__dict__.update(zip(self.names, refs))


def start_sources(sources, targets, bank_hbm, bank_ref, sems):
    pairs = tuple(zip(sources, targets))
    return start_copies(pairs + in_parts(bank_hbm, bank_ref, BANK_COPIES), sems)


def build_held(lon_count, list_ref, slot_ref, targets, copies, held):
    labels_ref, tap_ref, out_factor_ref, bias_ref = targets
    places, rows = find_rows(list_ref, slot_ref, lon_count, held.bank.shape[0])
    even = (lax.axis_index("lon") % 2) == 0
    order = list(places[0])
    order += [jnp.where(even, places[2][nth], places[1][nth]) for nth in range(PER_OWNER)]
    order += [jnp.where(even, places[1][nth], places[2][nth]) for nth in range(PER_OWNER)]
    labels = labels_ref[...]
    position = jnp.zeros(labels.shape, jnp.int32)
    for index, place in enumerate(order):
        position = jnp.where(labels == place, index, position)
    held.position[...] = position

    rank, out_channels = out_factor_ref.shape
    half = rank // 2
    tap_rank, taps = tap_ref.shape
    shape = (tap_rank * half, taps * half)
    spread = (
        lax.broadcasted_iota(jnp.int32, (shape[0], tap_rank), 0) // half == lane_index((shape[0], tap_rank))
    ).astype(BF16)
    repeat = (
        lax.broadcasted_iota(jnp.int32, (taps, shape[1]), 0) == lane_index((taps, shape[1])) // half
    ).astype(BF16)
    tall = jnp.dot(spread, tap_ref[...], preferred_element_type=F32).astype(BF16)
    wide = jnp.dot(tall, repeat, preferred_element_type=F32)
    same = lax.broadcasted_iota(jnp.int32, shape, 0) % half == lane_index(shape) % half
    held.weights[...] = jnp.where(same, wide, 0.0).astype(BF16)

    shape = (out_channels * GROUP, rank * GROUP)
    spread = (
        lax.broadcasted_iota(jnp.int32, (shape[0], out_channels), 0) // GROUP
        == lane_index((shape[0], out_channels))
    ).astype(BF16)
    repeat = (
        lax.broadcasted_iota(jnp.int32, (rank, shape[1]), 0) == lane_index((rank, shape[1])) % rank
    ).astype(BF16)
    tall = lax.dot_general(
        spread, out_factor_ref[...], (((1,), (1,)), ((), ())), preferred_element_type=F32
    ).astype(BF16)
    wide = jnp.dot(tall, repeat, preferred_element_type=F32)
    same = lax.broadcasted_iota(jnp.int32, shape, 0) % GROUP == lane_index(shape) // rank
    held.mixer[...] = jnp.where(same, wide, 0.0).astype(BF16)

    shape = (out_channels * GROUP, out_channels)
    mine = lax.broadcasted_iota(jnp.int32, shape, 0) // GROUP == lane_index(shape)
    offset = jnp.sum(jnp.where(mine, bias_ref[...], 0.0), axis=1, keepdims=True)
    held.offset[...] = jnp.broadcast_to(offset, held.offset.shape)
    for copy in copies:
        copy.wait()
    for nth in range(PER_OWNER):
        held.own[nth] = held.bank[rows[0][nth]]


def asked_rows(list_ref, slots_ref, owner, held):
    lane = lane_index((1, LANES))
    found = []
    for i in range(list_ref.shape[2]):
        region = list_ref[0, 0, i]
        row = slots_ref[pl.ds(region // LANES, 1), :]
        found.append(jnp.where(lane == region % LANES, row - owner * held, -1))
    local = jnp.max(jnp.concatenate(found, axis=0), axis=1, keepdims=True)
    hit = (local >= 0) & (local < held)
    least = jnp.min(jnp.where(hit, local, held - 1), axis=0, keepdims=True)
    greatest = jnp.max(jnp.where(hit, local, 0), axis=0, keepdims=True)
    return least, greatest


def edge_kernel(lon_count, *refs):
    list_hbm, slot_hbm, feat_hbm, in_hbm, bank_hbm = refs[:5]
    sources, slots_hbm, (pay_a_ref, pay_b_ref), held_refs = refs[5:9], refs[9], refs[10:12], refs[12:18]
    list_ref, slot_ref, feat_ref, in_ref, turned_ref, slots_ref = refs[18:24]
    targets, sems, held_sems = refs[24:28], refs[28], refs[29]
    held = Held(held_refs)
    channels, lat_len, lon_len = feat_ref.shape
    rank = in_ref.shape[0]
    batch = LANES // EDGE
    pairs = in_parts(feat_hbm, feat_ref, IN_COPIES)
    pairs += ((slots_hbm, slots_ref), (list_hbm, list_ref), (in_hbm, in_ref))
    copies = start_copies(pairs, sems)
    for copy in copies:
        copy.wait()
    lane = lane_index((lat_len, LANES))
    for part in range(channels // batch):
        packed = jnp.zeros((lat_len, LANES), F32)
        for c in range(batch):
            moved = pltpu.roll(feat_ref[part * batch + c].astype(F32), (EDGE * c + REACH) % LANES, 1)
            packed = jnp.where(lane // EDGE == c, moved, packed)
        turned_ref[part * LANES : (part + 1) * LANES, :] = jnp.transpose(packed)
    columns = jnp.concatenate(
        [turned_ref[pl.ds(j, channels, stride=EDGE), :].astype(BF16) for j in range(EDGE)], axis=1
    )
    edges = jnp.dot(in_ref[...], columns, preferred_element_type=F32)
    edges = jnp.concatenate([edges, jnp.zeros((rank, LANES - EDGE * lat_len), F32)], axis=1)
    me = lax.axis_index("lon")
    even = (me % 2) == 0
    prev, following = lax.rem(me + lon_count - 1, lon_count), lax.rem(me + 1, lon_count)
    lane = lane_index((rank, LANES))
    for out_ref, owner in (
        (pay_a_ref, jnp.where(even, following, prev)),
        (pay_b_ref, jnp.where(even, prev, following)),
    ):
        load = edges
        for nth, row in enumerate(asked_rows(list_ref, slots_ref, owner, held.bank.shape[0])):
            load = jnp.where(lane == EDGE * lat_len + nth, row.astype(F32), load)
        out_ref[...] = load.astype(BF16)

    @pl.when(is_early())
    def _():
        copies = start_sources(sources, targets, bank_hbm, held.bank, held_sems)
        scalars = pltpu.make_async_copy(slot_hbm, slot_ref, sems.at[0])
        scalars.start()
        for copy in [scalars, *copies[: len(targets)]]:
            copy.wait()
        build_held(lon_count, list_ref, slot_ref, targets, copies[len(targets) :], held)


def reduce_tile(lat_len, feat_ref, in_ref, rows_ref, red_ref):
    channels, lon_len = feat_ref.shape[0], feat_ref.shape[2]
    rows_ref[...] = feat_ref[...].astype(F32).reshape(channels * lat_len, lon_len)
    cells = jnp.concatenate(
        [rows_ref[pl.ds(p, channels, stride=lat_len), :].astype(BF16) for p in range(lat_len)], axis=1
    )
    red_ref[...] = jnp.dot(in_ref[...], cells, preferred_element_type=F32).astype(BF16)


def prepare_kernel(lon_count, lat_len, *refs):
    list_hbm, slot_hbm, feat_hbm, in_hbm, bank_hbm = refs[:5]
    sources, given = refs[5:9], Held((None, *refs[9:14]))
    red_ref, held = refs[14], Held(refs[15:21])
    list_ref, slot_ref, feat_ref, in_ref, rows_ref = refs[21:26]
    targets, sems, held_sems = refs[26:30], refs[30], refs[31]
    early = is_early()
    shared = in_parts(feat_hbm, feat_ref, IN_COPIES) + ((in_hbm, in_ref),)
    lists = ((slot_hbm, slot_ref), (list_hbm, list_ref))

    @pl.when(early)
    def _():
        copies = start_copies(shared, sems)
        for name in held.names[1:]:
            getattr(held, name)[...] = getattr(given, name)[...]
        for copy in copies:
            copy.wait()
        reduce_tile(lat_len, feat_ref, in_ref, rows_ref, red_ref)

    @pl.when(jnp.logical_not(early))
    def _():
        copies = start_copies(shared + lists, sems)
        others = start_sources(sources, targets, bank_hbm, held.bank, held_sems)
        for copy in copies + others[: len(targets)]:
            copy.wait()
        reduce_tile(lat_len, feat_ref, in_ref, rows_ref, red_ref)
        build_held(lon_count, list_ref, slot_ref, targets, others[len(targets) :], held)


def pick_kernel(lat_len, got_b_ref, got_a_ref, early_bank_ref, late_bank_ref, core_a_ref, core_b_ref):
    early = is_early()
    lane = lane_index((1, LANES))
    for got_ref, core_ref in ((got_b_ref, core_b_ref), (got_a_ref, core_a_ref)):
        head = got_ref[...].astype(F32)[0:1, :]
        for nth in range(PER_OWNER):
            row = jnp.sum(jnp.where(lane == EDGE * lat_len + nth, head, 0.0)).astype(jnp.int32)
            core_ref[nth] = jnp.where(early, early_bank_ref[row], late_bank_ref[row])


def rows_kernel(lat_len, got_b_ref, got_a_ref, core_ref, red_ref, edge_ref, row_a_ref, row_b_ref):
    lon_len = red_ref.shape[1] // lat_len
    even = (lax.axis_index("lon") % 2) == 0
    from_prev = lane_index(got_a_ref.shape) < REACH * lat_len
    got = jnp.where(from_prev == even, got_b_ref[...].astype(F32), got_a_ref[...].astype(F32)).astype(BF16)
    source = lax.broadcasted_iota(jnp.int32, (LANES, LANES), 0)
    target = lane_index((LANES, LANES))
    order = (source == (target % EDGE) * lat_len + target // EDGE) & (target < EDGE * lat_len)
    edges = jnp.dot(got, order.astype(BF16), preferred_element_type=F32).astype(BF16)
    edge_ref[...] = edges
    even = (lax.axis_index("lat") % 2) == 0
    head = red_ref[:, : REACH * lon_len].astype(F32)
    tail = red_ref[:, (lat_len - REACH) * lon_len :].astype(F32)
    row_a_ref[:, : REACH * lon_len] = jnp.where(even, tail, head).astype(BF16)
    row_b_ref[:, : REACH * lon_len] = jnp.where(even, head, tail).astype(BF16)
    row_a_ref[:, REACH * lon_len :] = edges
    row_b_ref[:, REACH * lon_len :] = edges


def shifted_columns(row, edges, place):
    lane = lane_index(row.shape)
    lon_len = row.shape[1]
    edges = pltpu.roll(edges, (LANES - REACH - EDGE * place) % LANES, 1)
    moved = []
    for col_off in range(KS):
        shift = REACH - col_off
        if shift > 0:
            piece = pltpu.roll(jnp.where(lane >= lon_len - shift, edges, row), shift, 1)
        elif shift < 0:
            piece = pltpu.roll(jnp.where(lane < -shift, edges, row), lon_len + shift, 1)
        else:
            piece = row
        moved.append(piece.astype(BF16))
    return moved


def stack_row(stack_ref, p, moved, slots, lon_len):
    half = moved[0].shape[0] // 2
    for col_off, piece in enumerate(moved):
        for row_off in range(KS):
            slot = slots.get(p + REACH - row_off)
            if slot is not None:
                k = row_off * KS + col_off
                for h in range(2):
                    stack_ref[h, k * half : (k + 1) * half, slot * lon_len : (slot + 1) * lon_len] = piece[
                        h * half : (h + 1) * half
                    ]


def apply_taps(rank, weights_ref, stacked, tapped_ref, lon_len):
    half = rank // 2
    tap_rank = tapped_ref.shape[0] // rank
    width = STEP * lon_len
    for start in range(0, tapped_ref.shape[1], width):
        parts = [
            jnp.dot(weights_ref[...], stacked(h, start, width), preferred_element_type=F32)
            .astype(BF16)
            .reshape(tap_rank, 1, half, width)
            for h in range(2)
        ]
        tapped_ref[:, start : start + width] = jnp.concatenate(parts, axis=1).reshape(tap_rank * rank, width)


def border_slots(lat_len):
    slots = {p: p for p in range(REACH)}
    slots.update({lat_len - REACH + p: REACH + p for p in range(REACH)})
    return slots


def inner_kernel(lat_len, red_ref, edge_ref, weights_ref, tapped_ref, halo_stack_ref, stack_ref):
    rank = red_ref.shape[0]
    lon_len = red_ref.shape[1] // lat_len
    slots = {p: p - REACH for p in range(REACH, lat_len - REACH)}
    edges = edge_ref[...].astype(F32)
    for p in range(lat_len):
        row = red_ref[:, p * lon_len : (p + 1) * lon_len].astype(F32)
        moved = shifted_columns(row, edges, p)
        stack_row(stack_ref, p, moved, slots, lon_len)
        stack_row(halo_stack_ref, p, moved, border_slots(lat_len), lon_len)
    apply_taps(rank, weights_ref, lambda h, start, width: stack_ref[h, :, start : start + width], tapped_ref, lon_len)


def border_kernel(lat_len, lat_count, row_b_ref, row_a_ref, weights_ref, own_stack_ref, tapped_ref, stack_ref):
    rank = row_a_ref.shape[0]
    lon_len = (row_a_ref.shape[1] - LANES) // REACH
    lat = lax.axis_index("lat")
    even = (lat % 2) == 0
    row_a = row_a_ref[...].astype(F32)
    row_b = row_b_ref[...].astype(F32)
    above = jnp.where(lat == 0, 0.0, jnp.where(even, row_b, row_a))
    below = jnp.where(lat == lat_count - 1, 0.0, jnp.where(even, row_a, row_b))
    slots = border_slots(lat_len)
    for i in range(REACH):
        for p, holder, place in ((i - REACH, above, lat_len - REACH + i), (lat_len + i, below, i)):
            row = holder[:, i * lon_len : (i + 1) * lon_len]
            moved = shifted_columns(row, holder[:, REACH * lon_len :], place)
            stack_row(stack_ref, p, moved, slots, lon_len)
    block = KS * rank // 2
    in_halo = {
        (slot, row_off)
        for p, slot in slots.items()
        for row_off in range(KS)
        if not 0 <= p + row_off - REACH < lat_len
    }

    def stacked(h, start, width):
        columns = []
        for slot in range(start // lon_len, (start + width) // lon_len):
            span = slice(slot * lon_len, (slot + 1) * lon_len)
            pieces = []
            for row_off in range(KS):
                ref = stack_ref if (slot, row_off) in in_halo else own_stack_ref
                pieces.append(ref[h, row_off * block : (row_off + 1) * block, span])
            columns.append(jnp.concatenate(pieces, axis=0))
        return jnp.concatenate(columns, axis=1)

    apply_taps(rank, weights_ref, stacked, tapped_ref, lon_len)


def mix_kernel(
    inner_ref,
    border_ref,
    core_a_ref,
    core_b_ref,
    own_ref,
    position_ref,
    mixer_ref,
    offset_ref,
    out_hbm,
    stage_ref,
    sems,
):
    lat_len, lon_len = position_ref.shape
    rank = own_ref.shape[1]
    cores = jnp.concatenate(
        [ref[...].reshape(PER_OWNER * rank, -1) for ref in (own_ref, core_a_ref, core_b_ref)], axis=0
    )
    chunks = [(border_ref, 0, [*range(REACH), *range(lat_len - REACH, lat_len)])]
    for start in range(REACH, lat_len - REACH, STEP):
        chunks.append((inner_ref, start - REACH, [*range(start, start + STEP)]))
    by_row = {}
    finished = []
    for ref, first, rows in chunks:
        width = len(rows) * lon_len
        every = jnp.dot(cores, ref[:, first * lon_len : first * lon_len + width], preferred_element_type=F32)
        position = jnp.concatenate([position_ref[r : r + 1, :] for r in rows], axis=1)
        hidden = jnp.zeros((rank, width), F32)
        for index in range(3 * PER_OWNER):
            hidden = jnp.where(position == index, every[index * rank : (index + 1) * rank], hidden)
        hidden = hidden.astype(BF16)
        for i, r in enumerate(rows):
            by_row[r] = hidden[:, i * lon_len : (i + 1) * lon_len]
        group = range(len(finished) * GROUP, (len(finished) + 1) * GROUP)
        if len(finished) * GROUP < lat_len and all(r in by_row for r in group):
            stacked = jnp.concatenate([by_row[r] for r in group], axis=0)
            output = jnp.dot(mixer_ref[...], stacked, preferred_element_type=F32) + offset_ref[...]
            finished.append(output / (1.0 + jnp.exp(-output)))
    channels = stage_ref.shape[0]
    share = channels // OUT_COPIES
    copies = []
    for part in range(OUT_COPIES):
        span = slice(part * share * GROUP, (part + 1) * share * GROUP)
        blocks = [mixed[span].reshape(share, GROUP, lon_len) for mixed in finished]
        held = slice(part * share, (part + 1) * share)
        stage_ref[held] = jnp.concatenate(blocks, axis=1).astype(BF16)
        copy = pltpu.make_async_copy(stage_ref.at[held], out_hbm.at[held], sems.at[part])
        copy.start()
        copies.append(copy)
    for copy in copies:
        copy.wait()


def on_device(
    features, labels, tile_regions, bank_slot, kernel_bank, in_factor, tap_factor, out_factor, out_bias
):
    channels, lat_len, lon_len = features.shape
    rank = in_factor.shape[0]
    held, core_rows, core_cols = kernel_bank.shape
    tap_rank, taps = tap_factor.shape
    out_channels = out_factor.shape[0]
    cells = lat_len * lon_len
    lon_count, lat_count = lax.axis_size("lon"), lax.axis_size("lat")
    lon_first, lon_second = swap_pairs(lon_count)
    lat_first, lat_second = swap_pairs(lat_count)
    edge_shape = jax.ShapeDtypeStruct((rank, LANES), BF16)
    core_shape = jax.ShapeDtypeStruct((PER_OWNER, core_rows, core_cols), BF16)
    held_shapes = (
        jax.ShapeDtypeStruct(kernel_bank.shape, BF16),
        core_shape,
        jax.ShapeDtypeStruct(labels.shape, jnp.int32),
        jax.ShapeDtypeStruct((tap_rank * rank // 2, taps * rank // 2), BF16),
        jax.ShapeDtypeStruct((out_channels * GROUP, rank * GROUP), BF16),
        jax.ShapeDtypeStruct((out_channels * GROUP, lon_len), F32),
    )
    lists = [
        pltpu.SMEM(tile_regions.shape, jnp.int32),
        pltpu.SMEM(bank_slot.shape, jnp.int32),
        pltpu.VMEM(features.shape, BF16),
        pltpu.VMEM(in_factor.shape, BF16),
    ]
    targets = [
        pltpu.VMEM(labels.shape, jnp.int32),
        pltpu.VMEM(tap_factor.shape, BF16),
        pltpu.VMEM(out_factor.shape[::-1], BF16),
        pltpu.VMEM((1, out_channels), F32),
    ]
    sources = tuple(
        in_hbm(x)
        for x in (
            tile_regions,
            bank_slot,
            features,
            in_factor,
            kernel_bank,
            labels,
            tap_factor,
            out_factor.T,
            out_bias.reshape(1, -1),
        )
    )
    pay_a, pay_b, early_bank, *given = pl.pallas_call(
        functools.partial(edge_kernel, lon_count),
        out_shape=(edge_shape, edge_shape, *held_shapes),
        in_specs=[HBM] * 10,
        out_specs=(VMEM,) * 8,
        scratch_shapes=[
            *lists,
            pltpu.VMEM((channels * EDGE, lat_len), F32),
            pltpu.VMEM((bank_slot.shape[0] // LANES, LANES), jnp.int32),
            *targets,
            pltpu.SemaphoreType.DMA((IN_COPIES + 3,)),
            pltpu.SemaphoreType.DMA((4 + BANK_COPIES,)),
        ],
        compiler_params=PARAMS,
    )(*sources, in_hbm(bank_slot.reshape(-1, LANES)))
    got_b = lax.ppermute(pay_b, "lon", lon_second)
    got_a = lax.ppermute(pay_a, "lon", lon_first)
    reduced, late_bank, own, position, weights, mixer, offset = pl.pallas_call(
        functools.partial(prepare_kernel, lon_count, lat_len),
        out_shape=(jax.ShapeDtypeStruct((rank, cells), BF16), *held_shapes),
        in_specs=[HBM] * 9 + [VMEM] * 5,
        out_specs=(VMEM,) * 7,
        scratch_shapes=[
            *lists,
            pltpu.VMEM((channels * lat_len, lon_len), F32),
            *targets,
            pltpu.SemaphoreType.DMA((IN_COPIES + 3,)),
            pltpu.SemaphoreType.DMA((4 + BANK_COPIES,)),
        ],
        compiler_params=PARAMS,
        cost_estimate=pl.CostEstimate(flops=10**6, bytes_accessed=kernel_bank.size * 4, transcendentals=0),
    )(*sources, *given)
    row_shape = jax.ShapeDtypeStruct((rank, REACH * lon_len + LANES), BF16)
    core_a, core_b = pl.pallas_call(
        functools.partial(pick_kernel, lat_len),
        out_shape=(core_shape, core_shape),
        in_specs=[VMEM] * 4,
        out_specs=(VMEM,) * 2,
        compiler_params=PARAMS,
    )(got_b, got_a, early_bank, late_bank)
    edges, row_a, row_b = pl.pallas_call(
        functools.partial(rows_kernel, lat_len),
        out_shape=(edge_shape, row_shape, row_shape),
        in_specs=[VMEM, VMEM, HBM, VMEM],
        out_specs=(VMEM,) * 3,
        compiler_params=PARAMS,
    )(got_b, got_a, core_b, reduced)
    core_b = lax.ppermute(core_b, "lon", lon_second)
    core_a = lax.ppermute(core_a, "lon", lon_first)
    row_a = lax.ppermute(row_a, "lat", lat_first)
    row_b = lax.ppermute(row_b, "lat", lat_second)
    border_cells = 2 * REACH * lon_len
    stack_rows = taps * rank // 2
    halo_stack_shape = jax.ShapeDtypeStruct((2, stack_rows, border_cells), BF16)
    inner, halo_stack = pl.pallas_call(
        functools.partial(inner_kernel, lat_len),
        out_shape=(jax.ShapeDtypeStruct((tap_rank * rank, cells - border_cells), BF16), halo_stack_shape),
        in_specs=[VMEM] * 3,
        out_specs=(VMEM,) * 2,
        scratch_shapes=[pltpu.VMEM((2, stack_rows, cells - border_cells), BF16)],
        compiler_params=PARAMS,
    )(reduced, edges, weights)
    border = pl.pallas_call(
        functools.partial(border_kernel, lat_len, lat_count),
        out_shape=jax.ShapeDtypeStruct((tap_rank * rank, border_cells), BF16),
        in_specs=[VMEM] * 4,
        out_specs=VMEM,
        scratch_shapes=[pltpu.VMEM(halo_stack_shape.shape, BF16)],
        compiler_params=PARAMS,
    )(row_b, row_a, weights, halo_stack)
    out_shape = (out_channels, lat_len, lon_len)
    return pl.pallas_call(
        mix_kernel,
        out_shape=jax.ShapeDtypeStruct(out_shape, BF16),
        in_specs=[VMEM] * 8,
        out_specs=HBM,
        scratch_shapes=[pltpu.VMEM(out_shape, BF16), pltpu.SemaphoreType.DMA((OUT_COPIES,))],
        compiler_params=PARAMS,
    )(inner, border, core_a, core_b, own, position, mixer, offset)


def solution(mesh):
    placed = (
        P(None, "lat", "lon"),
        P("lat", "lon"),
        P("lat", "lon", None),
        P(),
        P("lon", None, None),
        P(),
        P(),
        P(),
        P(),
    )
    return jax.shard_map(
        on_device, mesh=mesh, in_specs=placed, out_specs=P(None, "lat", "lon"), check_vma=False
    )
```

```python
import functools

import jax
import jax.numpy as jnp
from jax import lax
from jax.experimental import pallas as pl
from jax.experimental.pallas import tpu as pltpu
from jax.sharding import PartitionSpec as P

KS = 5
REACH = KS // 2
PER_OWNER = 2
LANES = 128
EDGE = 2 * REACH
GROUP = 8
STEP = 4
OUT_COPIES = 4
IN_COPIES = 4
F32 = jnp.float32
BF16 = jnp.bfloat16
VMEM = pl.BlockSpec(memory_space=pltpu.VMEM)
SMEM = pl.BlockSpec(memory_space=pltpu.SMEM)
HBM = pl.BlockSpec(memory_space=pltpu.HBM)
PARAMS = pltpu.CompilerParams(vmem_limit_bytes=24 * 1024 * 1024)


def swap_pairs(count):
    first = [(i, i ^ 1) for i in range(count)]
    second = [(i, (i + 1 if i % 2 else i - 1) % count) for i in range(count)]
    return first, second


def in_hbm(array):
    return pltpu.with_memory_space_constraint(array, pltpu.HBM)


def lane_index(shape):
    return lax.broadcasted_iota(jnp.int32, shape, 1)


def start_copies(pairs, sems):
    copies = [pltpu.make_async_copy(source, target, sems.at[i]) for i, (source, target) in enumerate(pairs)]
    for copy in copies:
        copy.start()
    return copies


def in_parts(source, target, count):
    share = target.shape[0] // count
    return tuple((source.at[pl.ds(i * share, share)], target.at[pl.ds(i * share, share)]) for i in range(count))


def find_rows(list_ref, slot_ref, lon_count, held):
    me = lax.axis_index("lon")
    owners = (me, lax.rem(me + lon_count - 1, lon_count), lax.rem(me + 1, lon_count))
    slots = [slot_ref[list_ref[0, 0, i]] for i in range(list_ref.shape[2])]
    places, rows = [], []
    for owner in owners:
        least, greatest = jnp.int32(held), jnp.int32(-1)
        first, last = jnp.int32(0), jnp.int32(0)
        for i, slot in enumerate(slots):
            local = slot - owner * held
            hit = (local >= 0) & (local < held)
            first = jnp.where(hit & (local < least), i, first)
            last = jnp.where(hit & (local > greatest), i, last)
            least = jnp.where(hit, jnp.minimum(local, least), least)
            greatest = jnp.where(hit, jnp.maximum(local, greatest), greatest)
        places.append([first, last])
        rows.append([jnp.minimum(least, held - 1), jnp.maximum(greatest, 0)])
    return places, rows


class Held:
    names = ("own", "position", "weights", "mixer", "offset")
    sources = ("labels", "tap", "out_factor", "bias")

    def __init__(self, refs):
        self.__dict__.update(zip(self.names, refs))


def build_held(places, targets, held):
    labels_ref, tap_ref, out_factor_ref, bias_ref = targets
    even = (lax.axis_index("lon") % 2) == 0
    order = list(places[0])
    order += [jnp.where(even, places[2][nth], places[1][nth]) for nth in range(PER_OWNER)]
    order += [jnp.where(even, places[1][nth], places[2][nth]) for nth in range(PER_OWNER)]
    labels = labels_ref[...]
    position = jnp.zeros(labels.shape, jnp.int32)
    for index, place in enumerate(order):
        position = jnp.where(labels == place, index, position)
    held.position[...] = position

    rank, out_channels = out_factor_ref.shape
    half = rank // 2
    tap_rank, taps = tap_ref.shape
    shape = (tap_rank * half, taps * half)
    spread = (
        lax.broadcasted_iota(jnp.int32, (shape[0], tap_rank), 0) // half == lane_index((shape[0], tap_rank))
    ).astype(BF16)
    repeat = (
        lax.broadcasted_iota(jnp.int32, (taps, shape[1]), 0) == lane_index((taps, shape[1])) // half
    ).astype(BF16)
    tall = jnp.dot(spread, tap_ref[...], preferred_element_type=F32).astype(BF16)
    wide = jnp.dot(tall, repeat, preferred_element_type=F32)
    same = lax.broadcasted_iota(jnp.int32, shape, 0) % half == lane_index(shape) % half
    held.weights[...] = jnp.where(same, wide, 0.0).astype(BF16)

    shape = (out_channels * GROUP, rank * GROUP)
    spread = (
        lax.broadcasted_iota(jnp.int32, (shape[0], out_channels), 0) // GROUP
        == lane_index((shape[0], out_channels))
    ).astype(BF16)
    repeat = (
        lax.broadcasted_iota(jnp.int32, (rank, shape[1]), 0) == lane_index((rank, shape[1])) % rank
    ).astype(BF16)
    tall = lax.dot_general(
        spread, out_factor_ref[...], (((1,), (1,)), ((), ())), preferred_element_type=F32
    ).astype(BF16)
    wide = jnp.dot(tall, repeat, preferred_element_type=F32)
    same = lax.broadcasted_iota(jnp.int32, shape, 0) % GROUP == lane_index(shape) // rank
    held.mixer[...] = jnp.where(same, wide, 0.0).astype(BF16)

    shape = (out_channels * GROUP, out_channels)
    mine = lax.broadcasted_iota(jnp.int32, shape, 0) // GROUP == lane_index(shape)
    offset = jnp.sum(jnp.where(mine, bias_ref[...], 0.0), axis=1, keepdims=True)
    held.offset[...] = jnp.broadcast_to(offset, held.offset.shape)


def asked_rows(list_ref, slots_ref, owner, held):
    lane = lane_index((1, LANES))
    found = []
    for i in range(list_ref.shape[2]):
        region = list_ref[0, 0, i]
        row = slots_ref[pl.ds(region // LANES, 1), :]
        found.append(jnp.where(lane == region % LANES, row - owner * held, -1))
    local = jnp.max(jnp.concatenate(found, axis=0), axis=1, keepdims=True)
    hit = (local >= 0) & (local < held)
    least = jnp.min(jnp.where(hit, local, held - 1), axis=0, keepdims=True)
    greatest = jnp.max(jnp.where(hit, local, 0), axis=0, keepdims=True)
    return least, greatest


def edge_kernel(lon_count, held_rows, *refs):
    list_hbm, slots_hbm, feat_hbm, in_hbm, pay_a_ref, pay_b_ref = refs[:6]
    list_ref, slots_ref, feat_ref, in_ref, turned_ref, sems = refs[6:]
    channels, lat_len, lon_len = feat_ref.shape
    rank = in_ref.shape[0]
    batch = LANES // EDGE
    pairs = in_parts(feat_hbm, feat_ref, IN_COPIES)
    pairs += ((slots_hbm, slots_ref), (list_hbm, list_ref), (in_hbm, in_ref))
    copies = start_copies(pairs, sems)
    for copy in copies:
        copy.wait()
    lane = lane_index((lat_len, LANES))
    for part in range(channels // batch):
        packed = jnp.zeros((lat_len, LANES), F32)
        for c in range(batch):
            moved = pltpu.roll(feat_ref[part * batch + c].astype(F32), (EDGE * c + REACH) % LANES, 1)
            packed = jnp.where(lane // EDGE == c, moved, packed)
        turned_ref[part * LANES : (part + 1) * LANES, :] = jnp.transpose(packed)
    columns = jnp.concatenate(
        [turned_ref[pl.ds(j, channels, stride=EDGE), :].astype(BF16) for j in range(EDGE)], axis=1
    )
    edges = jnp.dot(in_ref[...], columns, preferred_element_type=F32)
    edges = jnp.concatenate([edges, jnp.zeros((rank, LANES - EDGE * lat_len), F32)], axis=1)
    me = lax.axis_index("lon")
    even = (me % 2) == 0
    prev, following = lax.rem(me + lon_count - 1, lon_count), lax.rem(me + 1, lon_count)
    lane = lane_index((rank, LANES))
    for out_ref, owner in (
        (pay_a_ref, jnp.where(even, following, prev)),
        (pay_b_ref, jnp.where(even, prev, following)),
    ):
        load = edges
        for nth, row in enumerate(asked_rows(list_ref, slots_ref, owner, held_rows)):
            load = jnp.where(lane == EDGE * lat_len + nth, row.astype(F32), load)
        out_ref[...] = load.astype(BF16)


def reduce_tile(lat_len, feat_ref, in_ref, rows_ref, red_ref):
    channels, lon_len = feat_ref.shape[0], feat_ref.shape[2]
    rows_ref[...] = feat_ref[...].astype(F32).reshape(channels * lat_len, lon_len)
    cells = jnp.concatenate(
        [rows_ref[pl.ds(p, channels, stride=lat_len), :].astype(BF16) for p in range(lat_len)], axis=1
    )
    red_ref[...] = jnp.dot(in_ref[...], cells, preferred_element_type=F32).astype(BF16)


def prepare_kernel(lon_count, lat_len, *refs):
    list_hbm, slot_hbm, feat_hbm, in_hbm, bank_hbm = refs[:5]
    sources, red_ref, held = refs[5:9], refs[10], Held(refs[11:16])
    list_ref, slot_ref, feat_ref, in_ref, rows_ref = refs[16:21]
    targets, sems = refs[21:25], refs[25]
    pairs = ((list_hbm, list_ref), (slot_hbm, slot_ref)) + in_parts(feat_hbm, feat_ref, IN_COPIES)
    pairs += ((in_hbm, in_ref), *zip(sources, targets))
    for copy in start_copies(pairs, sems):
        copy.wait()
    places, rows = find_rows(list_ref, slot_ref, lon_count, bank_hbm.shape[0])
    own = start_copies(tuple((bank_hbm.at[row], held.own.at[nth]) for nth, row in enumerate(rows[0])), sems)
    reduce_tile(lat_len, feat_ref, in_ref, rows_ref, red_ref)
    build_held(places, targets, held)
    for copy in own:
        copy.wait()


def pick_kernel(lat_len, got_b_ref, got_a_ref, own_hbm, bank_ref, core_a_ref, core_b_ref):
    lane = lane_index((1, LANES))
    for got_ref, core_ref in ((got_b_ref, core_b_ref), (got_a_ref, core_a_ref)):
        head = got_ref[...].astype(F32)[0:1, :]
        for nth in range(PER_OWNER):
            row = jnp.sum(jnp.where(lane == EDGE * lat_len + nth, head, 0.0)).astype(jnp.int32)
            core_ref[nth] = bank_ref[row]


def rows_kernel(lat_len, got_b_ref, got_a_ref, core_ref, red_ref, edge_ref, row_a_ref, row_b_ref):
    lon_len = red_ref.shape[1] // lat_len
    even = (lax.axis_index("lon") % 2) == 0
    from_prev = lane_index(got_a_ref.shape) < REACH * lat_len
    got = jnp.where(from_prev == even, got_b_ref[...].astype(F32), got_a_ref[...].astype(F32)).astype(BF16)
    source = lax.broadcasted_iota(jnp.int32, (LANES, LANES), 0)
    target = lane_index((LANES, LANES))
    order = (source == (target % EDGE) * lat_len + target // EDGE) & (target < EDGE * lat_len)
    edges = jnp.dot(got, order.astype(BF16), preferred_element_type=F32).astype(BF16)
    edge_ref[...] = edges
    even = (lax.axis_index("lat") % 2) == 0
    head = red_ref[:, : REACH * lon_len].astype(F32)
    tail = red_ref[:, (lat_len - REACH) * lon_len :].astype(F32)
    row_a_ref[:, : REACH * lon_len] = jnp.where(even, tail, head).astype(BF16)
    row_b_ref[:, : REACH * lon_len] = jnp.where(even, head, tail).astype(BF16)
    row_a_ref[:, REACH * lon_len :] = edges
    row_b_ref[:, REACH * lon_len :] = edges


def shifted_columns(row, edges, place):
    lane = lane_index(row.shape)
    lon_len = row.shape[1]
    edges = pltpu.roll(edges, (LANES - REACH - EDGE * place) % LANES, 1)
    moved = []
    for col_off in range(KS):
        shift = REACH - col_off
        if shift > 0:
            piece = pltpu.roll(jnp.where(lane >= lon_len - shift, edges, row), shift, 1)
        elif shift < 0:
            piece = pltpu.roll(jnp.where(lane < -shift, edges, row), lon_len + shift, 1)
        else:
            piece = row
        moved.append(piece.astype(BF16))
    return moved


def stack_row(stack_ref, p, moved, slots, lon_len):
    half = moved[0].shape[0] // 2
    for col_off, piece in enumerate(moved):
        for row_off in range(KS):
            slot = slots.get(p + REACH - row_off)
            if slot is not None:
                k = row_off * KS + col_off
                for h in range(2):
                    stack_ref[h, k * half : (k + 1) * half, slot * lon_len : (slot + 1) * lon_len] = piece[
                        h * half : (h + 1) * half
                    ]


def apply_taps(rank, weights_ref, stacked, tapped_ref, lon_len):
    half = rank // 2
    tap_rank = tapped_ref.shape[0] // rank
    width = STEP * lon_len
    for start in range(0, tapped_ref.shape[1], width):
        parts = [
            jnp.dot(weights_ref[...], stacked(h, start, width), preferred_element_type=F32)
            .astype(BF16)
            .reshape(tap_rank, 1, half, width)
            for h in range(2)
        ]
        tapped_ref[:, start : start + width] = jnp.concatenate(parts, axis=1).reshape(tap_rank * rank, width)


def border_slots(lat_len):
    slots = {p: p for p in range(REACH)}
    slots.update({lat_len - REACH + p: REACH + p for p in range(REACH)})
    return slots


def inner_kernel(lat_len, red_ref, edge_ref, weights_ref, tapped_ref, halo_stack_ref, stack_ref):
    rank = red_ref.shape[0]
    lon_len = red_ref.shape[1] // lat_len
    slots = {p: p - REACH for p in range(REACH, lat_len - REACH)}
    edges = edge_ref[...].astype(F32)
    for p in range(lat_len):
        row = red_ref[:, p * lon_len : (p + 1) * lon_len].astype(F32)
        moved = shifted_columns(row, edges, p)
        stack_row(stack_ref, p, moved, slots, lon_len)
        stack_row(halo_stack_ref, p, moved, border_slots(lat_len), lon_len)
    apply_taps(rank, weights_ref, lambda h, start, width: stack_ref[h, :, start : start + width], tapped_ref, lon_len)


def border_kernel(lat_len, lat_count, row_b_ref, row_a_ref, weights_ref, own_stack_ref, tapped_ref, stack_ref):
    rank = row_a_ref.shape[0]
    lon_len = (row_a_ref.shape[1] - LANES) // REACH
    lat = lax.axis_index("lat")
    even = (lat % 2) == 0
    row_a = row_a_ref[...].astype(F32)
    row_b = row_b_ref[...].astype(F32)
    above = jnp.where(lat == 0, 0.0, jnp.where(even, row_b, row_a))
    below = jnp.where(lat == lat_count - 1, 0.0, jnp.where(even, row_a, row_b))
    slots = border_slots(lat_len)
    for i in range(REACH):
        for p, holder, place in ((i - REACH, above, lat_len - REACH + i), (lat_len + i, below, i)):
            row = holder[:, i * lon_len : (i + 1) * lon_len]
            moved = shifted_columns(row, holder[:, REACH * lon_len :], place)
            stack_row(stack_ref, p, moved, slots, lon_len)
    block = KS * rank // 2
    in_halo = {
        (slot, row_off)
        for p, slot in slots.items()
        for row_off in range(KS)
        if not 0 <= p + row_off - REACH < lat_len
    }

    def stacked(h, start, width):
        columns = []
        for slot in range(start // lon_len, (start + width) // lon_len):
            span = slice(slot * lon_len, (slot + 1) * lon_len)
            pieces = []
            for row_off in range(KS):
                ref = stack_ref if (slot, row_off) in in_halo else own_stack_ref
                pieces.append(ref[h, row_off * block : (row_off + 1) * block, span])
            columns.append(jnp.concatenate(pieces, axis=0))
        return jnp.concatenate(columns, axis=1)

    apply_taps(rank, weights_ref, stacked, tapped_ref, lon_len)


def mix_kernel(
    inner_ref,
    border_ref,
    core_a_ref,
    core_b_ref,
    own_ref,
    position_ref,
    mixer_ref,
    offset_ref,
    out_hbm,
    stage_ref,
    sems,
):
    lat_len, lon_len = position_ref.shape
    rank = own_ref.shape[1]
    cores = jnp.concatenate(
        [ref[...].reshape(PER_OWNER * rank, -1) for ref in (own_ref, core_a_ref, core_b_ref)], axis=0
    )
    chunks = [(border_ref, 0, [*range(REACH), *range(lat_len - REACH, lat_len)])]
    for start in range(REACH, lat_len - REACH, STEP):
        chunks.append((inner_ref, start - REACH, [*range(start, start + STEP)]))
    by_row = {}
    for ref, first, rows in chunks:
        width = len(rows) * lon_len
        every = jnp.dot(cores, ref[:, first * lon_len : first * lon_len + width], preferred_element_type=F32)
        position = jnp.concatenate([position_ref[r : r + 1, :] for r in rows], axis=1)
        hidden = jnp.zeros((rank, width), F32)
        for index in range(3 * PER_OWNER):
            hidden = jnp.where(position == index, every[index * rank : (index + 1) * rank], hidden)
        hidden = hidden.astype(BF16)
        for i, r in enumerate(rows):
            by_row[r] = hidden[:, i * lon_len : (i + 1) * lon_len]
    pieces = [by_row[r] for r in range(lat_len)]
    groups = [jnp.concatenate(pieces[g : g + GROUP], axis=0) for g in range(0, lat_len, GROUP)]
    channels = stage_ref.shape[0]
    share = channels // OUT_COPIES
    outputs = [jnp.dot(mixer_ref[...], hidden, preferred_element_type=F32) for hidden in groups]
    copies = []
    for part in range(OUT_COPIES):
        span = slice(part * share * GROUP, (part + 1) * share * GROUP)
        blocks = []
        for output in outputs:
            output = output[span] + offset_ref[span, :]
            mixed = 0.5 * output * (1.0 + jnp.tanh(0.5 * output))
            blocks.append(mixed.reshape(share, GROUP, lon_len))
        held = slice(part * share, (part + 1) * share)
        stage_ref[held] = jnp.concatenate(blocks, axis=1).astype(BF16)
        copy = pltpu.make_async_copy(stage_ref.at[held], out_hbm.at[held], sems.at[part])
        copy.start()
        copies.append(copy)
    for copy in copies:
        copy.wait()


def on_device(
    features, labels, tile_regions, bank_slot, kernel_bank, in_factor, tap_factor, out_factor, out_bias
):
    channels, lat_len, lon_len = features.shape
    rank = in_factor.shape[0]
    held, core_rows, core_cols = kernel_bank.shape
    tap_rank, taps = tap_factor.shape
    out_channels = out_factor.shape[0]
    cells = lat_len * lon_len
    lon_count, lat_count = lax.axis_size("lon"), lax.axis_size("lat")
    lon_first, lon_second = swap_pairs(lon_count)
    lat_first, lat_second = swap_pairs(lat_count)
    edge_shape = jax.ShapeDtypeStruct((rank, LANES), BF16)
    core_shape = jax.ShapeDtypeStruct((PER_OWNER, core_rows, core_cols), BF16)
    held_shapes = (
        core_shape,
        jax.ShapeDtypeStruct(labels.shape, jnp.int32),
        jax.ShapeDtypeStruct((tap_rank * rank // 2, taps * rank // 2), BF16),
        jax.ShapeDtypeStruct((out_channels * GROUP, rank * GROUP), BF16),
        jax.ShapeDtypeStruct((out_channels * GROUP, lon_len), F32),
    )
    lists = [
        pltpu.SMEM(tile_regions.shape, jnp.int32),
        pltpu.SMEM(bank_slot.shape, jnp.int32),
        pltpu.VMEM(features.shape, BF16),
        pltpu.VMEM(in_factor.shape, BF16),
    ]
    targets = [
        pltpu.VMEM(labels.shape, jnp.int32),
        pltpu.VMEM(tap_factor.shape, BF16),
        pltpu.VMEM(out_factor.shape[::-1], BF16),
        pltpu.VMEM((1, out_channels), F32),
    ]
    sources = tuple(
        in_hbm(x)
        for x in (
            tile_regions,
            bank_slot,
            features,
            in_factor,
            kernel_bank,
            labels,
            tap_factor,
            out_factor.T,
            out_bias.reshape(1, -1),
        )
    )
    pay_a, pay_b = pl.pallas_call(
        functools.partial(edge_kernel, lon_count, held),
        out_shape=(edge_shape, edge_shape),
        in_specs=[HBM] * 4,
        out_specs=(VMEM,) * 2,
        scratch_shapes=[
            lists[0],
            pltpu.VMEM((bank_slot.shape[0] // LANES, LANES), jnp.int32),
            *lists[2:],
            pltpu.VMEM((channels * EDGE, lat_len), F32),
            pltpu.SemaphoreType.DMA((IN_COPIES + 3,)),
        ],
        compiler_params=PARAMS,
        cost_estimate=pl.CostEstimate(flops=2 * 10**9, bytes_accessed=4 * 10**6, transcendentals=0),
    )(sources[0], in_hbm(bank_slot.reshape(-1, LANES)), *sources[2:4])
    got_b = lax.ppermute(pay_b, "lon", lon_second)
    got_a = lax.ppermute(pay_a, "lon", lon_first)
    reduced, own, position, weights, mixer, offset = pl.pallas_call(
        functools.partial(prepare_kernel, lon_count, lat_len),
        out_shape=(jax.ShapeDtypeStruct((rank, cells), BF16), *held_shapes),
        in_specs=[HBM] * 9 + [HBM],
        out_specs=(VMEM,) * 6,
        scratch_shapes=[
            *lists,
            pltpu.VMEM((channels * lat_len, lon_len), F32),
            *targets,
            pltpu.SemaphoreType.DMA((IN_COPIES + 7,)),
        ],
        compiler_params=PARAMS,
        cost_estimate=pl.CostEstimate(flops=10**5, bytes_accessed=10**5, transcendentals=0),
    )(*sources, pay_a)
    row_shape = jax.ShapeDtypeStruct((rank, REACH * lon_len + LANES), BF16)
    core_a, core_b = pl.pallas_call(
        functools.partial(pick_kernel, lat_len),
        out_shape=(core_shape, core_shape),
        in_specs=[VMEM, VMEM, HBM, VMEM],
        out_specs=(VMEM,) * 2,
        compiler_params=PARAMS,
    )(got_b, got_a, own, kernel_bank)
    edges, row_a, row_b = pl.pallas_call(
        functools.partial(rows_kernel, lat_len),
        out_shape=(edge_shape, row_shape, row_shape),
        in_specs=[VMEM, VMEM, HBM, VMEM],
        out_specs=(VMEM,) * 3,
        compiler_params=PARAMS,
    )(got_b, got_a, core_b, reduced)
    core_b = lax.ppermute(core_b, "lon", lon_second)
    core_a = lax.ppermute(core_a, "lon", lon_first)
    row_a = lax.ppermute(row_a, "lat", lat_first)
    row_b = lax.ppermute(row_b, "lat", lat_second)
    border_cells = 2 * REACH * lon_len
    stack_rows = taps * rank // 2
    halo_stack_shape = jax.ShapeDtypeStruct((2, stack_rows, border_cells), BF16)
    inner, halo_stack = pl.pallas_call(
        functools.partial(inner_kernel, lat_len),
        out_shape=(jax.ShapeDtypeStruct((tap_rank * rank, cells - border_cells), BF16), halo_stack_shape),
        in_specs=[VMEM] * 3,
        out_specs=(VMEM,) * 2,
        scratch_shapes=[pltpu.VMEM((2, stack_rows, cells - border_cells), BF16)],
        compiler_params=PARAMS,
    )(reduced, edges, weights)
    border = pl.pallas_call(
        functools.partial(border_kernel, lat_len, lat_count),
        out_shape=jax.ShapeDtypeStruct((tap_rank * rank, border_cells), BF16),
        in_specs=[VMEM] * 4,
        out_specs=VMEM,
        scratch_shapes=[pltpu.VMEM(halo_stack_shape.shape, BF16)],
        compiler_params=PARAMS,
    )(row_b, row_a, weights, halo_stack)
    out_shape = (out_channels, lat_len, lon_len)
    return pl.pallas_call(
        mix_kernel,
        out_shape=jax.ShapeDtypeStruct(out_shape, BF16),
        in_specs=[VMEM] * 8,
        out_specs=HBM,
        scratch_shapes=[pltpu.VMEM(out_shape, BF16), pltpu.SemaphoreType.DMA((OUT_COPIES,))],
        compiler_params=PARAMS,
    )(inner, border, core_a, core_b, own, position, mixer, offset)


def solution(mesh):
    placed = (
        P(None, "lat", "lon"),
        P("lat", "lon"),
        P("lat", "lon", None),
        P(),
        P("lon", None, None),
        P(),
        P(),
        P(),
        P(),
    )
    return jax.shard_map(
        on_device, mesh=mesh, in_specs=placed, out_specs=P(None, "lat", "lon"), check_vma=False
    )
```

```python
import functools

import jax
import jax.numpy as jnp
from jax import lax
from jax.experimental import pallas as pl
from jax.experimental.pallas import tpu as pltpu
from jax.sharding import PartitionSpec as P

KS = 5
REACH = KS // 2
PER_OWNER = 2
LANES = 128
EDGE = 2 * REACH
GROUP = 8
STEP = 4
OUT_COPIES = 4
IN_COPIES = 4
F32 = jnp.float32
BF16 = jnp.bfloat16
VMEM = pl.BlockSpec(memory_space=pltpu.VMEM)
SMEM = pl.BlockSpec(memory_space=pltpu.SMEM)
HBM = pl.BlockSpec(memory_space=pltpu.HBM)
PARAMS = pltpu.CompilerParams(vmem_limit_bytes=24 * 1024 * 1024)


def swap_pairs(count):
    first = [(i, i ^ 1) for i in range(count)]
    second = [(i, (i + 1 if i % 2 else i - 1) % count) for i in range(count)]
    return first, second


def in_hbm(array):
    return pltpu.with_memory_space_constraint(array, pltpu.HBM)


def lane_index(shape):
    return lax.broadcasted_iota(jnp.int32, shape, 1)


def start_copies(pairs, sems):
    copies = [pltpu.make_async_copy(source, target, sems.at[i]) for i, (source, target) in enumerate(pairs)]
    for copy in copies:
        copy.start()
    return copies


def in_parts(source, target, count):
    share = target.shape[0] // count
    return tuple((source.at[pl.ds(i * share, share)], target.at[pl.ds(i * share, share)]) for i in range(count))


def find_rows(list_ref, slot_ref, lon_count, held):
    me = lax.axis_index("lon")
    owners = (me, lax.rem(me + lon_count - 1, lon_count), lax.rem(me + 1, lon_count))
    slots = [slot_ref[list_ref[0, 0, i]] for i in range(list_ref.shape[2])]
    places, rows = [], []
    for owner in owners:
        least, greatest = jnp.int32(held), jnp.int32(-1)
        first, last = jnp.int32(0), jnp.int32(0)
        for i, slot in enumerate(slots):
            local = slot - owner * held
            hit = (local >= 0) & (local < held)
            first = jnp.where(hit & (local < least), i, first)
            last = jnp.where(hit & (local > greatest), i, last)
            least = jnp.where(hit, jnp.minimum(local, least), least)
            greatest = jnp.where(hit, jnp.maximum(local, greatest), greatest)
        places.append([first, last])
        rows.append([jnp.minimum(least, held - 1), jnp.maximum(greatest, 0)])
    return places, rows


class Held:
    names = ("own", "position", "weights")
    sources = ("labels", "tap")

    def __init__(self, refs):
        self.__dict__.update(zip(self.names, refs))


def build_held(places, targets, held):
    labels_ref, tap_ref = targets
    even = (lax.axis_index("lon") % 2) == 0
    order = list(places[0])
    order += [jnp.where(even, places[2][nth], places[1][nth]) for nth in range(PER_OWNER)]
    order += [jnp.where(even, places[1][nth], places[2][nth]) for nth in range(PER_OWNER)]
    labels = labels_ref[...]
    position = jnp.zeros(labels.shape, jnp.int32)
    for index, place in enumerate(order):
        position = jnp.where(labels == place, index, position)
    held.position[...] = position

    tap_rank, taps = tap_ref.shape
    half = held.weights.shape[0] // tap_rank
    shape = (tap_rank * half, taps * half)
    spread = (
        lax.broadcasted_iota(jnp.int32, (shape[0], tap_rank), 0) // half == lane_index((shape[0], tap_rank))
    ).astype(BF16)
    repeat = (
        lax.broadcasted_iota(jnp.int32, (taps, shape[1]), 0) == lane_index((taps, shape[1])) // half
    ).astype(BF16)
    tall = jnp.dot(spread, tap_ref[...], preferred_element_type=F32).astype(BF16)
    wide = jnp.dot(tall, repeat, preferred_element_type=F32)
    same = lax.broadcasted_iota(jnp.int32, shape, 0) % half == lane_index(shape) % half
    held.weights[...] = jnp.where(same, wide, 0.0).astype(BF16)


def build_mixer(out_factor_ref, bias_ref, mixer_ref, offset_ref):
    rank, out_channels = out_factor_ref.shape
    shape = (out_channels * GROUP, rank * GROUP)
    spread = (
        lax.broadcasted_iota(jnp.int32, (shape[0], out_channels), 0) // GROUP
        == lane_index((shape[0], out_channels))
    ).astype(BF16)
    repeat = (
        lax.broadcasted_iota(jnp.int32, (rank, shape[1]), 0) == lane_index((rank, shape[1])) % rank
    ).astype(BF16)
    tall = lax.dot_general(
        spread, out_factor_ref[...], (((1,), (1,)), ((), ())), preferred_element_type=F32
    ).astype(BF16)
    wide = jnp.dot(tall, repeat, preferred_element_type=F32)
    same = lax.broadcasted_iota(jnp.int32, shape, 0) % GROUP == lane_index(shape) // rank
    mixer_ref[...] = jnp.where(same, wide, 0.0).astype(BF16)

    square = (out_channels, out_channels)
    diagonal = lax.broadcasted_iota(jnp.int32, square, 0) == lane_index(square)
    column = jnp.sum(jnp.where(diagonal, bias_ref[...], 0.0), axis=1, keepdims=True)
    rest = jnp.broadcast_to(column, (out_channels, offset_ref.shape[1]))
    total = jnp.zeros(offset_ref.shape, F32)
    for _ in range(3):
        piece = rest.astype(BF16)
        rest = rest - piece.astype(F32)
        total = total + jnp.dot(spread, piece, preferred_element_type=F32)
    offset_ref[...] = total


def asked_rows(list_ref, slots_ref, owner, held):
    lane = lane_index((1, LANES))
    found = []
    for i in range(list_ref.shape[2]):
        region = list_ref[0, 0, i]
        row = slots_ref[pl.ds(region // LANES, 1), :]
        found.append(jnp.where(lane == region % LANES, row - owner * held, -1))
    local = jnp.max(jnp.concatenate(found, axis=0), axis=1, keepdims=True)
    hit = (local >= 0) & (local < held)
    least = jnp.min(jnp.where(hit, local, held - 1), axis=0, keepdims=True)
    greatest = jnp.max(jnp.where(hit, local, 0), axis=0, keepdims=True)
    return least, greatest


def edge_kernel(lon_count, held_rows, *refs):
    list_hbm, slots_hbm, feat_hbm, in_hbm, pay_a_ref, pay_b_ref = refs[:6]
    list_ref, slots_ref, feat_ref, in_ref, turned_ref, sems = refs[6:]
    channels, lat_len, lon_len = feat_ref.shape
    rank = in_ref.shape[0]
    batch = LANES // EDGE
    pairs = in_parts(feat_hbm, feat_ref, IN_COPIES)
    pairs += ((slots_hbm, slots_ref), (list_hbm, list_ref), (in_hbm, in_ref))
    copies = start_copies(pairs, sems)
    for copy in copies:
        copy.wait()
    lane = lane_index((lat_len, LANES))
    for part in range(channels // batch):
        packed = jnp.zeros((lat_len, LANES), F32)
        for c in range(batch):
            moved = pltpu.roll(feat_ref[part * batch + c].astype(F32), (EDGE * c + REACH) % LANES, 1)
            packed = jnp.where(lane // EDGE == c, moved, packed)
        turned_ref[part * LANES : (part + 1) * LANES, :] = jnp.transpose(packed)
    columns = jnp.concatenate(
        [turned_ref[pl.ds(j, channels, stride=EDGE), :].astype(BF16) for j in range(EDGE)], axis=1
    )
    edges = jnp.dot(in_ref[...], columns, preferred_element_type=F32)
    edges = jnp.concatenate([edges, jnp.zeros((rank, LANES - EDGE * lat_len), F32)], axis=1)
    me = lax.axis_index("lon")
    even = (me % 2) == 0
    prev, following = lax.rem(me + lon_count - 1, lon_count), lax.rem(me + 1, lon_count)
    lane = lane_index((rank, LANES))
    for out_ref, owner in (
        (pay_a_ref, jnp.where(even, following, prev)),
        (pay_b_ref, jnp.where(even, prev, following)),
    ):
        load = edges
        for nth, row in enumerate(asked_rows(list_ref, slots_ref, owner, held_rows)):
            load = jnp.where(lane == EDGE * lat_len + nth, row.astype(F32), load)
        out_ref[...] = load.astype(BF16)


def reduce_tile(lat_len, feat_ref, in_ref, rows_ref, red_ref):
    channels, lon_len = feat_ref.shape[0], feat_ref.shape[2]
    rows_ref[...] = feat_ref[...].astype(F32).reshape(channels * lat_len, lon_len)
    cells = jnp.concatenate(
        [rows_ref[pl.ds(p, channels, stride=lat_len), :].astype(BF16) for p in range(lat_len)], axis=1
    )
    red_ref[...] = jnp.dot(in_ref[...], cells, preferred_element_type=F32).astype(BF16)


def prepare_kernel(lon_count, lat_len, *refs):
    list_hbm, slot_hbm, feat_hbm, in_hbm, bank_hbm = refs[:5]
    sources, red_ref, held = refs[5:7], refs[8], Held(refs[9:12])
    list_ref, slot_ref, feat_ref, in_ref, rows_ref = refs[12:17]
    targets, sems = refs[17:19], refs[19]
    pairs = ((list_hbm, list_ref), (slot_hbm, slot_ref)) + in_parts(feat_hbm, feat_ref, IN_COPIES)
    pairs += ((in_hbm, in_ref), *zip(sources, targets))
    for copy in start_copies(pairs, sems):
        copy.wait()
    places, rows = find_rows(list_ref, slot_ref, lon_count, bank_hbm.shape[0])
    own = start_copies(tuple((bank_hbm.at[row], held.own.at[nth]) for nth, row in enumerate(rows[0])), sems)
    reduce_tile(lat_len, feat_ref, in_ref, rows_ref, red_ref)
    build_held(places, targets, held)
    for copy in own:
        copy.wait()


def pick_kernel(lat_len, got_b_ref, got_a_ref, own_hbm, bank_ref, core_a_ref, core_b_ref):
    lane = lane_index((1, LANES))
    for got_ref, core_ref in ((got_b_ref, core_b_ref), (got_a_ref, core_a_ref)):
        head = got_ref[...].astype(F32)[0:1, :]
        for nth in range(PER_OWNER):
            row = jnp.sum(jnp.where(lane == EDGE * lat_len + nth, head, 0.0)).astype(jnp.int32)
            core_ref[nth] = bank_ref[row]


def rows_kernel(lat_len, got_b_ref, got_a_ref, core_ref, red_ref, edge_ref, row_a_ref, row_b_ref):
    lon_len = red_ref.shape[1] // lat_len
    even = (lax.axis_index("lon") % 2) == 0
    from_prev = lane_index(got_a_ref.shape) < REACH * lat_len
    got = jnp.where(from_prev == even, got_b_ref[...].astype(F32), got_a_ref[...].astype(F32)).astype(BF16)
    source = lax.broadcasted_iota(jnp.int32, (LANES, LANES), 0)
    target = lane_index((LANES, LANES))
    order = (source == (target % EDGE) * lat_len + target // EDGE) & (target < EDGE * lat_len)
    edges = jnp.dot(got, order.astype(BF16), preferred_element_type=F32).astype(BF16)
    edge_ref[...] = edges
    even = (lax.axis_index("lat") % 2) == 0
    head = red_ref[:, : REACH * lon_len].astype(F32)
    tail = red_ref[:, (lat_len - REACH) * lon_len :].astype(F32)
    row_a_ref[:, : REACH * lon_len] = jnp.where(even, tail, head).astype(BF16)
    row_b_ref[:, : REACH * lon_len] = jnp.where(even, head, tail).astype(BF16)
    row_a_ref[:, REACH * lon_len :] = edges
    row_b_ref[:, REACH * lon_len :] = edges


def shifted_columns(row, edges, place):
    lane = lane_index(row.shape)
    lon_len = row.shape[1]
    edges = pltpu.roll(edges, (LANES - REACH - EDGE * place) % LANES, 1)
    moved = []
    for col_off in range(KS):
        shift = REACH - col_off
        if shift > 0:
            piece = pltpu.roll(jnp.where(lane >= lon_len - shift, edges, row), shift, 1)
        elif shift < 0:
            piece = pltpu.roll(jnp.where(lane < -shift, edges, row), lon_len + shift, 1)
        else:
            piece = row
        moved.append(piece.astype(BF16))
    return moved


def stack_row(stack_ref, p, moved, slots, lon_len):
    half = moved[0].shape[0] // 2
    for col_off, piece in enumerate(moved):
        for row_off in range(KS):
            slot = slots.get(p + REACH - row_off)
            if slot is not None:
                k = row_off * KS + col_off
                for h in range(2):
                    stack_ref[h, k * half : (k + 1) * half, slot * lon_len : (slot + 1) * lon_len] = piece[
                        h * half : (h + 1) * half
                    ]


def apply_taps(rank, weights_ref, stacked, tapped_ref, lon_len):
    half = rank // 2
    tap_rank = tapped_ref.shape[0] // rank
    width = STEP * lon_len
    for start in range(0, tapped_ref.shape[1], width):
        parts = [
            jnp.dot(weights_ref[...], stacked(h, start, width), preferred_element_type=F32)
            .astype(BF16)
            .reshape(tap_rank, 1, half, width)
            for h in range(2)
        ]
        tapped_ref[:, start : start + width] = jnp.concatenate(parts, axis=1).reshape(tap_rank * rank, width)


def border_slots(lat_len):
    slots = {p: p for p in range(REACH)}
    slots.update({lat_len - REACH + p: REACH + p for p in range(REACH)})
    return slots


def inner_kernel(
    lat_len,
    red_ref,
    edge_ref,
    weights_ref,
    out_factor_ref,
    bias_ref,
    tapped_ref,
    halo_stack_ref,
    mixer_ref,
    offset_ref,
    stack_ref,
):
    rank = red_ref.shape[0]
    build_mixer(out_factor_ref, bias_ref, mixer_ref, offset_ref)
    lon_len = red_ref.shape[1] // lat_len
    slots = {p: p - REACH for p in range(REACH, lat_len - REACH)}
    edges = edge_ref[...].astype(F32)
    for p in range(lat_len):
        row = red_ref[:, p * lon_len : (p + 1) * lon_len].astype(F32)
        moved = shifted_columns(row, edges, p)
        stack_row(stack_ref, p, moved, slots, lon_len)
        stack_row(halo_stack_ref, p, moved, border_slots(lat_len), lon_len)
    apply_taps(rank, weights_ref, lambda h, start, width: stack_ref[h, :, start : start + width], tapped_ref, lon_len)


def border_kernel(lat_len, lat_count, row_b_ref, row_a_ref, weights_ref, own_stack_ref, tapped_ref, stack_ref):
    rank = row_a_ref.shape[0]
    lon_len = (row_a_ref.shape[1] - LANES) // REACH
    lat = lax.axis_index("lat")
    even = (lat % 2) == 0
    row_a = row_a_ref[...].astype(F32)
    row_b = row_b_ref[...].astype(F32)
    above = jnp.where(lat == 0, 0.0, jnp.where(even, row_b, row_a))
    below = jnp.where(lat == lat_count - 1, 0.0, jnp.where(even, row_a, row_b))
    slots = border_slots(lat_len)
    for i in range(REACH):
        for p, holder, place in ((i - REACH, above, lat_len - REACH + i), (lat_len + i, below, i)):
            row = holder[:, i * lon_len : (i + 1) * lon_len]
            moved = shifted_columns(row, holder[:, REACH * lon_len :], place)
            stack_row(stack_ref, p, moved, slots, lon_len)
    block = KS * rank // 2
    in_halo = {
        (slot, row_off)
        for p, slot in slots.items()
        for row_off in range(KS)
        if not 0 <= p + row_off - REACH < lat_len
    }

    def stacked(h, start, width):
        columns = []
        for slot in range(start // lon_len, (start + width) // lon_len):
            span = slice(slot * lon_len, (slot + 1) * lon_len)
            pieces = []
            for row_off in range(KS):
                ref = stack_ref if (slot, row_off) in in_halo else own_stack_ref
                pieces.append(ref[h, row_off * block : (row_off + 1) * block, span])
            columns.append(jnp.concatenate(pieces, axis=0))
        return jnp.concatenate(columns, axis=1)

    apply_taps(rank, weights_ref, stacked, tapped_ref, lon_len)


def mix_kernel(
    inner_ref,
    border_ref,
    core_a_ref,
    core_b_ref,
    own_ref,
    position_ref,
    mixer_ref,
    offset_ref,
    out_hbm,
    stage_ref,
    sems,
):
    lat_len, lon_len = position_ref.shape
    rank = own_ref.shape[1]
    cores = jnp.concatenate(
        [ref[...].reshape(PER_OWNER * rank, -1) for ref in (own_ref, core_a_ref, core_b_ref)], axis=0
    )
    chunks = [(border_ref, 0, [*range(REACH), *range(lat_len - REACH, lat_len)])]
    for start in range(REACH, lat_len - REACH, STEP):
        chunks.append((inner_ref, start - REACH, [*range(start, start + STEP)]))
    by_row = {}
    for ref, first, rows in chunks:
        width = len(rows) * lon_len
        every = jnp.dot(cores, ref[:, first * lon_len : first * lon_len + width], preferred_element_type=F32)
        position = jnp.concatenate([position_ref[r : r + 1, :] for r in rows], axis=1)
        hidden = jnp.zeros((rank, width), F32)
        for index in range(3 * PER_OWNER):
            hidden = jnp.where(position == index, every[index * rank : (index + 1) * rank], hidden)
        hidden = hidden.astype(BF16)
        for i, r in enumerate(rows):
            by_row[r] = hidden[:, i * lon_len : (i + 1) * lon_len]
    pieces = [by_row[r] for r in range(lat_len)]
    groups = [jnp.concatenate(pieces[g : g + GROUP], axis=0) for g in range(0, lat_len, GROUP)]
    channels = stage_ref.shape[0]
    share = channels // OUT_COPIES
    outputs = [jnp.dot(mixer_ref[...], hidden, preferred_element_type=F32) for hidden in groups]
    copies = []
    for part in range(OUT_COPIES):
        span = slice(part * share * GROUP, (part + 1) * share * GROUP)
        blocks = []
        for output in outputs:
            output = output[span] + offset_ref[span, :]
            mixed = 0.5 * output * (1.0 + jnp.tanh(0.5 * output))
            blocks.append(mixed.reshape(share, GROUP, lon_len))
        held = slice(part * share, (part + 1) * share)
        stage_ref[held] = jnp.concatenate(blocks, axis=1).astype(BF16)
        copy = pltpu.make_async_copy(stage_ref.at[held], out_hbm.at[held], sems.at[part])
        copy.start()
        copies.append(copy)
    for copy in copies:
        copy.wait()


def on_device(
    features, labels, tile_regions, bank_slot, kernel_bank, in_factor, tap_factor, out_factor, out_bias
):
    channels, lat_len, lon_len = features.shape
    rank = in_factor.shape[0]
    held, core_rows, core_cols = kernel_bank.shape
    tap_rank, taps = tap_factor.shape
    out_channels = out_factor.shape[0]
    cells = lat_len * lon_len
    lon_count, lat_count = lax.axis_size("lon"), lax.axis_size("lat")
    lon_first, lon_second = swap_pairs(lon_count)
    lat_first, lat_second = swap_pairs(lat_count)
    edge_shape = jax.ShapeDtypeStruct((rank, LANES), BF16)
    core_shape = jax.ShapeDtypeStruct((PER_OWNER, core_rows, core_cols), BF16)
    held_shapes = (
        core_shape,
        jax.ShapeDtypeStruct(labels.shape, jnp.int32),
        jax.ShapeDtypeStruct((tap_rank * rank // 2, taps * rank // 2), BF16),
    )
    lists = [
        pltpu.SMEM(tile_regions.shape, jnp.int32),
        pltpu.SMEM(bank_slot.shape, jnp.int32),
        pltpu.VMEM(features.shape, BF16),
        pltpu.VMEM(in_factor.shape, BF16),
    ]
    targets = [
        pltpu.VMEM(labels.shape, jnp.int32),
        pltpu.VMEM(tap_factor.shape, BF16),
    ]
    sources = tuple(
        in_hbm(x)
        for x in (
            tile_regions,
            bank_slot,
            features,
            in_factor,
            kernel_bank,
            labels,
            tap_factor,
        )
    )
    pay_a, pay_b = pl.pallas_call(
        functools.partial(edge_kernel, lon_count, held),
        out_shape=(edge_shape, edge_shape),
        in_specs=[HBM] * 4,
        out_specs=(VMEM,) * 2,
        scratch_shapes=[
            lists[0],
            pltpu.VMEM((bank_slot.shape[0] // LANES, LANES), jnp.int32),
            *lists[2:],
            pltpu.VMEM((channels * EDGE, lat_len), F32),
            pltpu.SemaphoreType.DMA((IN_COPIES + 3,)),
        ],
        compiler_params=PARAMS,
        cost_estimate=pl.CostEstimate(flops=2 * 10**9, bytes_accessed=4 * 10**6, transcendentals=0),
    )(sources[0], in_hbm(bank_slot.reshape(-1, LANES)), *sources[2:4])
    got_b = lax.ppermute(pay_b, "lon", lon_second)
    got_a = lax.ppermute(pay_a, "lon", lon_first)
    reduced, own, position, weights = pl.pallas_call(
        functools.partial(prepare_kernel, lon_count, lat_len),
        out_shape=(jax.ShapeDtypeStruct((rank, cells), BF16), *held_shapes),
        in_specs=[HBM] * 8,
        out_specs=(VMEM,) * 4,
        scratch_shapes=[
            *lists,
            pltpu.VMEM((channels * lat_len, lon_len), F32),
            *targets,
            pltpu.SemaphoreType.DMA((IN_COPIES + 5,)),
        ],
        compiler_params=PARAMS,
        cost_estimate=pl.CostEstimate(flops=10**5, bytes_accessed=10**5, transcendentals=0),
    )(*sources, pay_a)
    row_shape = jax.ShapeDtypeStruct((rank, REACH * lon_len + LANES), BF16)
    core_a, core_b = pl.pallas_call(
        functools.partial(pick_kernel, lat_len),
        out_shape=(core_shape, core_shape),
        in_specs=[VMEM, VMEM, HBM, VMEM],
        out_specs=(VMEM,) * 2,
        compiler_params=PARAMS,
    )(got_b, got_a, own, kernel_bank)
    edges, row_a, row_b = pl.pallas_call(
        functools.partial(rows_kernel, lat_len),
        out_shape=(edge_shape, row_shape, row_shape),
        in_specs=[VMEM, VMEM, HBM, VMEM],
        out_specs=(VMEM,) * 3,
        compiler_params=PARAMS,
    )(got_b, got_a, core_b, reduced)
    core_b = lax.ppermute(core_b, "lon", lon_second)
    core_a = lax.ppermute(core_a, "lon", lon_first)
    row_a = lax.ppermute(row_a, "lat", lat_first)
    row_b = lax.ppermute(row_b, "lat", lat_second)
    border_cells = 2 * REACH * lon_len
    stack_rows = taps * rank // 2
    halo_stack_shape = jax.ShapeDtypeStruct((2, stack_rows, border_cells), BF16)
    inner, halo_stack, mixer, offset = pl.pallas_call(
        functools.partial(inner_kernel, lat_len),
        out_shape=(
            jax.ShapeDtypeStruct((tap_rank * rank, cells - border_cells), BF16),
            halo_stack_shape,
            jax.ShapeDtypeStruct((out_channels * GROUP, rank * GROUP), BF16),
            jax.ShapeDtypeStruct((out_channels * GROUP, lon_len), F32),
        ),
        in_specs=[VMEM] * 5,
        out_specs=(VMEM,) * 4,
        scratch_shapes=[pltpu.VMEM((2, stack_rows, cells - border_cells), BF16)],
        compiler_params=PARAMS,
    )(reduced, edges, weights, out_factor.T, out_bias.reshape(1, -1))
    border = pl.pallas_call(
        functools.partial(border_kernel, lat_len, lat_count),
        out_shape=jax.ShapeDtypeStruct((tap_rank * rank, border_cells), BF16),
        in_specs=[VMEM] * 4,
        out_specs=VMEM,
        scratch_shapes=[pltpu.VMEM(halo_stack_shape.shape, BF16)],
        compiler_params=PARAMS,
    )(row_b, row_a, weights, halo_stack)
    out_shape = (out_channels, lat_len, lon_len)
    return pl.pallas_call(
        mix_kernel,
        out_shape=jax.ShapeDtypeStruct(out_shape, BF16),
        in_specs=[VMEM] * 8,
        out_specs=HBM,
        scratch_shapes=[pltpu.VMEM(out_shape, BF16), pltpu.SemaphoreType.DMA((OUT_COPIES,))],
        compiler_params=PARAMS,
    )(inner, border, core_a, core_b, own, position, mixer, offset)


def solution(mesh):
    placed = (
        P(None, "lat", "lon"),
        P("lat", "lon"),
        P("lat", "lon", None),
        P(),
        P("lon", None, None),
        P(),
        P(),
        P(),
        P(),
    )
    return jax.shard_map(
        on_device, mesh=mesh, in_specs=placed, out_specs=P(None, "lat", "lon"), check_vma=False
    )
```

```python
import functools

import jax
import jax.numpy as jnp
from jax import lax
from jax.experimental import pallas as pl
from jax.experimental.pallas import tpu as pltpu
from jax.sharding import PartitionSpec as P

KS = 5
REACH = KS // 2
PER_OWNER = 2
LANES = 128
EDGE = 2 * REACH
GROUP = 8
STEP = 4
OUT_COPIES = 4
IN_COPIES = 4
F32 = jnp.float32
BF16 = jnp.bfloat16
VMEM = pl.BlockSpec(memory_space=pltpu.VMEM)
SMEM = pl.BlockSpec(memory_space=pltpu.SMEM)
HBM = pl.BlockSpec(memory_space=pltpu.HBM)
PARAMS = pltpu.CompilerParams(vmem_limit_bytes=24 * 1024 * 1024)


def swap_pairs(count):
    first = [(i, i ^ 1) for i in range(count)]
    second = [(i, (i + 1 if i % 2 else i - 1) % count) for i in range(count)]
    return first, second


def in_hbm(array):
    return pltpu.with_memory_space_constraint(array, pltpu.HBM)


def lane_index(shape):
    return lax.broadcasted_iota(jnp.int32, shape, 1)


def start_copies(pairs, sems):
    copies = [pltpu.make_async_copy(source, target, sems.at[i]) for i, (source, target) in enumerate(pairs)]
    for copy in copies:
        copy.start()
    return copies


def in_parts(source, target, count):
    share = target.shape[0] // count
    return tuple((source.at[pl.ds(i * share, share)], target.at[pl.ds(i * share, share)]) for i in range(count))


def find_rows(list_ref, slot_ref, lon_count, held):
    me = lax.axis_index("lon")
    owners = (me, lax.rem(me + lon_count - 1, lon_count), lax.rem(me + 1, lon_count))
    slots = [slot_ref[list_ref[0, 0, i]] for i in range(list_ref.shape[2])]
    places, rows = [], []
    for owner in owners:
        least, greatest = jnp.int32(held), jnp.int32(-1)
        first, last = jnp.int32(0), jnp.int32(0)
        for i, slot in enumerate(slots):
            local = slot - owner * held
            hit = (local >= 0) & (local < held)
            first = jnp.where(hit & (local < least), i, first)
            last = jnp.where(hit & (local > greatest), i, last)
            least = jnp.where(hit, jnp.minimum(local, least), least)
            greatest = jnp.where(hit, jnp.maximum(local, greatest), greatest)
        places.append([first, last])
        rows.append([jnp.minimum(least, held - 1), jnp.maximum(greatest, 0)])
    return places, rows


class Held:
    names = ("own_rows", "position", "weights")
    sources = ("labels", "tap")

    def __init__(self, refs):
        self.__dict__.update(zip(self.names, refs))


def build_held(places, targets, held):
    labels_ref, tap_ref = targets
    even = (lax.axis_index("lon") % 2) == 0
    order = list(places[0])
    order += [jnp.where(even, places[2][nth], places[1][nth]) for nth in range(PER_OWNER)]
    order += [jnp.where(even, places[1][nth], places[2][nth]) for nth in range(PER_OWNER)]
    labels = labels_ref[...]
    position = jnp.zeros(labels.shape, jnp.int32)
    for index, place in enumerate(order):
        position = jnp.where(labels == place, index, position)
    held.position[...] = position

    tap_rank, taps = tap_ref.shape
    half = held.weights.shape[0] // tap_rank
    shape = (tap_rank * half, taps * half)
    spread = (
        lax.broadcasted_iota(jnp.int32, (shape[0], tap_rank), 0) // half == lane_index((shape[0], tap_rank))
    ).astype(BF16)
    repeat = (
        lax.broadcasted_iota(jnp.int32, (taps, shape[1]), 0) == lane_index((taps, shape[1])) // half
    ).astype(BF16)
    tall = jnp.dot(spread, tap_ref[...], preferred_element_type=F32).astype(BF16)
    wide = jnp.dot(tall, repeat, preferred_element_type=F32)
    same = lax.broadcasted_iota(jnp.int32, shape, 0) % half == lane_index(shape) % half
    held.weights[...] = jnp.where(same, wide, 0.0).astype(BF16)


def build_mixer(out_factor_ref, bias_ref, mixer_ref, offset_ref):
    rank, out_channels = out_factor_ref.shape
    shape = (out_channels * GROUP, rank * GROUP)
    spread = (
        lax.broadcasted_iota(jnp.int32, (shape[0], out_channels), 0) // GROUP
        == lane_index((shape[0], out_channels))
    ).astype(BF16)
    repeat = (
        lax.broadcasted_iota(jnp.int32, (rank, shape[1]), 0) == lane_index((rank, shape[1])) % rank
    ).astype(BF16)
    tall = lax.dot_general(
        spread, out_factor_ref[...], (((1,), (1,)), ((), ())), preferred_element_type=F32
    ).astype(BF16)
    wide = jnp.dot(tall, repeat, preferred_element_type=F32)
    same = lax.broadcasted_iota(jnp.int32, shape, 0) % GROUP == lane_index(shape) // rank
    mixer_ref[...] = jnp.where(same, wide, 0.0).astype(BF16)

    square = (out_channels, out_channels)
    diagonal = lax.broadcasted_iota(jnp.int32, square, 0) == lane_index(square)
    column = jnp.sum(jnp.where(diagonal, bias_ref[...], 0.0), axis=1, keepdims=True)
    rest = jnp.broadcast_to(column, (out_channels, offset_ref.shape[1]))
    total = jnp.zeros(offset_ref.shape, F32)
    for _ in range(3):
        piece = rest.astype(BF16)
        rest = rest - piece.astype(F32)
        total = total + jnp.dot(spread, piece, preferred_element_type=F32)
    offset_ref[...] = total


def asked_rows(list_ref, slots_ref, owner, held):
    lane = lane_index((1, LANES))
    found = []
    for i in range(list_ref.shape[2]):
        region = list_ref[0, 0, i]
        row = slots_ref[pl.ds(region // LANES, 1), :]
        found.append(jnp.where(lane == region % LANES, row - owner * held, -1))
    local = jnp.max(jnp.concatenate(found, axis=0), axis=1, keepdims=True)
    hit = (local >= 0) & (local < held)
    least = jnp.min(jnp.where(hit, local, held - 1), axis=0, keepdims=True)
    greatest = jnp.max(jnp.where(hit, local, 0), axis=0, keepdims=True)
    return least, greatest


def edge_kernel(lon_count, held_rows, *refs):
    list_hbm, slots_hbm, feat_hbm, in_hbm, pay_a_ref, pay_b_ref = refs[:6]
    list_ref, slots_ref, feat_ref, in_ref, turned_ref, sems = refs[6:]
    channels, lat_len, lon_len = feat_ref.shape
    rank = in_ref.shape[0]
    batch = LANES // EDGE
    pairs = in_parts(feat_hbm, feat_ref, IN_COPIES)
    pairs += ((slots_hbm, slots_ref), (list_hbm, list_ref), (in_hbm, in_ref))
    copies = start_copies(pairs, sems)
    for copy in copies:
        copy.wait()
    lane = lane_index((lat_len, LANES))
    for part in range(channels // batch):
        packed = jnp.zeros((lat_len, LANES), F32)
        for c in range(batch):
            moved = pltpu.roll(feat_ref[part * batch + c].astype(F32), (EDGE * c + REACH) % LANES, 1)
            packed = jnp.where(lane // EDGE == c, moved, packed)
        turned_ref[part * LANES : (part + 1) * LANES, :] = jnp.transpose(packed)
    columns = jnp.concatenate(
        [turned_ref[pl.ds(j, channels, stride=EDGE), :].astype(BF16) for j in range(EDGE)], axis=1
    )
    edges = jnp.dot(in_ref[...], columns, preferred_element_type=F32)
    edges = jnp.concatenate([edges, jnp.zeros((rank, LANES - EDGE * lat_len), F32)], axis=1)
    me = lax.axis_index("lon")
    even = (me % 2) == 0
    prev, following = lax.rem(me + lon_count - 1, lon_count), lax.rem(me + 1, lon_count)
    lane = lane_index((rank, LANES))
    for out_ref, owner in (
        (pay_a_ref, jnp.where(even, following, prev)),
        (pay_b_ref, jnp.where(even, prev, following)),
    ):
        load = edges
        for nth, row in enumerate(asked_rows(list_ref, slots_ref, owner, held_rows)):
            load = jnp.where(lane == EDGE * lat_len + nth, row.astype(F32), load)
        out_ref[...] = load.astype(BF16)


def reduce_tile(lat_len, feat_ref, in_ref, rows_ref, red_ref):
    channels, lon_len = feat_ref.shape[0], feat_ref.shape[2]
    rows_ref[...] = feat_ref[...].astype(F32).reshape(channels * lat_len, lon_len)
    cells = jnp.concatenate(
        [rows_ref[pl.ds(p, channels, stride=lat_len), :].astype(BF16) for p in range(lat_len)], axis=1
    )
    red_ref[...] = jnp.dot(in_ref[...], cells, preferred_element_type=F32).astype(BF16)


def prepare_kernel(lon_count, lat_len, *refs):
    list_hbm, slot_hbm, feat_hbm, in_hbm, bank_hbm = refs[:5]
    sources, red_ref, held = refs[5:7], refs[8], Held(refs[9:12])
    list_ref, slot_ref, feat_ref, in_ref, rows_ref = refs[12:17]
    targets, sems = refs[17:19], refs[19]
    pairs = ((list_hbm, list_ref), (slot_hbm, slot_ref)) + in_parts(feat_hbm, feat_ref, IN_COPIES)
    pairs += ((in_hbm, in_ref), *zip(sources, targets))
    for copy in start_copies(pairs, sems):
        copy.wait()
    places, rows = find_rows(list_ref, slot_ref, lon_count, bank_hbm.shape[0])
    lane = lane_index((1, LANES))
    own_rows = jnp.zeros((1, LANES), jnp.int32)
    for nth, row in enumerate(rows[0]):
        own_rows = jnp.where(lane == nth, row, own_rows)
    held.own_rows[...] = own_rows
    reduce_tile(lat_len, feat_ref, in_ref, rows_ref, red_ref)
    build_held(places, targets, held)


def pick_kernel(lat_len, got_b_ref, got_a_ref, own_rows_hbm, bank_ref, core_a_ref, core_b_ref):
    lane = lane_index((1, LANES))
    for got_ref, core_ref in ((got_b_ref, core_b_ref), (got_a_ref, core_a_ref)):
        head = got_ref[...].astype(F32)[0:1, :]
        for nth in range(PER_OWNER):
            row = jnp.sum(jnp.where(lane == EDGE * lat_len + nth, head, 0.0)).astype(jnp.int32)
            core_ref[nth] = bank_ref[row]


def rows_kernel(lat_len, got_b_ref, got_a_ref, core_ref, red_ref, edge_ref, row_a_ref, row_b_ref):
    lon_len = red_ref.shape[1] // lat_len
    even = (lax.axis_index("lon") % 2) == 0
    from_prev = lane_index(got_a_ref.shape) < REACH * lat_len
    got = jnp.where(from_prev == even, got_b_ref[...].astype(F32), got_a_ref[...].astype(F32)).astype(BF16)
    source = lax.broadcasted_iota(jnp.int32, (LANES, LANES), 0)
    target = lane_index((LANES, LANES))
    order = (source == (target % EDGE) * lat_len + target // EDGE) & (target < EDGE * lat_len)
    edges = jnp.dot(got, order.astype(BF16), preferred_element_type=F32).astype(BF16)
    edge_ref[...] = edges
    even = (lax.axis_index("lat") % 2) == 0
    head = red_ref[:, : REACH * lon_len].astype(F32)
    tail = red_ref[:, (lat_len - REACH) * lon_len :].astype(F32)
    row_a_ref[:, : REACH * lon_len] = jnp.where(even, tail, head).astype(BF16)
    row_b_ref[:, : REACH * lon_len] = jnp.where(even, head, tail).astype(BF16)
    row_a_ref[:, REACH * lon_len :] = edges
    row_b_ref[:, REACH * lon_len :] = edges


def shifted_columns(row, edges, place):
    lane = lane_index(row.shape)
    lon_len = row.shape[1]
    edges = pltpu.roll(edges, (LANES - REACH - EDGE * place) % LANES, 1)
    moved = []
    for col_off in range(KS):
        shift = REACH - col_off
        if shift > 0:
            piece = pltpu.roll(jnp.where(lane >= lon_len - shift, edges, row), shift, 1)
        elif shift < 0:
            piece = pltpu.roll(jnp.where(lane < -shift, edges, row), lon_len + shift, 1)
        else:
            piece = row
        moved.append(piece.astype(BF16))
    return moved


def stack_row(stack_ref, p, moved, slots, lon_len):
    half = moved[0].shape[0] // 2
    for col_off, piece in enumerate(moved):
        for row_off in range(KS):
            slot = slots.get(p + REACH - row_off)
            if slot is not None:
                k = row_off * KS + col_off
                for h in range(2):
                    stack_ref[h, k * half : (k + 1) * half, slot * lon_len : (slot + 1) * lon_len] = piece[
                        h * half : (h + 1) * half
                    ]


def apply_taps(rank, weights_ref, stacked, tapped_ref, lon_len):
    half = rank // 2
    tap_rank = tapped_ref.shape[0] // rank
    width = STEP * lon_len
    for start in range(0, tapped_ref.shape[1], width):
        parts = [
            jnp.dot(weights_ref[...], stacked(h, start, width), preferred_element_type=F32)
            .astype(BF16)
            .reshape(tap_rank, 1, half, width)
            for h in range(2)
        ]
        tapped_ref[:, start : start + width] = jnp.concatenate(parts, axis=1).reshape(tap_rank * rank, width)


def border_slots(lat_len):
    slots = {p: p for p in range(REACH)}
    slots.update({lat_len - REACH + p: REACH + p for p in range(REACH)})
    return slots


def inner_kernel(
    lat_len,
    red_ref,
    edge_ref,
    weights_ref,
    out_factor_ref,
    bias_ref,
    own_rows_ref,
    bank_ref,
    tapped_ref,
    halo_stack_ref,
    mixer_ref,
    offset_ref,
    own_ref,
    stack_ref,
):
    rank = red_ref.shape[0]
    head = own_rows_ref[...].astype(F32)
    for nth in range(PER_OWNER):
        row = jnp.sum(jnp.where(lane_index((1, LANES)) == nth, head, 0.0)).astype(jnp.int32)
        own_ref[nth] = bank_ref[row]
    build_mixer(out_factor_ref, bias_ref, mixer_ref, offset_ref)
    lon_len = red_ref.shape[1] // lat_len
    slots = {p: p - REACH for p in range(REACH, lat_len - REACH)}
    edges = edge_ref[...].astype(F32)
    for p in range(lat_len):
        row = red_ref[:, p * lon_len : (p + 1) * lon_len].astype(F32)
        moved = shifted_columns(row, edges, p)
        stack_row(stack_ref, p, moved, slots, lon_len)
        stack_row(halo_stack_ref, p, moved, border_slots(lat_len), lon_len)
    apply_taps(rank, weights_ref, lambda h, start, width: stack_ref[h, :, start : start + width], tapped_ref, lon_len)


def border_kernel(lat_len, lat_count, row_b_ref, row_a_ref, weights_ref, own_stack_ref, tapped_ref, stack_ref):
    rank = row_a_ref.shape[0]
    lon_len = (row_a_ref.shape[1] - LANES) // REACH
    lat = lax.axis_index("lat")
    even = (lat % 2) == 0
    row_a = row_a_ref[...].astype(F32)
    row_b = row_b_ref[...].astype(F32)
    above = jnp.where(lat == 0, 0.0, jnp.where(even, row_b, row_a))
    below = jnp.where(lat == lat_count - 1, 0.0, jnp.where(even, row_a, row_b))
    slots = border_slots(lat_len)
    for i in range(REACH):
        for p, holder, place in ((i - REACH, above, lat_len - REACH + i), (lat_len + i, below, i)):
            row = holder[:, i * lon_len : (i + 1) * lon_len]
            moved = shifted_columns(row, holder[:, REACH * lon_len :], place)
            stack_row(stack_ref, p, moved, slots, lon_len)
    block = KS * rank // 2
    in_halo = {
        (slot, row_off)
        for p, slot in slots.items()
        for row_off in range(KS)
        if not 0 <= p + row_off - REACH < lat_len
    }

    def stacked(h, start, width):
        columns = []
        for slot in range(start // lon_len, (start + width) // lon_len):
            span = slice(slot * lon_len, (slot + 1) * lon_len)
            pieces = []
            for row_off in range(KS):
                ref = stack_ref if (slot, row_off) in in_halo else own_stack_ref
                pieces.append(ref[h, row_off * block : (row_off + 1) * block, span])
            columns.append(jnp.concatenate(pieces, axis=0))
        return jnp.concatenate(columns, axis=1)

    apply_taps(rank, weights_ref, stacked, tapped_ref, lon_len)


def mix_kernel(
    inner_ref,
    border_ref,
    core_a_ref,
    core_b_ref,
    own_ref,
    position_ref,
    mixer_ref,
    offset_ref,
    out_hbm,
    stage_ref,
    sems,
):
    lat_len, lon_len = position_ref.shape
    rank = own_ref.shape[1]
    cores = jnp.concatenate(
        [ref[...].reshape(PER_OWNER * rank, -1) for ref in (own_ref, core_a_ref, core_b_ref)], axis=0
    )
    chunks = [(border_ref, 0, [*range(REACH), *range(lat_len - REACH, lat_len)])]
    for start in range(REACH, lat_len - REACH, STEP):
        chunks.append((inner_ref, start - REACH, [*range(start, start + STEP)]))
    by_row = {}
    for ref, first, rows in chunks:
        width = len(rows) * lon_len
        every = jnp.dot(cores, ref[:, first * lon_len : first * lon_len + width], preferred_element_type=F32)
        position = jnp.concatenate([position_ref[r : r + 1, :] for r in rows], axis=1)
        hidden = jnp.zeros((rank, width), F32)
        for index in range(3 * PER_OWNER):
            hidden = jnp.where(position == index, every[index * rank : (index + 1) * rank], hidden)
        hidden = hidden.astype(BF16)
        for i, r in enumerate(rows):
            by_row[r] = hidden[:, i * lon_len : (i + 1) * lon_len]
    pieces = [by_row[r] for r in range(lat_len)]
    groups = [jnp.concatenate(pieces[g : g + GROUP], axis=0) for g in range(0, lat_len, GROUP)]
    channels = stage_ref.shape[0]
    share = channels // OUT_COPIES
    outputs = [jnp.dot(mixer_ref[...], hidden, preferred_element_type=F32) for hidden in groups]
    copies = []
    for part in range(OUT_COPIES):
        span = slice(part * share * GROUP, (part + 1) * share * GROUP)
        blocks = []
        for output in outputs:
            output = output[span] + offset_ref[span, :]
            mixed = 0.5 * output * (1.0 + jnp.tanh(0.5 * output))
            blocks.append(mixed.reshape(share, GROUP, lon_len))
        held = slice(part * share, (part + 1) * share)
        stage_ref[held] = jnp.concatenate(blocks, axis=1).astype(BF16)
        copy = pltpu.make_async_copy(stage_ref.at[held], out_hbm.at[held], sems.at[part])
        copy.start()
        copies.append(copy)
    for copy in copies:
        copy.wait()


def on_device(
    features, labels, tile_regions, bank_slot, kernel_bank, in_factor, tap_factor, out_factor, out_bias
):
    channels, lat_len, lon_len = features.shape
    rank = in_factor.shape[0]
    held, core_rows, core_cols = kernel_bank.shape
    tap_rank, taps = tap_factor.shape
    out_channels = out_factor.shape[0]
    cells = lat_len * lon_len
    lon_count, lat_count = lax.axis_size("lon"), lax.axis_size("lat")
    lon_first, lon_second = swap_pairs(lon_count)
    lat_first, lat_second = swap_pairs(lat_count)
    edge_shape = jax.ShapeDtypeStruct((rank, LANES), BF16)
    core_shape = jax.ShapeDtypeStruct((PER_OWNER, core_rows, core_cols), BF16)
    held_shapes = (
        jax.ShapeDtypeStruct((1, LANES), jnp.int32),
        jax.ShapeDtypeStruct(labels.shape, jnp.int32),
        jax.ShapeDtypeStruct((tap_rank * rank // 2, taps * rank // 2), BF16),
    )
    lists = [
        pltpu.SMEM(tile_regions.shape, jnp.int32),
        pltpu.SMEM(bank_slot.shape, jnp.int32),
        pltpu.VMEM(features.shape, BF16),
        pltpu.VMEM(in_factor.shape, BF16),
    ]
    targets = [
        pltpu.VMEM(labels.shape, jnp.int32),
        pltpu.VMEM(tap_factor.shape, BF16),
    ]
    sources = tuple(
        in_hbm(x)
        for x in (
            tile_regions,
            bank_slot,
            features,
            in_factor,
            kernel_bank,
            labels,
            tap_factor,
        )
    )
    pay_a, pay_b = pl.pallas_call(
        functools.partial(edge_kernel, lon_count, held),
        out_shape=(edge_shape, edge_shape),
        in_specs=[HBM] * 4,
        out_specs=(VMEM,) * 2,
        scratch_shapes=[
            lists[0],
            pltpu.VMEM((bank_slot.shape[0] // LANES, LANES), jnp.int32),
            *lists[2:],
            pltpu.VMEM((channels * EDGE, lat_len), F32),
            pltpu.SemaphoreType.DMA((IN_COPIES + 3,)),
        ],
        compiler_params=PARAMS,
        cost_estimate=pl.CostEstimate(flops=2 * 10**9, bytes_accessed=4 * 10**6, transcendentals=0),
    )(sources[0], in_hbm(bank_slot.reshape(-1, LANES)), *sources[2:4])
    got_b = lax.ppermute(pay_b, "lon", lon_second)
    got_a = lax.ppermute(pay_a, "lon", lon_first)
    reduced, own_rows, position, weights = pl.pallas_call(
        functools.partial(prepare_kernel, lon_count, lat_len),
        out_shape=(jax.ShapeDtypeStruct((rank, cells), BF16), *held_shapes),
        in_specs=[HBM] * 8,
        out_specs=(VMEM,) * 4,
        scratch_shapes=[
            *lists,
            pltpu.VMEM((channels * lat_len, lon_len), F32),
            *targets,
            pltpu.SemaphoreType.DMA((IN_COPIES + 5,)),
        ],
        compiler_params=PARAMS,
        cost_estimate=pl.CostEstimate(flops=10**5, bytes_accessed=10**5, transcendentals=0),
    )(*sources, pay_a)
    row_shape = jax.ShapeDtypeStruct((rank, REACH * lon_len + LANES), BF16)
    core_a, core_b = pl.pallas_call(
        functools.partial(pick_kernel, lat_len),
        out_shape=(core_shape, core_shape),
        in_specs=[VMEM, VMEM, HBM, VMEM],
        out_specs=(VMEM,) * 2,
        compiler_params=PARAMS,
    )(got_b, got_a, own_rows, kernel_bank)
    edges, row_a, row_b = pl.pallas_call(
        functools.partial(rows_kernel, lat_len),
        out_shape=(edge_shape, row_shape, row_shape),
        in_specs=[VMEM, VMEM, HBM, VMEM],
        out_specs=(VMEM,) * 3,
        compiler_params=PARAMS,
    )(got_b, got_a, core_b, reduced)
    core_b = lax.ppermute(core_b, "lon", lon_second)
    core_a = lax.ppermute(core_a, "lon", lon_first)
    row_a = lax.ppermute(row_a, "lat", lat_first)
    row_b = lax.ppermute(row_b, "lat", lat_second)
    border_cells = 2 * REACH * lon_len
    stack_rows = taps * rank // 2
    halo_stack_shape = jax.ShapeDtypeStruct((2, stack_rows, border_cells), BF16)
    inner, halo_stack, mixer, offset, own = pl.pallas_call(
        functools.partial(inner_kernel, lat_len),
        out_shape=(
            jax.ShapeDtypeStruct((tap_rank * rank, cells - border_cells), BF16),
            halo_stack_shape,
            jax.ShapeDtypeStruct((out_channels * GROUP, rank * GROUP), BF16),
            jax.ShapeDtypeStruct((out_channels * GROUP, lon_len), F32),
            core_shape,
        ),
        in_specs=[VMEM] * 7,
        out_specs=(VMEM,) * 5,
        scratch_shapes=[pltpu.VMEM((2, stack_rows, cells - border_cells), BF16)],
        compiler_params=PARAMS,
    )(reduced, edges, weights, out_factor.T, out_bias.reshape(1, -1), own_rows, kernel_bank)
    border = pl.pallas_call(
        functools.partial(border_kernel, lat_len, lat_count),
        out_shape=jax.ShapeDtypeStruct((tap_rank * rank, border_cells), BF16),
        in_specs=[VMEM] * 4,
        out_specs=VMEM,
        scratch_shapes=[pltpu.VMEM(halo_stack_shape.shape, BF16)],
        compiler_params=PARAMS,
    )(row_b, row_a, weights, halo_stack)
    out_shape = (out_channels, lat_len, lon_len)
    return pl.pallas_call(
        mix_kernel,
        out_shape=jax.ShapeDtypeStruct(out_shape, BF16),
        in_specs=[VMEM] * 8,
        out_specs=HBM,
        scratch_shapes=[pltpu.VMEM(out_shape, BF16), pltpu.SemaphoreType.DMA((OUT_COPIES,))],
        compiler_params=PARAMS,
    )(inner, border, core_a, core_b, own, position, mixer, offset)


def solution(mesh):
    placed = (
        P(None, "lat", "lon"),
        P("lat", "lon"),
        P("lat", "lon", None),
        P(),
        P("lon", None, None),
        P(),
        P(),
        P(),
        P(),
    )
    return jax.shard_map(
        on_device, mesh=mesh, in_specs=placed, out_specs=P(None, "lat", "lon"), check_vma=False
    )
```

```python
import functools

import jax
import jax.numpy as jnp
from jax import lax
from jax.experimental import pallas as pl
from jax.experimental.pallas import tpu as pltpu
from jax.sharding import PartitionSpec as P

KS = 5
REACH = KS // 2
PER_OWNER = 2
LANES = 128
EDGE = 2 * REACH
GROUP = 8
STEP = 4
OUT_COPIES = 4
IN_COPIES = 1
F32 = jnp.float32
BF16 = jnp.bfloat16
VMEM = pl.BlockSpec(memory_space=pltpu.VMEM)
SMEM = pl.BlockSpec(memory_space=pltpu.SMEM)
HBM = pl.BlockSpec(memory_space=pltpu.HBM)
PARAMS = pltpu.CompilerParams(vmem_limit_bytes=24 * 1024 * 1024)


def swap_pairs(count):
    first = [(i, i ^ 1) for i in range(count)]
    second = [(i, (i + 1 if i % 2 else i - 1) % count) for i in range(count)]
    return first, second


def in_hbm(array):
    return pltpu.with_memory_space_constraint(array, pltpu.HBM)


def lane_index(shape):
    return lax.broadcasted_iota(jnp.int32, shape, 1)


def start_copies(pairs, sems):
    copies = [pltpu.make_async_copy(source, target, sems.at[i]) for i, (source, target) in enumerate(pairs)]
    for copy in copies:
        copy.start()
    return copies


def in_parts(source, target, count):
    share = target.shape[0] // count
    return tuple((source.at[pl.ds(i * share, share)], target.at[pl.ds(i * share, share)]) for i in range(count))


def find_rows(list_ref, slot_ref, lon_count, held):
    me = lax.axis_index("lon")
    owners = (me, lax.rem(me + lon_count - 1, lon_count), lax.rem(me + 1, lon_count))
    slots = [slot_ref[list_ref[0, 0, i]] for i in range(list_ref.shape[2])]
    places, rows = [], []
    for owner in owners:
        least, greatest = jnp.int32(held), jnp.int32(-1)
        first, last = jnp.int32(0), jnp.int32(0)
        for i, slot in enumerate(slots):
            local = slot - owner * held
            hit = (local >= 0) & (local < held)
            first = jnp.where(hit & (local < least), i, first)
            last = jnp.where(hit & (local > greatest), i, last)
            least = jnp.where(hit, jnp.minimum(local, least), least)
            greatest = jnp.where(hit, jnp.maximum(local, greatest), greatest)
        places.append([first, last])
        rows.append([jnp.minimum(least, held - 1), jnp.maximum(greatest, 0)])
    return places, rows


class Held:
    names = ("own_rows", "position", "weights")
    sources = ("labels", "tap")

    def __init__(self, refs):
        self.__dict__.update(zip(self.names, refs))


def build_held(places, targets, held):
    labels_ref, tap_ref = targets
    even = (lax.axis_index("lon") % 2) == 0
    order = list(places[0])
    order += [jnp.where(even, places[2][nth], places[1][nth]) for nth in range(PER_OWNER)]
    order += [jnp.where(even, places[1][nth], places[2][nth]) for nth in range(PER_OWNER)]
    labels = labels_ref[...]
    position = jnp.zeros(labels.shape, jnp.int32)
    for index, place in enumerate(order):
        position = jnp.where(labels == place, index, position)
    held.position[...] = position

    tap_rank, taps = tap_ref.shape
    half = held.weights.shape[0] // tap_rank
    shape = (tap_rank * half, taps * half)
    spread = (
        lax.broadcasted_iota(jnp.int32, (shape[0], tap_rank), 0) // half == lane_index((shape[0], tap_rank))
    ).astype(BF16)
    repeat = (
        lax.broadcasted_iota(jnp.int32, (taps, shape[1]), 0) == lane_index((taps, shape[1])) // half
    ).astype(BF16)
    tall = jnp.dot(spread, tap_ref[...], preferred_element_type=F32).astype(BF16)
    wide = jnp.dot(tall, repeat, preferred_element_type=F32)
    same = lax.broadcasted_iota(jnp.int32, shape, 0) % half == lane_index(shape) % half
    held.weights[...] = jnp.where(same, wide, 0.0).astype(BF16)


def build_mixer(out_factor_ref, bias_ref, mixer_ref, offset_ref):
    rank, out_channels = out_factor_ref.shape
    shape = (out_channels * GROUP, rank * GROUP)
    spread = (
        lax.broadcasted_iota(jnp.int32, (shape[0], out_channels), 0) // GROUP
        == lane_index((shape[0], out_channels))
    ).astype(BF16)
    repeat = (
        lax.broadcasted_iota(jnp.int32, (rank, shape[1]), 0) == lane_index((rank, shape[1])) % rank
    ).astype(BF16)
    tall = lax.dot_general(
        spread, out_factor_ref[...], (((1,), (1,)), ((), ())), preferred_element_type=F32
    ).astype(BF16)
    wide = jnp.dot(tall, repeat, preferred_element_type=F32)
    same = lax.broadcasted_iota(jnp.int32, shape, 0) % GROUP == lane_index(shape) // rank
    mixer_ref[...] = jnp.where(same, wide, 0.0).astype(BF16)

    square = (out_channels, out_channels)
    diagonal = lax.broadcasted_iota(jnp.int32, square, 0) == lane_index(square)
    column = jnp.sum(jnp.where(diagonal, bias_ref[...], 0.0), axis=1, keepdims=True)
    rest = jnp.broadcast_to(column, (out_channels, offset_ref.shape[1]))
    total = jnp.zeros(offset_ref.shape, F32)
    for _ in range(3):
        piece = rest.astype(BF16)
        rest = rest - piece.astype(F32)
        total = total + jnp.dot(spread, piece, preferred_element_type=F32)
    offset_ref[...] = total


def asked_rows(list_ref, slots_ref, owner, held):
    lane = lane_index((1, LANES))
    found = []
    for i in range(list_ref.shape[2]):
        region = list_ref[0, 0, i]
        row = slots_ref[pl.ds(region // LANES, 1), :]
        found.append(jnp.where(lane == region % LANES, row - owner * held, -1))
    local = jnp.max(jnp.concatenate(found, axis=0), axis=1, keepdims=True)
    hit = (local >= 0) & (local < held)
    least = jnp.min(jnp.where(hit, local, held - 1), axis=0, keepdims=True)
    greatest = jnp.max(jnp.where(hit, local, 0), axis=0, keepdims=True)
    return least, greatest


def edge_kernel(lon_count, held_rows, *refs):
    list_hbm, slots_hbm, feat_hbm, in_hbm, pay_a_ref, pay_b_ref = refs[:6]
    list_ref, slots_ref, feat_ref, in_ref, turned_ref, sems = refs[6:]
    channels, lat_len, lon_len = feat_ref.shape
    rank = in_ref.shape[0]
    batch = LANES // EDGE
    pairs = in_parts(feat_hbm, feat_ref, IN_COPIES)
    pairs += ((slots_hbm, slots_ref), (list_hbm, list_ref), (in_hbm, in_ref))
    copies = start_copies(pairs, sems)
    for copy in copies:
        copy.wait()
    lane = lane_index((lat_len, LANES))
    for part in range(channels // batch):
        packed = jnp.zeros((lat_len, LANES), F32)
        for c in range(batch):
            moved = pltpu.roll(feat_ref[part * batch + c].astype(F32), (EDGE * c + REACH) % LANES, 1)
            packed = jnp.where(lane // EDGE == c, moved, packed)
        turned_ref[part * LANES : (part + 1) * LANES, :] = jnp.transpose(packed)
    columns = jnp.concatenate(
        [turned_ref[pl.ds(j, channels, stride=EDGE), :].astype(BF16) for j in range(EDGE)], axis=1
    )
    edges = jnp.dot(in_ref[...], columns, preferred_element_type=F32)
    edges = jnp.concatenate([edges, jnp.zeros((rank, LANES - EDGE * lat_len), F32)], axis=1)
    me = lax.axis_index("lon")
    even = (me % 2) == 0
    prev, following = lax.rem(me + lon_count - 1, lon_count), lax.rem(me + 1, lon_count)
    lane = lane_index((rank, LANES))
    for out_ref, owner in (
        (pay_a_ref, jnp.where(even, following, prev)),
        (pay_b_ref, jnp.where(even, prev, following)),
    ):
        load = edges
        for nth, row in enumerate(asked_rows(list_ref, slots_ref, owner, held_rows)):
            load = jnp.where(lane == EDGE * lat_len + nth, row.astype(F32), load)
        out_ref[...] = load.astype(BF16)


def reduce_tile(lat_len, feat_ref, in_ref, rows_ref, red_ref):
    channels, lon_len = feat_ref.shape[0], feat_ref.shape[2]
    rows_ref[...] = feat_ref[...].astype(F32).reshape(channels * lat_len, lon_len)
    cells = jnp.concatenate(
        [rows_ref[pl.ds(p, channels, stride=lat_len), :].astype(BF16) for p in range(lat_len)], axis=1
    )
    red_ref[...] = jnp.dot(in_ref[...], cells, preferred_element_type=F32).astype(BF16)


def prepare_kernel(lon_count, lat_len, *refs):
    list_hbm, slot_hbm, feat_hbm, in_hbm, bank_hbm = refs[:5]
    sources, red_ref, held = refs[5:7], refs[8], Held(refs[9:12])
    list_ref, slot_ref, feat_ref, in_ref, rows_ref = refs[12:17]
    targets, sems = refs[17:19], refs[19]
    pairs = ((list_hbm, list_ref), (slot_hbm, slot_ref)) + in_parts(feat_hbm, feat_ref, IN_COPIES)
    pairs += ((in_hbm, in_ref), *zip(sources, targets))
    for copy in start_copies(pairs, sems):
        copy.wait()
    places, rows = find_rows(list_ref, slot_ref, lon_count, bank_hbm.shape[0])
    lane = lane_index((1, LANES))
    own_rows = jnp.zeros((1, LANES), jnp.int32)
    for nth, row in enumerate(rows[0]):
        own_rows = jnp.where(lane == nth, row, own_rows)
    held.own_rows[...] = own_rows
    reduce_tile(lat_len, feat_ref, in_ref, rows_ref, red_ref)
    build_held(places, targets, held)


def pick_kernel(lat_len, got_b_ref, got_a_ref, own_rows_hbm, bank_ref, core_a_ref, core_b_ref):
    lane = lane_index((1, LANES))
    for got_ref, core_ref in ((got_b_ref, core_b_ref), (got_a_ref, core_a_ref)):
        head = got_ref[...].astype(F32)[0:1, :]
        for nth in range(PER_OWNER):
            row = jnp.sum(jnp.where(lane == EDGE * lat_len + nth, head, 0.0)).astype(jnp.int32)
            core_ref[nth] = bank_ref[row]


def rows_kernel(lat_len, got_b_ref, got_a_ref, core_ref, red_ref, edge_ref, row_a_ref, row_b_ref):
    lon_len = red_ref.shape[1] // lat_len
    even = (lax.axis_index("lon") % 2) == 0
    from_prev = lane_index(got_a_ref.shape) < REACH * lat_len
    got = jnp.where(from_prev == even, got_b_ref[...].astype(F32), got_a_ref[...].astype(F32)).astype(BF16)
    source = lax.broadcasted_iota(jnp.int32, (LANES, LANES), 0)
    target = lane_index((LANES, LANES))
    order = (source == (target % EDGE) * lat_len + target // EDGE) & (target < EDGE * lat_len)
    edges = jnp.dot(got, order.astype(BF16), preferred_element_type=F32).astype(BF16)
    edge_ref[...] = edges
    even = (lax.axis_index("lat") % 2) == 0
    head = red_ref[:, : REACH * lon_len].astype(F32)
    tail = red_ref[:, (lat_len - REACH) * lon_len :].astype(F32)
    row_a_ref[:, : REACH * lon_len] = jnp.where(even, tail, head).astype(BF16)
    row_b_ref[:, : REACH * lon_len] = jnp.where(even, head, tail).astype(BF16)
    row_a_ref[:, REACH * lon_len :] = edges
    row_b_ref[:, REACH * lon_len :] = edges


def shifted_columns(row, edges, place):
    lane = lane_index(row.shape)
    lon_len = row.shape[1]
    edges = pltpu.roll(edges, (LANES - REACH - EDGE * place) % LANES, 1)
    moved = []
    for col_off in range(KS):
        shift = REACH - col_off
        if shift > 0:
            piece = pltpu.roll(jnp.where(lane >= lon_len - shift, edges, row), shift, 1)
        elif shift < 0:
            piece = pltpu.roll(jnp.where(lane < -shift, edges, row), lon_len + shift, 1)
        else:
            piece = row
        moved.append(piece.astype(BF16))
    return moved


def stack_row(stack_ref, p, moved, slots, lon_len):
    half = moved[0].shape[0] // 2
    for col_off, piece in enumerate(moved):
        for row_off in range(KS):
            slot = slots.get(p + REACH - row_off)
            if slot is not None:
                k = row_off * KS + col_off
                for h in range(2):
                    stack_ref[h, k * half : (k + 1) * half, slot * lon_len : (slot + 1) * lon_len] = piece[
                        h * half : (h + 1) * half
                    ]


def apply_taps(rank, weights_ref, stacked, tapped_ref, lon_len):
    half = rank // 2
    tap_rank = tapped_ref.shape[0] // rank
    width = STEP * lon_len
    for start in range(0, tapped_ref.shape[1], width):
        parts = [
            jnp.dot(weights_ref[...], stacked(h, start, width), preferred_element_type=F32)
            .astype(BF16)
            .reshape(tap_rank, 1, half, width)
            for h in range(2)
        ]
        tapped_ref[:, start : start + width] = jnp.concatenate(parts, axis=1).reshape(tap_rank * rank, width)


def border_slots(lat_len):
    slots = {p: p for p in range(REACH)}
    slots.update({lat_len - REACH + p: REACH + p for p in range(REACH)})
    return slots


def inner_kernel(
    lat_len,
    red_ref,
    edge_ref,
    weights_ref,
    out_factor_ref,
    bias_ref,
    own_rows_ref,
    bank_ref,
    tapped_ref,
    halo_stack_ref,
    mixer_ref,
    offset_ref,
    own_ref,
    stack_ref,
):
    rank = red_ref.shape[0]
    head = own_rows_ref[...].astype(F32)
    for nth in range(PER_OWNER):
        row = jnp.sum(jnp.where(lane_index((1, LANES)) == nth, head, 0.0)).astype(jnp.int32)
        own_ref[nth] = bank_ref[row]
    build_mixer(out_factor_ref, bias_ref, mixer_ref, offset_ref)
    lon_len = red_ref.shape[1] // lat_len
    slots = {p: p - REACH for p in range(REACH, lat_len - REACH)}
    edges = edge_ref[...].astype(F32)
    for p in range(lat_len):
        row = red_ref[:, p * lon_len : (p + 1) * lon_len].astype(F32)
        moved = shifted_columns(row, edges, p)
        stack_row(stack_ref, p, moved, slots, lon_len)
        stack_row(halo_stack_ref, p, moved, border_slots(lat_len), lon_len)
    apply_taps(rank, weights_ref, lambda h, start, width: stack_ref[h, :, start : start + width], tapped_ref, lon_len)


def border_kernel(lat_len, lat_count, row_b_ref, row_a_ref, weights_ref, own_stack_ref, tapped_ref, stack_ref):
    rank = row_a_ref.shape[0]
    lon_len = (row_a_ref.shape[1] - LANES) // REACH
    lat = lax.axis_index("lat")
    even = (lat % 2) == 0
    row_a = row_a_ref[...].astype(F32)
    row_b = row_b_ref[...].astype(F32)
    above = jnp.where(lat == 0, 0.0, jnp.where(even, row_b, row_a))
    below = jnp.where(lat == lat_count - 1, 0.0, jnp.where(even, row_a, row_b))
    slots = border_slots(lat_len)
    for i in range(REACH):
        for p, holder, place in ((i - REACH, above, lat_len - REACH + i), (lat_len + i, below, i)):
            row = holder[:, i * lon_len : (i + 1) * lon_len]
            moved = shifted_columns(row, holder[:, REACH * lon_len :], place)
            stack_row(stack_ref, p, moved, slots, lon_len)
    block = KS * rank // 2
    in_halo = {
        (slot, row_off)
        for p, slot in slots.items()
        for row_off in range(KS)
        if not 0 <= p + row_off - REACH < lat_len
    }

    def stacked(h, start, width):
        columns = []
        for slot in range(start // lon_len, (start + width) // lon_len):
            span = slice(slot * lon_len, (slot + 1) * lon_len)
            pieces = []
            for row_off in range(KS):
                ref = stack_ref if (slot, row_off) in in_halo else own_stack_ref
                pieces.append(ref[h, row_off * block : (row_off + 1) * block, span])
            columns.append(jnp.concatenate(pieces, axis=0))
        return jnp.concatenate(columns, axis=1)

    apply_taps(rank, weights_ref, stacked, tapped_ref, lon_len)


def mix_kernel(
    inner_ref,
    border_ref,
    core_a_ref,
    core_b_ref,
    own_ref,
    position_ref,
    mixer_ref,
    offset_ref,
    out_hbm,
    stage_ref,
    sems,
):
    lat_len, lon_len = position_ref.shape
    rank = own_ref.shape[1]
    cores = jnp.concatenate(
        [ref[...].reshape(PER_OWNER * rank, -1) for ref in (own_ref, core_a_ref, core_b_ref)], axis=0
    )
    chunks = [(border_ref, 0, [*range(REACH), *range(lat_len - REACH, lat_len)])]
    for start in range(REACH, lat_len - REACH, STEP):
        chunks.append((inner_ref, start - REACH, [*range(start, start + STEP)]))
    by_row = {}
    for ref, first, rows in chunks:
        width = len(rows) * lon_len
        every = jnp.dot(cores, ref[:, first * lon_len : first * lon_len + width], preferred_element_type=F32)
        position = jnp.concatenate([position_ref[r : r + 1, :] for r in rows], axis=1)
        hidden = jnp.zeros((rank, width), F32)
        for index in range(3 * PER_OWNER):
            hidden = jnp.where(position == index, every[index * rank : (index + 1) * rank], hidden)
        hidden = hidden.astype(BF16)
        for i, r in enumerate(rows):
            by_row[r] = hidden[:, i * lon_len : (i + 1) * lon_len]
    pieces = [by_row[r] for r in range(lat_len)]
    groups = [jnp.concatenate(pieces[g : g + GROUP], axis=0) for g in range(0, lat_len, GROUP)]
    channels = stage_ref.shape[0]
    share = channels // OUT_COPIES
    outputs = [jnp.dot(mixer_ref[...], hidden, preferred_element_type=F32) for hidden in groups]
    copies = []
    for part in range(OUT_COPIES):
        span = slice(part * share * GROUP, (part + 1) * share * GROUP)
        blocks = []
        for output in outputs:
            output = output[span] + offset_ref[span, :]
            mixed = 0.5 * output * (1.0 + jnp.tanh(0.5 * output))
            blocks.append(mixed.reshape(share, GROUP, lon_len))
        held = slice(part * share, (part + 1) * share)
        stage_ref[held] = jnp.concatenate(blocks, axis=1).astype(BF16)
        copy = pltpu.make_async_copy(stage_ref.at[held], out_hbm.at[held], sems.at[part])
        copy.start()
        copies.append(copy)
    for copy in copies:
        copy.wait()


def on_device(
    features, labels, tile_regions, bank_slot, kernel_bank, in_factor, tap_factor, out_factor, out_bias
):
    channels, lat_len, lon_len = features.shape
    rank = in_factor.shape[0]
    held, core_rows, core_cols = kernel_bank.shape
    tap_rank, taps = tap_factor.shape
    out_channels = out_factor.shape[0]
    cells = lat_len * lon_len
    lon_count, lat_count = lax.axis_size("lon"), lax.axis_size("lat")
    lon_first, lon_second = swap_pairs(lon_count)
    lat_first, lat_second = swap_pairs(lat_count)
    edge_shape = jax.ShapeDtypeStruct((rank, LANES), BF16)
    core_shape = jax.ShapeDtypeStruct((PER_OWNER, core_rows, core_cols), BF16)
    held_shapes = (
        jax.ShapeDtypeStruct((1, LANES), jnp.int32),
        jax.ShapeDtypeStruct(labels.shape, jnp.int32),
        jax.ShapeDtypeStruct((tap_rank * rank // 2, taps * rank // 2), BF16),
    )
    lists = [
        pltpu.SMEM(tile_regions.shape, jnp.int32),
        pltpu.SMEM(bank_slot.shape, jnp.int32),
        pltpu.VMEM(features.shape, BF16),
        pltpu.VMEM(in_factor.shape, BF16),
    ]
    targets = [
        pltpu.VMEM(labels.shape, jnp.int32),
        pltpu.VMEM(tap_factor.shape, BF16),
    ]
    sources = tuple(
        in_hbm(x)
        for x in (
            tile_regions,
            bank_slot,
            features,
            in_factor,
            kernel_bank,
            labels,
            tap_factor,
        )
    )
    pay_a, pay_b = pl.pallas_call(
        functools.partial(edge_kernel, lon_count, held),
        out_shape=(edge_shape, edge_shape),
        in_specs=[HBM] * 4,
        out_specs=(VMEM,) * 2,
        scratch_shapes=[
            lists[0],
            pltpu.VMEM((bank_slot.shape[0] // LANES, LANES), jnp.int32),
            *lists[2:],
            pltpu.VMEM((channels * EDGE, lat_len), F32),
            pltpu.SemaphoreType.DMA((IN_COPIES + 3,)),
        ],
        compiler_params=PARAMS,
        cost_estimate=pl.CostEstimate(flops=2 * 10**9, bytes_accessed=4 * 10**6, transcendentals=0),
    )(sources[0], in_hbm(bank_slot.reshape(-1, LANES)), *sources[2:4])
    got_b = lax.ppermute(pay_b, "lon", lon_second)
    got_a = lax.ppermute(pay_a, "lon", lon_first)
    reduced, own_rows, position, weights = pl.pallas_call(
        functools.partial(prepare_kernel, lon_count, lat_len),
        out_shape=(jax.ShapeDtypeStruct((rank, cells), BF16), *held_shapes),
        in_specs=[HBM] * 8,
        out_specs=(VMEM,) * 4,
        scratch_shapes=[
            *lists,
            pltpu.VMEM((channels * lat_len, lon_len), F32),
            *targets,
            pltpu.SemaphoreType.DMA((IN_COPIES + 5,)),
        ],
        compiler_params=PARAMS,
        cost_estimate=pl.CostEstimate(flops=10**5, bytes_accessed=10**5, transcendentals=0),
    )(*sources, pay_a)
    row_shape = jax.ShapeDtypeStruct((rank, REACH * lon_len + LANES), BF16)
    core_a, core_b = pl.pallas_call(
        functools.partial(pick_kernel, lat_len),
        out_shape=(core_shape, core_shape),
        in_specs=[VMEM, VMEM, HBM, VMEM],
        out_specs=(VMEM,) * 2,
        compiler_params=PARAMS,
    )(got_b, got_a, own_rows, kernel_bank)
    edges, row_a, row_b = pl.pallas_call(
        functools.partial(rows_kernel, lat_len),
        out_shape=(edge_shape, row_shape, row_shape),
        in_specs=[VMEM, VMEM, HBM, VMEM],
        out_specs=(VMEM,) * 3,
        compiler_params=PARAMS,
    )(got_b, got_a, core_b, reduced)
    core_b = lax.ppermute(core_b, "lon", lon_second)
    core_a = lax.ppermute(core_a, "lon", lon_first)
    row_a = lax.ppermute(row_a, "lat", lat_first)
    row_b = lax.ppermute(row_b, "lat", lat_second)
    border_cells = 2 * REACH * lon_len
    stack_rows = taps * rank // 2
    halo_stack_shape = jax.ShapeDtypeStruct((2, stack_rows, border_cells), BF16)
    inner, halo_stack, mixer, offset, own = pl.pallas_call(
        functools.partial(inner_kernel, lat_len),
        out_shape=(
            jax.ShapeDtypeStruct((tap_rank * rank, cells - border_cells), BF16),
            halo_stack_shape,
            jax.ShapeDtypeStruct((out_channels * GROUP, rank * GROUP), BF16),
            jax.ShapeDtypeStruct((out_channels * GROUP, lon_len), F32),
            core_shape,
        ),
        in_specs=[VMEM] * 7,
        out_specs=(VMEM,) * 5,
        scratch_shapes=[pltpu.VMEM((2, stack_rows, cells - border_cells), BF16)],
        compiler_params=PARAMS,
    )(reduced, edges, weights, out_factor.T, out_bias.reshape(1, -1), own_rows, kernel_bank)
    border = pl.pallas_call(
        functools.partial(border_kernel, lat_len, lat_count),
        out_shape=jax.ShapeDtypeStruct((tap_rank * rank, border_cells), BF16),
        in_specs=[VMEM] * 4,
        out_specs=VMEM,
        scratch_shapes=[pltpu.VMEM(halo_stack_shape.shape, BF16)],
        compiler_params=PARAMS,
    )(row_b, row_a, weights, halo_stack)
    out_shape = (out_channels, lat_len, lon_len)
    return pl.pallas_call(
        mix_kernel,
        out_shape=jax.ShapeDtypeStruct(out_shape, BF16),
        in_specs=[VMEM] * 8,
        out_specs=HBM,
        scratch_shapes=[pltpu.VMEM(out_shape, BF16), pltpu.SemaphoreType.DMA((OUT_COPIES,))],
        compiler_params=PARAMS,
    )(inner, border, core_a, core_b, own, position, mixer, offset)


def solution(mesh):
    placed = (
        P(None, "lat", "lon"),
        P("lat", "lon"),
        P("lat", "lon", None),
        P(),
        P("lon", None, None),
        P(),
        P(),
        P(),
        P(),
    )
    return jax.shard_map(
        on_device, mesh=mesh, in_specs=placed, out_specs=P(None, "lat", "lon"), check_vma=False
    )
```

```python
import functools

import jax
import jax.numpy as jnp
from jax import lax
from jax.experimental import pallas as pl
from jax.experimental.pallas import tpu as pltpu
from jax.sharding import PartitionSpec as P

KS = 5
REACH = KS // 2
PER_OWNER = 2
LANES = 128
EDGE = 2 * REACH
GROUP = 8
STEP = 4
OUT_COPIES = 2
IN_COPIES = 1
F32 = jnp.float32
BF16 = jnp.bfloat16
VMEM = pl.BlockSpec(memory_space=pltpu.VMEM)
SMEM = pl.BlockSpec(memory_space=pltpu.SMEM)
HBM = pl.BlockSpec(memory_space=pltpu.HBM)
PARAMS = pltpu.CompilerParams(vmem_limit_bytes=24 * 1024 * 1024)


def swap_pairs(count):
    first = [(i, i ^ 1) for i in range(count)]
    second = [(i, (i + 1 if i % 2 else i - 1) % count) for i in range(count)]
    return first, second


def in_hbm(array):
    return pltpu.with_memory_space_constraint(array, pltpu.HBM)


def lane_index(shape):
    return lax.broadcasted_iota(jnp.int32, shape, 1)


def start_copies(pairs, sems):
    copies = [pltpu.make_async_copy(source, target, sems.at[i]) for i, (source, target) in enumerate(pairs)]
    for copy in copies:
        copy.start()
    return copies


def in_parts(source, target, count):
    share = target.shape[0] // count
    return tuple((source.at[pl.ds(i * share, share)], target.at[pl.ds(i * share, share)]) for i in range(count))


def find_rows(list_ref, slot_ref, lon_count, held):
    me = lax.axis_index("lon")
    owners = (me, lax.rem(me + lon_count - 1, lon_count), lax.rem(me + 1, lon_count))
    slots = [slot_ref[list_ref[0, 0, i]] for i in range(list_ref.shape[2])]
    places, rows = [], []
    for owner in owners:
        least, greatest = jnp.int32(held), jnp.int32(-1)
        first, last = jnp.int32(0), jnp.int32(0)
        for i, slot in enumerate(slots):
            local = slot - owner * held
            hit = (local >= 0) & (local < held)
            first = jnp.where(hit & (local < least), i, first)
            last = jnp.where(hit & (local > greatest), i, last)
            least = jnp.where(hit, jnp.minimum(local, least), least)
            greatest = jnp.where(hit, jnp.maximum(local, greatest), greatest)
        places.append([first, last])
        rows.append([jnp.minimum(least, held - 1), jnp.maximum(greatest, 0)])
    return places, rows


class Held:
    names = ("own_rows", "position", "weights")
    sources = ("labels", "tap")

    def __init__(self, refs):
        self.__dict__.update(zip(self.names, refs))


def build_held(places, targets, held):
    labels_ref, tap_ref = targets
    even = (lax.axis_index("lon") % 2) == 0
    order = list(places[0])
    order += [jnp.where(even, places[2][nth], places[1][nth]) for nth in range(PER_OWNER)]
    order += [jnp.where(even, places[1][nth], places[2][nth]) for nth in range(PER_OWNER)]
    labels = labels_ref[...]
    position = jnp.zeros(labels.shape, jnp.int32)
    for index, place in enumerate(order):
        position = jnp.where(labels == place, index, position)
    held.position[...] = position

    tap_rank, taps = tap_ref.shape
    half = held.weights.shape[0] // tap_rank
    shape = (tap_rank * half, taps * half)
    spread = (
        lax.broadcasted_iota(jnp.int32, (shape[0], tap_rank), 0) // half == lane_index((shape[0], tap_rank))
    ).astype(BF16)
    repeat = (
        lax.broadcasted_iota(jnp.int32, (taps, shape[1]), 0) == lane_index((taps, shape[1])) // half
    ).astype(BF16)
    tall = jnp.dot(spread, tap_ref[...], preferred_element_type=F32).astype(BF16)
    wide = jnp.dot(tall, repeat, preferred_element_type=F32)
    same = lax.broadcasted_iota(jnp.int32, shape, 0) % half == lane_index(shape) % half
    held.weights[...] = jnp.where(same, wide, 0.0).astype(BF16)


def build_mixer(out_factor_ref, bias_ref, mixer_ref, offset_ref):
    rank, out_channels = out_factor_ref.shape
    shape = (out_channels * GROUP, rank * GROUP)
    spread = (
        lax.broadcasted_iota(jnp.int32, (shape[0], out_channels), 0) // GROUP
        == lane_index((shape[0], out_channels))
    ).astype(BF16)
    repeat = (
        lax.broadcasted_iota(jnp.int32, (rank, shape[1]), 0) == lane_index((rank, shape[1])) % rank
    ).astype(BF16)
    tall = lax.dot_general(
        spread, out_factor_ref[...], (((1,), (1,)), ((), ())), preferred_element_type=F32
    ).astype(BF16)
    wide = jnp.dot(tall, repeat, preferred_element_type=F32)
    same = lax.broadcasted_iota(jnp.int32, shape, 0) % GROUP == lane_index(shape) // rank
    mixer_ref[...] = jnp.where(same, wide, 0.0).astype(BF16)

    square = (out_channels, out_channels)
    diagonal = lax.broadcasted_iota(jnp.int32, square, 0) == lane_index(square)
    column = jnp.sum(jnp.where(diagonal, bias_ref[...], 0.0), axis=1, keepdims=True)
    rest = jnp.broadcast_to(column, (out_channels, offset_ref.shape[1]))
    total = jnp.zeros(offset_ref.shape, F32)
    for _ in range(3):
        piece = rest.astype(BF16)
        rest = rest - piece.astype(F32)
        total = total + jnp.dot(spread, piece, preferred_element_type=F32)
    offset_ref[...] = total


def asked_rows(list_ref, slots_ref, owner, held):
    lane = lane_index((1, LANES))
    found = []
    for i in range(list_ref.shape[2]):
        region = list_ref[0, 0, i]
        row = slots_ref[pl.ds(region // LANES, 1), :]
        found.append(jnp.where(lane == region % LANES, row - owner * held, -1))
    local = jnp.max(jnp.concatenate(found, axis=0), axis=1, keepdims=True)
    hit = (local >= 0) & (local < held)
    least = jnp.min(jnp.where(hit, local, held - 1), axis=0, keepdims=True)
    greatest = jnp.max(jnp.where(hit, local, 0), axis=0, keepdims=True)
    return least, greatest


def edge_kernel(lon_count, held_rows, *refs):
    list_hbm, slots_hbm, feat_hbm, in_hbm, pay_a_ref, pay_b_ref = refs[:6]
    list_ref, slots_ref, feat_ref, in_ref, turned_ref, sems = refs[6:]
    channels, lat_len, lon_len = feat_ref.shape
    rank = in_ref.shape[0]
    batch = LANES // EDGE
    pairs = in_parts(feat_hbm, feat_ref, IN_COPIES)
    pairs += ((slots_hbm, slots_ref), (list_hbm, list_ref), (in_hbm, in_ref))
    copies = start_copies(pairs, sems)
    for copy in copies:
        copy.wait()
    lane = lane_index((lat_len, LANES))
    for part in range(channels // batch):
        packed = jnp.zeros((lat_len, LANES), F32)
        for c in range(batch):
            moved = pltpu.roll(feat_ref[part * batch + c].astype(F32), (EDGE * c + REACH) % LANES, 1)
            packed = jnp.where(lane // EDGE == c, moved, packed)
        turned_ref[part * LANES : (part + 1) * LANES, :] = jnp.transpose(packed)
    columns = jnp.concatenate(
        [turned_ref[pl.ds(j, channels, stride=EDGE), :].astype(BF16) for j in range(EDGE)], axis=1
    )
    edges = jnp.dot(in_ref[...], columns, preferred_element_type=F32)
    edges = jnp.concatenate([edges, jnp.zeros((rank, LANES - EDGE * lat_len), F32)], axis=1)
    me = lax.axis_index("lon")
    even = (me % 2) == 0
    prev, following = lax.rem(me + lon_count - 1, lon_count), lax.rem(me + 1, lon_count)
    lane = lane_index((rank, LANES))
    for out_ref, owner in (
        (pay_a_ref, jnp.where(even, following, prev)),
        (pay_b_ref, jnp.where(even, prev, following)),
    ):
        load = edges
        for nth, row in enumerate(asked_rows(list_ref, slots_ref, owner, held_rows)):
            load = jnp.where(lane == EDGE * lat_len + nth, row.astype(F32), load)
        out_ref[...] = load.astype(BF16)


def reduce_tile(lat_len, feat_ref, in_ref, rows_ref, red_ref):
    channels, lon_len = feat_ref.shape[0], feat_ref.shape[2]
    rows_ref[...] = feat_ref[...].astype(F32).reshape(channels * lat_len, lon_len)
    cells = jnp.concatenate(
        [rows_ref[pl.ds(p, channels, stride=lat_len), :].astype(BF16) for p in range(lat_len)], axis=1
    )
    red_ref[...] = jnp.dot(in_ref[...], cells, preferred_element_type=F32).astype(BF16)


def prepare_kernel(lon_count, lat_len, *refs):
    list_hbm, slot_hbm, feat_hbm, in_hbm, bank_hbm = refs[:5]
    sources, red_ref, held = refs[5:7], refs[8], Held(refs[9:12])
    list_ref, slot_ref, feat_ref, in_ref, rows_ref = refs[12:17]
    targets, sems = refs[17:19], refs[19]
    pairs = ((list_hbm, list_ref), (slot_hbm, slot_ref)) + in_parts(feat_hbm, feat_ref, IN_COPIES)
    pairs += ((in_hbm, in_ref), *zip(sources, targets))
    for copy in start_copies(pairs, sems):
        copy.wait()
    places, rows = find_rows(list_ref, slot_ref, lon_count, bank_hbm.shape[0])
    lane = lane_index((1, LANES))
    own_rows = jnp.zeros((1, LANES), jnp.int32)
    for nth, row in enumerate(rows[0]):
        own_rows = jnp.where(lane == nth, row, own_rows)
    held.own_rows[...] = own_rows
    reduce_tile(lat_len, feat_ref, in_ref, rows_ref, red_ref)
    build_held(places, targets, held)


def pick_kernel(lat_len, got_b_ref, got_a_ref, own_rows_hbm, bank_ref, core_a_ref, core_b_ref):
    lane = lane_index((1, LANES))
    for got_ref, core_ref in ((got_b_ref, core_b_ref), (got_a_ref, core_a_ref)):
        head = got_ref[...].astype(F32)[0:1, :]
        for nth in range(PER_OWNER):
            row = jnp.sum(jnp.where(lane == EDGE * lat_len + nth, head, 0.0)).astype(jnp.int32)
            core_ref[nth] = bank_ref[row]


def rows_kernel(lat_len, got_b_ref, got_a_ref, core_ref, red_ref, edge_ref, row_a_ref, row_b_ref):
    lon_len = red_ref.shape[1] // lat_len
    even = (lax.axis_index("lon") % 2) == 0
    from_prev = lane_index(got_a_ref.shape) < REACH * lat_len
    got = jnp.where(from_prev == even, got_b_ref[...].astype(F32), got_a_ref[...].astype(F32)).astype(BF16)
    source = lax.broadcasted_iota(jnp.int32, (LANES, LANES), 0)
    target = lane_index((LANES, LANES))
    order = (source == (target % EDGE) * lat_len + target // EDGE) & (target < EDGE * lat_len)
    edges = jnp.dot(got, order.astype(BF16), preferred_element_type=F32).astype(BF16)
    edge_ref[...] = edges
    even = (lax.axis_index("lat") % 2) == 0
    head = red_ref[:, : REACH * lon_len].astype(F32)
    tail = red_ref[:, (lat_len - REACH) * lon_len :].astype(F32)
    row_a_ref[:, : REACH * lon_len] = jnp.where(even, tail, head).astype(BF16)
    row_b_ref[:, : REACH * lon_len] = jnp.where(even, head, tail).astype(BF16)
    row_a_ref[:, REACH * lon_len :] = edges
    row_b_ref[:, REACH * lon_len :] = edges


def shifted_columns(row, edges, place):
    lane = lane_index(row.shape)
    lon_len = row.shape[1]
    edges = pltpu.roll(edges, (LANES - REACH - EDGE * place) % LANES, 1)
    moved = []
    for col_off in range(KS):
        shift = REACH - col_off
        if shift > 0:
            piece = pltpu.roll(jnp.where(lane >= lon_len - shift, edges, row), shift, 1)
        elif shift < 0:
            piece = pltpu.roll(jnp.where(lane < -shift, edges, row), lon_len + shift, 1)
        else:
            piece = row
        moved.append(piece.astype(BF16))
    return moved


def stack_row(stack_ref, p, moved, slots, lon_len):
    half = moved[0].shape[0] // 2
    for col_off, piece in enumerate(moved):
        for row_off in range(KS):
            slot = slots.get(p + REACH - row_off)
            if slot is not None:
                k = row_off * KS + col_off
                for h in range(2):
                    stack_ref[h, k * half : (k + 1) * half, slot * lon_len : (slot + 1) * lon_len] = piece[
                        h * half : (h + 1) * half
                    ]


def apply_taps(rank, weights_ref, stacked, tapped_ref, lon_len):
    half = rank // 2
    tap_rank = tapped_ref.shape[0] // rank
    width = STEP * lon_len
    for start in range(0, tapped_ref.shape[1], width):
        parts = [
            jnp.dot(weights_ref[...], stacked(h, start, width), preferred_element_type=F32)
            .astype(BF16)
            .reshape(tap_rank, 1, half, width)
            for h in range(2)
        ]
        tapped_ref[:, start : start + width] = jnp.concatenate(parts, axis=1).reshape(tap_rank * rank, width)


def border_slots(lat_len):
    slots = {p: p for p in range(REACH)}
    slots.update({lat_len - REACH + p: REACH + p for p in range(REACH)})
    return slots


def inner_kernel(
    lat_len,
    red_ref,
    edge_ref,
    weights_ref,
    out_factor_ref,
    bias_ref,
    own_rows_ref,
    bank_ref,
    tapped_ref,
    halo_stack_ref,
    mixer_ref,
    offset_ref,
    own_ref,
    stack_ref,
):
    rank = red_ref.shape[0]
    head = own_rows_ref[...].astype(F32)
    for nth in range(PER_OWNER):
        row = jnp.sum(jnp.where(lane_index((1, LANES)) == nth, head, 0.0)).astype(jnp.int32)
        own_ref[nth] = bank_ref[row]
    build_mixer(out_factor_ref, bias_ref, mixer_ref, offset_ref)
    lon_len = red_ref.shape[1] // lat_len
    slots = {p: p - REACH for p in range(REACH, lat_len - REACH)}
    edges = edge_ref[...].astype(F32)
    for p in range(lat_len):
        row = red_ref[:, p * lon_len : (p + 1) * lon_len].astype(F32)
        moved = shifted_columns(row, edges, p)
        stack_row(stack_ref, p, moved, slots, lon_len)
        stack_row(halo_stack_ref, p, moved, border_slots(lat_len), lon_len)
    apply_taps(rank, weights_ref, lambda h, start, width: stack_ref[h, :, start : start + width], tapped_ref, lon_len)


def border_kernel(lat_len, lat_count, row_b_ref, row_a_ref, weights_ref, own_stack_ref, tapped_ref, stack_ref):
    rank = row_a_ref.shape[0]
    lon_len = (row_a_ref.shape[1] - LANES) // REACH
    lat = lax.axis_index("lat")
    even = (lat % 2) == 0
    row_a = row_a_ref[...].astype(F32)
    row_b = row_b_ref[...].astype(F32)
    above = jnp.where(lat == 0, 0.0, jnp.where(even, row_b, row_a))
    below = jnp.where(lat == lat_count - 1, 0.0, jnp.where(even, row_a, row_b))
    slots = border_slots(lat_len)
    for i in range(REACH):
        for p, holder, place in ((i - REACH, above, lat_len - REACH + i), (lat_len + i, below, i)):
            row = holder[:, i * lon_len : (i + 1) * lon_len]
            moved = shifted_columns(row, holder[:, REACH * lon_len :], place)
            stack_row(stack_ref, p, moved, slots, lon_len)
    block = KS * rank // 2
    in_halo = {
        (slot, row_off)
        for p, slot in slots.items()
        for row_off in range(KS)
        if not 0 <= p + row_off - REACH < lat_len
    }

    def stacked(h, start, width):
        columns = []
        for slot in range(start // lon_len, (start + width) // lon_len):
            span = slice(slot * lon_len, (slot + 1) * lon_len)
            pieces = []
            for row_off in range(KS):
                ref = stack_ref if (slot, row_off) in in_halo else own_stack_ref
                pieces.append(ref[h, row_off * block : (row_off + 1) * block, span])
            columns.append(jnp.concatenate(pieces, axis=0))
        return jnp.concatenate(columns, axis=1)

    apply_taps(rank, weights_ref, stacked, tapped_ref, lon_len)


def mix_kernel(
    inner_ref,
    border_ref,
    core_a_ref,
    core_b_ref,
    own_ref,
    position_ref,
    mixer_ref,
    offset_ref,
    out_hbm,
    stage_ref,
    sems,
):
    lat_len, lon_len = position_ref.shape
    rank = own_ref.shape[1]
    cores = jnp.concatenate(
        [ref[...].reshape(PER_OWNER * rank, -1) for ref in (own_ref, core_a_ref, core_b_ref)], axis=0
    )
    chunks = [(border_ref, 0, [*range(REACH), *range(lat_len - REACH, lat_len)])]
    for start in range(REACH, lat_len - REACH, STEP):
        chunks.append((inner_ref, start - REACH, [*range(start, start + STEP)]))
    by_row = {}
    for ref, first, rows in chunks:
        width = len(rows) * lon_len
        every = jnp.dot(cores, ref[:, first * lon_len : first * lon_len + width], preferred_element_type=F32)
        position = jnp.concatenate([position_ref[r : r + 1, :] for r in rows], axis=1)
        hidden = jnp.zeros((rank, width), F32)
        for index in range(3 * PER_OWNER):
            hidden = jnp.where(position == index, every[index * rank : (index + 1) * rank], hidden)
        hidden = hidden.astype(BF16)
        for i, r in enumerate(rows):
            by_row[r] = hidden[:, i * lon_len : (i + 1) * lon_len]
    pieces = [by_row[r] for r in range(lat_len)]
    groups = [jnp.concatenate(pieces[g : g + GROUP], axis=0) for g in range(0, lat_len, GROUP)]
    channels = stage_ref.shape[0]
    share = channels // OUT_COPIES
    outputs = [jnp.dot(mixer_ref[...], hidden, preferred_element_type=F32) for hidden in groups]
    copies = []
    for part in range(OUT_COPIES):
        span = slice(part * share * GROUP, (part + 1) * share * GROUP)
        blocks = []
        for output in outputs:
            output = output[span] + offset_ref[span, :]
            mixed = 0.5 * output * (1.0 + jnp.tanh(0.5 * output))
            blocks.append(mixed.reshape(share, GROUP, lon_len))
        held = slice(part * share, (part + 1) * share)
        stage_ref[held] = jnp.concatenate(blocks, axis=1).astype(BF16)
        copy = pltpu.make_async_copy(stage_ref.at[held], out_hbm.at[held], sems.at[part])
        copy.start()
        copies.append(copy)
    for copy in copies:
        copy.wait()


def on_device(
    features, labels, tile_regions, bank_slot, kernel_bank, in_factor, tap_factor, out_factor, out_bias
):
    channels, lat_len, lon_len = features.shape
    rank = in_factor.shape[0]
    held, core_rows, core_cols = kernel_bank.shape
    tap_rank, taps = tap_factor.shape
    out_channels = out_factor.shape[0]
    cells = lat_len * lon_len
    lon_count, lat_count = lax.axis_size("lon"), lax.axis_size("lat")
    lon_first, lon_second = swap_pairs(lon_count)
    lat_first, lat_second = swap_pairs(lat_count)
    edge_shape = jax.ShapeDtypeStruct((rank, LANES), BF16)
    core_shape = jax.ShapeDtypeStruct((PER_OWNER, core_rows, core_cols), BF16)
    held_shapes = (
        jax.ShapeDtypeStruct((1, LANES), jnp.int32),
        jax.ShapeDtypeStruct(labels.shape, jnp.int32),
        jax.ShapeDtypeStruct((tap_rank * rank // 2, taps * rank // 2), BF16),
    )
    lists = [
        pltpu.SMEM(tile_regions.shape, jnp.int32),
        pltpu.SMEM(bank_slot.shape, jnp.int32),
        pltpu.VMEM(features.shape, BF16),
        pltpu.VMEM(in_factor.shape, BF16),
    ]
    targets = [
        pltpu.VMEM(labels.shape, jnp.int32),
        pltpu.VMEM(tap_factor.shape, BF16),
    ]
    sources = tuple(
        in_hbm(x)
        for x in (
            tile_regions,
            bank_slot,
            features,
            in_factor,
            kernel_bank,
            labels,
            tap_factor,
        )
    )
    pay_a, pay_b = pl.pallas_call(
        functools.partial(edge_kernel, lon_count, held),
        out_shape=(edge_shape, edge_shape),
        in_specs=[HBM] * 4,
        out_specs=(VMEM,) * 2,
        scratch_shapes=[
            lists[0],
            pltpu.VMEM((bank_slot.shape[0] // LANES, LANES), jnp.int32),
            *lists[2:],
            pltpu.VMEM((channels * EDGE, lat_len), F32),
            pltpu.SemaphoreType.DMA((IN_COPIES + 3,)),
        ],
        compiler_params=PARAMS,
        cost_estimate=pl.CostEstimate(flops=2 * 10**9, bytes_accessed=4 * 10**6, transcendentals=0),
    )(sources[0], in_hbm(bank_slot.reshape(-1, LANES)), *sources[2:4])
    got_b = lax.ppermute(pay_b, "lon", lon_second)
    got_a = lax.ppermute(pay_a, "lon", lon_first)
    reduced, own_rows, position, weights = pl.pallas_call(
        functools.partial(prepare_kernel, lon_count, lat_len),
        out_shape=(jax.ShapeDtypeStruct((rank, cells), BF16), *held_shapes),
        in_specs=[HBM] * 8,
        out_specs=(VMEM,) * 4,
        scratch_shapes=[
            *lists,
            pltpu.VMEM((channels * lat_len, lon_len), F32),
            *targets,
            pltpu.SemaphoreType.DMA((IN_COPIES + 5,)),
        ],
        compiler_params=PARAMS,
        cost_estimate=pl.CostEstimate(flops=10**5, bytes_accessed=10**5, transcendentals=0),
    )(*sources, pay_a)
    row_shape = jax.ShapeDtypeStruct((rank, REACH * lon_len + LANES), BF16)
    core_a, core_b = pl.pallas_call(
        functools.partial(pick_kernel, lat_len),
        out_shape=(core_shape, core_shape),
        in_specs=[VMEM, VMEM, HBM, VMEM],
        out_specs=(VMEM,) * 2,
        compiler_params=PARAMS,
    )(got_b, got_a, own_rows, kernel_bank)
    edges, row_a, row_b = pl.pallas_call(
        functools.partial(rows_kernel, lat_len),
        out_shape=(edge_shape, row_shape, row_shape),
        in_specs=[VMEM, VMEM, HBM, VMEM],
        out_specs=(VMEM,) * 3,
        compiler_params=PARAMS,
    )(got_b, got_a, core_b, reduced)
    core_b = lax.ppermute(core_b, "lon", lon_second)
    core_a = lax.ppermute(core_a, "lon", lon_first)
    row_a = lax.ppermute(row_a, "lat", lat_first)
    row_b = lax.ppermute(row_b, "lat", lat_second)
    border_cells = 2 * REACH * lon_len
    stack_rows = taps * rank // 2
    halo_stack_shape = jax.ShapeDtypeStruct((2, stack_rows, border_cells), BF16)
    inner, halo_stack, mixer, offset, own = pl.pallas_call(
        functools.partial(inner_kernel, lat_len),
        out_shape=(
            jax.ShapeDtypeStruct((tap_rank * rank, cells - border_cells), BF16),
            halo_stack_shape,
            jax.ShapeDtypeStruct((out_channels * GROUP, rank * GROUP), BF16),
            jax.ShapeDtypeStruct((out_channels * GROUP, lon_len), F32),
            core_shape,
        ),
        in_specs=[VMEM] * 7,
        out_specs=(VMEM,) * 5,
        scratch_shapes=[pltpu.VMEM((2, stack_rows, cells - border_cells), BF16)],
        compiler_params=PARAMS,
    )(reduced, edges, weights, out_factor.T, out_bias.reshape(1, -1), own_rows, kernel_bank)
    border = pl.pallas_call(
        functools.partial(border_kernel, lat_len, lat_count),
        out_shape=jax.ShapeDtypeStruct((tap_rank * rank, border_cells), BF16),
        in_specs=[VMEM] * 4,
        out_specs=VMEM,
        scratch_shapes=[pltpu.VMEM(halo_stack_shape.shape, BF16)],
        compiler_params=PARAMS,
    )(row_b, row_a, weights, halo_stack)
    out_shape = (out_channels, lat_len, lon_len)
    return pl.pallas_call(
        mix_kernel,
        out_shape=jax.ShapeDtypeStruct(out_shape, BF16),
        in_specs=[VMEM] * 8,
        out_specs=HBM,
        scratch_shapes=[pltpu.VMEM(out_shape, BF16), pltpu.SemaphoreType.DMA((OUT_COPIES,))],
        compiler_params=PARAMS,
    )(inner, border, core_a, core_b, own, position, mixer, offset)


def solution(mesh):
    placed = (
        P(None, "lat", "lon"),
        P("lat", "lon"),
        P("lat", "lon", None),
        P(),
        P("lon", None, None),
        P(),
        P(),
        P(),
        P(),
    )
    return jax.shard_map(
        on_device, mesh=mesh, in_specs=placed, out_specs=P(None, "lat", "lon"), check_vma=False
    )
```
